32 devices in a mesh: dp: 8 (over z, y), state: 4 (over x, core).
Axes of the slice: x: 2, y: 2, z: 4, core: 2. Of those that a mesh axis runs over, the one named last changes fastest.
Arguments:
- tokens: bfloat16 [8192, 1024], P(('dp', 'state')), may hold values from -6 to 6
- state_in: bfloat16 [8, 512, 1024], P('dp', 'state'), may hold values from -6 to 6
- cotangent: bfloat16 [8192, 1024], P(('dp', 'state')), may hold values from -6 to 6
- state_cotangent: bfloat16 [8, 512, 1024], P('dp', 'state'), may hold values from -6 to 6
- seq_len: int32 [8], P('dp'), may hold values from 769 to 1024, as said below
- bucket_table: int32 [512], replicated, may hold values from 0 to 31, as said below
- w_qkv: bfloat16 [1024, 3072], P('dp', 'state'), may hold values from -0.1875 to 0.1875
- w_out: bfloat16 [1024, 1024], P('dp', 'state'), may hold values from -3 to 3
- w_sqkv: bfloat16 [1024, 3072], P('dp', 'state'), may hold values from -0.1875 to 0.1875
- w_sout: bfloat16 [1024, 1024], P('dp', 'state'), may hold values from -6 to 6
- w_up: bfloat16 [1024, 4096], P('dp', 'state'), may hold values from -0.1875 to 0.1875
- w_down: bfloat16 [4096, 1024], P('state', 'dp'), may hold values from -0.09375 to 0.09375
- rel_table: float32 [32, 8], replicated, may hold values from -4 to 4
- norm_gain: float32 [3, 1024], replicated, may hold values from 0.5 to 1.5
- norm_shift: float32 [3, 1024], replicated, may hold values from -2 to 2
- gate_bias: float32 [1024], replicated, may hold values from 0.5 to 2.5
Outputs:
- output: bfloat16 [8192, 1024], P(('dp', 'state'))
- next_state: bfloat16 [8, 512, 1024], P('dp', 'state')
- grad_tokens: bfloat16 [8192, 1024], P(('dp', 'state'))
- grad_state: bfloat16 [8, 512, 1024], P('dp', 'state')
- grad_qkv: float32 [1024, 3072], P('dp', 'state')
- grad_out: float32 [1024, 1024], P('dp', 'state')
- grad_sqkv: float32 [1024, 3072], P('dp', 'state')
- grad_sout: float32 [1024, 1024], P('dp', 'state')
- grad_up: float32 [1024, 4096], P('dp', 'state')
- grad_down: float32 [4096, 1024], P('state', 'dp')
- grad_rel: float32 [32, 8], replicated
- grad_gain: float32 [3, 1024], replicated
- grad_shift: float32 [3, 1024], replicated
- grad_gate: float32 [1024], replicated
The draws below stay inside these ranges and needn't reach their ends.
Inputs may be any that keep to these rules, and one draw needn't show every extreme that they name: Each sequence's live tokens are the first seq_len of its 1024 slots; some sequence has all 1024 live and some has the fewest. `bucket_table`: never falls as the distance grows, is 0 at distance 0, and every bucket occurs.
All inputs are finite; a program needn't handle non-finite values.
Results may differ from the reference program's by a relative error of at most 0.014.
Values may be sent and summed in bfloat16 or wider, within the bound.
A program may use at most 256 MiB of HBM per device.

```python
import jax
import jax.numpy as jnp
from jax import lax

D = 1024
HEADS = 8
HEAD_DIM = 128
FF = 4096
STATES = 512
WIN = 512
BUCKETS = 32
GRP_TOK = 1024
GROUPS = 8
TOKENS = 8192


def draw_seq_len(key, part):
    key = jax.random.fold_in(key, 11)
    first_key, second_key = jax.random.split(key, 2)
    shortest = 3 * GRP_TOK // 4 + 1
    lengths = jax.random.randint(first_key, (GROUPS,), shortest, GRP_TOK + 1)
    shuffled = jax.random.permutation(second_key, GROUPS)
    lengths = lengths.at[shuffled[0]].set(GRP_TOK).at[shuffled[1]].set(shortest)
    return lengths.astype(jnp.int32)


def draw_bucket_table(key, part):
    key = jax.random.fold_in(key, 7)
    shuffled = jax.random.permutation(key, WIN - 1) + 1
    cut_points = shuffled[:BUCKETS - 1]
    distance = jnp.arange(WIN)
    return jnp.sum((cut_points[None, :] <= distance[:, None]).astype(jnp.int32), axis=1).astype(jnp.int32)


def raised(drawn, stream_key, source, target, shards_of, factor):
    owner, partner = [(jnp.arange(drawn.shape[axis_at]) // (drawn.shape[axis_at] // shards_of)).reshape([-1 if axis == axis_at else 1 for axis in range(drawn.ndim)]) for axis_at in (source, target)]
    chosen = jax.random.permutation(stream_key, shards_of)[partner]
    strong = (owner == chosen) | (owner == (partner + shards_of // 2) % shards_of)
    return jnp.where(strong, factor * drawn, drawn)


def block_levels(own_key, shape, pieces, smallest, largest):
    def one(axis_at, shards_of):
        steps = jax.random.uniform(jax.random.fold_in(jax.random.fold_in(own_key, 6), axis_at), (shards_of,), jnp.float32, smallest / len(pieces), largest / len(pieces))
        return jnp.repeat(jnp.exp(steps), shape[axis_at] // shards_of).reshape((-1,) + (1,) * (len(shape) - axis_at - 1))

    level = one(*pieces[0])
    for cut in pieces[1:]:
        level = level * one(*cut)
    return level


def bell_draw(own_key, shape, deviation, most, cuts=(), kind=jnp.bfloat16):
    entries = deviation * jax.random.normal(own_key, shape, jnp.float32)
    if cuts:
        entries = entries * block_levels(own_key, shape, cuts, -0.22, 0.18)
    return jnp.clip(entries, -most, most).astype(kind)


def heavy_noise(key, dims, scale, most, cuts, heavy, held_as=jnp.bfloat16):
    result = scale * jax.random.normal(key, dims, jnp.float32)
    if cuts:
        result = result * block_levels(key, dims, cuts, -0.22, 0.18)
    return jnp.clip(raised(result, jax.random.fold_in(key, 3), *heavy), -most, most).astype(held_as)


def setup_inputs(seed: int = 0) -> dict:
    key_of = jax.random.split(jax.random.key(seed), 17)
    return {
        "tokens": bell_draw(key_of[0], (TOKENS, D), 1.0, 6.0, ((0, 32),)),
        "state_in": bell_draw(key_of[1], (GROUPS, STATES, D), 1.0, 6.0, ((0, 8), (1, 4))),
        "cotangent": heavy_noise(key_of[2], (TOKENS, D), 1.0, 6.0, ((0, 32),), (0, 1, 32, 2.75)),
        "state_cotangent": bell_draw(key_of[3], (GROUPS, STATES, D), 1.0, 6.0, ((0, 8), (1, 4))),
        "seq_len": draw_seq_len(jax.random.fold_in(key_of[16], 71), 0),
        "bucket_table": draw_bucket_table(jax.random.fold_in(key_of[16], 71), 0),
        "w_qkv": bell_draw(key_of[6], (D, 3 * D), D ** -0.5, 0.1875, ((0, 8), (1, 4))),
        "w_out": bell_draw(key_of[7], (D, D), (max(D // 256, 1)) ** -0.5, 3.0, ((0, 8), (1, 4))),
        "w_sqkv": bell_draw(key_of[8], (D, 3 * D), D ** -0.5, 0.1875, ((0, 8), (1, 4))),
        "w_sout": bell_draw(key_of[9], (D, D), 1 ** -0.5, 6.0, ((0, 8), (1, 4))),
        "w_up": bell_draw(key_of[10], (D, FF), D ** -0.5, 0.1875, ((0, 8), (1, 4))),
        "w_down": bell_draw(key_of[11], (FF, D), FF ** -0.5, 0.09375, ((0, 4), (1, 8))),
        "rel_table": bell_draw(key_of[12], (BUCKETS, HEADS), 1.0, 4.0, (), jnp.float32),
        "norm_gain": jnp.clip(1.0 + 0.1 * jax.random.normal(key_of[13], (3, D), jnp.float32), 0.5, 1.5),
        "norm_shift": bell_draw(key_of[14], (3, D), 0.3, 2.0, (), jnp.float32),
        "gate_bias": jnp.clip(jax.random.uniform(key_of[15], (D,), jnp.float32, 0.5, 2.5), 0.5, 2.5),
    }


@jax.custom_vjp
def low(v):
    return lax.optimization_barrier(v.astype(jnp.bfloat16)).astype(jnp.float32)

@jax.custom_vjp
def low_back(v):
    return v

def low_keep(v):
    return (low(v), None)

def low_pass(kept, grad):
    return (grad,)

def back_keep(v):
    return (v, None)

def back_low(kept, grad):
    return (low(grad),)
low.defvjp(low_keep, low_pass)
low_back.defvjp(back_keep, back_low)
epsilon = 1e-05
masked_value = -1e+30
highest = lax.Precision.HIGHEST

def layer_norm(values, gain, shift):
    centre = lax.optimization_barrier(jnp.mean(values, axis=-1, keepdims=True))
    centred = values - centre
    spread = lax.optimization_barrier(jnp.mean(centred * centred, axis=-1, keepdims=True))
    return centred * lax.rsqrt(spread + epsilon) * gain + shift

def product(left, right):
    return jnp.dot(left, right, precision=highest, preferred_element_type=jnp.float32)

def split_heads(values):
    return values.reshape(values.shape[0], HEADS, HEAD_DIM)

def window_block(query, keys, values, rel_bias, block_start, length):
    raw_scores = low_back(jnp.einsum('qhd,khd->hqk', query, keys, precision=highest))
    row_at = jnp.arange(WIN)[:, None]
    col_at = jnp.arange(2 * WIN)[None, :]
    distance = WIN + row_at - col_at
    key_at = block_start - WIN + col_at
    allowed = (distance >= 0) & (distance < WIN) & (key_at >= 0) & ((key_at < length) | (distance == 0))
    bias_block = rel_bias[:, jnp.clip(distance, 0, WIN - 1)]
    scores = jnp.where(allowed[None], raw_scores * HEAD_DIM ** (-0.5) + bias_block, masked_value)
    weights = low(jax.nn.softmax(scores, axis=-1))
    return jnp.einsum('hqk,khd->qhd', weights, values, precision=highest)

def local_attention(query, keys, values, rel_bias, length):
    front = jnp.zeros((WIN, HEADS, HEAD_DIM), jnp.float32)
    keys_padded = jnp.concatenate([front, keys], axis=0)
    values_padded = jnp.concatenate([front, values], axis=0)

    def one_block(block_index):
        block_start = block_index * WIN
        return window_block(lax.dynamic_slice_in_dim(query, block_start, WIN, 0), lax.dynamic_slice_in_dim(keys_padded, block_start, 2 * WIN, 0), lax.dynamic_slice_in_dim(values_padded, block_start, 2 * WIN, 0), rel_bias, block_start, length)
    blocks = lax.map(jax.checkpoint(one_block), jnp.arange(GRP_TOK // WIN, dtype=jnp.int32))
    return blocks.reshape(GRP_TOK, D)

def state_attention(query, state_keys, state_values, keys, values, length):
    score_scale = HEAD_DIM ** (-0.5)
    own_part = low_back(jnp.einsum('qhd,khd->hqk', query, state_keys, precision=highest)) * score_scale
    token_part = low_back(jnp.einsum('qhd,khd->hqk', query, keys, precision=highest)) * score_scale
    live_keys = jnp.arange(GRP_TOK) < length
    token_part = jnp.where(live_keys[None, None, :], token_part, masked_value)
    weights = low(jax.nn.softmax(jnp.concatenate([own_part, token_part], axis=-1), axis=-1))
    state_read = jnp.einsum('hqk,khd->qhd', weights[:, :, :STATES], state_values, precision=highest)
    state_read = state_read + jnp.einsum('hqk,khd->qhd', weights[:, :, STATES:], values, precision=highest)
    return state_read.reshape(STATES, D)

def group_forward(group_tokens, group_state, params, length, bucket_table):
    w_qkv, w_out, w_sqkv, w_sout, w_up, w_down, rel_table, norm_gain, norm_shift, gate_bias = params
    first_norm = low(layer_norm(group_tokens, norm_gain[0], norm_shift[0]))
    tok_qkv = low(low_back(product(first_norm, w_qkv)))
    query = split_heads(tok_qkv[:, :D])
    keys = split_heads(tok_qkv[:, D:2 * D])
    values = split_heads(tok_qkv[:, 2 * D:])
    rel_bias = jnp.take(rel_table, bucket_table, axis=0).T
    mixed_rows = low(low_back(local_attention(query, keys, values, rel_bias, length)))
    residual = group_tokens + low_back(product(mixed_rows, w_out))
    second_norm = low(layer_norm(residual, norm_gain[1], norm_shift[1]))
    hidden = low(jax.nn.gelu(low_back(product(second_norm, w_up))))
    output = residual + product(hidden, w_down)
    state_norm = low(layer_norm(group_state, norm_gain[2], norm_shift[2]))
    state_qkv = low(low_back(product(state_norm, w_sqkv)))
    state_read = state_attention(split_heads(state_qkv[:, :D]), split_heads(state_qkv[:, D:2 * D]), split_heads(state_qkv[:, 2 * D:]), keys, values, length)
    state_read = low(low_back(state_read))
    update = low_back(product(state_read, w_sout))
    gate_open = jax.nn.sigmoid(gate_bias)
    return (output, gate_open * group_state + (1.0 - gate_open) * update)

def reference(tokens, state_in, cotangent, state_cotangent, seq_len, bucket_table, w_qkv, w_out, w_sqkv, w_sout, w_up, w_down, rel_table, norm_gain, norm_shift, gate_bias):
    params = (w_qkv.astype(jnp.float32), w_out.astype(jnp.float32), w_sqkv.astype(jnp.float32), w_sout.astype(jnp.float32), w_up.astype(jnp.float32), w_down.astype(jnp.float32), rel_table.astype(jnp.float32), norm_gain.astype(jnp.float32), norm_shift.astype(jnp.float32), gate_bias.astype(jnp.float32))
    token_groups = tokens.astype(jnp.float32).reshape(GROUPS, GRP_TOK, D)
    cot_groups = cotangent.astype(jnp.float32).reshape(GROUPS, GRP_TOK, D)

    def one_group(totals, inputs):
        group_tokens, group_state, group_cot, group_state_cot, length = inputs

        def forward(layer_in, state_vectors, weights):
            return group_forward(layer_in, state_vectors, weights, length, bucket_table)
        outputs, pullback = jax.vjp(forward, group_tokens, group_state, params)
        grads = pullback((group_cot, group_state_cot))
        totals = tuple((running + fresh for running, fresh in zip(totals, grads[2])))
        return (totals, (outputs[0].astype(jnp.bfloat16), outputs[1].astype(jnp.bfloat16), grads[0].astype(jnp.bfloat16), grads[1].astype(jnp.bfloat16)))
    zeros = tuple((jnp.zeros_like(weight) for weight in params))
    totals, outs = lax.scan(one_group, zeros, (token_groups, state_in.astype(jnp.float32), cot_groups, state_cotangent.astype(jnp.float32), seq_len))
    output, next_state, grad_tokens, grad_state = outs
    return (output.reshape(TOKENS, D), next_state, grad_tokens.reshape(TOKENS, D), grad_state, totals[0], totals[1], totals[2], totals[3], totals[4], totals[5], totals[6], totals[7], totals[8], totals[9])
```

```python
import functools

import jax
import jax.numpy as jnp
from jax import lax
from jax.experimental import pallas as pl
from jax.experimental.pallas import tpu as pltpu
from jax.sharding import PartitionSpec as P

epsilon = 1e-05
masked_value = -1e30
f32 = jnp.float32
bf16 = jnp.bfloat16

PLACES = (0, 2, 1, 3)
DP_STEPS = (2, 4, 1)
DP_PLACES = (0, 2, 4, 6, 1, 3, 5, 7)


def dot(left, right):
    return lax.dot_general(left, right, (((1,), (0,)), ((), ())), preferred_element_type=f32)


def dot_rt(left, right):
    return lax.dot_general(left, right, (((1,), (1,)), ((), ())), preferred_element_type=f32)


def dot_lt(left, right):
    return lax.dot_general(left, right, (((0,), (0,)), ((), ())), preferred_element_type=f32)


def where_from(sender, place):
    return PLACES.index(PLACES[sender] ^ PLACES[place])


def normalized(values):
    centre = jnp.mean(values, axis=-1, keepdims=True)
    centred = values - centre
    spread = jnp.mean(centred * centred, axis=-1, keepdims=True)
    inverse = lax.rsqrt(spread + epsilon)
    return centred * inverse, inverse


def place_of(scal, q):
    return scal[0] ^ PLACES[q]


def aligned(start, size):
    return pl.ds(pl.multiple_of(start, size), size)


def block_at(scal, q):
    return scal[2 + q]


def position_of(scal, block, blocks):
    return scal[2 + blocks + block]


def rows_in_order(scal, target, source):
    blocks, depth = source.shape[0], source.shape[1]
    for q in range(blocks):
        target[aligned(block_at(scal, q) * depth, depth), :] = source[q]


def columns_in_order(scal, target, source):
    blocks, depth = source.shape[0], source.shape[2]
    for q in range(blocks):
        target[:, aligned(block_at(scal, q) * depth, depth)] = source[q]


def put_rows(scal, target, start, value):
    blocks, depth = target.shape[0], target.shape[1]
    rows = value.shape[0]
    if depth >= rows:
        target[position_of(scal, start // depth, blocks), aligned(start % depth, rows), :] = value
    else:
        for i in range(rows // depth):
            position = position_of(scal, start // depth + i, blocks)
            target[position] = value[i * depth : (i + 1) * depth]


def put_columns(scal, target, start, value):
    blocks, depth = target.shape[0], target.shape[2]
    columns = value.shape[1]
    if depth >= columns:
        target[position_of(scal, start // depth, blocks), :, aligned(start % depth, columns)] = value
    else:
        for i in range(columns // depth):
            position = position_of(scal, start // depth + i, blocks)
            target[position] = value[:, i * depth : (i + 1) * depth]


def call(body, name, outs, scratch, flops, exps, *args):
    sizes = sum(a.size * a.dtype.itemsize for a in args) + sum(
        a.size * a.dtype.itemsize for a in outs
    )
    in_specs = [pl.BlockSpec(memory_space=pltpu.SMEM)] + [
        pl.BlockSpec(memory_space=pltpu.VMEM) for _ in args[1:]
    ]
    return pl.pallas_call(
        body,
        out_shape=outs,
        in_specs=in_specs,
        out_specs=[pl.BlockSpec(memory_space=pltpu.VMEM) for _ in outs],
        scratch_shapes=scratch,
        compiler_params=pltpu.CompilerParams(vmem_limit_bytes=56 << 20),
        cost_estimate=pl.CostEstimate(flops=flops, bytes_accessed=sizes, transcendentals=exps),
        name=name,
    )(*args)


def out(shape, kind=bf16):
    return jax.ShapeDtypeStruct(shape, kind)


def by_distance(scores):
    rows, span = scores.shape
    row_at = lax.broadcasted_iota(jnp.int32, scores.shape, 0)
    step = 1
    while step < rows:
        scores = jnp.where(row_at & step != 0, pltpu.roll(scores, span - step, 1), scores)
        step *= 2
    return scores


def bias_blocks(tb, bias):
    heads, rows, span = tb.shape
    for h in range(heads):
        row = jnp.broadcast_to(bias[h : h + 1, :], (rows, span))
        tb[h] = pltpu.roll(row, 0, 1, stride=1, stride_axis=0)


def window_probs(scal, query, keys, tb_block, last, scale):
    rows, span = tb_block.shape
    count = keys.shape[0]
    scores = dot_rt(query, keys) * scale + tb_block[:, span - count :]
    if last:
        row_at = lax.broadcasted_iota(jnp.int32, scores.shape, 0)
        col_at = lax.broadcasted_iota(jnp.int32, scores.shape, 1)
        ahead = col_at - (count - rows)
        live = (ahead < scal[1] - last) | (ahead == row_at)
        scores = jnp.where(live, scores, masked_value)
    top = jnp.max(scores, axis=-1, keepdims=True)
    grown = jnp.exp(scores - top)
    return grown * (1.0 / jnp.sum(grown, axis=-1, keepdims=True))


def state_probs(scal, query, state_keys, keys, scale):
    own = dot_rt(query, state_keys) * scale
    token = dot_rt(query, keys) * scale
    col_at = lax.broadcasted_iota(jnp.int32, token.shape, 1)
    token = jnp.where(col_at < scal[1], token, masked_value)
    top = jnp.maximum(
        jnp.max(own, axis=-1, keepdims=True), jnp.max(token, axis=-1, keepdims=True)
    )
    own = jnp.exp(own - top)
    token = jnp.exp(token - top)
    total = jnp.sum(own, axis=-1, keepdims=True) + jnp.sum(token, axis=-1, keepdims=True)
    inverse = 1.0 / total
    return own * inverse, token * inverse


def head_cols(block, h, heads, head_dim):
    start = (block * heads + h) * head_dim
    return slice(start, start + head_dim)


def token_forward(head_dim, scal, tokens, gain, shift, w_qkv, bias, first, qkv, mixed, w_nat, tb):
    places, rows, width = tokens.shape
    heads = bias.shape[0]
    span = bias.shape[1]
    scale = head_dim ** (-0.5)
    rows_in_order(scal, w_nat, w_qkv)
    bias_blocks(tb, bias)
    for q in range(places):
        hat, _ = normalized(tokens[q].astype(f32))
        normed = (hat * gain[...] + shift[...]).astype(bf16)
        at = aligned(place_of(scal, q) * rows, rows)
        first[at, :] = normed
        qkv[at, :] = dot(normed, w_nat[...]).astype(bf16)
    for c in range(places):
        count = min(span, (c + 1) * rows)
        low, high = (c + 1) * rows - count, (c + 1) * rows
        last = c * rows if c == places - 1 else 0
        parts = []
        for h in range(heads):
            probs = window_probs(
                scal,
                qkv[c * rows : high, head_cols(0, h, heads, head_dim)],
                qkv[low:high, head_cols(1, h, heads, head_dim)],
                tb[h],
                last,
                scale,
            )
            parts.append(
                dot(probs.astype(bf16), qkv[low:high, head_cols(2, h, heads, head_dim)])
            )
        mixed[c] = jnp.concatenate(parts, axis=1).astype(bf16)


def state_forward(
    head_dim, scal, state, gain, shift, w_sqkv, qkv, normed_out, sqkv, read, w_nat
):
    places, rows, width = state.shape
    heads = qkv.shape[1] // (3 * head_dim)
    scale = head_dim ** (-0.5)
    rows_in_order(scal, w_nat, w_sqkv)
    for q in range(places):
        hat, _ = normalized(state[q].astype(f32))
        normed = (hat * gain[...] + shift[...]).astype(bf16)
        normed_out[q * rows : (q + 1) * rows, :] = normed
        sqkv[q * rows : (q + 1) * rows, :] = dot(normed, w_nat[...]).astype(bf16)
    for q in range(places):
        parts = []
        for h in range(heads):
            own, token = state_probs(
                scal,
                sqkv[q * rows : (q + 1) * rows, head_cols(0, h, heads, head_dim)],
                sqkv[:, head_cols(1, h, heads, head_dim)],
                qkv[:, head_cols(1, h, heads, head_dim)],
                scale,
            )
            parts.append(
                dot(own.astype(bf16), sqkv[:, head_cols(2, h, heads, head_dim)])
                + dot(token.astype(bf16), qkv[:, head_cols(2, h, heads, head_dim)])
            )
        read[q] = jnp.concatenate(parts, axis=1).astype(bf16)


def assembled(scal, target, parts):
    for p, part in enumerate(parts):
        blocks, depth, columns = part.shape
        at = aligned(place_of(scal, p) * columns, columns)
        for q in range(blocks):
            target[aligned(block_at(scal, q) * depth, depth), at] = part[q]


def state_backward(
    head_dim,
    scal,
    state_own,
    state_cot,
    gate_bias,
    state,
    read0,
    read1,
    read2,
    read3,
    out0,
    out1,
    out2,
    out3,
    sqkv,
    qkv,
    normed,
    w_sqkv,
    next_state,
    grad_gate,
    grad_sout,
    token_back,
    grad_sqkv,
    back_norm,
    grad_norm,
    w_nat,
    w_out,
    back_update,
    back_read,
    back_sqkv,
    own_sum,
):
    places, rows, width = state_cot.shape
    reads = (read0, read1, read2, read3)
    heads = qkv.shape[1] // (3 * head_dim)
    lanes = heads * head_dim
    scale = head_dim ** (-0.5)
    rows_in_order(scal, w_nat, w_sqkv)
    assembled(scal, w_out, (out0, out1, out2, out3))
    gate = jax.nn.sigmoid(gate_bias[...])
    update = None
    for p in range(places):
        term = dot(reads[p][p], w_out[aligned(place_of(scal, p) * lanes, lanes), :])
        update = term if update is None else update + term
    held = state_own[...].astype(f32)
    cot = state_cot[0].astype(f32)
    next_state[...] = (gate * held + (1.0 - gate) * update).astype(bf16)
    grad_gate[...] = jnp.sum(cot * (held - update), axis=0, keepdims=True) * (gate * (1.0 - gate))
    for q in range(places):
        back_update[q * rows : (q + 1) * rows, :] = (
            (1.0 - gate) * state_cot[q].astype(f32)
        ).astype(bf16)
    own_columns = back_update[:, aligned(scal[0] * lanes, lanes)]
    for p in range(places):
        stack = jnp.concatenate([reads[p][where_from(p, q)] for q in range(places)], axis=0)
        put_rows(
            scal, grad_sout, place_of(scal, p) * lanes, dot_lt(stack, own_columns).astype(bf16)
        )
    back_read[...] = dot_rt(
        back_update[...], w_out[aligned(scal[0] * lanes, lanes), :]
    ).astype(bf16)
    for h in range(heads):
        key_at, value_at = head_cols(1, h, heads, head_dim), head_cols(2, h, heads, head_dim)
        query_at, read_at = head_cols(0, h, heads, head_dim), slice(h * head_dim, (h + 1) * head_dim)
        for q in range(places):
            at = slice(q * rows, (q + 1) * rows)
            query, back = sqkv[at, query_at], back_read[at, read_at]
            own, token = state_probs(scal, query, sqkv[:, key_at], qkv[:, key_at], scale)
            back_own = dot_rt(back, sqkv[:, value_at])
            back_token = dot_rt(back, qkv[:, value_at])
            row_dot = jnp.sum(own * back_own, axis=-1, keepdims=True) + jnp.sum(
                token * back_token, axis=-1, keepdims=True
            )
            own_raw = (own * (back_own - row_dot) * scale).astype(bf16)
            token_raw = (token * (back_token - row_dot) * scale).astype(bf16)
            back_sqkv[at, query_at] = (
                dot(own_raw, sqkv[:, key_at]) + dot(token_raw, qkv[:, key_at])
            ).astype(bf16)
            terms = (
                (own_sum, key_at, dot_lt(own_raw, query)),
                (own_sum, value_at, dot_lt(own.astype(bf16), back)),
                (token_back, key_at, dot_lt(token_raw, query)),
                (token_back, value_at, dot_lt(token.astype(bf16), back)),
            )
            for target, columns, term in terms:
                columns = slice(columns.start - lanes, columns.stop - lanes)
                if q == 0:
                    target[:, columns] = term
                else:
                    target[:, columns] += term
    back_sqkv[:, lanes:] = own_sum[...].astype(bf16)
    for start in range(0, width, 256):
        put_rows(
            scal,
            grad_sqkv,
            start,
            dot_lt(normed[:, start : start + 256], back_sqkv[...]).astype(bf16),
        )
    gain_sum, shift_sum = None, None
    for q in range(places):
        back = dot_rt(back_sqkv[q * rows : (q + 1) * rows, :], w_nat[...])
        back_norm[q] = back.astype(bf16)
        hat, _ = normalized(state[q].astype(f32))
        gain_term = jnp.sum(back * hat, axis=0, keepdims=True)
        shift_term = jnp.sum(back, axis=0, keepdims=True)
        gain_sum = gain_term if q == 0 else gain_sum + gain_term
        shift_sum = shift_term if q == 0 else shift_sum + shift_term
    grad_norm[0:1, :] = gain_sum
    grad_norm[1:2, :] = shift_sum


def ffn_up(
    scal,
    tokens,
    mixed0,
    mixed1,
    mixed2,
    mixed3,
    out0,
    out1,
    out2,
    out3,
    gain,
    shift,
    w_up,
    cot,
    residual,
    second,
    hidden,
    slope,
    out_rows,
    grad_down,
    w_out,
    w_nat,
):
    places, rows, width = tokens.shape
    mixed = (mixed0, mixed1, mixed2, mixed3)
    lanes = mixed0.shape[2]
    assembled(scal, w_out, (out0, out1, out2, out3))
    out_rows[...] = w_out[aligned(scal[0] * lanes, lanes), :]
    rows_in_order(scal, w_nat, w_up)
    for q in range(places):
        total = tokens[q].astype(f32)
        for p in range(places):
            total += dot(
                mixed[p][place_of(scal, q)], w_out[aligned(place_of(scal, p) * lanes, lanes), :]
            )
        residual[q] = total
        hat, _ = normalized(total)
        normed = (hat * gain[...] + shift[...]).astype(bf16)
        at = slice(q * rows, (q + 1) * rows)
        second[at, :] = normed
        inner = dot(normed, w_nat[...])
        root = 0.7978845608028654
        square = inner * inner
        bend = jnp.tanh(root * inner * (1.0 + 0.044715 * square))
        half = 0.5 * (1.0 + bend)
        hidden[at, :] = (inner * half).astype(bf16)
        slope[at, :] = (
            half + (0.5 * root) * inner * (1.0 - bend * bend) * (1.0 + (3 * 0.044715) * square)
        ).astype(bf16)
    for start in range(0, width, 256):
        columns = jnp.concatenate([cot[q, :, start : start + 256] for q in range(places)], axis=0)
        put_columns(scal, grad_down, start, dot_lt(hidden[...], columns).astype(bf16))


def ffn_back(
    scal,
    cot,
    w_down,
    w_up,
    slope,
    residual,
    back_second,
    back_input,
    grad_norm,
    w_nat,
    w_up_nat,
):
    places, rows, width = cot.shape
    columns_in_order(scal, w_nat, w_down)
    rows_in_order(scal, w_up_nat, w_up)
    gain_sum, shift_sum = None, None
    for q in range(places):
        at = slice(q * rows, (q + 1) * rows)
        inner = (dot_rt(cot[q], w_nat[...]) * slope[at, :].astype(f32)).astype(bf16)
        back_input[at, :] = inner
        back = dot_rt(inner, w_up_nat[...])
        back_second[q] = back.astype(bf16)
        hat, _ = normalized(residual[q])
        gain_term = jnp.sum(back * hat, axis=0, keepdims=True)
        shift_term = jnp.sum(back, axis=0, keepdims=True)
        gain_sum = gain_term if q == 0 else gain_sum + gain_term
        shift_sum = shift_term if q == 0 else shift_sum + shift_term
    grad_norm[0:1, :] = gain_sum
    grad_norm[1:2, :] = shift_sum


def ffn_rest(scal, hidden, w_down, second, back_input, partial, grad_up, w_nat):
    places, rows, width = partial.shape
    for start in range(0, width, 256):
        put_rows(
            scal,
            grad_up,
            start,
            dot_lt(second[:, start : start + 256], back_input[...]).astype(bf16),
        )
    columns_in_order(scal, w_nat, w_down)
    for q in range(places):
        partial[q] = dot(hidden[q * rows : (q + 1) * rows, :], w_nat[...]).astype(bf16)


def out_grad(scal, back_branch, mixed0, mixed1, mixed2, mixed3, grad_out):
    places, rows, width = back_branch.shape
    mixed = (mixed0, mixed1, mixed2, mixed3)
    lanes = mixed0.shape[2]
    own_at = aligned(scal[0] * lanes, lanes)
    own_columns = jnp.concatenate([back_branch[q, :, own_at] for q in range(places)], axis=0)
    for p in range(places):
        stack = jnp.concatenate([mixed[p][place_of(scal, q)] for q in range(places)], axis=0)
        put_rows(
            scal, grad_out, place_of(scal, p) * lanes, dot_lt(stack, own_columns).astype(bf16)
        )


def token_backward(
    head_dim,
    scal,
    back_branch,
    out_rows,
    qkv,
    bias,
    token_back,
    first,
    tokens,
    w_qkv,
    grad_qkv,
    back_first,
    grad_norm,
    distance,
    w_nat,
    tb,
    back_mixed,
    back_qkv,
    key_sum,
    band,
):
    places, rows, width = back_branch.shape
    heads, span = bias.shape
    lanes = heads * head_dim
    scale = head_dim ** (-0.5)
    rows_in_order(scal, w_nat, w_qkv)
    bias_blocks(tb, bias)
    for q in range(places):
        back_mixed[aligned(place_of(scal, q) * rows, rows), :] = dot_rt(
            back_branch[q], out_rows[...]
        ).astype(bf16)
    key_sum[...] = token_back[...]
    for h in range(heads):
        key_at, value_at = head_cols(1, h, heads, head_dim), head_cols(2, h, heads, head_dim)
        query_at, read_at = head_cols(0, h, heads, head_dim), slice(h * head_dim, (h + 1) * head_dim)
        for c in reversed(range(places)):
            count = min(span, (c + 1) * rows)
            low, high = (c + 1) * rows - count, (c + 1) * rows
            last = c * rows if c == places - 1 else 0
            query, back = qkv[c * rows : high, query_at], back_mixed[c * rows : high, read_at]
            keys = qkv[low:high, key_at]
            probs = window_probs(scal, query, keys, tb[h], last, scale)
            back_probs = dot_rt(back, qkv[low:high, value_at])
            row_dot = jnp.sum(probs * back_probs, axis=-1, keepdims=True)
            back_scores = probs * (back_probs - row_dot)
            if c == places - 1:
                band[...] = back_scores
            else:
                band[:, span - count :] += back_scores
            raw = (back_scores * scale).astype(bf16)
            back_qkv[c * rows : high, query_at] = dot(raw, keys).astype(bf16)
            key_to = slice(key_at.start - lanes, key_at.stop - lanes)
            value_to = slice(value_at.start - lanes, value_at.stop - lanes)
            key_sum[low:high, key_to] += dot_lt(raw, query)
            key_sum[low:high, value_to] += dot_lt(probs.astype(bf16), back)
        distance[h : h + 1, :] = jnp.sum(by_distance(band[...]), axis=0, keepdims=True)
    back_qkv[:, lanes:] = key_sum[...].astype(bf16)
    for start in range(0, width, 256):
        put_rows(
            scal,
            grad_qkv,
            start,
            dot_lt(first[:, start : start + 256], back_qkv[...]).astype(bf16),
        )
    gain_sum, shift_sum = None, None
    for q in range(places):
        back = dot_rt(back_qkv[aligned(place_of(scal, q) * rows, rows), :], w_nat[...])
        back_first[q] = back.astype(bf16)
        hat, _ = normalized(tokens[q].astype(f32))
        gain_term = jnp.sum(back * hat, axis=0, keepdims=True)
        shift_term = jnp.sum(back, axis=0, keepdims=True)
        gain_sum = gain_term if q == 0 else gain_sum + gain_term
        shift_sum = shift_term if q == 0 else shift_sum + shift_term
    grad_norm[0:1, :] = gain_sum
    grad_norm[1:2, :] = shift_sum


def norm_back(values, back, gain):
    hat, inverse = normalized(values)
    grown = back * gain
    return inverse * (
        grown
        - jnp.mean(grown, axis=-1, keepdims=True)
        - hat * jnp.mean(grown * hat, axis=-1, keepdims=True)
    )


def per_device(
    tokens,
    state_in,
    cotangent,
    state_cotangent,
    seq_len,
    bucket_table,
    w_qkv,
    w_out,
    w_sqkv,
    w_sout,
    w_up,
    w_down,
    rel_table,
    norm_gain,
    norm_shift,
    gate_bias,
):
    rows, width = tokens.shape
    bucket_count, head_count = rel_table.shape
    window = bucket_table.shape[0]
    state_rows = state_in.shape[1]
    places = lax.axis_size("state")
    assert places == len(PLACES)
    dp_count = lax.axis_size("dp")
    here, dp_here = lax.axis_index("state"), lax.axis_index("dp")
    head_dim = width // head_count
    heads = head_count // places
    lanes = heads * head_dim
    span = window + rows
    group_rows = rows * places
    all_states = state_rows * places
    inner_width = w_up.shape[1]
    hops = dp_count == len(DP_PLACES)
    blocks = dp_count if hops else 1

    def swap(value, axis, bit):
        count = lax.axis_size(axis)
        return lax.ppermute(value, axis, [(i, i ^ bit) for i in range(count)])

    def from_group(value):
        pair = jnp.stack([value, swap(value, "state", 2)])
        return jnp.concatenate([pair, swap(pair, "state", 1)], axis=0)

    def list_from_group(value):
        across = swap(value, "state", 2)
        return [value, across, swap(value, "state", 1), swap(across, "state", 1)]

    def sum_to_owner(partial):
        half = partial.shape[0] // 2
        pair = partial[:half].astype(f32) + swap(partial[half:], "state", 1).astype(f32)
        return pair[0] + swap(pair[1].astype(bf16), "state", 2).astype(f32)

    def from_dp(block, axis):
        if not hops:
            return lax.all_gather(block, "dp", axis=axis, tiled=True)[None]
        gathered = block[None]
        for bit in DP_STEPS:
            gathered = jnp.concatenate([gathered, swap(gathered, "dp", bit)], axis=0)
        return gathered

    def sum_over_dp(partial, axis):
        if not hops:
            return lax.psum_scatter(partial[0], "dp", scatter_dimension=axis, tiled=True).astype(f32)
        for bit in reversed(DP_STEPS):
            half = partial.shape[0] // 2
            arrived = swap(partial[half:], "dp", bit)
            total = partial[:half].astype(f32) + arrived.astype(f32)
            partial = total.astype(bf16)
        return total[0]

    def sum_over_all(vector):
        if not hops:
            return lax.psum(vector, ("dp", "state"))
        for axis, bit in (("state", 1), ("state", 2), ("dp", 1), ("dp", 2), ("dp", 4)):
            vector = vector + swap(vector, axis, bit)
        return vector

    even = here % 2 == 0

    def pick(*by_place):
        value = by_place[-1]
        for i in reversed(range(places - 1)):
            value = jnp.where(here == i, by_place[i], value)
        return value

    def to_heads(shard):
        left, middle, right = (shard[:, i * lanes : (i + 1) * lanes] for i in range(3))
        own = jnp.where(even, left, right)
        across = swap(jnp.where(even, right, left), "state", 2)
        beside = swap(middle, "state", 1)
        query = pick(own, beside, across, across)
        keys = pick(beside, own, own, beside)
        values = pick(across, across, beside, own)
        return jnp.concatenate([query, keys, values], axis=1)

    def from_heads(grads):
        query, keys, values = (grads[:, i * lanes : (i + 1) * lanes] for i in range(3))
        own = pick(query, keys, keys, values)
        beside = swap(pick(keys, query, values, keys), "state", 1)
        across = swap(pick(values, values, query, query), "state", 2)
        return jnp.concatenate(
            [jnp.where(even, own, across), beside, jnp.where(even, across, own)], axis=1
        )

    if hops:
        block_list = dp_here ^ jnp.array(DP_PLACES, jnp.int32)
        position_list = jnp.array(
            [DP_PLACES.index(i) for i in range(dp_count)], jnp.int32
        )[dp_here ^ jnp.arange(dp_count)]
    else:
        block_list = position_list = jnp.zeros((1,), jnp.int32)
    scal = jnp.concatenate(
        [here[None].astype(jnp.int32), seq_len.astype(jnp.int32), block_list, position_list]
    ).astype(jnp.int32)

    both = to_heads(jnp.concatenate([w_qkv, w_sqkv], axis=0))
    depth = w_qkv.shape[0]
    full_qkv = from_dp(both[:depth], 0)
    all_tokens = from_group(tokens)
    full_sqkv = from_dp(both[depth:], 0)
    all_state = from_group(state_in[0])
    all_cot = from_group(cotangent)
    all_state_cot = from_group(state_cotangent[0])
    outs_pair = from_dp(jnp.concatenate([w_out, w_sout], axis=1), 0)
    half = outs_pair.shape[2] // 2
    full_sout = list_from_group(outs_pair[:, :, half:])
    full_out = list_from_group(outs_pair[:, :, :half])
    full_up = from_dp(w_up, 0)
    full_down = from_dp(w_down, 1)

    lookup = (bucket_table[:, None] == jnp.arange(bucket_count)[None, :]).astype(f32)
    own_table = lax.dynamic_slice_in_dim(rel_table, here * heads, heads, 1)
    bias_rows = jnp.dot(
        own_table.T, lookup.T, precision=lax.Precision.HIGHEST, preferred_element_type=f32
    )
    bias = jnp.concatenate(
        [
            jnp.full((heads, 1), masked_value, f32),
            bias_rows[:, ::-1],
            jnp.full((heads, span - window - 1), masked_value, f32),
        ],
        axis=1,
    )
    gains = [norm_gain[i : i + 1] for i in range(3)]
    shifts = [norm_shift[i : i + 1] for i in range(3)]

    first, qkv, mixed = call(
        functools.partial(token_forward, head_dim),
        "token_forward",
        [out((group_rows, width)), out((group_rows, 3 * lanes)), out((places, rows, lanes))],
        [pltpu.VMEM((width, 3 * lanes), bf16), pltpu.VMEM((heads, rows, span), f32)],
        2 * group_rows * width * 3 * lanes,
        group_rows * span * heads,
        scal,
        all_tokens,
        gains[0],
        shifts[0],
        full_qkv,
        bias,
    )
    mixed_parts = list_from_group(mixed)

    state_norm, sqkv, read = call(
        functools.partial(state_forward, head_dim),
        "state_forward",
        [
            out((all_states, width)),
            out((all_states, 3 * lanes)),
            out((places, state_rows, lanes)),
        ],
        [pltpu.VMEM((width, 3 * lanes), bf16)],
        2 * all_states * width * 3 * lanes,
        all_states * (all_states + group_rows) * heads,
        scal,
        all_state,
        gains[2],
        shifts[2],
        full_sqkv,
        qkv,
    )
    read_parts = list_from_group(read)

    next_state, grad_gate, grad_sout, token_back, grad_sqkv, back_state_norm, state_sums = call(
        functools.partial(state_backward, head_dim),
        "state_backward",
        [
            out((state_rows, width)),
            out((1, width), f32),
            out((blocks, width // blocks, lanes)),
            out((group_rows, 2 * lanes), f32),
            out((blocks, width // blocks, 3 * lanes)),
            out((places, state_rows, width)),
            out((2, width), f32),
        ],
        [
            pltpu.VMEM((width, 3 * lanes), bf16),
            pltpu.VMEM((width, width), bf16),
            pltpu.VMEM((all_states, width), bf16),
            pltpu.VMEM((all_states, lanes), bf16),
            pltpu.VMEM((all_states, 3 * lanes), bf16),
            pltpu.VMEM((all_states, 2 * lanes), f32),
        ],
        4 * all_states * width * 4 * lanes,
        all_states * (all_states + group_rows) * heads,
        scal,
        state_in[0],
        all_state_cot,
        gate_bias[None],
        all_state,
        *read_parts,
        *full_sout,
        sqkv,
        qkv,
        state_norm,
        full_sqkv,
    )
    own_grad_sout = sum_over_dp(grad_sout, 0)
    own_grad_sqkv = sum_over_dp(grad_sqkv, 0)
    back_state = sum_to_owner(back_state_norm)
    gate_open = jax.nn.sigmoid(gate_bias)
    grad_state = (
        gate_open * state_cotangent[0].astype(f32)
        + norm_back(state_in[0].astype(f32), back_state, norm_gain[2])
    ).astype(bf16)

    residual, second, hidden, slope, out_rows, grad_down = call(
        ffn_up,
        "ffn_up",
        [
            out((places, rows, width), f32),
            out((group_rows, width)),
            out((group_rows, inner_width)),
            out((group_rows, inner_width)),
            out((lanes, width)),
            out((blocks, inner_width, width // blocks)),
        ],
        [pltpu.VMEM((width, width), bf16), pltpu.VMEM((width, inner_width), bf16)],
        2 * group_rows * width * (width + 2 * inner_width),
        group_rows * inner_width,
        scal,
        all_tokens,
        *mixed_parts,
        *full_out,
        gains[1],
        shifts[1],
        full_up,
        all_cot,
    )
    own_grad_down = sum_over_dp(grad_down, 1)

    back_second, back_input, mid_sums = call(
        ffn_back,
        "ffn_back",
        [
            out((places, rows, width)),
            out((group_rows, inner_width)),
            out((2, width), f32),
        ],
        [pltpu.VMEM((inner_width, width), bf16), pltpu.VMEM((width, inner_width), bf16)],
        4 * group_rows * width * inner_width,
        0,
        scal,
        all_cot,
        full_down,
        full_up,
        slope,
        residual,
    )
    back_second = sum_to_owner(back_second)
    back_residual = cotangent.astype(f32) + norm_back(residual[0], back_second, norm_gain[1])
    back_branch = from_group(back_residual.astype(bf16))

    ffn_partial, grad_up = call(
        ffn_rest,
        "ffn_rest",
        [out((places, rows, width)), out((blocks, width // blocks, inner_width))],
        [pltpu.VMEM((inner_width, width), bf16)],
        4 * group_rows * width * inner_width,
        0,
        scal,
        hidden,
        full_down,
        second,
        back_input,
    )
    own_grad_up = sum_over_dp(grad_up, 0)
    output = (residual[0] + sum_to_owner(ffn_partial)).astype(bf16)

    (grad_out,) = call(
        out_grad,
        "out_grad",
        [out((blocks, width // blocks, lanes))],
        [],
        2 * group_rows * width * lanes,
        0,
        scal,
        back_branch,
        *mixed_parts,
    )
    own_grad_out = sum_over_dp(grad_out, 0)

    grad_qkv, back_first, first_sums, distance = call(
        functools.partial(token_backward, head_dim),
        "token_backward",
        [
            out((blocks, width // blocks, 3 * lanes)),
            out((places, rows, width)),
            out((2, width), f32),
            out((heads, span), f32),
        ],
        [
            pltpu.VMEM((width, 3 * lanes), bf16),
            pltpu.VMEM((heads, rows, span), f32),
            pltpu.VMEM((group_rows, lanes), bf16),
            pltpu.VMEM((group_rows, 3 * lanes), bf16),
            pltpu.VMEM((group_rows, 2 * lanes), f32),
            pltpu.VMEM((rows, span), f32),
        ],
        2 * group_rows * width * 7 * lanes,
        group_rows * span * heads,
        scal,
        back_branch,
        out_rows,
        qkv,
        bias,
        token_back,
        first,
        all_tokens,
        full_qkv,
    )
    back_first = sum_to_owner(back_first)
    grad_tokens = (
        norm_back(tokens.astype(f32), back_first, norm_gain[0]) + back_residual
    ).astype(bf16)
    own_grad_qkv = sum_over_dp(grad_qkv, 0)
    both_grads = from_heads(
        jnp.concatenate([own_grad_qkv, own_grad_sqkv], axis=0).astype(bf16)
    ).astype(f32)

    per_distance = distance[:, 1 : window + 1][:, ::-1]
    own_rel = jnp.dot(
        per_distance, lookup, precision=lax.Precision.HIGHEST, preferred_element_type=f32
    ).T
    grad_rel = lax.dynamic_update_slice_in_dim(
        jnp.zeros((bucket_count, head_count), f32), own_rel, here * heads, 1
    )
    small = [
        jnp.stack([first_sums[0], mid_sums[0], state_sums[0]]),
        jnp.stack([first_sums[1], mid_sums[1], state_sums[1]]),
        grad_gate[0],
        grad_rel,
    ]
    packed = sum_over_all(jnp.concatenate([v.reshape(-1, 128) for v in small], axis=0))
    unpacked, start = [], 0
    for v in small:
        count = v.size // 128
        unpacked.append(packed[start : start + count].reshape(v.shape))
        start += count
    return (
        output,
        next_state[None],
        grad_tokens,
        grad_state[None],
        both_grads[:depth],
        own_grad_out,
        both_grads[depth:],
        own_grad_sout,
        own_grad_up,
        own_grad_down,
        unpacked[3],
        unpacked[0],
        unpacked[1],
        unpacked[2],
    )


def solution(mesh):
    rows_spec = P(("dp", "state"), None)
    state_spec = P("dp", "state", None)
    weight_spec = P("dp", "state")
    return jax.shard_map(
        per_device,
        mesh=mesh,
        in_specs=(
            rows_spec,
            state_spec,
            rows_spec,
            state_spec,
            P("dp"),
            P(),
            weight_spec,
            weight_spec,
            weight_spec,
            weight_spec,
            weight_spec,
            P("state", "dp"),
            P(),
            P(),
            P(),
            P(),
        ),
        out_specs=(
            rows_spec,
            state_spec,
            rows_spec,
            state_spec,
            weight_spec,
            weight_spec,
            weight_spec,
            weight_spec,
            weight_spec,
            P("state", "dp"),
            P(),
            P(),
            P(),
            P(),
        ),
        check_vma=False,
    )
```

```python
import functools

import jax
import jax.numpy as jnp
from jax import lax
from jax.experimental import pallas as pl
from jax.experimental.pallas import tpu as pltpu
from jax.sharding import PartitionSpec as P

epsilon = 1e-05
masked_value = -1e30
f32 = jnp.float32
bf16 = jnp.bfloat16

PLACES = (0, 2, 1, 3)
DP_STEPS = (2, 4, 1)
DP_PLACES = (0, 2, 4, 6, 1, 3, 5, 7)


def dot(left, right):
    return lax.dot_general(left, right, (((1,), (0,)), ((), ())), preferred_element_type=f32)


def dot_rt(left, right):
    return lax.dot_general(left, right, (((1,), (1,)), ((), ())), preferred_element_type=f32)


def dot_lt(left, right):
    return lax.dot_general(left, right, (((0,), (0,)), ((), ())), preferred_element_type=f32)


def where_from(sender, place):
    return PLACES.index(PLACES[sender] ^ PLACES[place])


def normalized(values):
    centre = jnp.mean(values, axis=-1, keepdims=True)
    centred = values - centre
    spread = jnp.mean(centred * centred, axis=-1, keepdims=True)
    inverse = lax.rsqrt(spread + epsilon)
    return centred * inverse, inverse


def place_of(scal, q):
    return scal[0] ^ PLACES[q]


def aligned(start, size):
    return pl.ds(pl.multiple_of(start, size), size)


def block_at(scal, q):
    return scal[2 + q]


def position_of(scal, block, blocks):
    return scal[2 + blocks + block]


def rows_in_order(scal, target, source):
    blocks, depth = source.shape[0], source.shape[1]
    for q in range(blocks):
        target[aligned(block_at(scal, q) * depth, depth), :] = source[q]


def columns_in_order(scal, target, source):
    blocks, depth = source.shape[0], source.shape[2]
    for q in range(blocks):
        target[:, aligned(block_at(scal, q) * depth, depth)] = source[q]


def put_rows(scal, target, start, value):
    blocks, depth = target.shape[0], target.shape[1]
    rows = value.shape[0]
    if depth >= rows:
        target[position_of(scal, start // depth, blocks), aligned(start % depth, rows), :] = value
    else:
        for i in range(rows // depth):
            position = position_of(scal, start // depth + i, blocks)
            target[position] = value[i * depth : (i + 1) * depth]


def put_columns(scal, target, start, value):
    blocks, depth = target.shape[0], target.shape[2]
    columns = value.shape[1]
    if depth >= columns:
        target[position_of(scal, start // depth, blocks), :, aligned(start % depth, columns)] = value
    else:
        for i in range(columns // depth):
            position = position_of(scal, start // depth + i, blocks)
            target[position] = value[:, i * depth : (i + 1) * depth]


def call(body, name, outs, scratch, flops, exps, *args):
    sizes = sum(a.size * a.dtype.itemsize for a in args) + sum(
        a.size * a.dtype.itemsize for a in outs
    )
    in_specs = [pl.BlockSpec(memory_space=pltpu.SMEM)] + [
        pl.BlockSpec(memory_space=pltpu.VMEM) for _ in args[1:]
    ]
    return pl.pallas_call(
        body,
        out_shape=outs,
        in_specs=in_specs,
        out_specs=[pl.BlockSpec(memory_space=pltpu.VMEM) for _ in outs],
        scratch_shapes=scratch,
        compiler_params=pltpu.CompilerParams(vmem_limit_bytes=56 << 20),
        cost_estimate=pl.CostEstimate(flops=flops, bytes_accessed=sizes, transcendentals=exps),
        name=name,
    )(*args)


def out(shape, kind=bf16):
    return jax.ShapeDtypeStruct(shape, kind)


def by_distance(scores):
    rows, span = scores.shape
    row_at = lax.broadcasted_iota(jnp.int32, scores.shape, 0)
    step = 1
    while step < rows:
        scores = jnp.where(row_at & step != 0, pltpu.roll(scores, span - step, 1), scores)
        step *= 2
    return scores


def bias_blocks(tb, bias):
    heads, rows, span = tb.shape
    for h in range(heads):
        row = jnp.broadcast_to(bias[h : h + 1, :], (rows, span))
        tb[h] = pltpu.roll(row, 0, 1, stride=1, stride_axis=0)


def window_probs(scal, query, keys, tb_block, last, scale):
    rows, span = tb_block.shape
    count = keys.shape[0]
    scores = dot_rt(query, keys) * scale + tb_block[:, span - count :]
    if last:
        row_at = lax.broadcasted_iota(jnp.int32, scores.shape, 0)
        col_at = lax.broadcasted_iota(jnp.int32, scores.shape, 1)
        ahead = col_at - (count - rows)
        live = (ahead < scal[1] - last) | (ahead == row_at)
        scores = jnp.where(live, scores, masked_value)
    top = jnp.max(scores, axis=-1, keepdims=True)
    grown = jnp.exp(scores - top)
    return grown * (1.0 / jnp.sum(grown, axis=-1, keepdims=True))


def state_probs(scal, query, state_keys, keys, scale):
    own = dot_rt(query, state_keys) * scale
    token = dot_rt(query, keys) * scale
    col_at = lax.broadcasted_iota(jnp.int32, token.shape, 1)
    token = jnp.where(col_at < scal[1], token, masked_value)
    top = jnp.maximum(
        jnp.max(own, axis=-1, keepdims=True), jnp.max(token, axis=-1, keepdims=True)
    )
    own = jnp.exp(own - top)
    token = jnp.exp(token - top)
    total = jnp.sum(own, axis=-1, keepdims=True) + jnp.sum(token, axis=-1, keepdims=True)
    inverse = 1.0 / total
    return own * inverse, token * inverse


def head_cols(block, h, heads, head_dim):
    start = (block * heads + h) * head_dim
    return slice(start, start + head_dim)


def token_forward(head_dim, scal, tokens, gain, shift, w_qkv, bias, first, qkv, mixed, w_nat, tb):
    places, rows, width = tokens.shape
    heads = bias.shape[0]
    span = bias.shape[1]
    scale = head_dim ** (-0.5)
    rows_in_order(scal, w_nat, w_qkv)
    bias_blocks(tb, bias)
    for q in range(places):
        hat, _ = normalized(tokens[q].astype(f32))
        normed = (hat * gain[...] + shift[...]).astype(bf16)
        at = aligned(place_of(scal, q) * rows, rows)
        first[at, :] = normed
        qkv[at, :] = dot(normed, w_nat[...]).astype(bf16)
    for c in range(places):
        count = min(span, (c + 1) * rows)
        low, high = (c + 1) * rows - count, (c + 1) * rows
        last = c * rows if c == places - 1 else 0
        parts = []
        for h in range(heads):
            probs = window_probs(
                scal,
                qkv[c * rows : high, head_cols(0, h, heads, head_dim)],
                qkv[low:high, head_cols(1, h, heads, head_dim)],
                tb[h],
                last,
                scale,
            )
            parts.append(
                dot(probs.astype(bf16), qkv[low:high, head_cols(2, h, heads, head_dim)])
            )
        mixed[c] = jnp.concatenate(parts, axis=1).astype(bf16)


def state_forward(
    head_dim, scal, state, gain, shift, w_sqkv, qkv, normed_out, sqkv, read, w_nat
):
    places, rows, width = state.shape
    heads = qkv.shape[1] // (3 * head_dim)
    scale = head_dim ** (-0.5)
    rows_in_order(scal, w_nat, w_sqkv)
    for q in range(places):
        hat, _ = normalized(state[q].astype(f32))
        normed = (hat * gain[...] + shift[...]).astype(bf16)
        normed_out[q * rows : (q + 1) * rows, :] = normed
        sqkv[q * rows : (q + 1) * rows, :] = dot(normed, w_nat[...]).astype(bf16)
    for q in range(places):
        parts = []
        for h in range(heads):
            own, token = state_probs(
                scal,
                sqkv[q * rows : (q + 1) * rows, head_cols(0, h, heads, head_dim)],
                sqkv[:, head_cols(1, h, heads, head_dim)],
                qkv[:, head_cols(1, h, heads, head_dim)],
                scale,
            )
            parts.append(
                dot(own.astype(bf16), sqkv[:, head_cols(2, h, heads, head_dim)])
                + dot(token.astype(bf16), qkv[:, head_cols(2, h, heads, head_dim)])
            )
        read[q] = jnp.concatenate(parts, axis=1).astype(bf16)


def assembled(scal, target, parts):
    for p, part in enumerate(parts):
        blocks, depth, columns = part.shape
        at = aligned(place_of(scal, p) * columns, columns)
        for q in range(blocks):
            target[aligned(block_at(scal, q) * depth, depth), at] = part[q]


def state_backward(
    head_dim,
    scal,
    state_own,
    state_cot,
    gate_bias,
    state,
    read0,
    read1,
    read2,
    read3,
    out0,
    out1,
    out2,
    out3,
    sqkv,
    qkv,
    normed,
    w_sqkv,
    next_state,
    grad_gate,
    grad_sout,
    token_back,
    grad_sqkv,
    back_norm,
    grad_norm,
    w_nat,
    w_out,
    back_update,
    back_read,
    back_sqkv,
    own_sum,
):
    places, rows, width = state_cot.shape
    reads = (read0, read1, read2, read3)
    heads = qkv.shape[1] // (3 * head_dim)
    lanes = heads * head_dim
    scale = head_dim ** (-0.5)
    rows_in_order(scal, w_nat, w_sqkv)
    assembled(scal, w_out, (out0, out1, out2, out3))
    gate = jax.nn.sigmoid(gate_bias[...])
    update = None
    for p in range(places):
        term = dot(reads[p][p], w_out[aligned(place_of(scal, p) * lanes, lanes), :])
        update = term if update is None else update + term
    held = state_own[...].astype(f32)
    cot = state_cot[0].astype(f32)
    next_state[...] = (gate * held + (1.0 - gate) * update).astype(bf16)
    grad_gate[...] = jnp.sum(cot * (held - update), axis=0, keepdims=True) * (gate * (1.0 - gate))
    for q in range(places):
        back_update[q * rows : (q + 1) * rows, :] = (
            (1.0 - gate) * state_cot[q].astype(f32)
        ).astype(bf16)
    own_columns = back_update[:, aligned(scal[0] * lanes, lanes)]
    for p in range(places):
        stack = jnp.concatenate([reads[p][where_from(p, q)] for q in range(places)], axis=0)
        put_rows(
            scal, grad_sout, place_of(scal, p) * lanes, dot_lt(stack, own_columns).astype(bf16)
        )
    back_read[...] = dot_rt(
        back_update[...], w_out[aligned(scal[0] * lanes, lanes), :]
    ).astype(bf16)
    for h in range(heads):
        key_at, value_at = head_cols(1, h, heads, head_dim), head_cols(2, h, heads, head_dim)
        query_at, read_at = head_cols(0, h, heads, head_dim), slice(h * head_dim, (h + 1) * head_dim)
        for q in range(places):
            at = slice(q * rows, (q + 1) * rows)
            query, back = sqkv[at, query_at], back_read[at, read_at]
            own, token = state_probs(scal, query, sqkv[:, key_at], qkv[:, key_at], scale)
            back_own = dot_rt(back, sqkv[:, value_at])
            back_token = dot_rt(back, qkv[:, value_at])
            row_dot = jnp.sum(own * back_own, axis=-1, keepdims=True) + jnp.sum(
                token * back_token, axis=-1, keepdims=True
            )
            own_raw = (own * (back_own - row_dot) * scale).astype(bf16)
            token_raw = (token * (back_token - row_dot) * scale).astype(bf16)
            back_sqkv[at, query_at] = (
                dot(own_raw, sqkv[:, key_at]) + dot(token_raw, qkv[:, key_at])
            ).astype(bf16)
            terms = (
                (own_sum, key_at, dot_lt(own_raw, query)),
                (own_sum, value_at, dot_lt(own.astype(bf16), back)),
                (token_back, key_at, dot_lt(token_raw, query)),
                (token_back, value_at, dot_lt(token.astype(bf16), back)),
            )
            for target, columns, term in terms:
                columns = slice(columns.start - lanes, columns.stop - lanes)
                if q == 0:
                    target[:, columns] = term
                else:
                    target[:, columns] += term
    back_sqkv[:, lanes:] = own_sum[...].astype(bf16)
    for start in range(0, width, 256):
        put_rows(
            scal,
            grad_sqkv,
            start,
            dot_lt(normed[:, start : start + 256], back_sqkv[...]).astype(bf16),
        )
    gain_sum, shift_sum = None, None
    for q in range(places):
        back = dot_rt(back_sqkv[q * rows : (q + 1) * rows, :], w_nat[...])
        back_norm[q] = back.astype(bf16)
        hat, _ = normalized(state[q].astype(f32))
        gain_term = jnp.sum(back * hat, axis=0, keepdims=True)
        shift_term = jnp.sum(back, axis=0, keepdims=True)
        gain_sum = gain_term if q == 0 else gain_sum + gain_term
        shift_sum = shift_term if q == 0 else shift_sum + shift_term
    grad_norm[0:1, :] = gain_sum
    grad_norm[1:2, :] = shift_sum


def ffn_up(
    scal,
    tokens,
    mixed0,
    mixed1,
    mixed2,
    mixed3,
    out0,
    out1,
    out2,
    out3,
    gain,
    shift,
    w_up,
    cot,
    residual,
    second,
    hidden,
    slope,
    out_rows,
    grad_down,
    w_out,
    w_nat,
):
    places, rows, width = tokens.shape
    mixed = (mixed0, mixed1, mixed2, mixed3)
    lanes = mixed0.shape[2]
    assembled(scal, w_out, (out0, out1, out2, out3))
    out_rows[...] = w_out[aligned(scal[0] * lanes, lanes), :]
    rows_in_order(scal, w_nat, w_up)
    for q in range(places):
        total = tokens[q].astype(f32)
        for p in range(places):
            total += dot(
                mixed[p][place_of(scal, q)], w_out[aligned(place_of(scal, p) * lanes, lanes), :]
            )
        residual[q] = total
        hat, _ = normalized(total)
        normed = (hat * gain[...] + shift[...]).astype(bf16)
        at = slice(q * rows, (q + 1) * rows)
        second[at, :] = normed
        inner = dot(normed, w_nat[...])
        root = 0.7978845608028654
        square = inner * inner
        bend = jnp.tanh(root * inner * (1.0 + 0.044715 * square))
        half = 0.5 * (1.0 + bend)
        hidden[at, :] = (inner * half).astype(bf16)
        slope[at, :] = (
            half + (0.5 * root) * inner * (1.0 - bend * bend) * (1.0 + (3 * 0.044715) * square)
        ).astype(bf16)
    for start in range(0, width, 256):
        columns = jnp.concatenate([cot[q, :, start : start + 256] for q in range(places)], axis=0)
        put_columns(scal, grad_down, start, dot_lt(hidden[...], columns).astype(bf16))


def ffn_back(
    scal,
    cot,
    w_down,
    w_up,
    slope,
    residual,
    back_second,
    back_input,
    grad_norm,
    w_nat,
    w_up_nat,
):
    places, rows, width = cot.shape
    columns_in_order(scal, w_nat, w_down)
    rows_in_order(scal, w_up_nat, w_up)
    gain_sum, shift_sum = None, None
    for q in range(places):
        at = slice(q * rows, (q + 1) * rows)
        inner = (dot_rt(cot[q], w_nat[...]) * slope[at, :].astype(f32)).astype(bf16)
        back_input[at, :] = inner
        back = dot_rt(inner, w_up_nat[...])
        back_second[q] = back.astype(bf16)
        hat, _ = normalized(residual[q])
        gain_term = jnp.sum(back * hat, axis=0, keepdims=True)
        shift_term = jnp.sum(back, axis=0, keepdims=True)
        gain_sum = gain_term if q == 0 else gain_sum + gain_term
        shift_sum = shift_term if q == 0 else shift_sum + shift_term
    grad_norm[0:1, :] = gain_sum
    grad_norm[1:2, :] = shift_sum


def ffn_rest(scal, hidden, w_down, second, back_input, partial, grad_up, w_nat):
    places, rows, width = partial.shape
    for start in range(0, width, 256):
        put_rows(
            scal,
            grad_up,
            start,
            dot_lt(second[:, start : start + 256], back_input[...]).astype(bf16),
        )
    columns_in_order(scal, w_nat, w_down)
    for q in range(places):
        partial[q] = dot(hidden[q * rows : (q + 1) * rows, :], w_nat[...]).astype(bf16)


def out_grad(scal, back_branch, mixed0, mixed1, mixed2, mixed3, grad_out):
    places, rows, width = back_branch.shape
    mixed = (mixed0, mixed1, mixed2, mixed3)
    lanes = mixed0.shape[2]
    own_at = aligned(scal[0] * lanes, lanes)
    own_columns = jnp.concatenate([back_branch[q, :, own_at] for q in range(places)], axis=0)
    for p in range(places):
        stack = jnp.concatenate([mixed[p][place_of(scal, q)] for q in range(places)], axis=0)
        put_rows(
            scal, grad_out, place_of(scal, p) * lanes, dot_lt(stack, own_columns).astype(bf16)
        )


def token_backward(
    head_dim,
    scal,
    back_branch,
    out_rows,
    qkv,
    bias,
    token_back,
    first,
    tokens,
    w_qkv,
    grad_qkv,
    back_first,
    grad_norm,
    distance,
    w_nat,
    tb,
    back_mixed,
    back_qkv,
    key_sum,
    band,
):
    places, rows, width = back_branch.shape
    heads, span = bias.shape
    lanes = heads * head_dim
    scale = head_dim ** (-0.5)
    rows_in_order(scal, w_nat, w_qkv)
    bias_blocks(tb, bias)
    for q in range(places):
        back_mixed[aligned(place_of(scal, q) * rows, rows), :] = dot_rt(
            back_branch[q], out_rows[...]
        ).astype(bf16)
    key_sum[...] = token_back[...]
    for h in range(heads):
        key_at, value_at = head_cols(1, h, heads, head_dim), head_cols(2, h, heads, head_dim)
        query_at, read_at = head_cols(0, h, heads, head_dim), slice(h * head_dim, (h + 1) * head_dim)
        for c in reversed(range(places)):
            count = min(span, (c + 1) * rows)
            low, high = (c + 1) * rows - count, (c + 1) * rows
            last = c * rows if c == places - 1 else 0
            query, back = qkv[c * rows : high, query_at], back_mixed[c * rows : high, read_at]
            keys = qkv[low:high, key_at]
            probs = window_probs(scal, query, keys, tb[h], last, scale)
            back_probs = dot_rt(back, qkv[low:high, value_at])
            row_dot = jnp.sum(probs * back_probs, axis=-1, keepdims=True)
            back_scores = probs * (back_probs - row_dot)
            if c == places - 1:
                band[...] = back_scores
            else:
                band[:, span - count :] += back_scores
            raw = (back_scores * scale).astype(bf16)
            back_qkv[c * rows : high, query_at] = dot(raw, keys).astype(bf16)
            key_to = slice(key_at.start - lanes, key_at.stop - lanes)
            value_to = slice(value_at.start - lanes, value_at.stop - lanes)
            key_sum[low:high, key_to] += dot_lt(raw, query)
            key_sum[low:high, value_to] += dot_lt(probs.astype(bf16), back)
        distance[h : h + 1, :] = jnp.sum(by_distance(band[...]), axis=0, keepdims=True)
    back_qkv[:, lanes:] = key_sum[...].astype(bf16)
    for start in range(0, width, 256):
        put_rows(
            scal,
            grad_qkv,
            start,
            dot_lt(first[:, start : start + 256], back_qkv[...]).astype(bf16),
        )
    gain_sum, shift_sum = None, None
    for q in range(places):
        back = dot_rt(back_qkv[aligned(place_of(scal, q) * rows, rows), :], w_nat[...])
        back_first[q] = back.astype(bf16)
        hat, _ = normalized(tokens[q].astype(f32))
        gain_term = jnp.sum(back * hat, axis=0, keepdims=True)
        shift_term = jnp.sum(back, axis=0, keepdims=True)
        gain_sum = gain_term if q == 0 else gain_sum + gain_term
        shift_sum = shift_term if q == 0 else shift_sum + shift_term
    grad_norm[0:1, :] = gain_sum
    grad_norm[1:2, :] = shift_sum


def flip_low(i):
    return i + 1 - 2 * (i % 2)


class Mover:
    def __init__(self, send, recv):
        self.send, self.recv, self.used = send, recv, 0

    def __call__(self, source, target, device):
        i = self.used
        self.used += 1
        return pltpu.make_async_remote_copy(
            src_ref=source,
            dst_ref=target,
            send_sem=self.send.at[i],
            recv_sem=self.recv.at[i],
            device_id=device,
            device_id_type=pl.DeviceIdType.MESH,
        )


class Links:
    def __init__(self):
        self.d, self.s = lax.axis_index("dp"), lax.axis_index("state")
        z, y = self.d // 2, self.d % 2
        self.over_z = [2 * (z + 1 - 2 * (z % 2)) + y, 2 * ((z + 2) % 4) + y, 2 * (3 - z) + y]
        self.over_y = flip_low(self.d)
        self.core, self.x = flip_low(self.s), (self.s + 2) % 4
        self.to_core, self.to_x = (self.d, self.core), (self.d, self.x)
        self.to_y = (self.over_y, self.s)
        self.to_z = [(other, self.s) for other in self.over_z]

    def greet(self):
        barrier = pltpu.get_barrier_semaphore()
        partners = [self.to_core, self.to_x, self.to_y, *self.to_z]
        for partner in partners:
            pl.semaphore_signal(
                barrier, inc=1, device_id=partner, device_id_type=pl.DeviceIdType.MESH
            )
        pl.semaphore_wait(barrier, len(partners))


class GroupGather:
    def __init__(self, mover, links, whole, at, source=None):
        self.links, self.parts = links, [links.s, links.core, links.x, flip_low(links.x)]
        own = whole.at[at(links.s)]
        source = own if source is None else source
        across = whole.at[at(links.x)]
        self.over_x = mover(source, own, links.to_x)
        self.beside = mover(source, own, links.to_core)
        self.passed = mover(across, across, links.to_core)

    def start(self):
        self.over_x.start()
        self.beside.start()

    def forward(self):
        self.over_x.wait_recv()
        self.passed.start()

    def finish(self):
        self.beside.wait_recv()
        self.passed.wait_recv()

    def sent(self):
        for copy in (self.over_x, self.beside, self.passed):
            copy.wait_send()


class WeightGather:
    def __init__(self, mover, links, whole, at, source):
        own = whole.at[at(links.d)]
        self.over_z = [mover(source, own, partner) for partner in links.to_z]
        self.own_y = mover(source, own, links.to_y)
        self.passed = []
        for other in links.over_z:
            block = whole.at[at(other)]
            self.passed.append(mover(block, block, links.to_y))

    def start_z(self):
        for copy in self.over_z:
            copy.start()

    def start_y(self):
        self.own_y.start()

    def forward(self, k):
        self.over_z[k].wait_recv()
        self.passed[k].start()

    def finish(self):
        self.own_y.wait_recv()
        for copy in self.passed:
            copy.wait_recv()

    def sent(self):
        for copy in (*self.over_z, self.own_y, *self.passed):
            copy.wait_send()


FRONT_COPIES = 72


def front(
    head_dim,
    length,
    tokens,
    state,
    cot,
    state_cot,
    w_qkv,
    w_out,
    w_sqkv,
    w_sout,
    w_up,
    w_down,
    bias,
    gains,
    shifts,
    gate_bias,
    next_state,
    grad_gate,
    grad_sout,
    grad_sqkv,
    back_state,
    state_sums,
    key_sum,
    first,
    qkv,
    mixed,
    residual,
    second,
    hidden,
    back_input,
    back_second,
    mid_sums,
    grad_down,
    qkv_nat,
    down_nat,
    out_nat,
    tok_all,
    send_sem,
    recv_sem,
    st_all,
    cot_all,
    scot_all,
    sqkv_nat,
    sout_nat,
    up_nat,
    slab,
    tb,
    state_norm,
    sqkv,
    read_all,
    back_update,
    back_read,
    back_sqkv,
    own_sum,
    slope,
    res_all,
):
    rows, width = tokens.shape
    state_rows = state.shape[0]
    heads, span = bias.shape
    lanes = heads * head_dim
    depth = w_qkv.shape[0]
    inner_width = up_nat.shape[1]
    scale = head_dim ** (-0.5)
    links = Links()
    s, d = links.s, links.d
    mover = Mover(send_sem, recv_sem)

    def block(i, size):
        return pl.ds(pl.multiple_of(i * size, size), size)

    def own_rows(size):
        return lambda i: (block(i, size), slice(None))

    def own_lanes(size):
        return lambda i: (slice(None), block(i, size))

    own_columns = block(s, lanes)
    to_slab = []
    for k, shard in enumerate((w_qkv, w_sqkv)):
        core_slot = 1 - links.core % 2 + links.core // 2
        x_slot = 2 - 2 * (links.x // 2)
        to_slab.append(
            (
                mover(
                    shard.at[:, block(2 - 2 * (s % 2), lanes)],
                    slab.at[k, :, block(x_slot, lanes)],
                    links.to_x,
                ),
                mover(
                    shard.at[:, lanes : 2 * lanes],
                    slab.at[k, :, block(core_slot, lanes)],
                    links.to_core,
                ),
            )
        )
    get_tokens = GroupGather(mover, links, tok_all, own_rows(rows), tokens)
    get_state = GroupGather(mover, links, st_all, own_rows(state_rows), state)
    get_scot = GroupGather(mover, links, scot_all, own_rows(state_rows), state_cot)
    get_cot = GroupGather(mover, links, cot_all, own_rows(rows), cot)

    def own_out(i):
        return (block(i, depth), own_columns)

    dp_sout = WeightGather(mover, links, sout_nat, own_out, w_sout)
    dp_out = WeightGather(mover, links, out_nat, own_out, w_out)
    dp_qkv = WeightGather(mover, links, qkv_nat, own_rows(depth), slab.at[0])
    dp_sqkv = WeightGather(mover, links, sqkv_nat, own_rows(depth), slab.at[1])
    dp_up = WeightGather(mover, links, up_nat, own_rows(depth), w_up)
    dp_down = WeightGather(mover, links, down_nat, own_lanes(depth), w_down)
    get_sout = GroupGather(mover, links, sout_nat, own_lanes(lanes))
    get_out = GroupGather(mover, links, out_nat, own_lanes(lanes))
    get_mixed = GroupGather(mover, links, mixed, own_lanes(lanes))
    get_read = GroupGather(mover, links, read_all, own_lanes(lanes))

    links.greet()
    for over_x, beside in to_slab:
        over_x.start()
        beside.start()
    dp_sout.start_z()
    dp_out.start_z()
    dp_sout.start_y()
    dp_out.start_y()
    get_tokens.start()
    for k, shard in enumerate((w_qkv, w_sqkv)):
        slab[k, :, block((s + 1) // 2, lanes)] = shard[:, block(2 * (s % 2), lanes)]
    for k, gather in enumerate((dp_qkv, dp_sqkv)):
        for copy in to_slab[k]:
            copy.wait_recv()
        gather.start_z()
        gather.start_y()
    dp_up.start_z()
    dp_down.start_z()
    get_state.start()
    get_scot.start()
    get_cot.start()
    qkv_nat[block(d, depth), :] = slab[0]
    sqkv_nat[block(d, depth), :] = slab[1]
    up_nat[block(d, depth), :] = w_up[...]
    down_nat[:, block(d, depth)] = w_down[...]
    out_nat[block(d, depth), own_columns] = w_out[...]
    sout_nat[block(d, depth), own_columns] = w_sout[...]
    tok_all[block(s, rows), :] = tokens[...]
    cot_all[block(s, rows), :] = cot[...]
    st_all[block(s, state_rows), :] = state[...]
    scot_all[block(s, state_rows), :] = state_cot[...]

    def token_norm(i):
        at = block(i, rows)
        hat, _ = normalized(tok_all[at, :].astype(f32))
        first[at, :] = (hat * gains[0:1, :] + shifts[0:1, :]).astype(bf16)

    token_norm(s)
    for k in range(3):
        dp_sout.forward(k)
        dp_out.forward(k)
    bias_blocks(tb, bias)
    get_tokens.beside.wait_recv()
    token_norm(links.core)
    get_tokens.forward()
    token_norm(links.x)
    dp_sout.finish()
    get_sout.start()
    dp_out.finish()
    get_out.start()
    get_tokens.passed.wait_recv()
    token_norm(flip_low(links.x))
    for k in range(3):
        dp_qkv.forward(k)
    dp_up.start_y()
    get_state.forward()
    get_scot.forward()
    dp_qkv.finish()

    def token_qkv(i, carry):
        at = block(i, rows)
        qkv[at, :] = dot(first[at, :], qkv_nat[...]).astype(bf16)
        return carry

    lax.fori_loop(0, 4, token_qkv, 0)
    for c in range(4):
        count = min(span, (c + 1) * rows)
        low, high = (c + 1) * rows - count, (c + 1) * rows
        last = c * rows if c == 3 else 0
        parts = []
        for h in range(heads):
            probs = window_probs(
                (0, length[0]),
                qkv[c * rows : high, head_cols(0, h, heads, head_dim)],
                qkv[low:high, head_cols(1, h, heads, head_dim)],
                tb[h],
                last,
                scale,
            )
            parts.append(
                dot(probs.astype(bf16), qkv[low:high, head_cols(2, h, heads, head_dim)])
            )
        mixed[c * rows : high, own_columns] = jnp.concatenate(parts, axis=1).astype(bf16)
        if c > 0:
            dp_sqkv.forward(c - 1)
    get_mixed.start()
    get_sout.forward()
    get_cot.forward()
    dp_down.start_y()

    get_state.finish()

    def state_norms(i, carry):
        at = block(i, state_rows)
        hat, _ = normalized(st_all[at, :].astype(f32))
        state_norm[at, :] = (hat * gains[2:3, :] + shifts[2:3, :]).astype(bf16)
        return carry

    lax.fori_loop(0, 4, state_norms, 0)
    dp_sqkv.finish()
    sqkv[...] = dot(state_norm[...], sqkv_nat[...]).astype(bf16)
    get_out.forward()
    dp_up.forward(0)

    def state_read(i, carry):
        at = block(i, state_rows)
        parts = []
        for h in range(heads):
            own, token = state_probs(
                (0, length[0]),
                sqkv[at, head_cols(0, h, heads, head_dim)],
                sqkv[:, head_cols(1, h, heads, head_dim)],
                qkv[:, head_cols(1, h, heads, head_dim)],
                scale,
            )
            parts.append(
                dot(own.astype(bf16), sqkv[:, head_cols(2, h, heads, head_dim)])
                + dot(token.astype(bf16), qkv[:, head_cols(2, h, heads, head_dim)])
            )
        read_all[at, own_columns] = jnp.concatenate(parts, axis=1).astype(bf16)
        return carry

    lax.fori_loop(0, 4, state_read, 0)
    get_read.start()
    dp_up.forward(1)
    get_mixed.forward()

    gate = jax.nn.sigmoid(gate_bias[...])
    get_scot.finish()

    def updates(i, carry):
        at = block(i, state_rows)
        back_update[at, :] = ((1.0 - gate) * scot_all[at, :].astype(f32)).astype(bf16)
        return carry

    lax.fori_loop(0, 4, updates, 0)
    get_sout.finish()
    back_read[...] = dot_rt(back_update[...], sout_nat[block(s, lanes), :]).astype(bf16)
    own_sum[...] = jnp.zeros_like(own_sum)
    key_sum[...] = jnp.zeros_like(key_sum)

    def state_back(h):
        key_at, value_at = head_cols(1, h, heads, head_dim), head_cols(2, h, heads, head_dim)
        query_at, read_at = head_cols(0, h, heads, head_dim), head_cols(0, h, heads, head_dim)

        def one(i, carry):
            at = block(i, state_rows)
            query, back = sqkv[at, query_at], back_read[at, read_at]
            own, token = state_probs(
                (0, length[0]), query, sqkv[:, key_at], qkv[:, key_at], scale
            )
            back_own = dot_rt(back, sqkv[:, value_at])
            back_token = dot_rt(back, qkv[:, value_at])
            row_dot = jnp.sum(own * back_own, axis=-1, keepdims=True) + jnp.sum(
                token * back_token, axis=-1, keepdims=True
            )
            own_raw = (own * (back_own - row_dot) * scale).astype(bf16)
            token_raw = (token * (back_token - row_dot) * scale).astype(bf16)
            back_sqkv[at, query_at] = (
                dot(own_raw, sqkv[:, key_at]) + dot(token_raw, qkv[:, key_at])
            ).astype(bf16)
            key_to = slice(key_at.start - lanes, key_at.stop - lanes)
            value_to = slice(value_at.start - lanes, value_at.stop - lanes)
            own_sum[:, key_to] += dot_lt(own_raw, query)
            own_sum[:, value_to] += dot_lt(own.astype(bf16), back)
            key_sum[:, key_to] += dot_lt(token_raw, query)
            key_sum[:, value_to] += dot_lt(token.astype(bf16), back)
            return carry

        lax.fori_loop(0, 4, one, 0)

    for h in range(heads):
        state_back(h)
        if h == 0:
            dp_up.forward(2)
    back_sqkv[:, lanes:] = own_sum[...].astype(bf16)
    dp_down.forward(0)

    def sqkv_grads(i, carry):
        at = block(i, 256)
        grad_sqkv[at, :] = dot_lt(state_norm[:, at], back_sqkv[...]).astype(bf16)
        return carry

    lax.fori_loop(0, width // 256, sqkv_grads, 0)
    state_sums[...] = jnp.zeros_like(state_sums)

    def state_partial(i, carry):
        at = block(i, state_rows)
        back = dot_rt(back_sqkv[at, :], sqkv_nat[...])
        back_state[at, :] = back.astype(bf16)
        hat, _ = normalized(st_all[at, :].astype(f32))
        state_sums[0:1, :] += jnp.sum(back * hat, axis=0, keepdims=True)
        state_sums[1:2, :] += jnp.sum(back, axis=0, keepdims=True)
        return carry

    lax.fori_loop(0, 4, state_partial, 0)
    get_read.forward()
    dp_down.forward(1)

    get_mixed.finish()
    get_out.finish()
    dp_up.finish()
    get_cot.finish()

    def ffn_rows(i, carry):
        at = block(i, rows)
        total = tok_all[at, :].astype(f32) + dot(mixed[at, :], out_nat[...])
        res_all[at, :] = total
        hat, _ = normalized(total)
        normed = (hat * gains[1:2, :] + shifts[1:2, :]).astype(bf16)
        second[at, :] = normed
        inner = dot(normed, up_nat[...])
        root = 0.7978845608028654
        square = inner * inner
        bend = jnp.tanh(root * inner * (1.0 + 0.044715 * square))
        half = 0.5 * (1.0 + bend)
        hidden[at, :] = (inner * half).astype(bf16)
        slope[at, :] = (
            half + (0.5 * root) * inner * (1.0 - bend * bend) * (1.0 + (3 * 0.044715) * square)
        ).astype(bf16)
        return carry

    lax.fori_loop(0, 4, ffn_rows, 0)
    residual[...] = res_all[block(s, rows), :]
    dp_down.forward(2)

    def down_grads(i, carry):
        at = block(i, 256)
        grad_down[:, at] = dot_lt(hidden[...], cot_all[:, at]).astype(bf16)
        return carry

    lax.fori_loop(0, width // 256, down_grads, 0)

    get_read.finish()
    own_state = block(s, state_rows)
    update = dot(read_all[own_state, :], sout_nat[...])
    held = state[...].astype(f32)
    own_cot = state_cot[...].astype(f32)
    next_state[...] = (gate * held + (1.0 - gate) * update).astype(bf16)
    grad_gate[...] = jnp.sum(own_cot * (held - update), axis=0, keepdims=True) * (
        gate * (1.0 - gate)
    )
    grad_sout[...] = dot_lt(read_all[...], back_update[:, own_columns]).astype(bf16)

    dp_down.finish()
    mid_sums[...] = jnp.zeros_like(mid_sums)

    def ffn_back_rows(i, carry):
        at = block(i, rows)
        inner = (dot_rt(cot_all[at, :], down_nat[...]) * slope[at, :].astype(f32)).astype(bf16)
        back_input[at, :] = inner
        back = dot_rt(inner, up_nat[...])
        back_second[at, :] = back.astype(bf16)
        hat, _ = normalized(res_all[at, :])
        mid_sums[0:1, :] += jnp.sum(back * hat, axis=0, keepdims=True)
        mid_sums[1:2, :] += jnp.sum(back, axis=0, keepdims=True)
        return carry

    lax.fori_loop(0, 4, ffn_back_rows, 0)
    for over_x, beside in to_slab:
        over_x.wait_send()
        beside.wait_send()
    for gather in (
        get_tokens,
        get_state,
        get_scot,
        get_cot,
        dp_sout,
        dp_out,
        dp_qkv,
        dp_sqkv,
        dp_up,
        dp_down,
        get_sout,
        get_out,
        get_mixed,
        get_read,
    ):
        gather.sent()
    assert mover.used <= FRONT_COPIES


def norm_back(values, back, gain):
    hat, inverse = normalized(values)
    grown = back * gain
    return inverse * (
        grown
        - jnp.mean(grown, axis=-1, keepdims=True)
        - hat * jnp.mean(grown * hat, axis=-1, keepdims=True)
    )


def per_device(
    tokens,
    state_in,
    cotangent,
    state_cotangent,
    seq_len,
    bucket_table,
    w_qkv,
    w_out,
    w_sqkv,
    w_sout,
    w_up,
    w_down,
    rel_table,
    norm_gain,
    norm_shift,
    gate_bias,
):
    rows, width = tokens.shape
    bucket_count, head_count = rel_table.shape
    window = bucket_table.shape[0]
    state_rows = state_in.shape[1]
    places = lax.axis_size("state")
    assert places == len(PLACES)
    dp_count = lax.axis_size("dp")
    here, dp_here = lax.axis_index("state"), lax.axis_index("dp")
    head_dim = width // head_count
    heads = head_count // places
    lanes = heads * head_dim
    span = window + rows
    group_rows = rows * places
    all_states = state_rows * places
    inner_width = w_up.shape[1]
    hops = dp_count == len(DP_PLACES)
    blocks = dp_count if hops else 1

    def swap(value, axis, bit):
        count = lax.axis_size(axis)
        return lax.ppermute(value, axis, [(i, i ^ bit) for i in range(count)])

    def from_group(value):
        pair = jnp.stack([value, swap(value, "state", 2)])
        return jnp.concatenate([pair, swap(pair, "state", 1)], axis=0)

    def list_from_group(value):
        across = swap(value, "state", 2)
        return [value, across, swap(value, "state", 1), swap(across, "state", 1)]

    def sum_to_owner(partial):
        half = partial.shape[0] // 2
        pair = partial[:half].astype(f32) + swap(partial[half:], "state", 1).astype(f32)
        return pair[0] + swap(pair[1].astype(bf16), "state", 2).astype(f32)

    def from_dp(block, axis):
        if not hops:
            return lax.all_gather(block, "dp", axis=axis, tiled=True)[None]
        gathered = block[None]
        for bit in DP_STEPS:
            gathered = jnp.concatenate([gathered, swap(gathered, "dp", bit)], axis=0)
        return gathered

    def sum_over_dp(partial, axis):
        if not hops:
            return lax.psum_scatter(partial[0], "dp", scatter_dimension=axis, tiled=True).astype(f32)
        for bit in reversed(DP_STEPS):
            half = partial.shape[0] // 2
            arrived = swap(partial[half:], "dp", bit)
            total = partial[:half].astype(f32) + arrived.astype(f32)
            partial = total.astype(bf16)
        return total[0]

    def sum_over_all(vector):
        if not hops:
            return lax.psum(vector, ("dp", "state"))
        for axis, bit in (("state", 1), ("state", 2), ("dp", 1), ("dp", 2), ("dp", 4)):
            vector = vector + swap(vector, axis, bit)
        return vector

    even = here % 2 == 0

    def pick(*by_place):
        value = by_place[-1]
        for i in reversed(range(places - 1)):
            value = jnp.where(here == i, by_place[i], value)
        return value

    def to_heads(shard):
        left, middle, right = (shard[:, i * lanes : (i + 1) * lanes] for i in range(3))
        own = jnp.where(even, left, right)
        across = swap(jnp.where(even, right, left), "state", 2)
        beside = swap(middle, "state", 1)
        query = pick(own, beside, across, across)
        keys = pick(beside, own, own, beside)
        values = pick(across, across, beside, own)
        return jnp.concatenate([query, keys, values], axis=1)

    def from_heads(grads):
        query, keys, values = (grads[:, i * lanes : (i + 1) * lanes] for i in range(3))
        own = pick(query, keys, keys, values)
        beside = swap(pick(keys, query, values, keys), "state", 1)
        across = swap(pick(values, values, query, query), "state", 2)
        return jnp.concatenate(
            [jnp.where(even, own, across), beside, jnp.where(even, across, own)], axis=1
        )

    if hops:
        block_list = dp_here ^ jnp.array(DP_PLACES, jnp.int32)
        position_list = jnp.array(
            [DP_PLACES.index(i) for i in range(dp_count)], jnp.int32
        )[dp_here ^ jnp.arange(dp_count)]
    else:
        block_list = position_list = jnp.zeros((1,), jnp.int32)
    scal = jnp.concatenate(
        [here[None].astype(jnp.int32), seq_len.astype(jnp.int32), block_list, position_list]
    ).astype(jnp.int32)

    lookup = (bucket_table[:, None] == jnp.arange(bucket_count)[None, :]).astype(f32)
    own_table = lax.dynamic_slice_in_dim(rel_table, here * heads, heads, 1)
    bias_rows = jnp.dot(
        own_table.T, lookup.T, precision=lax.Precision.HIGHEST, preferred_element_type=f32
    )
    bias = jnp.concatenate(
        [
            jnp.full((heads, 1), masked_value, f32),
            bias_rows[:, ::-1],
            jnp.full((heads, span - window - 1), masked_value, f32),
        ],
        axis=1,
    )
    gains = [norm_gain[i : i + 1] for i in range(3)]
    shifts = [norm_shift[i : i + 1] for i in range(3)]

    depth = w_qkv.shape[0]
    if hops:
        (
            next_state,
            grad_gate,
            grad_sout,
            grad_sqkv,
            back_state_norm,
            state_sums,
            token_back,
            first,
            qkv,
            mixed,
            residual_own,
            second,
            hidden,
            back_input,
            back_second,
            mid_sums,
            grad_down,
            qkv_nat,
            down_nat,
            out_nat,
            tok_all,
        ) = pl.pallas_call(
            functools.partial(front, head_dim),
            out_shape=[
                out((state_rows, width)),
                out((1, width), f32),
                out((width, lanes)),
                out((width, 3 * lanes)),
                out((all_states, width)),
                out((2, width), f32),
                out((group_rows, 2 * lanes), f32),
                out((group_rows, width)),
                out((group_rows, 3 * lanes)),
                out((group_rows, width)),
                out((rows, width), f32),
                out((group_rows, width)),
                out((group_rows, inner_width)),
                out((group_rows, inner_width)),
                out((group_rows, width)),
                out((2, width), f32),
                out((inner_width, width)),
                out((width, 3 * lanes)),
                out((inner_width, width)),
                out((width, width)),
                out((group_rows, width)),
            ],
            in_specs=[pl.BlockSpec(memory_space=pltpu.SMEM)]
            + [pl.BlockSpec(memory_space=pltpu.VMEM)] * 14,
            out_specs=[pl.BlockSpec(memory_space=pltpu.VMEM)] * 21,
            scratch_shapes=[
                pltpu.SemaphoreType.DMA((FRONT_COPIES,)),
                pltpu.SemaphoreType.DMA((FRONT_COPIES,)),
                pltpu.VMEM((all_states, width), bf16),
                pltpu.VMEM((group_rows, width), bf16),
                pltpu.VMEM((all_states, width), bf16),
                pltpu.VMEM((width, 3 * lanes), bf16),
                pltpu.VMEM((width, width), bf16),
                pltpu.VMEM((width, inner_width), bf16),
                pltpu.VMEM((2, depth, 3 * lanes), bf16),
                pltpu.VMEM((heads, rows, span), f32),
                pltpu.VMEM((all_states, width), bf16),
                pltpu.VMEM((all_states, 3 * lanes), bf16),
                pltpu.VMEM((all_states, width), bf16),
                pltpu.VMEM((all_states, width), bf16),
                pltpu.VMEM((all_states, lanes), bf16),
                pltpu.VMEM((all_states, 3 * lanes), bf16),
                pltpu.VMEM((all_states, 2 * lanes), f32),
                pltpu.VMEM((group_rows, inner_width), bf16),
                pltpu.VMEM((group_rows, width), f32),
            ],
            compiler_params=pltpu.CompilerParams(
                collective_id=0, has_side_effects=True, vmem_limit_bytes=64 << 20
            ),
            name="front",
        )(
            seq_len,
            tokens,
            state_in[0],
            cotangent,
            state_cotangent[0],
            w_qkv,
            w_out,
            w_sqkv,
            w_sout,
            w_up,
            w_down,
            bias,
            norm_gain,
            norm_shift,
            gate_bias[None],
        )
        turned = here ^ jnp.array(PLACES, jnp.int32)
        to_places = lambda v: v.reshape(places, -1, v.shape[-1])[turned]
        to_blocks = lambda v: v.reshape(blocks, -1, v.shape[-1])[block_list]
        lane_blocks = lambda v: v.reshape(v.shape[0], blocks, -1).transpose(1, 0, 2)[block_list]
        grad_sout, grad_sqkv = to_blocks(grad_sout), to_blocks(grad_sqkv)
        grad_down = lane_blocks(grad_down)
        back_state_norm, back_second = to_places(back_state_norm), to_places(back_second)
        full_qkv, full_down = to_blocks(qkv_nat), lane_blocks(down_nat)
        out_rows = lax.dynamic_slice_in_dim(out_nat, here * lanes, lanes, 0)
        all_tokens = to_places(tok_all)
        mixed_parts = [
            lax.dynamic_slice_in_dim(mixed, turned[p] * lanes, lanes, 1).reshape(places, rows, lanes)
            for p in range(places)
        ]
    else:
        both = to_heads(jnp.concatenate([w_qkv, w_sqkv], axis=0))
        full_qkv = from_dp(both[:depth], 0)
        all_tokens = from_group(tokens)
        full_sqkv = from_dp(both[depth:], 0)
        all_state = from_group(state_in[0])
        all_cot = from_group(cotangent)
        all_state_cot = from_group(state_cotangent[0])
        outs_pair = from_dp(jnp.concatenate([w_out, w_sout], axis=1), 0)
        half = outs_pair.shape[2] // 2
        full_sout = list_from_group(outs_pair[:, :, half:])
        full_out = list_from_group(outs_pair[:, :, :half])
        full_up = from_dp(w_up, 0)
        full_down = from_dp(w_down, 1)

        first, qkv, mixed = call(
            functools.partial(token_forward, head_dim),
            "token_forward",
            [out((group_rows, width)), out((group_rows, 3 * lanes)), out((places, rows, lanes))],
            [pltpu.VMEM((width, 3 * lanes), bf16), pltpu.VMEM((heads, rows, span), f32)],
            2 * group_rows * width * 3 * lanes,
            group_rows * span * heads,
            scal,
            all_tokens,
            gains[0],
            shifts[0],
            full_qkv,
            bias,
        )
        mixed_parts = list_from_group(mixed)

        state_norm, sqkv, read = call(
            functools.partial(state_forward, head_dim),
            "state_forward",
            [
                out((all_states, width)),
                out((all_states, 3 * lanes)),
                out((places, state_rows, lanes)),
            ],
            [pltpu.VMEM((width, 3 * lanes), bf16)],
            2 * all_states * width * 3 * lanes,
            all_states * (all_states + group_rows) * heads,
            scal,
            all_state,
            gains[2],
            shifts[2],
            full_sqkv,
            qkv,
        )
        read_parts = list_from_group(read)

        next_state, grad_gate, grad_sout, token_back, grad_sqkv, back_state_norm, state_sums = call(
            functools.partial(state_backward, head_dim),
            "state_backward",
            [
                out((state_rows, width)),
                out((1, width), f32),
                out((blocks, width // blocks, lanes)),
                out((group_rows, 2 * lanes), f32),
                out((blocks, width // blocks, 3 * lanes)),
                out((places, state_rows, width)),
                out((2, width), f32),
            ],
            [
                pltpu.VMEM((width, 3 * lanes), bf16),
                pltpu.VMEM((width, width), bf16),
                pltpu.VMEM((all_states, width), bf16),
                pltpu.VMEM((all_states, lanes), bf16),
                pltpu.VMEM((all_states, 3 * lanes), bf16),
                pltpu.VMEM((all_states, 2 * lanes), f32),
            ],
            4 * all_states * width * 4 * lanes,
            all_states * (all_states + group_rows) * heads,
            scal,
            state_in[0],
            all_state_cot,
            gate_bias[None],
            all_state,
            *read_parts,
            *full_sout,
            sqkv,
            qkv,
            state_norm,
            full_sqkv,
        )
        residual, second, hidden, slope, out_rows, grad_down = call(
            ffn_up,
            "ffn_up",
            [
                out((places, rows, width), f32),
                out((group_rows, width)),
                out((group_rows, inner_width)),
                out((group_rows, inner_width)),
                out((lanes, width)),
                out((blocks, inner_width, width // blocks)),
            ],
            [pltpu.VMEM((width, width), bf16), pltpu.VMEM((width, inner_width), bf16)],
            2 * group_rows * width * (width + 2 * inner_width),
            group_rows * inner_width,
            scal,
            all_tokens,
            *mixed_parts,
            *full_out,
            gains[1],
            shifts[1],
            full_up,
            all_cot,
        )

        back_second, back_input, mid_sums = call(
            ffn_back,
            "ffn_back",
            [
                out((places, rows, width)),
                out((group_rows, inner_width)),
                out((2, width), f32),
            ],
            [pltpu.VMEM((inner_width, width), bf16), pltpu.VMEM((width, inner_width), bf16)],
            4 * group_rows * width * inner_width,
            0,
            scal,
            all_cot,
            full_down,
            full_up,
            slope,
            residual,
        )
        residual_own = residual[0]
    own_grad_sout = sum_over_dp(grad_sout, 0)
    own_grad_sqkv = sum_over_dp(grad_sqkv, 0)
    back_state = sum_to_owner(back_state_norm)
    gate_open = jax.nn.sigmoid(gate_bias)
    grad_state = (
        gate_open * state_cotangent[0].astype(f32)
        + norm_back(state_in[0].astype(f32), back_state, norm_gain[2])
    ).astype(bf16)

    own_grad_down = sum_over_dp(grad_down, 1)
    back_second = sum_to_owner(back_second)
    back_residual = cotangent.astype(f32) + norm_back(residual_own, back_second, norm_gain[1])
    back_branch = from_group(back_residual.astype(bf16))

    ffn_partial, grad_up = call(
        ffn_rest,
        "ffn_rest",
        [out((places, rows, width)), out((blocks, width // blocks, inner_width))],
        [pltpu.VMEM((inner_width, width), bf16)],
        4 * group_rows * width * inner_width,
        0,
        scal,
        hidden,
        full_down,
        second,
        back_input,
    )
    own_grad_up = sum_over_dp(grad_up, 0)
    if hops:
        ffn_partial = to_places(ffn_partial)
    output = (residual_own + sum_to_owner(ffn_partial)).astype(bf16)

    (grad_out,) = call(
        out_grad,
        "out_grad",
        [out((blocks, width // blocks, lanes))],
        [],
        2 * group_rows * width * lanes,
        0,
        scal,
        back_branch,
        *mixed_parts,
    )
    own_grad_out = sum_over_dp(grad_out, 0)

    grad_qkv, back_first, first_sums, distance = call(
        functools.partial(token_backward, head_dim),
        "token_backward",
        [
            out((blocks, width // blocks, 3 * lanes)),
            out((places, rows, width)),
            out((2, width), f32),
            out((heads, span), f32),
        ],
        [
            pltpu.VMEM((width, 3 * lanes), bf16),
            pltpu.VMEM((heads, rows, span), f32),
            pltpu.VMEM((group_rows, lanes), bf16),
            pltpu.VMEM((group_rows, 3 * lanes), bf16),
            pltpu.VMEM((group_rows, 2 * lanes), f32),
            pltpu.VMEM((rows, span), f32),
        ],
        2 * group_rows * width * 7 * lanes,
        group_rows * span * heads,
        scal,
        back_branch,
        out_rows,
        qkv,
        bias,
        token_back,
        first,
        all_tokens,
        full_qkv,
    )
    back_first = sum_to_owner(back_first)
    grad_tokens = (
        norm_back(tokens.astype(f32), back_first, norm_gain[0]) + back_residual
    ).astype(bf16)
    own_grad_qkv = sum_over_dp(grad_qkv, 0)
    both_grads = from_heads(
        jnp.concatenate([own_grad_qkv, own_grad_sqkv], axis=0).astype(bf16)
    ).astype(f32)

    per_distance = distance[:, 1 : window + 1][:, ::-1]
    own_rel = jnp.dot(
        per_distance, lookup, precision=lax.Precision.HIGHEST, preferred_element_type=f32
    ).T
    grad_rel = lax.dynamic_update_slice_in_dim(
        jnp.zeros((bucket_count, head_count), f32), own_rel, here * heads, 1
    )
    small = [
        jnp.stack([first_sums[0], mid_sums[0], state_sums[0]]),
        jnp.stack([first_sums[1], mid_sums[1], state_sums[1]]),
        grad_gate[0],
        grad_rel,
    ]
    packed = sum_over_all(jnp.concatenate([v.reshape(-1, 128) for v in small], axis=0))
    unpacked, start = [], 0
    for v in small:
        count = v.size // 128
        unpacked.append(packed[start : start + count].reshape(v.shape))
        start += count
    return (
        output,
        next_state[None],
        grad_tokens,
        grad_state[None],
        both_grads[:depth],
        own_grad_out,
        both_grads[depth:],
        own_grad_sout,
        own_grad_up,
        own_grad_down,
        unpacked[3],
        unpacked[0],
        unpacked[1],
        unpacked[2],
    )


def solution(mesh):
    rows_spec = P(("dp", "state"), None)
    state_spec = P("dp", "state", None)
    weight_spec = P("dp", "state")
    return jax.shard_map(
        per_device,
        mesh=mesh,
        in_specs=(
            rows_spec,
            state_spec,
            rows_spec,
            state_spec,
            P("dp"),
            P(),
            weight_spec,
            weight_spec,
            weight_spec,
            weight_spec,
            weight_spec,
            P("state", "dp"),
            P(),
            P(),
            P(),
            P(),
        ),
        out_specs=(
            rows_spec,
            state_spec,
            rows_spec,
            state_spec,
            weight_spec,
            weight_spec,
            weight_spec,
            weight_spec,
            weight_spec,
            P("state", "dp"),
            P(),
            P(),
            P(),
            P(),
        ),
        check_vma=False,
    )
```

```python
import functools

import jax
import jax.numpy as jnp
from jax import lax
from jax.experimental import pallas as pl
from jax.experimental.pallas import tpu as pltpu
from jax.sharding import PartitionSpec as P

epsilon = 1e-05
masked_value = -1e30
f32 = jnp.float32
bf16 = jnp.bfloat16

PLACES = (0, 2, 1, 3)
DP_STEPS = (2, 4, 1)
DP_PLACES = (0, 2, 4, 6, 1, 3, 5, 7)


def dot(left, right):
    return lax.dot_general(left, right, (((1,), (0,)), ((), ())), preferred_element_type=f32)


def dot_rt(left, right):
    return lax.dot_general(left, right, (((1,), (1,)), ((), ())), preferred_element_type=f32)


def dot_lt(left, right):
    return lax.dot_general(left, right, (((0,), (0,)), ((), ())), preferred_element_type=f32)


def where_from(sender, place):
    return PLACES.index(PLACES[sender] ^ PLACES[place])


def normalized(values):
    centre = jnp.mean(values, axis=-1, keepdims=True)
    centred = values - centre
    spread = jnp.mean(centred * centred, axis=-1, keepdims=True)
    inverse = lax.rsqrt(spread + epsilon)
    return centred * inverse, inverse


def normed_back(back, hat, inverse, gain):
    grown = back * gain
    return inverse * (
        grown
        - jnp.mean(grown, axis=-1, keepdims=True)
        - hat * jnp.mean(grown * hat, axis=-1, keepdims=True)
    )


def place_of(scal, q):
    return scal[0] ^ PLACES[q]


def aligned(start, size):
    return pl.ds(pl.multiple_of(start, size), size)


def block_at(scal, q):
    return scal[2 + q]


def position_of(scal, block, blocks):
    return scal[2 + blocks + block]


def rows_in_order(scal, target, source):
    blocks, depth = source.shape[0], source.shape[1]
    for q in range(blocks):
        target[aligned(block_at(scal, q) * depth, depth), :] = source[q]


def columns_in_order(scal, target, source):
    blocks, depth = source.shape[0], source.shape[2]
    for q in range(blocks):
        target[:, aligned(block_at(scal, q) * depth, depth)] = source[q]


def put_rows(scal, target, start, value):
    blocks, depth = target.shape[0], target.shape[1]
    rows = value.shape[0]
    if depth >= rows:
        target[position_of(scal, start // depth, blocks), aligned(start % depth, rows), :] = value
    else:
        for i in range(rows // depth):
            position = position_of(scal, start // depth + i, blocks)
            target[position] = value[i * depth : (i + 1) * depth]


def put_columns(scal, target, start, value):
    blocks, depth = target.shape[0], target.shape[2]
    columns = value.shape[1]
    if depth >= columns:
        target[position_of(scal, start // depth, blocks), :, aligned(start % depth, columns)] = value
    else:
        for i in range(columns // depth):
            position = position_of(scal, start // depth + i, blocks)
            target[position] = value[:, i * depth : (i + 1) * depth]


def call(body, name, outs, scratch, flops, exps, *args):
    sizes = sum(a.size * a.dtype.itemsize for a in args) + sum(
        a.size * a.dtype.itemsize for a in outs
    )
    in_specs = [pl.BlockSpec(memory_space=pltpu.SMEM)] + [
        pl.BlockSpec(memory_space=pltpu.VMEM) for _ in args[1:]
    ]
    return pl.pallas_call(
        body,
        out_shape=outs,
        in_specs=in_specs,
        out_specs=[pl.BlockSpec(memory_space=pltpu.VMEM) for _ in outs],
        scratch_shapes=scratch,
        compiler_params=pltpu.CompilerParams(vmem_limit_bytes=56 << 20),
        cost_estimate=pl.CostEstimate(flops=flops, bytes_accessed=sizes, transcendentals=exps),
        name=name,
    )(*args)


def out(shape, kind=bf16):
    return jax.ShapeDtypeStruct(shape, kind)


def by_distance(scores):
    rows, span = scores.shape
    row_at = lax.broadcasted_iota(jnp.int32, scores.shape, 0)
    step = 1
    while step < rows:
        scores = jnp.where(row_at & step != 0, pltpu.roll(scores, span - step, 1), scores)
        step *= 2
    return scores


def bias_blocks(tb, bias):
    heads, rows, span = tb.shape
    for h in range(heads):
        row = jnp.broadcast_to(bias[h : h + 1, :], (rows, span))
        tb[h] = pltpu.roll(row, 0, 1, stride=1, stride_axis=0)


def window_probs(scal, query, keys, tb_block, last, scale):
    rows, span = tb_block.shape
    count = keys.shape[0]
    scores = dot_rt(query, keys) * scale + tb_block[:, span - count :]
    if last:
        row_at = lax.broadcasted_iota(jnp.int32, scores.shape, 0)
        col_at = lax.broadcasted_iota(jnp.int32, scores.shape, 1)
        ahead = col_at - (count - rows)
        live = (ahead < scal[1] - last) | (ahead == row_at)
        scores = jnp.where(live, scores, masked_value)
    top = jnp.max(scores, axis=-1, keepdims=True)
    grown = jnp.exp(scores - top)
    return grown * (1.0 / jnp.sum(grown, axis=-1, keepdims=True))


def state_probs(scal, query, state_keys, keys, scale):
    own = dot_rt(query, state_keys) * scale
    token = dot_rt(query, keys) * scale
    col_at = lax.broadcasted_iota(jnp.int32, token.shape, 1)
    token = jnp.where(col_at < scal[1], token, masked_value)
    top = jnp.maximum(
        jnp.max(own, axis=-1, keepdims=True), jnp.max(token, axis=-1, keepdims=True)
    )
    own = jnp.exp(own - top)
    token = jnp.exp(token - top)
    total = jnp.sum(own, axis=-1, keepdims=True) + jnp.sum(token, axis=-1, keepdims=True)
    inverse = 1.0 / total
    return own * inverse, token * inverse


def head_cols(block, h, heads, head_dim):
    start = (block * heads + h) * head_dim
    return slice(start, start + head_dim)


def token_forward(head_dim, scal, tokens, gain, shift, w_qkv, bias, first, qkv, mixed, w_nat, tb):
    places, rows, width = tokens.shape
    heads = bias.shape[0]
    span = bias.shape[1]
    scale = head_dim ** (-0.5)
    rows_in_order(scal, w_nat, w_qkv)
    bias_blocks(tb, bias)
    for q in range(places):
        hat, _ = normalized(tokens[q].astype(f32))
        normed = (hat * gain[...] + shift[...]).astype(bf16)
        at = aligned(place_of(scal, q) * rows, rows)
        first[at, :] = normed
        qkv[at, :] = dot(normed, w_nat[...]).astype(bf16)
    for c in range(places):
        count = min(span, (c + 1) * rows)
        low, high = (c + 1) * rows - count, (c + 1) * rows
        last = c * rows if c == places - 1 else 0
        parts = []
        for h in range(heads):
            probs = window_probs(
                scal,
                qkv[c * rows : high, head_cols(0, h, heads, head_dim)],
                qkv[low:high, head_cols(1, h, heads, head_dim)],
                tb[h],
                last,
                scale,
            )
            parts.append(
                dot(probs.astype(bf16), qkv[low:high, head_cols(2, h, heads, head_dim)])
            )
        mixed[c] = jnp.concatenate(parts, axis=1).astype(bf16)


def state_forward(
    head_dim, scal, state, gain, shift, w_sqkv, qkv, normed_out, sqkv, read, w_nat
):
    places, rows, width = state.shape
    heads = qkv.shape[1] // (3 * head_dim)
    scale = head_dim ** (-0.5)
    rows_in_order(scal, w_nat, w_sqkv)
    for q in range(places):
        hat, _ = normalized(state[q].astype(f32))
        normed = (hat * gain[...] + shift[...]).astype(bf16)
        normed_out[q * rows : (q + 1) * rows, :] = normed
        sqkv[q * rows : (q + 1) * rows, :] = dot(normed, w_nat[...]).astype(bf16)
    for q in range(places):
        parts = []
        for h in range(heads):
            own, token = state_probs(
                scal,
                sqkv[q * rows : (q + 1) * rows, head_cols(0, h, heads, head_dim)],
                sqkv[:, head_cols(1, h, heads, head_dim)],
                qkv[:, head_cols(1, h, heads, head_dim)],
                scale,
            )
            parts.append(
                dot(own.astype(bf16), sqkv[:, head_cols(2, h, heads, head_dim)])
                + dot(token.astype(bf16), qkv[:, head_cols(2, h, heads, head_dim)])
            )
        read[q] = jnp.concatenate(parts, axis=1).astype(bf16)


def assembled(scal, target, parts):
    for p, part in enumerate(parts):
        blocks, depth, columns = part.shape
        at = aligned(place_of(scal, p) * columns, columns)
        for q in range(blocks):
            target[aligned(block_at(scal, q) * depth, depth), at] = part[q]


def state_backward(
    head_dim,
    scal,
    state_own,
    state_cot,
    gate_bias,
    state,
    read0,
    read1,
    read2,
    read3,
    out0,
    out1,
    out2,
    out3,
    sqkv,
    qkv,
    normed,
    w_sqkv,
    next_state,
    grad_gate,
    grad_sout,
    token_back,
    grad_sqkv,
    back_norm,
    grad_norm,
    w_nat,
    w_out,
    back_update,
    back_read,
    back_sqkv,
    own_sum,
):
    places, rows, width = state_cot.shape
    reads = (read0, read1, read2, read3)
    heads = qkv.shape[1] // (3 * head_dim)
    lanes = heads * head_dim
    scale = head_dim ** (-0.5)
    rows_in_order(scal, w_nat, w_sqkv)
    assembled(scal, w_out, (out0, out1, out2, out3))
    gate = jax.nn.sigmoid(gate_bias[...])
    update = None
    for p in range(places):
        term = dot(reads[p][p], w_out[aligned(place_of(scal, p) * lanes, lanes), :])
        update = term if update is None else update + term
    held = state_own[...].astype(f32)
    cot = state_cot[0].astype(f32)
    next_state[...] = (gate * held + (1.0 - gate) * update).astype(bf16)
    grad_gate[...] = jnp.sum(cot * (held - update), axis=0, keepdims=True) * (gate * (1.0 - gate))
    for q in range(places):
        back_update[q * rows : (q + 1) * rows, :] = (
            (1.0 - gate) * state_cot[q].astype(f32)
        ).astype(bf16)
    own_columns = back_update[:, aligned(scal[0] * lanes, lanes)]
    for p in range(places):
        stack = jnp.concatenate([reads[p][where_from(p, q)] for q in range(places)], axis=0)
        put_rows(
            scal, grad_sout, place_of(scal, p) * lanes, dot_lt(stack, own_columns).astype(bf16)
        )
    back_read[...] = dot_rt(
        back_update[...], w_out[aligned(scal[0] * lanes, lanes), :]
    ).astype(bf16)
    for h in range(heads):
        key_at, value_at = head_cols(1, h, heads, head_dim), head_cols(2, h, heads, head_dim)
        query_at, read_at = head_cols(0, h, heads, head_dim), slice(h * head_dim, (h + 1) * head_dim)
        for q in range(places):
            at = slice(q * rows, (q + 1) * rows)
            query, back = sqkv[at, query_at], back_read[at, read_at]
            own, token = state_probs(scal, query, sqkv[:, key_at], qkv[:, key_at], scale)
            back_own = dot_rt(back, sqkv[:, value_at])
            back_token = dot_rt(back, qkv[:, value_at])
            row_dot = jnp.sum(own * back_own, axis=-1, keepdims=True) + jnp.sum(
                token * back_token, axis=-1, keepdims=True
            )
            own_raw = (own * (back_own - row_dot) * scale).astype(bf16)
            token_raw = (token * (back_token - row_dot) * scale).astype(bf16)
            back_sqkv[at, query_at] = (
                dot(own_raw, sqkv[:, key_at]) + dot(token_raw, qkv[:, key_at])
            ).astype(bf16)
            terms = (
                (own_sum, key_at, dot_lt(own_raw, query)),
                (own_sum, value_at, dot_lt(own.astype(bf16), back)),
                (token_back, key_at, dot_lt(token_raw, query)),
                (token_back, value_at, dot_lt(token.astype(bf16), back)),
            )
            for target, columns, term in terms:
                columns = slice(columns.start - lanes, columns.stop - lanes)
                if q == 0:
                    target[:, columns] = term
                else:
                    target[:, columns] += term
    back_sqkv[:, lanes:] = own_sum[...].astype(bf16)
    for start in range(0, width, 256):
        put_rows(
            scal,
            grad_sqkv,
            start,
            dot_lt(normed[:, start : start + 256], back_sqkv[...]).astype(bf16),
        )
    gain_sum, shift_sum = None, None
    for q in range(places):
        back = dot_rt(back_sqkv[q * rows : (q + 1) * rows, :], w_nat[...])
        back_norm[q] = back.astype(bf16)
        hat, _ = normalized(state[q].astype(f32))
        gain_term = jnp.sum(back * hat, axis=0, keepdims=True)
        shift_term = jnp.sum(back, axis=0, keepdims=True)
        gain_sum = gain_term if q == 0 else gain_sum + gain_term
        shift_sum = shift_term if q == 0 else shift_sum + shift_term
    grad_norm[0:1, :] = gain_sum
    grad_norm[1:2, :] = shift_sum


def ffn_up(
    scal,
    tokens,
    mixed0,
    mixed1,
    mixed2,
    mixed3,
    out0,
    out1,
    out2,
    out3,
    gain,
    shift,
    w_up,
    cot,
    residual,
    second,
    hidden,
    slope,
    out_rows,
    grad_down,
    w_out,
    w_nat,
):
    places, rows, width = tokens.shape
    mixed = (mixed0, mixed1, mixed2, mixed3)
    lanes = mixed0.shape[2]
    assembled(scal, w_out, (out0, out1, out2, out3))
    out_rows[...] = w_out[aligned(scal[0] * lanes, lanes), :]
    rows_in_order(scal, w_nat, w_up)
    for q in range(places):
        total = tokens[q].astype(f32)
        for p in range(places):
            total += dot(
                mixed[p][place_of(scal, q)], w_out[aligned(place_of(scal, p) * lanes, lanes), :]
            )
        residual[q] = total
        hat, _ = normalized(total)
        normed = (hat * gain[...] + shift[...]).astype(bf16)
        at = slice(q * rows, (q + 1) * rows)
        second[at, :] = normed
        inner = dot(normed, w_nat[...])
        root = 0.7978845608028654
        square = inner * inner
        bend = jnp.tanh(root * inner * (1.0 + 0.044715 * square))
        half = 0.5 * (1.0 + bend)
        hidden[at, :] = (inner * half).astype(bf16)
        slope[at, :] = (
            half + (0.5 * root) * inner * (1.0 - bend * bend) * (1.0 + (3 * 0.044715) * square)
        ).astype(bf16)
    for start in range(0, width, 256):
        columns = jnp.concatenate([cot[q, :, start : start + 256] for q in range(places)], axis=0)
        put_columns(scal, grad_down, start, dot_lt(hidden[...], columns).astype(bf16))


def ffn_back(
    scal,
    cot,
    w_down,
    w_up,
    slope,
    residual,
    back_second,
    back_input,
    grad_norm,
    w_nat,
    w_up_nat,
):
    places, rows, width = cot.shape
    columns_in_order(scal, w_nat, w_down)
    rows_in_order(scal, w_up_nat, w_up)
    gain_sum, shift_sum = None, None
    for q in range(places):
        at = slice(q * rows, (q + 1) * rows)
        inner = (dot_rt(cot[q], w_nat[...]) * slope[at, :].astype(f32)).astype(bf16)
        back_input[at, :] = inner
        back = dot_rt(inner, w_up_nat[...])
        back_second[q] = back.astype(bf16)
        hat, _ = normalized(residual[q])
        gain_term = jnp.sum(back * hat, axis=0, keepdims=True)
        shift_term = jnp.sum(back, axis=0, keepdims=True)
        gain_sum = gain_term if q == 0 else gain_sum + gain_term
        shift_sum = shift_term if q == 0 else shift_sum + shift_term
    grad_norm[0:1, :] = gain_sum
    grad_norm[1:2, :] = shift_sum


def ffn_rest(scal, hidden, w_down, second, back_input, partial, grad_up, w_nat):
    places, rows, width = partial.shape
    for start in range(0, width, 256):
        put_rows(
            scal,
            grad_up,
            start,
            dot_lt(second[:, start : start + 256], back_input[...]).astype(bf16),
        )
    columns_in_order(scal, w_nat, w_down)
    for q in range(places):
        partial[q] = dot(hidden[q * rows : (q + 1) * rows, :], w_nat[...]).astype(bf16)


def out_grad(scal, back_branch, mixed0, mixed1, mixed2, mixed3, grad_out):
    places, rows, width = back_branch.shape
    mixed = (mixed0, mixed1, mixed2, mixed3)
    lanes = mixed0.shape[2]
    own_at = aligned(scal[0] * lanes, lanes)
    own_columns = jnp.concatenate([back_branch[q, :, own_at] for q in range(places)], axis=0)
    for p in range(places):
        stack = jnp.concatenate([mixed[p][place_of(scal, q)] for q in range(places)], axis=0)
        put_rows(
            scal, grad_out, place_of(scal, p) * lanes, dot_lt(stack, own_columns).astype(bf16)
        )


def token_backward(
    head_dim,
    scal,
    back_branch,
    out_rows,
    qkv,
    bias,
    token_back,
    first,
    tokens,
    w_qkv,
    grad_qkv,
    back_first,
    grad_norm,
    distance,
    w_nat,
    tb,
    back_mixed,
    back_qkv,
    key_sum,
    band,
):
    places, rows, width = back_branch.shape
    heads, span = bias.shape
    lanes = heads * head_dim
    scale = head_dim ** (-0.5)
    rows_in_order(scal, w_nat, w_qkv)
    bias_blocks(tb, bias)
    for q in range(places):
        back_mixed[aligned(place_of(scal, q) * rows, rows), :] = dot_rt(
            back_branch[q], out_rows[...]
        ).astype(bf16)
    key_sum[...] = token_back[...]
    for h in range(heads):
        key_at, value_at = head_cols(1, h, heads, head_dim), head_cols(2, h, heads, head_dim)
        query_at, read_at = head_cols(0, h, heads, head_dim), slice(h * head_dim, (h + 1) * head_dim)
        for c in reversed(range(places)):
            count = min(span, (c + 1) * rows)
            low, high = (c + 1) * rows - count, (c + 1) * rows
            last = c * rows if c == places - 1 else 0
            query, back = qkv[c * rows : high, query_at], back_mixed[c * rows : high, read_at]
            keys = qkv[low:high, key_at]
            probs = window_probs(scal, query, keys, tb[h], last, scale)
            back_probs = dot_rt(back, qkv[low:high, value_at])
            row_dot = jnp.sum(probs * back_probs, axis=-1, keepdims=True)
            back_scores = probs * (back_probs - row_dot)
            if c == places - 1:
                band[...] = back_scores
            else:
                band[:, span - count :] += back_scores
            raw = (back_scores * scale).astype(bf16)
            back_qkv[c * rows : high, query_at] = dot(raw, keys).astype(bf16)
            key_to = slice(key_at.start - lanes, key_at.stop - lanes)
            value_to = slice(value_at.start - lanes, value_at.stop - lanes)
            key_sum[low:high, key_to] += dot_lt(raw, query)
            key_sum[low:high, value_to] += dot_lt(probs.astype(bf16), back)
        distance[h : h + 1, :] = jnp.sum(by_distance(band[...]), axis=0, keepdims=True)
    back_qkv[:, lanes:] = key_sum[...].astype(bf16)
    for start in range(0, width, 256):
        put_rows(
            scal,
            grad_qkv,
            start,
            dot_lt(first[:, start : start + 256], back_qkv[...]).astype(bf16),
        )
    gain_sum, shift_sum = None, None
    for q in range(places):
        back = dot_rt(back_qkv[aligned(place_of(scal, q) * rows, rows), :], w_nat[...])
        back_first[q] = back.astype(bf16)
        hat, _ = normalized(tokens[q].astype(f32))
        gain_term = jnp.sum(back * hat, axis=0, keepdims=True)
        shift_term = jnp.sum(back, axis=0, keepdims=True)
        gain_sum = gain_term if q == 0 else gain_sum + gain_term
        shift_sum = shift_term if q == 0 else shift_sum + shift_term
    grad_norm[0:1, :] = gain_sum
    grad_norm[1:2, :] = shift_sum


def flip_low(i):
    return i + 1 - 2 * (i % 2)


class Mover:
    def __init__(self, send, recv):
        self.send, self.recv, self.used = send, recv, 0

    def __call__(self, source, target, device):
        i = self.used
        self.used += 1
        return pltpu.make_async_remote_copy(
            src_ref=source,
            dst_ref=target,
            send_sem=self.send.at[i],
            recv_sem=self.recv.at[i],
            device_id=device,
            device_id_type=pl.DeviceIdType.MESH,
        )


class Links:
    def __init__(self):
        self.d, self.s = lax.axis_index("dp"), lax.axis_index("state")
        z, y = self.d // 2, self.d % 2
        self.over_z = [2 * (z + 1 - 2 * (z % 2)) + y, 2 * ((z + 2) % 4) + y, 2 * (3 - z) + y]
        self.over_y = flip_low(self.d)
        self.core, self.x = flip_low(self.s), (self.s + 2) % 4
        self.to_core, self.to_x = (self.d, self.core), (self.d, self.x)
        self.to_y = (self.over_y, self.s)
        self.to_z = [(other, self.s) for other in self.over_z]

    def greet(self):
        barrier = pltpu.get_barrier_semaphore()
        partners = [self.to_core, self.to_x, self.to_y, *self.to_z]
        for partner in partners:
            pl.semaphore_signal(
                barrier, inc=1, device_id=partner, device_id_type=pl.DeviceIdType.MESH
            )
        pl.semaphore_wait(barrier, len(partners))


class GroupGather:
    def __init__(self, mover, links, whole, at, source=None):
        self.links, self.parts = links, [links.s, links.core, links.x, flip_low(links.x)]
        own = whole.at[at(links.s)]
        source = own if source is None else source
        across = whole.at[at(links.x)]
        self.over_x = mover(source, own, links.to_x)
        self.beside = mover(source, own, links.to_core)
        self.passed = mover(across, across, links.to_core)

    def start(self):
        self.over_x.start()
        self.beside.start()

    def forward(self):
        self.over_x.wait_recv()
        self.passed.start()

    def finish(self):
        self.beside.wait_recv()
        self.passed.wait_recv()

    def sent(self):
        for copy in (self.over_x, self.beside, self.passed):
            copy.wait_send()


class WeightGather:
    def __init__(self, mover, links, whole, at, source):
        own = whole.at[at(links.d)]
        self.over_z = [mover(source, own, partner) for partner in links.to_z]
        self.own_y = mover(source, own, links.to_y)
        self.passed = []
        for other in links.over_z:
            block = whole.at[at(other)]
            self.passed.append(mover(block, block, links.to_y))

    def start_z(self):
        for copy in self.over_z:
            copy.start()

    def start_y(self):
        self.own_y.start()

    def forward(self, k):
        self.over_z[k].wait_recv()
        self.passed[k].start()

    def finish(self):
        self.own_y.wait_recv()
        for copy in self.passed:
            copy.wait_recv()

    def sent(self):
        for copy in (*self.over_z, self.own_y, *self.passed):
            copy.wait_send()


class GroupSum:
    def __init__(self, mover, links, partial, at, beside, across):
        self.partial, self.at, self.links = partial, at, links
        self.from_core, self.from_x = beside, across
        diagonal = flip_low(links.x)
        self.far = mover(partial.at[at(diagonal)], beside.at[1], links.to_core)
        self.near = mover(partial.at[at(links.core)], beside.at[0], links.to_core)
        self.over = mover(partial.at[at(links.x)], across, links.to_x)

    def start(self):
        self.far.start()
        self.near.start()

    def middle(self):
        self.far.wait_recv()
        place = self.at(self.links.x)
        total = self.partial[place].astype(f32) + self.from_core[1].astype(f32)
        self.partial[place] = total.astype(bf16)
        self.over.start()

    def finish(self):
        self.near.wait_recv()
        pair = self.partial[self.at(self.links.s)].astype(f32) + self.from_core[0].astype(f32)
        self.over.wait_recv()
        return pair + self.from_x[...].astype(f32)

    def sent(self):
        for copy in (self.far, self.near, self.over):
            copy.wait_send()


class WeightSum:
    def __init__(self, mover, links, grads, at, from_y, from_z):
        self.grads, self.at, self.links = grads, at, links
        self.from_y, self.from_z = from_y, from_z
        self.over_y = [
            mover(grads.at[at(flip_low(i))], from_y.at[k], links.to_y)
            for k, i in enumerate([links.d, *links.over_z])
        ]
        self.over_z = [
            mover(grads.at[at(i)], from_z.at[k], partner)
            for k, (i, partner) in enumerate(zip(links.over_z, links.to_z))
        ]

    def start(self):
        for k in (2, 3, 1, 0):
            self.over_y[k].start()

    def forward(self):
        for k in (1, 2, 0):
            self.over_y[k + 1].wait_recv()
            place = self.at(self.links.over_z[k])
            total = self.grads[place].astype(f32) + self.from_y[k + 1].astype(f32)
            self.grads[place] = total.astype(bf16)
            self.over_z[k].start()

    def finish(self):
        self.over_y[0].wait_recv()
        total = self.grads[self.at(self.links.d)].astype(f32) + self.from_y[0].astype(f32)
        for k in range(3):
            self.over_z[k].wait_recv()
            total += self.from_z[k].astype(f32)
        return total

    def sent(self):
        for copy in (*self.over_y, *self.over_z):
            copy.wait_send()


class SmallSum:
    def __init__(self, mover, links, value, arrived):
        self.value, self.arrived = value, arrived
        partners = [links.to_y, links.to_z[0], links.to_z[1], links.to_x, links.to_core]
        self.copies = [mover(value.at[k], arrived.at[k], to) for k, to in enumerate(partners)]

    def start(self):
        self.copies[0].start()

    def step(self, k):
        self.copies[k].wait_recv()
        self.value[k + 1] = self.value[k] + self.arrived[k]
        if k + 1 < len(self.copies):
            self.copies[k + 1].start()

    def sent(self):
        for copy in self.copies:
            copy.wait_send()


LAYER_COPIES = 160


def layer(
    head_dim,
    length,
    tokens,
    state,
    cot,
    state_cot,
    w_qkv,
    w_out,
    w_sqkv,
    w_sout,
    w_up,
    w_down,
    bias,
    buckets,
    gains,
    shifts,
    gate_bias,
    output,
    next_state,
    grad_tokens,
    grad_state,
    grad_qkv,
    grad_out,
    grad_sqkv,
    grad_sout,
    grad_up,
    grad_down,
    grad_rel,
    grad_norm,
    send_sem,
    recv_sem,
    local_sem,
    slab,
    qkv_nat,
    sqkv_nat,
    out_nat,
    sout_nat,
    up_nat,
    down_nat,
    tok_all,
    cot_all,
    state_all,
    mixed,
    read_all,
    hid,
    first,
    qkv,
    second,
    sqkv,
    back_read,
    back_sqkv,
    own_sum,
    key_sum,
    res_own,
    tb,
    band,
    back_mixed,
    out_rows,
    state_grads,
    down_grads,
    y_state,
    y_down,
    y_up,
    y_out,
    z_state,
    z_down,
    z_up,
    z_out,
    beside_rows,
    across_rows,
    beside_ffn,
    across_ffn,
    small,
    small_in,
    distance,
    landed,
    credit,
):
    rows, width = tokens.shape
    state_rows = state.shape[0]
    heads, span = bias.shape
    lanes = heads * head_dim
    depth = w_qkv.shape[0]
    inner_width = up_nat.shape[1]
    all_states = 4 * state_rows
    group_rows = 4 * rows
    scale = head_dim ** (-0.5)
    links = Links()
    s, d = links.s, links.d
    mover = Mover(send_sem, recv_sem)
    back_qkv, back_second, back_input = sqkv_nat, out_nat, sout_nat
    ffn_partial, back_first, back_branch = up_nat, down_nat, cot_all
    slope, up_grads = state_all, state_all
    back_state, ship, back_res = second, slab, own_sum
    hidden, token_grads = hid, hid

    def block(i, size):
        return pl.ds(pl.multiple_of(i * size, size), size)

    def own_rows(size):
        return lambda i: (block(i, size), slice(None))

    def own_lanes(size):
        return lambda i: (slice(None), block(i, size))

    def cot_rows(i):
        return (pl.ds(pl.multiple_of(all_states + i * state_rows, state_rows), state_rows), slice(None))

    own_columns = block(s, lanes)

    def own_out(i):
        return (block(i, depth), own_columns)

    def lanes_from(start, size):
        return pl.ds(pl.multiple_of(start * lanes, lanes), size * lanes)

    to_slab = []
    for k, shard in enumerate((w_qkv, w_sqkv)):
        core_slot = 1 - links.core % 2 + links.core // 2
        x_slot = 2 - 2 * (links.x // 2)
        to_slab.append(
            (
                mover(
                    shard.at[:, block(2 - 2 * (s % 2), lanes)],
                    slab.at[k, :, block(x_slot, lanes)],
                    links.to_x,
                ),
                mover(
                    shard.at[:, lanes : 2 * lanes],
                    slab.at[k, :, block(core_slot, lanes)],
                    links.to_core,
                ),
            )
        )
    get_tokens = GroupGather(mover, links, tok_all, own_rows(rows), tokens)
    get_state = GroupGather(mover, links, state_all, own_rows(state_rows), state)
    get_scot = GroupGather(mover, links, state_all, cot_rows, state_cot)
    get_cot = GroupGather(mover, links, cot_all, own_rows(rows), cot)
    dp_sout = WeightGather(mover, links, sout_nat, own_out, w_sout)
    dp_out = WeightGather(mover, links, out_nat, own_out, w_out)
    dp_qkv = WeightGather(mover, links, qkv_nat, own_rows(depth), slab.at[0])
    dp_sqkv = WeightGather(mover, links, sqkv_nat, own_rows(depth), slab.at[1])
    dp_up = WeightGather(mover, links, up_nat, own_rows(depth), w_up)
    dp_down = WeightGather(mover, links, down_nat, own_lanes(depth), w_down)
    get_sout = GroupGather(mover, links, sout_nat, own_lanes(lanes))
    get_out = GroupGather(mover, links, out_nat, own_lanes(lanes))
    get_mixed = GroupGather(mover, links, mixed, own_lanes(lanes))
    get_read = GroupGather(mover, links, read_all, own_lanes(lanes))
    get_branch = GroupGather(mover, links, back_branch, own_rows(rows))
    sum_state = GroupSum(
        mover,
        links,
        back_state,
        own_rows(state_rows),
        beside_ffn.at[:, 0:state_rows, :],
        across_ffn.at[0:state_rows, :],
    )
    sum_second = GroupSum(mover, links, back_second, own_rows(rows), beside_rows, across_rows)
    sum_ffn = GroupSum(mover, links, ffn_partial, own_rows(rows), beside_ffn, across_ffn)
    sum_first = GroupSum(mover, links, back_first, own_rows(rows), beside_rows, across_rows)
    dp_state = WeightSum(mover, links, state_grads, own_rows(depth), y_state, z_state)
    dp_grad_down = WeightSum(mover, links, down_grads, own_lanes(depth), y_down, z_down)
    dp_grad_up = WeightSum(mover, links, up_grads, own_rows(depth), y_up, z_up)
    dp_grad_out = WeightSum(
        mover,
        links,
        token_grads,
        lambda i: (block(i, depth), slice(3 * lanes, 4 * lanes)),
        y_out,
        z_out,
    )
    dp_grad_qkv = WeightSum(
        mover,
        links,
        token_grads,
        lambda i: (block(i, depth), slice(0, 3 * lanes)),
        y_state.at[:, :, 0 : 3 * lanes],
        z_state.at[:, :, 0 : 3 * lanes],
    )
    sum_small = SmallSum(mover, links, small, small_in)
    to_owner = [
        (
            mover(
                ship.at[k, :, block(2 - 2 * (s // 2), lanes)],
                landed.at[k, :, block(2 - 2 * (s % 2), lanes)],
                links.to_x,
            ),
            mover(
                ship.at[k, :, block(1 - s % 2 + s // 2, lanes)],
                landed.at[k, :, lanes : 2 * lanes],
                links.to_core,
            ),
        )
        for k in range(2)
    ]
    assert mover.used <= LAYER_COPIES

    local = []
    for source, target in (
        (w_qkv.at[:, block(2 * (s % 2), lanes)], slab.at[0, :, block((s + 1) // 2, lanes)]),
        (w_sqkv.at[:, block(2 * (s % 2), lanes)], slab.at[1, :, block((s + 1) // 2, lanes)]),
        (tokens, tok_all.at[block(s, rows), :]),
        (state, state_all.at[block(s, state_rows), :]),
        (state_cot, state_all.at[cot_rows(s)]),
        (cot, cot_all.at[block(s, rows), :]),
        (w_up, up_nat.at[block(d, depth), :]),
        (w_down, down_nat.at[:, block(d, depth)]),
        (w_out, out_nat.at[block(d, depth), own_columns]),
        (w_sout, sout_nat.at[block(d, depth), own_columns]),
    ):
        local.append(pltpu.make_async_copy(source, target, local_sem.at[len(local)]))

    links.greet()
    for over_x, beside in to_slab:
        over_x.start()
        beside.start()
    dp_sout.start_z()
    dp_out.start_z()
    dp_sout.start_y()
    dp_out.start_y()
    get_tokens.start()
    for copy in local:
        copy.start()
    small[0] = jnp.zeros(small.shape[1:], f32)
    distance[...] = jnp.zeros_like(distance)
    key_sum[...] = jnp.zeros_like(key_sum)
    own_sum[...] = jnp.zeros_like(own_sum)
    for k, gather in enumerate((dp_qkv, dp_sqkv)):
        for copy in (*to_slab[k],):
            copy.wait_recv()
        local[k].wait()
        gather.start_z()
        gather.start_y()
    dp_up.start_z()
    dp_down.start_z()
    get_state.start()
    get_scot.start()
    get_cot.start()
    qkv_nat[block(d, depth), :] = slab[0]
    sqkv_nat[block(d, depth), :] = slab[1]
    for copy in local[2:]:
        copy.wait()

    def token_norm(i):
        at = block(i, rows)
        hat, _ = normalized(tok_all[at, :].astype(f32))
        first[at, :] = (hat * gains[0:1, :] + shifts[0:1, :]).astype(bf16)

    token_norm(s)
    for k in range(3):
        dp_sout.forward(k)
        dp_out.forward(k)
    bias_blocks(tb, bias)
    get_tokens.beside.wait_recv()
    token_norm(links.core)
    get_tokens.forward()
    token_norm(links.x)
    dp_sout.finish()
    get_sout.start()
    dp_out.finish()
    get_out.start()
    get_tokens.passed.wait_recv()
    token_norm(flip_low(links.x))
    for k in range(3):
        dp_qkv.forward(k)
    dp_up.start_y()
    get_state.forward()
    get_scot.forward()
    dp_qkv.finish()

    def token_qkv(i, carry):
        at = block(i, rows)
        qkv[at, :] = dot(first[at, :], qkv_nat[...]).astype(bf16)
        return carry

    lax.fori_loop(0, 4, token_qkv, 0)
    for c in range(4):
        count = min(span, (c + 1) * rows)
        low, high = (c + 1) * rows - count, (c + 1) * rows
        last = c * rows if c == 3 else 0
        parts = []
        for h in range(heads):
            probs = window_probs(
                (0, length[0]),
                qkv[c * rows : high, head_cols(0, h, heads, head_dim)],
                qkv[low:high, head_cols(1, h, heads, head_dim)],
                tb[h],
                last,
                scale,
            )
            parts.append(
                dot(probs.astype(bf16), qkv[low:high, head_cols(2, h, heads, head_dim)])
            )
        mixed[c * rows : high, own_columns] = jnp.concatenate(parts, axis=1).astype(bf16)
        if c > 0:
            dp_sqkv.forward(c - 1)
    get_mixed.start()
    get_sout.forward()
    get_cot.forward()
    dp_down.start_y()

    get_state.finish()

    def state_norms(i, carry):
        at = block(i, state_rows)
        hat, _ = normalized(state_all[at, :].astype(f32))
        hid[at, :] = (hat * gains[2:3, :] + shifts[2:3, :]).astype(bf16)
        return carry

    lax.fori_loop(0, 4, state_norms, 0)
    dp_sqkv.finish()
    state_norm, back_update = slice(0, all_states), slice(all_states, 2 * all_states)
    sqkv[...] = dot(hid[state_norm, :], sqkv_nat[...]).astype(bf16)
    get_out.forward()
    dp_up.forward(0)

    def state_read(i, carry):
        at = block(i, state_rows)
        parts = []
        for h in range(heads):
            own, token = state_probs(
                (0, length[0]),
                sqkv[at, head_cols(0, h, heads, head_dim)],
                sqkv[:, head_cols(1, h, heads, head_dim)],
                qkv[:, head_cols(1, h, heads, head_dim)],
                scale,
            )
            parts.append(
                dot(own.astype(bf16), sqkv[:, head_cols(2, h, heads, head_dim)])
                + dot(token.astype(bf16), qkv[:, head_cols(2, h, heads, head_dim)])
            )
        read_all[at, own_columns] = jnp.concatenate(parts, axis=1).astype(bf16)
        return carry

    lax.fori_loop(0, 4, state_read, 0)
    get_read.start()
    dp_up.forward(1)
    get_mixed.forward()

    gate = jax.nn.sigmoid(gate_bias[...])
    get_scot.finish()

    def updates(i, carry):
        hid[cot_rows(i)] = ((1.0 - gate) * state_all[cot_rows(i)].astype(f32)).astype(bf16)
        return carry

    lax.fori_loop(0, 4, updates, 0)
    get_sout.finish()
    back_read[...] = dot_rt(hid[back_update, :], sout_nat[block(s, lanes), :]).astype(bf16)

    def state_back(h):
        key_at, value_at = head_cols(1, h, heads, head_dim), head_cols(2, h, heads, head_dim)
        query_at, read_at = head_cols(0, h, heads, head_dim), head_cols(0, h, heads, head_dim)

        def one(i, carry):
            at = block(i, state_rows)
            query, back = sqkv[at, query_at], back_read[at, read_at]
            own, token = state_probs(
                (0, length[0]), query, sqkv[:, key_at], qkv[:, key_at], scale
            )
            back_own = dot_rt(back, sqkv[:, value_at])
            back_token = dot_rt(back, qkv[:, value_at])
            row_dot = jnp.sum(own * back_own, axis=-1, keepdims=True) + jnp.sum(
                token * back_token, axis=-1, keepdims=True
            )
            own_raw = (own * (back_own - row_dot) * scale).astype(bf16)
            token_raw = (token * (back_token - row_dot) * scale).astype(bf16)
            back_sqkv[at, query_at] = (
                dot(own_raw, sqkv[:, key_at]) + dot(token_raw, qkv[:, key_at])
            ).astype(bf16)
            key_to = slice(key_at.start - lanes, key_at.stop - lanes)
            value_to = slice(value_at.start - lanes, value_at.stop - lanes)
            own_sum[:, key_to] += dot_lt(own_raw, query)
            own_sum[:, value_to] += dot_lt(own.astype(bf16), back)
            key_sum[:, key_to] += dot_lt(token_raw, query)
            key_sum[:, value_to] += dot_lt(token.astype(bf16), back)
            return carry

        lax.fori_loop(0, 4, one, 0)

    for h in range(heads):
        state_back(h)
        if h == 0:
            dp_up.forward(2)
    back_sqkv[:, lanes:] = own_sum[...].astype(bf16)
    dp_down.forward(0)

    def state_partial(i, carry):
        at = block(i, state_rows)
        back_state[at, :] = dot_rt(back_sqkv[at, :], sqkv_nat[...]).astype(bf16)
        return carry

    lax.fori_loop(0, 4, state_partial, 0)
    sum_state.start()

    def sqkv_grads(i, carry):
        at = block(i, 256)
        state_grads[at, 0 : 3 * lanes] = dot_lt(hid[state_norm, at], back_sqkv[...]).astype(bf16)
        return carry

    lax.fori_loop(0, width // 256, sqkv_grads, 0)
    sum_state.middle()
    get_read.forward()
    dp_down.forward(1)

    get_read.finish()
    update = dot(read_all[block(s, state_rows), :], sout_nat[...])
    held = state_all[block(s, state_rows), :].astype(f32)
    own_cot = state_all[cot_rows(s)].astype(f32)
    next_state[...] = (gate * held + (1.0 - gate) * update).astype(bf16)
    small[0, 6:7, :] = jnp.sum(own_cot * (held - update), axis=0, keepdims=True) * (
        gate * (1.0 - gate)
    )
    state_grads[:, 3 * lanes : 4 * lanes] = dot_lt(
        read_all[...], hid[back_update, own_columns]
    ).astype(bf16)
    hat_state, inverse_state = normalized(held)
    kept_state = gate * own_cot
    back_own_state = sum_state.finish()
    small[0, 2:3, :] = jnp.sum(back_own_state * hat_state, axis=0, keepdims=True)
    small[0, 5:6, :] = jnp.sum(back_own_state, axis=0, keepdims=True)
    grad_state[...] = (
        kept_state + normed_back(back_own_state, hat_state, inverse_state, gains[2:3, :])
    ).astype(bf16)

    get_mixed.finish()
    get_out.finish()
    dp_up.finish()
    get_cot.finish()
    for gather in (get_state, get_scot, get_sout, dp_sout, get_out, dp_out, dp_sqkv, sum_state):
        gather.sent()
    out_rows[...] = out_nat[block(s, lanes), :]

    def ffn_rows(i, carry):
        at = block(i, rows)
        total = tok_all[at, :].astype(f32) + dot(mixed[at, :], out_nat[...])

        @pl.when(i == s)
        def _():
            res_own[...] = total

        hat, _ = normalized(total)
        normed = (hat * gains[1:2, :] + shifts[1:2, :]).astype(bf16)
        second[at, :] = normed
        inner = dot(normed, up_nat[...])
        root = 0.7978845608028654
        square = inner * inner
        bend = jnp.tanh(root * inner * (1.0 + 0.044715 * square))
        half = 0.5 * (1.0 + bend)
        hidden[at, :] = (inner * half).astype(bf16)
        slope[at, :] = (
            half + (0.5 * root) * inner * (1.0 - bend * bend) * (1.0 + (3 * 0.044715) * square)
        ).astype(bf16)
        return carry

    lax.fori_loop(0, 4, ffn_rows, 0)
    dp_down.forward(2)
    dp_state.start()

    def down_columns(i, carry):
        at = block(i, 256)
        down_grads[:, at] = dot_lt(hidden[...], cot_all[:, at]).astype(bf16)
        return carry

    lax.fori_loop(0, width // 256, down_columns, 0)
    dp_grad_down.start()
    get_cot.sent()
    dp_down.finish()

    def ffn_back_rows(i, carry):
        at = block(i, rows)
        inner = (dot_rt(cot_all[at, :], down_nat[...]) * slope[at, :].astype(f32)).astype(bf16)
        back_input[at, :] = inner
        back_second[at, :] = dot_rt(inner, up_nat[...]).astype(bf16)
        return carry

    lax.fori_loop(0, 4, ffn_back_rows, 0)
    kept_cot = cot_all[block(s, rows), :].astype(f32)
    sum_second.start()

    def up_columns(i, carry):
        at = block(i, 256)
        up_grads[at, :] = dot_lt(second[:, at], back_input[...]).astype(bf16)
        return carry

    lax.fori_loop(0, width // 256, up_columns, 0)
    dp_grad_up.start()
    sum_second.middle()
    dp_up.sent()

    def ffn_out_rows(i, carry):
        at = block(i, rows)
        ffn_partial[at, :] = dot(hidden[at, :], down_nat[...]).astype(bf16)
        return carry

    lax.fori_loop(0, 4, ffn_out_rows, 0)
    sum_ffn.start()
    dp_down.sent()
    dp_state.forward()

    hat_mid, inverse_mid = normalized(res_own[...])
    back_own = sum_second.finish()
    own_back = kept_cot + normed_back(back_own, hat_mid, inverse_mid, gains[1:2, :])
    back_branch[block(s, rows), :] = own_back.astype(bf16)
    get_branch.start()
    back_res[0:rows, :] = own_back[:, 0 : width // 2]
    back_res[rows : 2 * rows, :] = own_back[:, width // 2 :]
    small[0, 1:2, :] = jnp.sum(back_own * hat_mid, axis=0, keepdims=True)
    small[0, 4:5, :] = jnp.sum(back_own, axis=0, keepdims=True)
    sum_ffn.middle()

    def mixed_back(i):
        back_mixed[block(i, rows), :] = dot_rt(
            back_branch[block(i, rows), :], out_rows[...]
        ).astype(bf16)

    mixed_back(s)
    dp_grad_down.forward()
    get_branch.beside.wait_recv()
    mixed_back(links.core)
    state_total = dp_state.finish()
    for partner in (links.to_y, *links.to_z):
        pl.semaphore_signal(credit, inc=1, device_id=partner, device_id_type=pl.DeviceIdType.MESH)
    dp_qkv.sent()
    grad_sout[...] = state_total[:, 3 * lanes :]
    ship[1] = state_total[:, : 3 * lanes].astype(bf16)
    grad_sqkv[:, block(2 * (s % 2), lanes)] = ship[1, :, block((s + 1) // 2, lanes)].astype(f32)
    for copy in to_owner[1]:
        copy.start()
    get_branch.forward()
    mixed_back(links.x)
    get_branch.passed.wait_recv()
    mixed_back(flip_low(links.x))
    token_grads[:, 3 * lanes : 4 * lanes] = dot_lt(
        mixed[...], back_branch[:, own_columns]
    ).astype(bf16)
    dp_grad_out.start()

    for h in range(heads):
        key_at, value_at = head_cols(1, h, heads, head_dim), head_cols(2, h, heads, head_dim)
        query_at, read_at = head_cols(0, h, heads, head_dim), head_cols(0, h, heads, head_dim)
        for c in reversed(range(4)):
            count = min(span, (c + 1) * rows)
            low, high = (c + 1) * rows - count, (c + 1) * rows
            last = c * rows if c == 3 else 0
            query, back = qkv[c * rows : high, query_at], back_mixed[c * rows : high, read_at]
            keys = qkv[low:high, key_at]
            probs = window_probs((0, length[0]), query, keys, tb[h], last, scale)
            back_probs = dot_rt(back, qkv[low:high, value_at])
            row_dot = jnp.sum(probs * back_probs, axis=-1, keepdims=True)
            back_scores = probs * (back_probs - row_dot)
            if c == 3:
                band[...] = back_scores
            else:
                band[:, span - count :] += back_scores
            raw = (back_scores * scale).astype(bf16)
            back_qkv[c * rows : high, query_at] = dot(raw, keys).astype(bf16)
            key_to = slice(key_at.start - lanes, key_at.stop - lanes)
            value_to = slice(value_at.start - lanes, value_at.stop - lanes)
            key_sum[low:high, key_to] += dot_lt(raw, query)
            key_sum[low:high, value_to] += dot_lt(probs.astype(bf16), back)
        distance[pl.ds(s * heads + h, 1), :] = jnp.sum(by_distance(band[...]), axis=0, keepdims=True)
    back_qkv[:, lanes:] = key_sum[...].astype(bf16)
    small[0, 0:1, :] = jnp.zeros((1, width), f32)
    small[0, 3:4, :] = jnp.zeros((1, width), f32)

    def first_partial(i, carry):
        at = block(i, rows)
        back = dot_rt(back_qkv[at, :], qkv_nat[...])
        back_first[at, :] = back.astype(bf16)
        hat, _ = normalized(tok_all[at, :].astype(f32))
        small[0, 0:1, :] += jnp.sum(back * hat, axis=0, keepdims=True)
        small[0, 3:4, :] += jnp.sum(back, axis=0, keepdims=True)
        return carry

    lax.fori_loop(0, 4, first_partial, 0)
    sum_first.start()
    small[0, 8:16, 0:128] = lax.dot_general(
        distance[...],
        buckets[...],
        (((1,), (0,)), ((), ())),
        precision=lax.Precision.HIGHEST,
        preferred_element_type=f32,
    )
    sum_small.start()

    def qkv_grads(i, carry):
        at = block(i, 256)
        token_grads[at, 0 : 3 * lanes] = dot_lt(first[:, at], back_qkv[...]).astype(bf16)
        return carry

    lax.fori_loop(0, width // 256, qkv_grads, 0)
    pl.semaphore_wait(credit, 4)
    dp_grad_qkv.start()
    sum_first.middle()
    dp_grad_up.forward()
    grad_down[...] = dp_grad_down.finish()
    output[...] = (res_own[...] + sum_ffn.finish()).astype(bf16)
    dp_grad_out.forward()
    hat_first, inverse_first = normalized(tok_all[block(s, rows), :].astype(f32))
    sum_small.step(0)
    back_own_first = sum_first.finish()
    own_back = jnp.concatenate([back_res[0:rows, :], back_res[rows : 2 * rows, :]], axis=1)
    grad_tokens[...] = (
        own_back + normed_back(back_own_first, hat_first, inverse_first, gains[0:1, :])
    ).astype(bf16)
    sum_small.step(1)
    dp_grad_qkv.forward()
    grad_up[...] = dp_grad_up.finish()
    sum_small.step(2)
    grad_out[...] = dp_grad_out.finish()
    sum_small.step(3)
    sum_small.step(4)
    grad_norm[...] = small[5, 0:8, :]
    grad_rel[...] = small[5, 8:16, 0:128]
    ship[0] = dp_grad_qkv.finish().astype(bf16)
    for copy in to_owner[0]:
        copy.start()
    grad_qkv[:, block(2 * (s % 2), lanes)] = ship[0, :, block((s + 1) // 2, lanes)].astype(f32)
    for k, grads in ((1, grad_sqkv), (0, grad_qkv)):
        for copy in to_owner[k]:
            copy.wait_recv()
        grads[:, lanes : 2 * lanes] = landed[k, :, lanes : 2 * lanes].astype(f32)
        x_at = block(2 - 2 * (s % 2), lanes)
        grads[:, x_at] = landed[k, :, x_at].astype(f32)
    for over_x, beside in (*to_slab, *to_owner):
        over_x.wait_send()
        beside.wait_send()
    for used in (
        get_tokens,
        get_mixed,
        get_read,
        get_branch,
        sum_second,
        sum_ffn,
        sum_first,
        dp_state,
        dp_grad_down,
        dp_grad_up,
        dp_grad_out,
        dp_grad_qkv,
        sum_small,
    ):
        used.sent()

def norm_back(values, back, gain):
    hat, inverse = normalized(values)
    return normed_back(back, hat, inverse, gain)


def per_device(
    tokens,
    state_in,
    cotangent,
    state_cotangent,
    seq_len,
    bucket_table,
    w_qkv,
    w_out,
    w_sqkv,
    w_sout,
    w_up,
    w_down,
    rel_table,
    norm_gain,
    norm_shift,
    gate_bias,
):
    rows, width = tokens.shape
    bucket_count, head_count = rel_table.shape
    window = bucket_table.shape[0]
    state_rows = state_in.shape[1]
    places = lax.axis_size("state")
    assert places == len(PLACES)
    dp_count = lax.axis_size("dp")
    here, dp_here = lax.axis_index("state"), lax.axis_index("dp")
    head_dim = width // head_count
    heads = head_count // places
    lanes = heads * head_dim
    span = window + rows
    group_rows = rows * places
    all_states = state_rows * places
    inner_width = w_up.shape[1]
    hops = dp_count == len(DP_PLACES)
    blocks = dp_count if hops else 1

    def swap(value, axis, bit):
        count = lax.axis_size(axis)
        return lax.ppermute(value, axis, [(i, i ^ bit) for i in range(count)])

    def from_group(value):
        pair = jnp.stack([value, swap(value, "state", 2)])
        return jnp.concatenate([pair, swap(pair, "state", 1)], axis=0)

    def list_from_group(value):
        across = swap(value, "state", 2)
        return [value, across, swap(value, "state", 1), swap(across, "state", 1)]

    def sum_to_owner(partial):
        half = partial.shape[0] // 2
        pair = partial[:half].astype(f32) + swap(partial[half:], "state", 1).astype(f32)
        return pair[0] + swap(pair[1].astype(bf16), "state", 2).astype(f32)

    def from_dp(block, axis):
        if not hops:
            return lax.all_gather(block, "dp", axis=axis, tiled=True)[None]
        gathered = block[None]
        for bit in DP_STEPS:
            gathered = jnp.concatenate([gathered, swap(gathered, "dp", bit)], axis=0)
        return gathered

    def sum_over_dp(partial, axis):
        if not hops:
            return lax.psum_scatter(partial[0], "dp", scatter_dimension=axis, tiled=True).astype(f32)
        for bit in reversed(DP_STEPS):
            half = partial.shape[0] // 2
            arrived = swap(partial[half:], "dp", bit)
            total = partial[:half].astype(f32) + arrived.astype(f32)
            partial = total.astype(bf16)
        return total[0]

    def sum_over_all(vector):
        if not hops:
            return lax.psum(vector, ("dp", "state"))
        for axis, bit in (("state", 1), ("state", 2), ("dp", 1), ("dp", 2), ("dp", 4)):
            vector = vector + swap(vector, axis, bit)
        return vector

    even = here % 2 == 0

    def pick(*by_place):
        value = by_place[-1]
        for i in reversed(range(places - 1)):
            value = jnp.where(here == i, by_place[i], value)
        return value

    def to_heads(shard):
        left, middle, right = (shard[:, i * lanes : (i + 1) * lanes] for i in range(3))
        own = jnp.where(even, left, right)
        across = swap(jnp.where(even, right, left), "state", 2)
        beside = swap(middle, "state", 1)
        query = pick(own, beside, across, across)
        keys = pick(beside, own, own, beside)
        values = pick(across, across, beside, own)
        return jnp.concatenate([query, keys, values], axis=1)

    def from_heads(grads):
        query, keys, values = (grads[:, i * lanes : (i + 1) * lanes] for i in range(3))
        own = pick(query, keys, keys, values)
        beside = swap(pick(keys, query, values, keys), "state", 1)
        across = swap(pick(values, values, query, query), "state", 2)
        return jnp.concatenate(
            [jnp.where(even, own, across), beside, jnp.where(even, across, own)], axis=1
        )

    if hops:
        block_list = dp_here ^ jnp.array(DP_PLACES, jnp.int32)
        position_list = jnp.array(
            [DP_PLACES.index(i) for i in range(dp_count)], jnp.int32
        )[dp_here ^ jnp.arange(dp_count)]
    else:
        block_list = position_list = jnp.zeros((1,), jnp.int32)
    scal = jnp.concatenate(
        [here[None].astype(jnp.int32), seq_len.astype(jnp.int32), block_list, position_list]
    ).astype(jnp.int32)

    lookup = (bucket_table[:, None] == jnp.arange(bucket_count)[None, :]).astype(f32)
    own_table = lax.dynamic_slice_in_dim(rel_table, here * heads, heads, 1)
    bias_rows = jnp.dot(
        own_table.T, lookup.T, precision=lax.Precision.HIGHEST, preferred_element_type=f32
    )
    bias = jnp.concatenate(
        [
            jnp.full((heads, 1), masked_value, f32),
            bias_rows[:, ::-1],
            jnp.full((heads, span - window - 1), masked_value, f32),
        ],
        axis=1,
    )
    gains = [norm_gain[i : i + 1] for i in range(3)]
    shifts = [norm_shift[i : i + 1] for i in range(3)]

    depth = w_qkv.shape[0]
    if hops:
        by_bucket = jnp.concatenate(
            [
                jnp.zeros((1, bucket_count), f32),
                lookup[::-1],
                jnp.zeros((span - window - 1, bucket_count), f32),
            ],
            axis=0,
        )
        by_bucket = jnp.pad(by_bucket, ((0, 0), (0, 128 - bucket_count)))
        whole = pl.BlockSpec(memory_space=pltpu.VMEM)
        anywhere = pl.BlockSpec(memory_space=pl.ANY)
        vmem = lambda shape, kind=bf16: pltpu.VMEM(shape, kind)
        square = vmem((width, width))
        (
            output,
            next_state,
            grad_tokens,
            grad_state,
            grad_qkv,
            grad_out,
            grad_sqkv,
            grad_sout,
            grad_up,
            grad_down,
            grad_rel,
            grad_norm,
        ) = pl.pallas_call(
            functools.partial(layer, head_dim),
            out_shape=[
                out((rows, width)),
                out((state_rows, width)),
                out((rows, width)),
                out((state_rows, width)),
                out((depth, 3 * lanes), f32),
                out((depth, lanes), f32),
                out((depth, 3 * lanes), f32),
                out((depth, lanes), f32),
                out((depth, inner_width), f32),
                out((inner_width, depth), f32),
                out((head_count, 128), f32),
                out((8, width), f32),
            ],
            in_specs=[pl.BlockSpec(memory_space=pltpu.SMEM)] + [anywhere] * 10 + [whole] * 5,
            out_specs=[whole] * 12,
            scratch_shapes=[
                pltpu.SemaphoreType.DMA((LAYER_COPIES,)),
                pltpu.SemaphoreType.DMA((LAYER_COPIES,)),
                pltpu.SemaphoreType.DMA((16,)),
                vmem((2, depth, 3 * lanes)),
                vmem((width, 3 * lanes)),
                vmem((width, 3 * lanes)),
                square,
                square,
                vmem((width, inner_width)),
                vmem((inner_width, width)),
                vmem((group_rows, width)),
                vmem((group_rows, width)),
                vmem((2 * all_states, width)),
                vmem((group_rows, width)),
                vmem((all_states, width)),
                vmem((2 * all_states, width)),
                vmem((group_rows, width)),
                vmem((group_rows, 3 * lanes)),
                vmem((group_rows, width)),
                vmem((all_states, 3 * lanes)),
                vmem((all_states, lanes)),
                vmem((all_states, 3 * lanes)),
                vmem((all_states, 2 * lanes), f32),
                vmem((group_rows, 2 * lanes), f32),
                vmem((rows, width), f32),
                vmem((heads, rows, span), f32),
                vmem((rows, span), f32),
                vmem((group_rows, lanes)),
                vmem((lanes, width)),
                square,
                vmem((inner_width, width)),
                vmem((4, depth, 4 * lanes)),
                vmem((4, inner_width, depth)),
                vmem((4, depth, inner_width)),
                vmem((4, depth, lanes)),
                vmem((3, depth, 4 * lanes)),
                vmem((3, inner_width, depth)),
                vmem((3, depth, inner_width)),
                vmem((3, depth, lanes)),
                vmem((2, rows, width)),
                vmem((rows, width)),
                vmem((2, rows, width)),
                vmem((rows, width)),
                vmem((6, 16, width), f32),
                vmem((5, 16, width), f32),
                vmem((8, span), f32),
                vmem((2, depth, 3 * lanes)),
                pltpu.SemaphoreType.REGULAR,
            ],
            compiler_params=pltpu.CompilerParams(
                collective_id=0, has_side_effects=True, vmem_limit_bytes=64 << 20
            ),
            name="layer",
        )(
            seq_len,
            tokens,
            state_in[0],
            cotangent,
            state_cotangent[0],
            w_qkv,
            w_out,
            w_sqkv,
            w_sout,
            w_up,
            w_down,
            bias,
            by_bucket,
            norm_gain,
            norm_shift,
            gate_bias[None],
        )
        return (
            output,
            next_state[None],
            grad_tokens,
            grad_state[None],
            grad_qkv,
            grad_out,
            grad_sqkv,
            grad_sout,
            grad_up,
            grad_down,
            grad_rel[:, :bucket_count].T,
            grad_norm[0:3],
            grad_norm[3:6],
            grad_norm[6],
        )

    both = to_heads(jnp.concatenate([w_qkv, w_sqkv], axis=0))
    full_qkv = from_dp(both[:depth], 0)
    all_tokens = from_group(tokens)
    full_sqkv = from_dp(both[depth:], 0)
    all_state = from_group(state_in[0])
    all_cot = from_group(cotangent)
    all_state_cot = from_group(state_cotangent[0])
    outs_pair = from_dp(jnp.concatenate([w_out, w_sout], axis=1), 0)
    half = outs_pair.shape[2] // 2
    full_sout = list_from_group(outs_pair[:, :, half:])
    full_out = list_from_group(outs_pair[:, :, :half])
    full_up = from_dp(w_up, 0)
    full_down = from_dp(w_down, 1)

    first, qkv, mixed = call(
        functools.partial(token_forward, head_dim),
        "token_forward",
        [out((group_rows, width)), out((group_rows, 3 * lanes)), out((places, rows, lanes))],
        [pltpu.VMEM((width, 3 * lanes), bf16), pltpu.VMEM((heads, rows, span), f32)],
        2 * group_rows * width * 3 * lanes,
        group_rows * span * heads,
        scal,
        all_tokens,
        gains[0],
        shifts[0],
        full_qkv,
        bias,
    )
    mixed_parts = list_from_group(mixed)

    state_norm, sqkv, read = call(
        functools.partial(state_forward, head_dim),
        "state_forward",
        [
            out((all_states, width)),
            out((all_states, 3 * lanes)),
            out((places, state_rows, lanes)),
        ],
        [pltpu.VMEM((width, 3 * lanes), bf16)],
        2 * all_states * width * 3 * lanes,
        all_states * (all_states + group_rows) * heads,
        scal,
        all_state,
        gains[2],
        shifts[2],
        full_sqkv,
        qkv,
    )
    read_parts = list_from_group(read)

    next_state, grad_gate, grad_sout, token_back, grad_sqkv, back_state_norm, state_sums = call(
        functools.partial(state_backward, head_dim),
        "state_backward",
        [
            out((state_rows, width)),
            out((1, width), f32),
            out((blocks, width // blocks, lanes)),
            out((group_rows, 2 * lanes), f32),
            out((blocks, width // blocks, 3 * lanes)),
            out((places, state_rows, width)),
            out((2, width), f32),
        ],
        [
            pltpu.VMEM((width, 3 * lanes), bf16),
            pltpu.VMEM((width, width), bf16),
            pltpu.VMEM((all_states, width), bf16),
            pltpu.VMEM((all_states, lanes), bf16),
            pltpu.VMEM((all_states, 3 * lanes), bf16),
            pltpu.VMEM((all_states, 2 * lanes), f32),
        ],
        4 * all_states * width * 4 * lanes,
        all_states * (all_states + group_rows) * heads,
        scal,
        state_in[0],
        all_state_cot,
        gate_bias[None],
        all_state,
        *read_parts,
        *full_sout,
        sqkv,
        qkv,
        state_norm,
        full_sqkv,
    )
    residual, second, hidden, slope, out_rows, grad_down = call(
        ffn_up,
        "ffn_up",
        [
            out((places, rows, width), f32),
            out((group_rows, width)),
            out((group_rows, inner_width)),
            out((group_rows, inner_width)),
            out((lanes, width)),
            out((blocks, inner_width, width // blocks)),
        ],
        [pltpu.VMEM((width, width), bf16), pltpu.VMEM((width, inner_width), bf16)],
        2 * group_rows * width * (width + 2 * inner_width),
        group_rows * inner_width,
        scal,
        all_tokens,
        *mixed_parts,
        *full_out,
        gains[1],
        shifts[1],
        full_up,
        all_cot,
    )

    back_second, back_input, mid_sums = call(
        ffn_back,
        "ffn_back",
        [
            out((places, rows, width)),
            out((group_rows, inner_width)),
            out((2, width), f32),
        ],
        [pltpu.VMEM((inner_width, width), bf16), pltpu.VMEM((width, inner_width), bf16)],
        4 * group_rows * width * inner_width,
        0,
        scal,
        all_cot,
        full_down,
        full_up,
        slope,
        residual,
    )
    residual_own = residual[0]
    own_grad_sout = sum_over_dp(grad_sout, 0)
    own_grad_sqkv = sum_over_dp(grad_sqkv, 0)
    back_state = sum_to_owner(back_state_norm)
    gate_open = jax.nn.sigmoid(gate_bias)
    grad_state = (
        gate_open * state_cotangent[0].astype(f32)
        + norm_back(state_in[0].astype(f32), back_state, norm_gain[2])
    ).astype(bf16)

    own_grad_down = sum_over_dp(grad_down, 1)
    back_second = sum_to_owner(back_second)
    back_residual = cotangent.astype(f32) + norm_back(residual_own, back_second, norm_gain[1])
    back_branch = from_group(back_residual.astype(bf16))

    ffn_partial, grad_up = call(
        ffn_rest,
        "ffn_rest",
        [out((places, rows, width)), out((blocks, width // blocks, inner_width))],
        [pltpu.VMEM((inner_width, width), bf16)],
        4 * group_rows * width * inner_width,
        0,
        scal,
        hidden,
        full_down,
        second,
        back_input,
    )
    own_grad_up = sum_over_dp(grad_up, 0)
    output = (residual_own + sum_to_owner(ffn_partial)).astype(bf16)

    (grad_out,) = call(
        out_grad,
        "out_grad",
        [out((blocks, width // blocks, lanes))],
        [],
        2 * group_rows * width * lanes,
        0,
        scal,
        back_branch,
        *mixed_parts,
    )
    own_grad_out = sum_over_dp(grad_out, 0)

    grad_qkv, back_first, first_sums, distance = call(
        functools.partial(token_backward, head_dim),
        "token_backward",
        [
            out((blocks, width // blocks, 3 * lanes)),
            out((places, rows, width)),
            out((2, width), f32),
            out((heads, span), f32),
        ],
        [
            pltpu.VMEM((width, 3 * lanes), bf16),
            pltpu.VMEM((heads, rows, span), f32),
            pltpu.VMEM((group_rows, lanes), bf16),
            pltpu.VMEM((group_rows, 3 * lanes), bf16),
            pltpu.VMEM((group_rows, 2 * lanes), f32),
            pltpu.VMEM((rows, span), f32),
        ],
        2 * group_rows * width * 7 * lanes,
        group_rows * span * heads,
        scal,
        back_branch,
        out_rows,
        qkv,
        bias,
        token_back,
        first,
        all_tokens,
        full_qkv,
    )
    back_first = sum_to_owner(back_first)
    grad_tokens = (
        norm_back(tokens.astype(f32), back_first, norm_gain[0]) + back_residual
    ).astype(bf16)
    own_grad_qkv = sum_over_dp(grad_qkv, 0)
    both_grads = from_heads(
        jnp.concatenate([own_grad_qkv, own_grad_sqkv], axis=0).astype(bf16)
    ).astype(f32)

    per_distance = distance[:, 1 : window + 1][:, ::-1]
    own_rel = jnp.dot(
        per_distance, lookup, precision=lax.Precision.HIGHEST, preferred_element_type=f32
    ).T
    grad_rel = lax.dynamic_update_slice_in_dim(
        jnp.zeros((bucket_count, head_count), f32), own_rel, here * heads, 1
    )
    small = [
        jnp.stack([first_sums[0], mid_sums[0], state_sums[0]]),
        jnp.stack([first_sums[1], mid_sums[1], state_sums[1]]),
        grad_gate[0],
        grad_rel,
    ]
    packed = sum_over_all(jnp.concatenate([v.reshape(-1, 128) for v in small], axis=0))
    unpacked, start = [], 0
    for v in small:
        count = v.size // 128
        unpacked.append(packed[start : start + count].reshape(v.shape))
        start += count
    return (
        output,
        next_state[None],
        grad_tokens,
        grad_state[None],
        both_grads[:depth],
        own_grad_out,
        both_grads[depth:],
        own_grad_sout,
        own_grad_up,
        own_grad_down,
        unpacked[3],
        unpacked[0],
        unpacked[1],
        unpacked[2],
    )


def solution(mesh):
    rows_spec = P(("dp", "state"), None)
    state_spec = P("dp", "state", None)
    weight_spec = P("dp", "state")
    return jax.shard_map(
        per_device,
        mesh=mesh,
        in_specs=(
            rows_spec,
            state_spec,
            rows_spec,
            state_spec,
            P("dp"),
            P(),
            weight_spec,
            weight_spec,
            weight_spec,
            weight_spec,
            weight_spec,
            P("state", "dp"),
            P(),
            P(),
            P(),
            P(),
        ),
        out_specs=(
            rows_spec,
            state_spec,
            rows_spec,
            state_spec,
            weight_spec,
            weight_spec,
            weight_spec,
            weight_spec,
            weight_spec,
            P("state", "dp"),
            P(),
            P(),
            P(),
            P(),
        ),
        check_vma=False,
    )
```

```python
import functools

import jax
import jax.numpy as jnp
from jax import lax
from jax.experimental import pallas as pl
from jax.experimental.pallas import tpu as pltpu
from jax.sharding import PartitionSpec as P

epsilon = 1e-05
masked_value = -1e30
f32 = jnp.float32
bf16 = jnp.bfloat16

PLACES = (0, 2, 1, 3)
DP_STEPS = (2, 4, 1)
DP_PLACES = (0, 2, 4, 6, 1, 3, 5, 7)


def dot(left, right):
    return lax.dot_general(left, right, (((1,), (0,)), ((), ())), preferred_element_type=f32)


def dot_rt(left, right):
    return lax.dot_general(left, right, (((1,), (1,)), ((), ())), preferred_element_type=f32)


def dot_lt(left, right):
    return lax.dot_general(left, right, (((0,), (0,)), ((), ())), preferred_element_type=f32)


def where_from(sender, place):
    return PLACES.index(PLACES[sender] ^ PLACES[place])


def normalized(values):
    centre = jnp.mean(values, axis=-1, keepdims=True)
    centred = values - centre
    spread = jnp.mean(centred * centred, axis=-1, keepdims=True)
    inverse = lax.rsqrt(spread + epsilon)
    return centred * inverse, inverse


def normed_back(back, hat, inverse, gain):
    grown = back * gain
    return inverse * (
        grown
        - jnp.mean(grown, axis=-1, keepdims=True)
        - hat * jnp.mean(grown * hat, axis=-1, keepdims=True)
    )


def place_of(scal, q):
    return scal[0] ^ PLACES[q]


def aligned(start, size):
    return pl.ds(pl.multiple_of(start, size), size)


def block_at(scal, q):
    return scal[2 + q]


def position_of(scal, block, blocks):
    return scal[2 + blocks + block]


def rows_in_order(scal, target, source):
    blocks, depth = source.shape[0], source.shape[1]
    for q in range(blocks):
        target[aligned(block_at(scal, q) * depth, depth), :] = source[q]


def columns_in_order(scal, target, source):
    blocks, depth = source.shape[0], source.shape[2]
    for q in range(blocks):
        target[:, aligned(block_at(scal, q) * depth, depth)] = source[q]


def put_rows(scal, target, start, value):
    blocks, depth = target.shape[0], target.shape[1]
    rows = value.shape[0]
    if depth >= rows:
        target[position_of(scal, start // depth, blocks), aligned(start % depth, rows), :] = value
    else:
        for i in range(rows // depth):
            position = position_of(scal, start // depth + i, blocks)
            target[position] = value[i * depth : (i + 1) * depth]


def put_columns(scal, target, start, value):
    blocks, depth = target.shape[0], target.shape[2]
    columns = value.shape[1]
    if depth >= columns:
        target[position_of(scal, start // depth, blocks), :, aligned(start % depth, columns)] = value
    else:
        for i in range(columns // depth):
            position = position_of(scal, start // depth + i, blocks)
            target[position] = value[:, i * depth : (i + 1) * depth]


def call(body, name, outs, scratch, flops, exps, *args):
    sizes = sum(a.size * a.dtype.itemsize for a in args) + sum(
        a.size * a.dtype.itemsize for a in outs
    )
    in_specs = [pl.BlockSpec(memory_space=pltpu.SMEM)] + [
        pl.BlockSpec(memory_space=pltpu.VMEM) for _ in args[1:]
    ]
    return pl.pallas_call(
        body,
        out_shape=outs,
        in_specs=in_specs,
        out_specs=[pl.BlockSpec(memory_space=pltpu.VMEM) for _ in outs],
        scratch_shapes=scratch,
        compiler_params=pltpu.CompilerParams(vmem_limit_bytes=56 << 20),
        cost_estimate=pl.CostEstimate(flops=flops, bytes_accessed=sizes, transcendentals=exps),
        name=name,
    )(*args)


def out(shape, kind=bf16):
    return jax.ShapeDtypeStruct(shape, kind)


def by_distance(scores):
    rows, span = scores.shape
    row_at = lax.broadcasted_iota(jnp.int32, scores.shape, 0)
    step = 1
    while step < rows:
        scores = jnp.where(row_at & step != 0, pltpu.roll(scores, span - step, 1), scores)
        step *= 2
    return scores


def bias_blocks(tb, bias):
    heads, rows, span = tb.shape
    for h in range(heads):
        row = jnp.broadcast_to(bias[h], (rows, span))
        tb[h] = pltpu.roll(row, 0, 1, stride=1, stride_axis=0)


def window_probs(scal, query, keys, tb_block, last, scale):
    rows, span = tb_block.shape
    count = keys.shape[0]
    scores = dot_rt(query, keys) * scale + tb_block[:, span - count :]
    if last:
        row_at = lax.broadcasted_iota(jnp.int32, scores.shape, 0)
        col_at = lax.broadcasted_iota(jnp.int32, scores.shape, 1)
        ahead = col_at - (count - rows)
        live = (ahead < scal[1] - last) | (ahead == row_at)
        scores = jnp.where(live, scores, masked_value)
    top = jnp.max(scores, axis=-1, keepdims=True)
    grown = jnp.exp(scores - top)
    return grown * (1.0 / jnp.sum(grown, axis=-1, keepdims=True))


def state_probs(scal, query, state_keys, keys, scale):
    own = dot_rt(query, state_keys) * scale
    token = dot_rt(query, keys) * scale
    col_at = lax.broadcasted_iota(jnp.int32, token.shape, 1)
    token = jnp.where(col_at < scal[1], token, masked_value)
    top = jnp.maximum(
        jnp.max(own, axis=-1, keepdims=True), jnp.max(token, axis=-1, keepdims=True)
    )
    own = jnp.exp(own - top)
    token = jnp.exp(token - top)
    total = jnp.sum(own, axis=-1, keepdims=True) + jnp.sum(token, axis=-1, keepdims=True)
    inverse = 1.0 / total
    return own * inverse, token * inverse


def head_cols(block, h, heads, head_dim):
    start = (block * heads + h) * head_dim
    return slice(start, start + head_dim)


def token_forward(head_dim, scal, tokens, gain, shift, w_qkv, bias, first, qkv, mixed, w_nat, tb):
    places, rows, width = tokens.shape
    heads = bias.shape[0]
    span = bias.shape[1]
    scale = head_dim ** (-0.5)
    rows_in_order(scal, w_nat, w_qkv)
    bias_blocks(tb, [bias[h : h + 1, :] for h in range(heads)])
    for q in range(places):
        hat, _ = normalized(tokens[q].astype(f32))
        normed = (hat * gain[...] + shift[...]).astype(bf16)
        at = aligned(place_of(scal, q) * rows, rows)
        first[at, :] = normed
        qkv[at, :] = dot(normed, w_nat[...]).astype(bf16)
    for c in range(places):
        count = min(span, (c + 1) * rows)
        low, high = (c + 1) * rows - count, (c + 1) * rows
        last = c * rows if c == places - 1 else 0
        parts = []
        for h in range(heads):
            probs = window_probs(
                scal,
                qkv[c * rows : high, head_cols(0, h, heads, head_dim)],
                qkv[low:high, head_cols(1, h, heads, head_dim)],
                tb[h],
                last,
                scale,
            )
            parts.append(
                dot(probs.astype(bf16), qkv[low:high, head_cols(2, h, heads, head_dim)])
            )
        mixed[c] = jnp.concatenate(parts, axis=1).astype(bf16)


def state_forward(
    head_dim, scal, state, gain, shift, w_sqkv, qkv, normed_out, sqkv, read, w_nat
):
    places, rows, width = state.shape
    heads = qkv.shape[1] // (3 * head_dim)
    scale = head_dim ** (-0.5)
    rows_in_order(scal, w_nat, w_sqkv)
    for q in range(places):
        hat, _ = normalized(state[q].astype(f32))
        normed = (hat * gain[...] + shift[...]).astype(bf16)
        normed_out[q * rows : (q + 1) * rows, :] = normed
        sqkv[q * rows : (q + 1) * rows, :] = dot(normed, w_nat[...]).astype(bf16)
    for q in range(places):
        parts = []
        for h in range(heads):
            own, token = state_probs(
                scal,
                sqkv[q * rows : (q + 1) * rows, head_cols(0, h, heads, head_dim)],
                sqkv[:, head_cols(1, h, heads, head_dim)],
                qkv[:, head_cols(1, h, heads, head_dim)],
                scale,
            )
            parts.append(
                dot(own.astype(bf16), sqkv[:, head_cols(2, h, heads, head_dim)])
                + dot(token.astype(bf16), qkv[:, head_cols(2, h, heads, head_dim)])
            )
        read[q] = jnp.concatenate(parts, axis=1).astype(bf16)


def assembled(scal, target, parts):
    for p, part in enumerate(parts):
        blocks, depth, columns = part.shape
        at = aligned(place_of(scal, p) * columns, columns)
        for q in range(blocks):
            target[aligned(block_at(scal, q) * depth, depth), at] = part[q]


def state_backward(
    head_dim,
    scal,
    state_own,
    state_cot,
    gate_bias,
    state,
    read0,
    read1,
    read2,
    read3,
    out0,
    out1,
    out2,
    out3,
    sqkv,
    qkv,
    normed,
    w_sqkv,
    next_state,
    grad_gate,
    grad_sout,
    token_back,
    grad_sqkv,
    back_norm,
    grad_norm,
    w_nat,
    w_out,
    back_update,
    back_read,
    back_sqkv,
    own_sum,
):
    places, rows, width = state_cot.shape
    reads = (read0, read1, read2, read3)
    heads = qkv.shape[1] // (3 * head_dim)
    lanes = heads * head_dim
    scale = head_dim ** (-0.5)
    rows_in_order(scal, w_nat, w_sqkv)
    assembled(scal, w_out, (out0, out1, out2, out3))
    gate = jax.nn.sigmoid(gate_bias[...])
    update = None
    for p in range(places):
        term = dot(reads[p][p], w_out[aligned(place_of(scal, p) * lanes, lanes), :])
        update = term if update is None else update + term
    held = state_own[...].astype(f32)
    cot = state_cot[0].astype(f32)
    next_state[...] = (gate * held + (1.0 - gate) * update).astype(bf16)
    grad_gate[...] = jnp.sum(cot * (held - update), axis=0, keepdims=True) * (gate * (1.0 - gate))
    for q in range(places):
        back_update[q * rows : (q + 1) * rows, :] = (
            (1.0 - gate) * state_cot[q].astype(f32)
        ).astype(bf16)
    own_columns = back_update[:, aligned(scal[0] * lanes, lanes)]
    for p in range(places):
        stack = jnp.concatenate([reads[p][where_from(p, q)] for q in range(places)], axis=0)
        put_rows(
            scal, grad_sout, place_of(scal, p) * lanes, dot_lt(stack, own_columns).astype(bf16)
        )
    back_read[...] = dot_rt(
        back_update[...], w_out[aligned(scal[0] * lanes, lanes), :]
    ).astype(bf16)
    for h in range(heads):
        key_at, value_at = head_cols(1, h, heads, head_dim), head_cols(2, h, heads, head_dim)
        query_at, read_at = head_cols(0, h, heads, head_dim), slice(h * head_dim, (h + 1) * head_dim)
        for q in range(places):
            at = slice(q * rows, (q + 1) * rows)
            query, back = sqkv[at, query_at], back_read[at, read_at]
            own, token = state_probs(scal, query, sqkv[:, key_at], qkv[:, key_at], scale)
            back_own = dot_rt(back, sqkv[:, value_at])
            back_token = dot_rt(back, qkv[:, value_at])
            row_dot = jnp.sum(own * back_own, axis=-1, keepdims=True) + jnp.sum(
                token * back_token, axis=-1, keepdims=True
            )
            own_raw = (own * (back_own - row_dot) * scale).astype(bf16)
            token_raw = (token * (back_token - row_dot) * scale).astype(bf16)
            back_sqkv[at, query_at] = (
                dot(own_raw, sqkv[:, key_at]) + dot(token_raw, qkv[:, key_at])
            ).astype(bf16)
            terms = (
                (own_sum, key_at, dot_lt(own_raw, query)),
                (own_sum, value_at, dot_lt(own.astype(bf16), back)),
                (token_back, key_at, dot_lt(token_raw, query)),
                (token_back, value_at, dot_lt(token.astype(bf16), back)),
            )
            for target, columns, term in terms:
                columns = slice(columns.start - lanes, columns.stop - lanes)
                if q == 0:
                    target[:, columns] = term
                else:
                    target[:, columns] += term
    back_sqkv[:, lanes:] = own_sum[...].astype(bf16)
    for start in range(0, width, 256):
        put_rows(
            scal,
            grad_sqkv,
            start,
            dot_lt(normed[:, start : start + 256], back_sqkv[...]).astype(bf16),
        )
    gain_sum, shift_sum = None, None
    for q in range(places):
        back = dot_rt(back_sqkv[q * rows : (q + 1) * rows, :], w_nat[...])
        back_norm[q] = back.astype(bf16)
        hat, _ = normalized(state[q].astype(f32))
        gain_term = jnp.sum(back * hat, axis=0, keepdims=True)
        shift_term = jnp.sum(back, axis=0, keepdims=True)
        gain_sum = gain_term if q == 0 else gain_sum + gain_term
        shift_sum = shift_term if q == 0 else shift_sum + shift_term
    grad_norm[0:1, :] = gain_sum
    grad_norm[1:2, :] = shift_sum


def ffn_up(
    scal,
    tokens,
    mixed0,
    mixed1,
    mixed2,
    mixed3,
    out0,
    out1,
    out2,
    out3,
    gain,
    shift,
    w_up,
    cot,
    residual,
    second,
    hidden,
    slope,
    out_rows,
    grad_down,
    w_out,
    w_nat,
):
    places, rows, width = tokens.shape
    mixed = (mixed0, mixed1, mixed2, mixed3)
    lanes = mixed0.shape[2]
    assembled(scal, w_out, (out0, out1, out2, out3))
    out_rows[...] = w_out[aligned(scal[0] * lanes, lanes), :]
    rows_in_order(scal, w_nat, w_up)
    for q in range(places):
        total = tokens[q].astype(f32)
        for p in range(places):
            total += dot(
                mixed[p][place_of(scal, q)], w_out[aligned(place_of(scal, p) * lanes, lanes), :]
            )
        residual[q] = total
        hat, _ = normalized(total)
        normed = (hat * gain[...] + shift[...]).astype(bf16)
        at = slice(q * rows, (q + 1) * rows)
        second[at, :] = normed
        inner = dot(normed, w_nat[...])
        root = 0.7978845608028654
        square = inner * inner
        bend = jnp.tanh(root * inner * (1.0 + 0.044715 * square))
        half = 0.5 * (1.0 + bend)
        hidden[at, :] = (inner * half).astype(bf16)
        slope[at, :] = (
            half + (0.5 * root) * inner * (1.0 - bend * bend) * (1.0 + (3 * 0.044715) * square)
        ).astype(bf16)
    for start in range(0, width, 256):
        columns = jnp.concatenate([cot[q, :, start : start + 256] for q in range(places)], axis=0)
        put_columns(scal, grad_down, start, dot_lt(hidden[...], columns).astype(bf16))


def ffn_back(
    scal,
    cot,
    w_down,
    w_up,
    slope,
    residual,
    back_second,
    back_input,
    grad_norm,
    w_nat,
    w_up_nat,
):
    places, rows, width = cot.shape
    columns_in_order(scal, w_nat, w_down)
    rows_in_order(scal, w_up_nat, w_up)
    gain_sum, shift_sum = None, None
    for q in range(places):
        at = slice(q * rows, (q + 1) * rows)
        inner = (dot_rt(cot[q], w_nat[...]) * slope[at, :].astype(f32)).astype(bf16)
        back_input[at, :] = inner
        back = dot_rt(inner, w_up_nat[...])
        back_second[q] = back.astype(bf16)
        hat, _ = normalized(residual[q])
        gain_term = jnp.sum(back * hat, axis=0, keepdims=True)
        shift_term = jnp.sum(back, axis=0, keepdims=True)
        gain_sum = gain_term if q == 0 else gain_sum + gain_term
        shift_sum = shift_term if q == 0 else shift_sum + shift_term
    grad_norm[0:1, :] = gain_sum
    grad_norm[1:2, :] = shift_sum


def ffn_rest(scal, hidden, w_down, second, back_input, partial, grad_up, w_nat):
    places, rows, width = partial.shape
    for start in range(0, width, 256):
        put_rows(
            scal,
            grad_up,
            start,
            dot_lt(second[:, start : start + 256], back_input[...]).astype(bf16),
        )
    columns_in_order(scal, w_nat, w_down)
    for q in range(places):
        partial[q] = dot(hidden[q * rows : (q + 1) * rows, :], w_nat[...]).astype(bf16)


def out_grad(scal, back_branch, mixed0, mixed1, mixed2, mixed3, grad_out):
    places, rows, width = back_branch.shape
    mixed = (mixed0, mixed1, mixed2, mixed3)
    lanes = mixed0.shape[2]
    own_at = aligned(scal[0] * lanes, lanes)
    own_columns = jnp.concatenate([back_branch[q, :, own_at] for q in range(places)], axis=0)
    for p in range(places):
        stack = jnp.concatenate([mixed[p][place_of(scal, q)] for q in range(places)], axis=0)
        put_rows(
            scal, grad_out, place_of(scal, p) * lanes, dot_lt(stack, own_columns).astype(bf16)
        )


def token_backward(
    head_dim,
    scal,
    back_branch,
    out_rows,
    qkv,
    bias,
    token_back,
    first,
    tokens,
    w_qkv,
    grad_qkv,
    back_first,
    grad_norm,
    distance,
    w_nat,
    tb,
    back_mixed,
    back_qkv,
    key_sum,
    band,
):
    places, rows, width = back_branch.shape
    heads, span = bias.shape
    lanes = heads * head_dim
    scale = head_dim ** (-0.5)
    rows_in_order(scal, w_nat, w_qkv)
    bias_blocks(tb, [bias[h : h + 1, :] for h in range(heads)])
    for q in range(places):
        back_mixed[aligned(place_of(scal, q) * rows, rows), :] = dot_rt(
            back_branch[q], out_rows[...]
        ).astype(bf16)
    key_sum[...] = token_back[...]
    for h in range(heads):
        key_at, value_at = head_cols(1, h, heads, head_dim), head_cols(2, h, heads, head_dim)
        query_at, read_at = head_cols(0, h, heads, head_dim), slice(h * head_dim, (h + 1) * head_dim)
        for c in reversed(range(places)):
            count = min(span, (c + 1) * rows)
            low, high = (c + 1) * rows - count, (c + 1) * rows
            last = c * rows if c == places - 1 else 0
            query, back = qkv[c * rows : high, query_at], back_mixed[c * rows : high, read_at]
            keys = qkv[low:high, key_at]
            probs = window_probs(scal, query, keys, tb[h], last, scale)
            back_probs = dot_rt(back, qkv[low:high, value_at])
            row_dot = jnp.sum(probs * back_probs, axis=-1, keepdims=True)
            back_scores = probs * (back_probs - row_dot)
            if c == places - 1:
                band[...] = back_scores
            else:
                band[:, span - count :] += back_scores
            raw = (back_scores * scale).astype(bf16)
            back_qkv[c * rows : high, query_at] = dot(raw, keys).astype(bf16)
            key_to = slice(key_at.start - lanes, key_at.stop - lanes)
            value_to = slice(value_at.start - lanes, value_at.stop - lanes)
            key_sum[low:high, key_to] += dot_lt(raw, query)
            key_sum[low:high, value_to] += dot_lt(probs.astype(bf16), back)
        distance[h : h + 1, :] = jnp.sum(by_distance(band[...]), axis=0, keepdims=True)
    back_qkv[:, lanes:] = key_sum[...].astype(bf16)
    for start in range(0, width, 256):
        put_rows(
            scal,
            grad_qkv,
            start,
            dot_lt(first[:, start : start + 256], back_qkv[...]).astype(bf16),
        )
    gain_sum, shift_sum = None, None
    for q in range(places):
        back = dot_rt(back_qkv[aligned(place_of(scal, q) * rows, rows), :], w_nat[...])
        back_first[q] = back.astype(bf16)
        hat, _ = normalized(tokens[q].astype(f32))
        gain_term = jnp.sum(back * hat, axis=0, keepdims=True)
        shift_term = jnp.sum(back, axis=0, keepdims=True)
        gain_sum = gain_term if q == 0 else gain_sum + gain_term
        shift_sum = shift_term if q == 0 else shift_sum + shift_term
    grad_norm[0:1, :] = gain_sum
    grad_norm[1:2, :] = shift_sum


def flip_low(i):
    return i + 1 - 2 * (i % 2)


class Mover:
    def __init__(self, send, recv):
        self.send, self.recv, self.sends, self.recvs = send, recv, 0, 0

    def send_slot(self):
        self.sends += 1
        return self.sends - 1

    def recv_slot(self):
        self.recvs += 1
        return self.recvs - 1

    def copy(self, source, target, device, send_slot, recv_slot):
        return pltpu.make_async_remote_copy(
            src_ref=source,
            dst_ref=target,
            send_sem=self.send.at[send_slot],
            recv_sem=self.recv.at[recv_slot],
            device_id=device,
            device_id_type=pl.DeviceIdType.MESH,
        )

    def __call__(self, source, target, device):
        return self.copy(source, target, device, self.send_slot(), self.recv_slot())


class Links:
    def __init__(self):
        self.d, self.s = lax.axis_index("dp"), lax.axis_index("state")
        z, y = self.d // 2, self.d % 2
        self.over_z = [2 * (z + 1 - 2 * (z % 2)) + y, 2 * ((z + 2) % 4) + y, 2 * (3 - z) + y]
        self.over_y = flip_low(self.d)
        self.core, self.x = flip_low(self.s), (self.s + 2) % 4
        self.to_core, self.to_x = (self.d, self.core), (self.d, self.x)
        self.to_y = (self.over_y, self.s)
        self.to_z = [(other, self.s) for other in self.over_z]
        self.in_middle = (z == 1) | (z == 2)
        self.far_middle = 2 * (2 - z // 2) + y
        self.far_end = 2 * (3 - 3 * (z // 2)) + y
        self.to_far = (self.far_middle, self.s)

    def greet(self):
        barrier = pltpu.get_barrier_semaphore()
        partners = [self.to_core, self.to_x, self.to_y, *self.to_z]
        for partner in partners:
            pl.semaphore_signal(
                barrier, inc=1, device_id=partner, device_id_type=pl.DeviceIdType.MESH
            )
        pl.semaphore_wait(barrier, len(partners))


class GroupGather:
    def __init__(self, mover, links, whole, at, source=None):
        self.links, self.parts = links, [links.s, links.core, links.x, flip_low(links.x)]
        own = whole.at[at(links.s)]
        source = own if source is None else source
        across = whole.at[at(links.x)]
        self.over_x = mover(source, own, links.to_x)
        self.beside = mover(source, own, links.to_core)
        self.passed = mover(across, across, links.to_core)

    def start(self):
        self.over_x.start()
        self.beside.start()

    def forward(self):
        self.over_x.wait_recv()
        self.passed.start()

    def finish(self):
        self.beside.wait_recv()
        self.passed.wait_recv()

    def sent(self):
        for copy in (self.over_x, self.beside, self.passed):
            copy.wait_send()


class WeightGather:
    def __init__(self, mover, links, whole, at, source):
        own = whole.at[at(links.d)]
        self.links = links
        near, far = mover.send_slot(), mover.send_slot()
        slots = [mover.recv_slot() for _ in range(3)]
        self.near = mover.copy(source, own, links.to_z[0], near, slots[0])
        self.far = [mover.copy(source, own, links.to_far, far, slots[k]) for k in (1, 2)]
        self.own_y = mover(source, own, links.to_y)
        self.passed, self.relayed = [], [None]
        for k, other in enumerate((links.over_z[0], links.far_middle, links.far_end)):
            block = whole.at[at(other)]
            self.passed.append(mover(block, block, links.to_y))
            if k:
                self.relayed.append(
                    mover.copy(block, block, links.to_z[0], mover.send_slot(), slots[k])
                )

    def start_z(self):
        self.near.start()

        @pl.when(self.links.in_middle)
        def _():
            self.far[0].start()

        @pl.when(jnp.logical_not(self.links.in_middle))
        def _():
            self.far[1].start()

    def start_y(self):
        self.own_y.start()

    def forward(self, k):
        if k == 0:
            self.near.wait_recv()
        else:
            self.relayed[k].wait_recv()

            @pl.when(self.links.in_middle)
            def _():
                self.relayed[k].start()

        self.passed[k].start()

    def finish(self):
        self.own_y.wait_recv()
        for copy in self.passed:
            copy.wait_recv()

    def sent(self):
        for copy in (self.near, self.far[0], self.own_y, *self.passed):
            copy.wait_send()

        @pl.when(self.links.in_middle)
        def _():
            for copy in self.relayed[1:]:
                copy.wait_send()


class GroupSum:
    def __init__(self, mover, links, partial, at, beside, across):
        self.partial, self.at, self.links = partial, at, links
        self.from_core, self.from_x = beside, across
        diagonal = flip_low(links.x)
        self.far = mover(partial.at[at(diagonal)], beside.at[1], links.to_core)
        self.near = mover(partial.at[at(links.core)], beside.at[0], links.to_core)
        self.over = mover(partial.at[at(links.x)], across, links.to_x)

    def start(self):
        self.far.start()
        self.near.start()

    def keep(self):
        self.near.wait_recv()
        pair = self.partial[self.at(self.links.s)].astype(f32) + self.from_core[0].astype(f32)
        self.from_core[0] = pair.astype(bf16)

    def finish_kept(self):
        self.over.wait_recv()
        return self.from_core[0].astype(f32) + self.from_x[...].astype(f32)

    def middle(self):
        self.far.wait_recv()
        place = self.at(self.links.x)
        total = self.partial[place].astype(f32) + self.from_core[1].astype(f32)
        self.partial[place] = total.astype(bf16)
        self.over.start()

    def finish(self):
        self.near.wait_recv()
        pair = self.partial[self.at(self.links.s)].astype(f32) + self.from_core[0].astype(f32)
        self.over.wait_recv()
        return pair + self.from_x[...].astype(f32)

    def sent(self):
        for copy in (self.far, self.near, self.over):
            copy.wait_send()


class WeightSum:
    def __init__(self, mover, links, grads, at, from_y, from_z):
        self.grads, self.at, self.links = grads, at, links
        self.from_y, self.from_z = from_y, from_z
        self.over_y = [
            mover(grads.at[at(flip_low(i))], from_y.at[k], links.to_y)
            for k, i in enumerate([links.d, *links.over_z])
        ]
        self.over_z = [
            mover(grads.at[at(i)], from_z.at[k], partner)
            for k, (i, partner) in enumerate(zip(links.over_z, links.to_z))
        ]

    def start(self):
        for k in (2, 3, 1, 0):
            self.over_y[k].start()

    def forward(self, *order):
        for k in order or (1, 2, 0):
            self.over_y[k + 1].wait_recv()
            place = self.at(self.links.over_z[k])
            total = self.grads[place].astype(f32) + self.from_y[k + 1].astype(f32)
            self.grads[place] = total.astype(bf16)
            self.over_z[k].start()

    def finish(self):
        self.over_y[0].wait_recv()
        total = self.grads[self.at(self.links.d)].astype(f32) + self.from_y[0].astype(f32)
        for k in range(3):
            self.over_z[k].wait_recv()
            total += self.from_z[k].astype(f32)
        return total

    def sent(self):
        for copy in (*self.over_y, *self.over_z):
            copy.wait_send()


class SmallSum:
    def __init__(self, mover, links, value, arrived):
        self.value, self.arrived = value, arrived
        partners = [links.to_core, links.to_x, links.to_z[0], links.to_z[1], links.to_y]
        self.copies = [mover(value.at[k], arrived.at[k], to) for k, to in enumerate(partners)]

    def start(self):
        self.copies[0].start()

    def step(self, k):
        self.copies[k].wait_recv()
        self.value[k + 1] = self.value[k] + self.arrived[k]
        if k + 1 < len(self.copies):
            self.copies[k + 1].start()

    def sent(self):
        for copy in self.copies:
            copy.wait_send()


LAYER_COPIES = 160


def layer(
    head_dim,
    length,
    tokens,
    state,
    cot,
    state_cot,
    w_qkv,
    w_out,
    w_sqkv,
    w_sout,
    w_up,
    w_down,
    buckets,
    rel_table,
    gains,
    shifts,
    gate_bias,
    output,
    next_state,
    grad_tokens,
    grad_state,
    grad_qkv,
    grad_out,
    grad_sqkv,
    grad_sout,
    grad_up,
    grad_down,
    grad_rel,
    grad_norm,
    send_sem,
    recv_sem,
    local_sem,
    slab,
    qkv_nat,
    sqkv_nat,
    out_nat,
    sout_nat,
    up_nat,
    down_nat,
    tok_all,
    cot_all,
    state_all,
    mixed,
    read_all,
    hid,
    first,
    qkv,
    second,
    sqkv,
    back_read,
    back_sqkv,
    own_sum,
    key_sum,
    res_own,
    tb,
    band,
    own_state,
    own_scot,
    beside_state,
    across_state,
    back_mixed,
    out_rows,
    state_grads,
    down_grads,
    y_state,
    y_down,
    y_up,
    y_out,
    z_state,
    z_down,
    z_up,
    z_out,
    beside_rows,
    across_rows,
    beside_ffn,
    across_ffn,
    small,
    small_in,
    distance,
    landed,
    credit,
):
    rows, width = tokens.shape
    state_rows = state.shape[0]
    heads, _, span = tb.shape
    lanes = heads * head_dim
    depth = w_qkv.shape[0]
    inner_width = up_nat.shape[1]
    all_states = 4 * state_rows
    group_rows = 4 * rows
    scale = head_dim ** (-0.5)
    links = Links()
    s, d = links.s, links.d
    mover = Mover(send_sem, recv_sem)
    back_qkv, back_second, back_input = sqkv_nat, out_nat, sout_nat
    ffn_partial, back_first, back_branch = up_nat, down_nat, cot_all
    slope, up_grads = state_all, state_all
    back_state, ship, back_res = down_grads, slab, own_sum
    hidden, token_grads = hid, hid

    def block(i, size):
        return pl.ds(pl.multiple_of(i * size, size), size)

    def own_rows(size):
        return lambda i: (block(i, size), slice(None))

    def own_lanes(size):
        return lambda i: (slice(None), block(i, size))

    def cot_rows(i):
        return (pl.ds(pl.multiple_of(all_states + i * state_rows, state_rows), state_rows), slice(None))

    own_columns = block(s, lanes)

    def own_out(i):
        return (block(i, depth), own_columns)

    def lanes_from(start, size):
        return pl.ds(pl.multiple_of(start * lanes, lanes), size * lanes)

    to_slab = []
    for k, shard in enumerate((w_qkv, w_sqkv)):
        core_slot = 1 - links.core % 2 + links.core // 2
        x_slot = 2 - 2 * (links.x // 2)
        to_slab.append(
            (
                mover(
                    shard.at[:, block(2 - 2 * (s % 2), lanes)],
                    slab.at[k, :, block(x_slot, lanes)],
                    links.to_x,
                ),
                mover(
                    shard.at[:, lanes : 2 * lanes],
                    slab.at[k, :, block(core_slot, lanes)],
                    links.to_core,
                ),
            )
        )
    get_tokens = GroupGather(mover, links, tok_all, own_rows(rows), tokens)
    get_state = GroupGather(mover, links, state_all, own_rows(state_rows), state)
    get_scot = GroupGather(mover, links, state_all, cot_rows, state_cot)
    get_cot = GroupGather(mover, links, cot_all, own_rows(rows), cot)
    dp_sout = WeightGather(mover, links, sout_nat, own_out, w_sout)
    dp_out = WeightGather(mover, links, out_nat, own_out, w_out)
    dp_qkv = WeightGather(mover, links, qkv_nat, own_rows(depth), slab.at[0])
    dp_sqkv = WeightGather(mover, links, sqkv_nat, own_rows(depth), slab.at[1])
    dp_up = WeightGather(mover, links, up_nat, own_rows(depth), w_up)
    dp_down = WeightGather(mover, links, down_nat, own_lanes(depth), w_down)
    get_sout = GroupGather(mover, links, sout_nat, own_lanes(lanes))
    get_out = GroupGather(mover, links, out_nat, own_lanes(lanes))
    get_mixed = GroupGather(mover, links, mixed, own_lanes(lanes))
    get_read = GroupGather(mover, links, read_all, own_lanes(lanes))
    get_branch = GroupGather(mover, links, back_branch, own_rows(rows))
    sum_state = GroupSum(
        mover,
        links,
        back_state,
        own_rows(state_rows),
        beside_state,
        across_state,
    )
    sum_second = GroupSum(mover, links, back_second, own_rows(rows), beside_rows, across_rows)
    sum_ffn = GroupSum(mover, links, ffn_partial, own_rows(rows), beside_ffn, across_ffn)
    sum_first = GroupSum(mover, links, back_first, own_rows(rows), beside_rows, across_rows)
    dp_state = WeightSum(mover, links, state_grads, own_rows(depth), y_state, z_state)
    dp_grad_down = WeightSum(mover, links, down_grads, own_lanes(depth), y_down, z_down)
    dp_grad_up = WeightSum(mover, links, up_grads, own_rows(depth), y_up, z_up)
    dp_grad_out = WeightSum(
        mover,
        links,
        token_grads,
        lambda i: (block(i, depth), slice(3 * lanes, 4 * lanes)),
        y_out,
        z_out,
    )
    dp_grad_qkv = WeightSum(
        mover,
        links,
        token_grads,
        lambda i: (block(i, depth), slice(0, 3 * lanes)),
        y_state.at[:, :, 0 : 3 * lanes],
        z_state.at[:, :, 0 : 3 * lanes],
    )
    sum_small = SmallSum(mover, links, small, small_in)
    to_owner = [
        (
            mover(
                ship.at[k, :, block(2 - 2 * (s // 2), lanes)],
                landed.at[k, :, block(2 - 2 * (s % 2), lanes)],
                links.to_x,
            ),
            mover(
                ship.at[k, :, block(1 - s % 2 + s // 2, lanes)],
                landed.at[k, :, lanes : 2 * lanes],
                links.to_core,
            ),
        )
        for k in range(2)
    ]
    assert max(mover.sends, mover.recvs) <= LAYER_COPIES

    local = []
    for source, target in (
        (w_qkv.at[:, block(2 * (s % 2), lanes)], slab.at[0, :, block((s + 1) // 2, lanes)]),
        (w_sqkv.at[:, block(2 * (s % 2), lanes)], slab.at[1, :, block((s + 1) // 2, lanes)]),
        (tokens, tok_all.at[block(s, rows), :]),
        (state, state_all.at[block(s, state_rows), :]),
        (state_cot, state_all.at[cot_rows(s)]),
        (cot, cot_all.at[block(s, rows), :]),
        (w_up, up_nat.at[block(d, depth), :]),
        (w_down, down_nat.at[:, block(d, depth)]),
        (w_out, out_nat.at[block(d, depth), own_columns]),
        (w_sout, sout_nat.at[block(d, depth), own_columns]),
        (state, own_state),
        (state_cot, own_scot),
    ):
        local.append(pltpu.make_async_copy(source, target, local_sem.at[len(local)]))

    links.greet()
    for over_x, beside in to_slab:
        over_x.start()
        beside.start()
    dp_sout.start_z()
    dp_sout.start_y()
    get_tokens.start()
    for copy in local:
        copy.start()
    small[0] = jnp.zeros(small.shape[1:], f32)
    key_sum[...] = jnp.zeros_like(key_sum)
    own_sum[...] = jnp.zeros_like(own_sum)
    for k, gather in enumerate((dp_qkv, dp_sqkv)):
        for copy in (*to_slab[k],):
            copy.wait_recv()
        local[k].wait()
        if k == 0:
            gather.start_z()
            gather.start_y()
    get_state.start()
    get_scot.start()
    get_cot.start()
    qkv_nat[block(d, depth), :] = slab[0]
    sqkv_nat[block(d, depth), :] = slab[1]
    for copy in local[2:]:
        copy.wait()

    def token_norm(i):
        at = block(i, rows)
        hat, _ = normalized(tok_all[at, :].astype(f32))
        first[at, :] = (hat * gains[0:1, :] + shifts[0:1, :]).astype(bf16)

    token_norm(s)
    for k in range(3):
        dp_sout.forward(k)
    dp_sqkv.start_z()
    bias = lax.dot_general(
        rel_table[...],
        buckets[:, 0 : rel_table.shape[0]],
        (((0,), (1,)), ((), ())),
        precision=lax.Precision.HIGHEST,
        preferred_element_type=f32,
    )
    column = lax.broadcasted_iota(jnp.int32, bias.shape, 1)
    distance[...] = jnp.where((column > 0) & (column <= span - rows), bias, masked_value)
    bias_blocks(tb, [distance[pl.ds(s * heads + h, 1), :] for h in range(heads)])
    distance[...] = jnp.zeros_like(distance)
    get_tokens.beside.wait_recv()
    token_norm(links.core)
    dp_qkv.forward(0)
    dp_qkv.forward(1)
    get_tokens.forward()
    token_norm(links.x)
    dp_qkv.forward(2)
    dp_out.start_z()
    dp_up.start_z()
    dp_sout.finish()
    get_sout.start()
    dp_sqkv.start_y()
    dp_sqkv.forward(0)
    get_tokens.passed.wait_recv()
    token_norm(flip_low(links.x))
    get_state.forward()
    dp_sqkv.forward(1)
    dp_qkv.finish()

    def token_qkv(i, carry):
        at = block(i, rows)
        qkv[at, :] = dot(first[at, :], qkv_nat[...]).astype(bf16)
        return carry

    lax.fori_loop(0, 4, token_qkv, 0)
    for c in range(4):
        count = min(span, (c + 1) * rows)
        low, high = (c + 1) * rows - count, (c + 1) * rows
        last = c * rows if c == 3 else 0
        parts = []
        for h in range(heads):
            probs = window_probs(
                (0, length[0]),
                qkv[c * rows : high, head_cols(0, h, heads, head_dim)],
                qkv[low:high, head_cols(1, h, heads, head_dim)],
                tb[h],
                last,
                scale,
            )
            parts.append(
                dot(probs.astype(bf16), qkv[low:high, head_cols(2, h, heads, head_dim)])
            )
        mixed[c * rows : high, own_columns] = jnp.concatenate(parts, axis=1).astype(bf16)
        if c == 0:
            dp_sqkv.forward(2)
            dp_down.start_z()
            dp_out.start_y()
        else:
            dp_out.forward(c - 1)
    get_mixed.start()
    dp_up.start_y()
    dp_up.forward(0)
    get_scot.forward()
    get_sout.forward()
    get_cot.forward()

    get_state.finish()

    def state_norms(i, carry):
        at = block(i, state_rows)
        hat, _ = normalized(state_all[at, :].astype(f32))
        hid[at, :] = (hat * gains[2:3, :] + shifts[2:3, :]).astype(bf16)
        return carry

    lax.fori_loop(0, 4, state_norms, 0)
    dp_sqkv.finish()
    state_norm, back_update = slice(0, all_states), slice(all_states, 2 * all_states)
    sqkv[...] = dot(hid[state_norm, :], sqkv_nat[...]).astype(bf16)
    dp_out.finish()
    get_out.start()
    dp_up.forward(1)

    def state_read(i, carry):
        at = block(i, state_rows)
        parts = []
        for h in range(heads):
            own, token = state_probs(
                (0, length[0]),
                sqkv[at, head_cols(0, h, heads, head_dim)],
                sqkv[:, head_cols(1, h, heads, head_dim)],
                qkv[:, head_cols(1, h, heads, head_dim)],
                scale,
            )
            parts.append(
                dot(own.astype(bf16), sqkv[:, head_cols(2, h, heads, head_dim)])
                + dot(token.astype(bf16), qkv[:, head_cols(2, h, heads, head_dim)])
            )
        read_all[at, own_columns] = jnp.concatenate(parts, axis=1).astype(bf16)
        return carry

    lax.fori_loop(0, 4, state_read, 0)
    get_read.start()
    dp_up.forward(2)
    dp_down.start_y()
    dp_down.forward(0)
    get_mixed.forward()

    gate = jax.nn.sigmoid(gate_bias[...])
    get_scot.finish()

    def updates(i, carry):
        hid[cot_rows(i)] = ((1.0 - gate) * state_all[cot_rows(i)].astype(f32)).astype(bf16)
        return carry

    lax.fori_loop(0, 4, updates, 0)
    get_sout.finish()
    back_read[...] = dot_rt(hid[back_update, :], sout_nat[block(s, lanes), :]).astype(bf16)

    def state_back(h):
        key_at, value_at = head_cols(1, h, heads, head_dim), head_cols(2, h, heads, head_dim)
        query_at, read_at = head_cols(0, h, heads, head_dim), head_cols(0, h, heads, head_dim)

        def one(i, carry):
            at = block(i, state_rows)
            query, back = sqkv[at, query_at], back_read[at, read_at]
            own, token = state_probs(
                (0, length[0]), query, sqkv[:, key_at], qkv[:, key_at], scale
            )
            back_own = dot_rt(back, sqkv[:, value_at])
            back_token = dot_rt(back, qkv[:, value_at])
            row_dot = jnp.sum(own * back_own, axis=-1, keepdims=True) + jnp.sum(
                token * back_token, axis=-1, keepdims=True
            )
            own_raw = (own * (back_own - row_dot) * scale).astype(bf16)
            token_raw = (token * (back_token - row_dot) * scale).astype(bf16)
            back_sqkv[at, query_at] = (
                dot(own_raw, sqkv[:, key_at]) + dot(token_raw, qkv[:, key_at])
            ).astype(bf16)
            key_to = slice(key_at.start - lanes, key_at.stop - lanes)
            value_to = slice(value_at.start - lanes, value_at.stop - lanes)
            own_sum[:, key_to] += dot_lt(own_raw, query)
            own_sum[:, value_to] += dot_lt(own.astype(bf16), back)
            key_sum[:, key_to] += dot_lt(token_raw, query)
            key_sum[:, value_to] += dot_lt(token.astype(bf16), back)
            return carry

        lax.fori_loop(0, 4, one, 0)

    for h in range(heads):
        state_back(h)
        if h == 0:
            dp_down.forward(1)
    back_sqkv[:, lanes:] = own_sum[...].astype(bf16)

    back_state[0:all_states, :] = dot_rt(back_sqkv[...], sqkv_nat[...]).astype(bf16)
    sum_state.start()
    dp_down.forward(2)

    for start in range(0, width, 256):
        at = slice(start, start + 256)
        state_grads[at, 0 : 3 * lanes] = dot_lt(hid[state_norm, at], back_sqkv[...]).astype(bf16)
    sum_state.middle()
    sum_state.keep()
    get_out.forward()
    get_read.forward()

    get_read.finish()
    update = dot(read_all[block(s, state_rows), :], sout_nat[...])
    held, own_cot = own_state[...].astype(f32), own_scot[...].astype(f32)
    next_state[...] = (gate * held + (1.0 - gate) * update).astype(bf16)
    small[0, 6:7, :] = jnp.sum(own_cot * (held - update), axis=0, keepdims=True) * (
        gate * (1.0 - gate)
    )
    state_grads[:, 3 * lanes : 4 * lanes] = dot_lt(
        read_all[...], hid[back_update, own_columns]
    ).astype(bf16)

    get_mixed.finish()
    get_out.finish()
    dp_up.finish()
    get_cot.finish()
    for gather in (get_state, get_scot, get_sout, dp_sout, get_out, dp_out, dp_sqkv):
        gather.sent()
    out_rows[...] = out_nat[block(s, lanes), :]
    dp_state.start()

    def ffn_rows(i, carry):
        at = block(i, rows)
        total = tok_all[at, :].astype(f32) + dot(mixed[at, :], out_nat[...])

        @pl.when(i == s)
        def _():
            res_own[...] = total

        hat, _ = normalized(total)
        normed = (hat * gains[1:2, :] + shifts[1:2, :]).astype(bf16)
        second[at, :] = normed
        inner = dot(normed, up_nat[...])
        root = 0.7978845608028654
        square = inner * inner
        bend = jnp.tanh(root * inner * (1.0 + 0.044715 * square))
        half = 0.5 * (1.0 + bend)
        hidden[at, :] = (inner * half).astype(bf16)
        slope[at, :] = (
            half + (0.5 * root) * inner * (1.0 - bend * bend) * (1.0 + (3 * 0.044715) * square)
        ).astype(bf16)
        return carry

    lax.fori_loop(0, 4, ffn_rows, 0)

    sum_state.sent()

    def down_columns(i, carry):
        at = block(i, 256)
        down_grads[:, at] = dot_lt(hidden[...], cot_all[:, at]).astype(bf16)
        return carry

    lax.fori_loop(0, width // 256, down_columns, 0)
    dp_grad_down.start()
    get_cot.sent()
    dp_down.finish()

    def ffn_back_rows(i, carry):
        at = block(i, rows)
        inner = (dot_rt(cot_all[at, :], down_nat[...]) * slope[at, :].astype(f32)).astype(bf16)
        back_input[at, :] = inner
        back_second[at, :] = dot_rt(inner, up_nat[...]).astype(bf16)
        return carry

    lax.fori_loop(0, 4, ffn_back_rows, 0)
    kept_cot = cot_all[block(s, rows), :].astype(f32)
    sum_second.start()

    def up_columns(i, carry):
        at = block(i, 256)
        up_grads[at, :] = dot_lt(second[:, at], back_input[...]).astype(bf16)
        return carry

    lax.fori_loop(0, width // 256, up_columns, 0)
    dp_grad_up.start()
    sum_second.middle()
    dp_state.forward(1)
    dp_up.sent()

    def ffn_out_rows(i, carry):
        at = block(i, rows)
        ffn_partial[at, :] = dot(hidden[at, :], down_nat[...]).astype(bf16)
        return carry

    lax.fori_loop(0, 4, ffn_out_rows, 0)
    sum_ffn.start()
    dp_down.sent()
    hat_state, inverse_state = normalized(own_state[...].astype(f32))
    back_own_state = sum_state.finish_kept()
    small[0, 2:3, :] = jnp.sum(back_own_state * hat_state, axis=0, keepdims=True)
    small[0, 5:6, :] = jnp.sum(back_own_state, axis=0, keepdims=True)
    grad_state[...] = (
        gate * own_scot[...].astype(f32)
        + normed_back(back_own_state, hat_state, inverse_state, gains[2:3, :])
    ).astype(bf16)
    dp_state.forward(2, 0)

    hat_mid, inverse_mid = normalized(res_own[...])
    back_own = sum_second.finish()
    own_back = kept_cot + normed_back(back_own, hat_mid, inverse_mid, gains[1:2, :])
    back_branch[block(s, rows), :] = own_back.astype(bf16)
    get_branch.start()
    back_res[0:rows, :] = own_back[:, 0 : width // 2]
    back_res[rows : 2 * rows, :] = own_back[:, width // 2 :]
    small[0, 1:2, :] = jnp.sum(back_own * hat_mid, axis=0, keepdims=True)
    small[0, 4:5, :] = jnp.sum(back_own, axis=0, keepdims=True)
    sum_ffn.middle()

    def mixed_back(i):
        back_mixed[block(i, rows), :] = dot_rt(
            back_branch[block(i, rows), :], out_rows[...]
        ).astype(bf16)

    mixed_back(s)
    get_branch.beside.wait_recv()
    mixed_back(links.core)
    dp_grad_down.forward(1)
    get_branch.forward()
    mixed_back(links.x)
    get_branch.passed.wait_recv()
    mixed_back(flip_low(links.x))
    token_grads[:, 3 * lanes : 4 * lanes] = dot_lt(
        mixed[...], back_branch[:, own_columns]
    ).astype(bf16)
    dp_grad_out.start()
    dp_grad_down.forward(2)
    state_total = dp_state.finish()
    for partner in (links.to_y, *links.to_z):
        pl.semaphore_signal(credit, inc=1, device_id=partner, device_id_type=pl.DeviceIdType.MESH)
    dp_qkv.sent()
    grad_sout[...] = state_total[:, 3 * lanes :].astype(bf16)
    ship[1] = state_total[:, : 3 * lanes].astype(bf16)
    grad_sqkv[:, block(2 * (s % 2), lanes)] = ship[1, :, block((s + 1) // 2, lanes)]
    for copy in to_owner[1]:
        copy.start()

    for h in range(heads):
        key_at, value_at = head_cols(1, h, heads, head_dim), head_cols(2, h, heads, head_dim)
        query_at, read_at = head_cols(0, h, heads, head_dim), head_cols(0, h, heads, head_dim)
        for c in reversed(range(4)):
            count = min(span, (c + 1) * rows)
            low, high = (c + 1) * rows - count, (c + 1) * rows
            last = c * rows if c == 3 else 0
            query, back = qkv[c * rows : high, query_at], back_mixed[c * rows : high, read_at]
            keys = qkv[low:high, key_at]
            probs = window_probs((0, length[0]), query, keys, tb[h], last, scale)
            back_probs = dot_rt(back, qkv[low:high, value_at])
            row_dot = jnp.sum(probs * back_probs, axis=-1, keepdims=True)
            back_scores = probs * (back_probs - row_dot)
            if c == 3:
                band[...] = back_scores
            else:
                band[:, span - count :] += back_scores
            raw = (back_scores * scale).astype(bf16)
            back_qkv[c * rows : high, query_at] = dot(raw, keys).astype(bf16)
            key_to = slice(key_at.start - lanes, key_at.stop - lanes)
            value_to = slice(value_at.start - lanes, value_at.stop - lanes)
            key_sum[low:high, key_to] += dot_lt(raw, query)
            key_sum[low:high, value_to] += dot_lt(probs.astype(bf16), back)
        distance[pl.ds(s * heads + h, 1), :] = jnp.sum(by_distance(band[...]), axis=0, keepdims=True)
        if h == 0:
            dp_grad_down.forward(0)
    back_qkv[:, lanes:] = key_sum[...].astype(bf16)
    small[0, 0:1, :] = jnp.zeros((1, width), f32)
    small[0, 3:4, :] = jnp.zeros((1, width), f32)

    def first_partial(i, carry):
        at = block(i, rows)
        back = dot_rt(back_qkv[at, :], qkv_nat[...])
        back_first[at, :] = back.astype(bf16)
        hat, _ = normalized(tok_all[at, :].astype(f32))
        small[0, 0:1, :] += jnp.sum(back * hat, axis=0, keepdims=True)
        small[0, 3:4, :] += jnp.sum(back, axis=0, keepdims=True)
        return carry

    lax.fori_loop(0, 4, first_partial, 0)
    sum_first.start()
    small[0, 8:16, 0:128] = lax.dot_general(
        distance[...],
        buckets[...],
        (((1,), (0,)), ((), ())),
        precision=lax.Precision.HIGHEST,
        preferred_element_type=f32,
    )
    sum_small.start()

    def qkv_grads(i, carry):
        at = block(i, 256)
        token_grads[at, 0 : 3 * lanes] = dot_lt(first[:, at], back_qkv[...]).astype(bf16)
        return carry

    lax.fori_loop(0, width // 256, qkv_grads, 0)
    pl.semaphore_wait(credit, 4)
    dp_grad_qkv.start()
    sum_first.middle()
    sum_small.step(0)
    dp_grad_up.forward(1)
    grad_down[...] = dp_grad_down.finish().astype(bf16)
    output[...] = (res_own[...] + sum_ffn.finish()).astype(bf16)
    dp_grad_up.forward(2)
    hat_first, inverse_first = normalized(tok_all[block(s, rows), :].astype(f32))
    sum_small.step(1)
    back_own_first = sum_first.finish()
    own_back = jnp.concatenate([back_res[0:rows, :], back_res[rows : 2 * rows, :]], axis=1)
    grad_tokens[...] = (
        own_back + normed_back(back_own_first, hat_first, inverse_first, gains[0:1, :])
    ).astype(bf16)
    dp_grad_up.forward(0)
    sum_small.step(2)
    dp_grad_out.forward()
    sum_small.step(3)
    dp_grad_qkv.forward()
    grad_up[...] = dp_grad_up.finish().astype(bf16)
    grad_out[...] = dp_grad_out.finish().astype(bf16)
    sum_small.step(4)
    grad_norm[...] = small[5, 0:8, :]
    grad_rel[...] = small[5, 8:16, 0:128]
    ship[0] = dp_grad_qkv.finish().astype(bf16)
    for copy in to_owner[0]:
        copy.start()
    grad_qkv[:, block(2 * (s % 2), lanes)] = ship[0, :, block((s + 1) // 2, lanes)]
    for k, grads in ((1, grad_sqkv), (0, grad_qkv)):
        for copy in to_owner[k]:
            copy.wait_recv()
        grads[:, lanes : 2 * lanes] = landed[k, :, lanes : 2 * lanes]
        x_at = block(2 - 2 * (s % 2), lanes)
        grads[:, x_at] = landed[k, :, x_at]
    for over_x, beside in (*to_slab, *to_owner):
        over_x.wait_send()
        beside.wait_send()
    for used in (
        get_tokens,
        get_mixed,
        get_read,
        get_branch,
        sum_second,
        sum_ffn,
        sum_first,
        dp_state,
        dp_grad_down,
        dp_grad_up,
        dp_grad_out,
        dp_grad_qkv,
        sum_small,
    ):
        used.sent()


def settle(
    output,
    next_state,
    grad_tokens,
    grad_state,
    grad_qkv,
    grad_out,
    grad_sqkv,
    grad_sout,
    grad_up,
    grad_down,
    grad_rel,
    grad_norm,
    *results,
):
    for result, value in zip(results, (output, next_state, grad_tokens, grad_state)):
        if len(result.shape) == 3:
            result[0] = value[...]
        else:
            result[...] = value[...]
    grads = (grad_qkv, grad_out, grad_sqkv, grad_sout, grad_up, grad_down)
    for result, value in zip(results[4:], grads):
        result[...] = value[...].astype(f32)
    rel, gain, shift, gate = results[10:]
    rel[...] = grad_rel[...].T[0 : rel.shape[0], :]
    gain[...] = grad_norm[0:3, :]
    shift[...] = grad_norm[3:6, :]
    gate[...] = grad_norm[6:7, :]


def norm_back(values, back, gain):
    hat, inverse = normalized(values)
    return normed_back(back, hat, inverse, gain)


def per_device(
    tokens,
    state_in,
    cotangent,
    state_cotangent,
    seq_len,
    bucket_table,
    w_qkv,
    w_out,
    w_sqkv,
    w_sout,
    w_up,
    w_down,
    rel_table,
    norm_gain,
    norm_shift,
    gate_bias,
):
    rows, width = tokens.shape
    bucket_count, head_count = rel_table.shape
    window = bucket_table.shape[0]
    state_rows = state_in.shape[1]
    places = lax.axis_size("state")
    assert places == len(PLACES)
    dp_count = lax.axis_size("dp")
    here, dp_here = lax.axis_index("state"), lax.axis_index("dp")
    head_dim = width // head_count
    heads = head_count // places
    lanes = heads * head_dim
    span = window + rows
    group_rows = rows * places
    all_states = state_rows * places
    inner_width = w_up.shape[1]
    hops = dp_count == len(DP_PLACES)
    blocks = dp_count if hops else 1

    def swap(value, axis, bit):
        count = lax.axis_size(axis)
        return lax.ppermute(value, axis, [(i, i ^ bit) for i in range(count)])

    def from_group(value):
        pair = jnp.stack([value, swap(value, "state", 2)])
        return jnp.concatenate([pair, swap(pair, "state", 1)], axis=0)

    def list_from_group(value):
        across = swap(value, "state", 2)
        return [value, across, swap(value, "state", 1), swap(across, "state", 1)]

    def sum_to_owner(partial):
        half = partial.shape[0] // 2
        pair = partial[:half].astype(f32) + swap(partial[half:], "state", 1).astype(f32)
        return pair[0] + swap(pair[1].astype(bf16), "state", 2).astype(f32)

    def from_dp(block, axis):
        if not hops:
            return lax.all_gather(block, "dp", axis=axis, tiled=True)[None]
        gathered = block[None]
        for bit in DP_STEPS:
            gathered = jnp.concatenate([gathered, swap(gathered, "dp", bit)], axis=0)
        return gathered

    def sum_over_dp(partial, axis):
        if not hops:
            return lax.psum_scatter(partial[0], "dp", scatter_dimension=axis, tiled=True).astype(f32)
        for bit in reversed(DP_STEPS):
            half = partial.shape[0] // 2
            arrived = swap(partial[half:], "dp", bit)
            total = partial[:half].astype(f32) + arrived.astype(f32)
            partial = total.astype(bf16)
        return total[0]

    def sum_over_all(vector):
        if not hops:
            return lax.psum(vector, ("dp", "state"))
        for axis, bit in (("state", 1), ("state", 2), ("dp", 1), ("dp", 2), ("dp", 4)):
            vector = vector + swap(vector, axis, bit)
        return vector

    even = here % 2 == 0

    def pick(*by_place):
        value = by_place[-1]
        for i in reversed(range(places - 1)):
            value = jnp.where(here == i, by_place[i], value)
        return value

    def to_heads(shard):
        left, middle, right = (shard[:, i * lanes : (i + 1) * lanes] for i in range(3))
        own = jnp.where(even, left, right)
        across = swap(jnp.where(even, right, left), "state", 2)
        beside = swap(middle, "state", 1)
        query = pick(own, beside, across, across)
        keys = pick(beside, own, own, beside)
        values = pick(across, across, beside, own)
        return jnp.concatenate([query, keys, values], axis=1)

    def from_heads(grads):
        query, keys, values = (grads[:, i * lanes : (i + 1) * lanes] for i in range(3))
        own = pick(query, keys, keys, values)
        beside = swap(pick(keys, query, values, keys), "state", 1)
        across = swap(pick(values, values, query, query), "state", 2)
        return jnp.concatenate(
            [jnp.where(even, own, across), beside, jnp.where(even, across, own)], axis=1
        )

    if hops:
        block_list = dp_here ^ jnp.array(DP_PLACES, jnp.int32)
        position_list = jnp.array(
            [DP_PLACES.index(i) for i in range(dp_count)], jnp.int32
        )[dp_here ^ jnp.arange(dp_count)]
    else:
        block_list = position_list = jnp.zeros((1,), jnp.int32)
    scal = jnp.concatenate(
        [here[None].astype(jnp.int32), seq_len.astype(jnp.int32), block_list, position_list]
    ).astype(jnp.int32)

    gains = [norm_gain[i : i + 1] for i in range(3)]
    shifts = [norm_shift[i : i + 1] for i in range(3)]

    depth = w_qkv.shape[0]
    lookup = (bucket_table[:, None] == jnp.arange(bucket_count)[None, :]).astype(f32)
    if hops:
        by_bucket = jnp.concatenate(
            [
                jnp.zeros((1, bucket_count), f32),
                lookup[::-1],
                jnp.zeros((span - window - 1, bucket_count), f32),
            ],
            axis=0,
        )
        by_bucket = jnp.pad(by_bucket, ((0, 0), (0, 128 - bucket_count)))
        whole = pl.BlockSpec(memory_space=pltpu.VMEM)
        anywhere = pl.BlockSpec(memory_space=pl.ANY)
        vmem = lambda shape, kind=bf16: pltpu.VMEM(shape, kind)
        square = vmem((width, width))
        summed = pl.pallas_call(
            functools.partial(layer, head_dim),
            out_shape=[
                out((rows, width)),
                out((state_rows, width)),
                out((rows, width)),
                out((state_rows, width)),
                out((depth, 3 * lanes)),
                out((depth, lanes)),
                out((depth, 3 * lanes)),
                out((depth, lanes)),
                out((depth, inner_width)),
                out((inner_width, depth)),
                out((head_count, 128), f32),
                out((8, width), f32),
            ],
            in_specs=[pl.BlockSpec(memory_space=pltpu.SMEM)] + [anywhere] * 10 + [whole] * 5,
            out_specs=[whole] * 12,
            scratch_shapes=[
                pltpu.SemaphoreType.DMA((LAYER_COPIES,)),
                pltpu.SemaphoreType.DMA((LAYER_COPIES,)),
                pltpu.SemaphoreType.DMA((16,)),
                vmem((2, depth, 3 * lanes)),
                vmem((width, 3 * lanes)),
                vmem((width, 3 * lanes)),
                square,
                square,
                vmem((width, inner_width)),
                vmem((inner_width, width)),
                vmem((group_rows, width)),
                vmem((group_rows, width)),
                vmem((2 * all_states, width)),
                vmem((group_rows, width)),
                vmem((all_states, width)),
                vmem((2 * all_states, width)),
                vmem((group_rows, width)),
                vmem((group_rows, 3 * lanes)),
                vmem((group_rows, width)),
                vmem((all_states, 3 * lanes)),
                vmem((all_states, lanes)),
                vmem((all_states, 3 * lanes)),
                vmem((all_states, 2 * lanes), f32),
                vmem((group_rows, 2 * lanes), f32),
                vmem((rows, width), f32),
                vmem((heads, rows, span), f32),
                vmem((rows, span), f32),
                vmem((state_rows, width)),
                vmem((state_rows, width)),
                vmem((2, state_rows, width)),
                vmem((state_rows, width)),
                vmem((group_rows, lanes)),
                vmem((lanes, width)),
                square,
                vmem((inner_width, width)),
                vmem((4, depth, 4 * lanes)),
                vmem((4, inner_width, depth)),
                vmem((4, depth, inner_width)),
                vmem((4, depth, lanes)),
                vmem((3, depth, 4 * lanes)),
                vmem((3, inner_width, depth)),
                vmem((3, depth, inner_width)),
                vmem((3, depth, lanes)),
                vmem((2, rows, width)),
                vmem((rows, width)),
                vmem((2, rows, width)),
                vmem((rows, width)),
                vmem((6, 16, width), f32),
                vmem((5, 16, width), f32),
                vmem((8, span), f32),
                vmem((2, depth, 3 * lanes)),
                pltpu.SemaphoreType.REGULAR,
            ],
            compiler_params=pltpu.CompilerParams(
                collective_id=0, has_side_effects=True, vmem_limit_bytes=64 << 20
            ),
            name="layer",
        )(
            seq_len,
            tokens,
            state_in[0],
            cotangent,
            state_cotangent[0],
            w_qkv,
            w_out,
            w_sqkv,
            w_sout,
            w_up,
            w_down,
            by_bucket,
            rel_table,
            norm_gain,
            norm_shift,
            gate_bias[None],
        )
        results = pl.pallas_call(
            settle,
            out_shape=[
                out((rows, width)),
                out((1, state_rows, width)),
                out((rows, width)),
                out((1, state_rows, width)),
                out((depth, 3 * lanes), f32),
                out((depth, lanes), f32),
                out((depth, 3 * lanes), f32),
                out((depth, lanes), f32),
                out((depth, inner_width), f32),
                out((inner_width, depth), f32),
                out((bucket_count, head_count), f32),
                out((3, width), f32),
                out((3, width), f32),
                out((1, width), f32),
            ],
            in_specs=[whole] * 12,
            out_specs=[whole] * 14,
            compiler_params=pltpu.CompilerParams(vmem_limit_bytes=24 << 20),
            name="settle",
        )(*summed)
        return (*results[:13], results[13][0])

    own_table = lax.dynamic_slice_in_dim(rel_table, here * heads, heads, 1)
    bias_rows = jnp.dot(
        own_table.T, lookup.T, precision=lax.Precision.HIGHEST, preferred_element_type=f32
    )
    bias = jnp.concatenate(
        [
            jnp.full((heads, 1), masked_value, f32),
            bias_rows[:, ::-1],
            jnp.full((heads, span - window - 1), masked_value, f32),
        ],
        axis=1,
    )
    both = to_heads(jnp.concatenate([w_qkv, w_sqkv], axis=0))
    full_qkv = from_dp(both[:depth], 0)
    all_tokens = from_group(tokens)
    full_sqkv = from_dp(both[depth:], 0)
    all_state = from_group(state_in[0])
    all_cot = from_group(cotangent)
    all_state_cot = from_group(state_cotangent[0])
    outs_pair = from_dp(jnp.concatenate([w_out, w_sout], axis=1), 0)
    half = outs_pair.shape[2] // 2
    full_sout = list_from_group(outs_pair[:, :, half:])
    full_out = list_from_group(outs_pair[:, :, :half])
    full_up = from_dp(w_up, 0)
    full_down = from_dp(w_down, 1)

    first, qkv, mixed = call(
        functools.partial(token_forward, head_dim),
        "token_forward",
        [out((group_rows, width)), out((group_rows, 3 * lanes)), out((places, rows, lanes))],
        [pltpu.VMEM((width, 3 * lanes), bf16), pltpu.VMEM((heads, rows, span), f32)],
        2 * group_rows * width * 3 * lanes,
        group_rows * span * heads,
        scal,
        all_tokens,
        gains[0],
        shifts[0],
        full_qkv,
        bias,
    )
    mixed_parts = list_from_group(mixed)

    state_norm, sqkv, read = call(
        functools.partial(state_forward, head_dim),
        "state_forward",
        [
            out((all_states, width)),
            out((all_states, 3 * lanes)),
            out((places, state_rows, lanes)),
        ],
        [pltpu.VMEM((width, 3 * lanes), bf16)],
        2 * all_states * width * 3 * lanes,
        all_states * (all_states + group_rows) * heads,
        scal,
        all_state,
        gains[2],
        shifts[2],
        full_sqkv,
        qkv,
    )
    read_parts = list_from_group(read)

    next_state, grad_gate, grad_sout, token_back, grad_sqkv, back_state_norm, state_sums = call(
        functools.partial(state_backward, head_dim),
        "state_backward",
        [
            out((state_rows, width)),
            out((1, width), f32),
            out((blocks, width // blocks, lanes)),
            out((group_rows, 2 * lanes), f32),
            out((blocks, width // blocks, 3 * lanes)),
            out((places, state_rows, width)),
            out((2, width), f32),
        ],
        [
            pltpu.VMEM((width, 3 * lanes), bf16),
            pltpu.VMEM((width, width), bf16),
            pltpu.VMEM((all_states, width), bf16),
            pltpu.VMEM((all_states, lanes), bf16),
            pltpu.VMEM((all_states, 3 * lanes), bf16),
            pltpu.VMEM((all_states, 2 * lanes), f32),
        ],
        4 * all_states * width * 4 * lanes,
        all_states * (all_states + group_rows) * heads,
        scal,
        state_in[0],
        all_state_cot,
        gate_bias[None],
        all_state,
        *read_parts,
        *full_sout,
        sqkv,
        qkv,
        state_norm,
        full_sqkv,
    )
    residual, second, hidden, slope, out_rows, grad_down = call(
        ffn_up,
        "ffn_up",
        [
            out((places, rows, width), f32),
            out((group_rows, width)),
            out((group_rows, inner_width)),
            out((group_rows, inner_width)),
            out((lanes, width)),
            out((blocks, inner_width, width // blocks)),
        ],
        [pltpu.VMEM((width, width), bf16), pltpu.VMEM((width, inner_width), bf16)],
        2 * group_rows * width * (width + 2 * inner_width),
        group_rows * inner_width,
        scal,
        all_tokens,
        *mixed_parts,
        *full_out,
        gains[1],
        shifts[1],
        full_up,
        all_cot,
    )

    back_second, back_input, mid_sums = call(
        ffn_back,
        "ffn_back",
        [
            out((places, rows, width)),
            out((group_rows, inner_width)),
            out((2, width), f32),
        ],
        [pltpu.VMEM((inner_width, width), bf16), pltpu.VMEM((width, inner_width), bf16)],
        4 * group_rows * width * inner_width,
        0,
        scal,
        all_cot,
        full_down,
        full_up,
        slope,
        residual,
    )
    residual_own = residual[0]
    own_grad_sout = sum_over_dp(grad_sout, 0)
    own_grad_sqkv = sum_over_dp(grad_sqkv, 0)
    back_state = sum_to_owner(back_state_norm)
    gate_open = jax.nn.sigmoid(gate_bias)
    grad_state = (
        gate_open * state_cotangent[0].astype(f32)
        + norm_back(state_in[0].astype(f32), back_state, norm_gain[2])
    ).astype(bf16)

    own_grad_down = sum_over_dp(grad_down, 1)
    back_second = sum_to_owner(back_second)
    back_residual = cotangent.astype(f32) + norm_back(residual_own, back_second, norm_gain[1])
    back_branch = from_group(back_residual.astype(bf16))

    ffn_partial, grad_up = call(
        ffn_rest,
        "ffn_rest",
        [out((places, rows, width)), out((blocks, width // blocks, inner_width))],
        [pltpu.VMEM((inner_width, width), bf16)],
        4 * group_rows * width * inner_width,
        0,
        scal,
        hidden,
        full_down,
        second,
        back_input,
    )
    own_grad_up = sum_over_dp(grad_up, 0)
    output = (residual_own + sum_to_owner(ffn_partial)).astype(bf16)

    (grad_out,) = call(
        out_grad,
        "out_grad",
        [out((blocks, width // blocks, lanes))],
        [],
        2 * group_rows * width * lanes,
        0,
        scal,
        back_branch,
        *mixed_parts,
    )
    own_grad_out = sum_over_dp(grad_out, 0)

    grad_qkv, back_first, first_sums, distance = call(
        functools.partial(token_backward, head_dim),
        "token_backward",
        [
            out((blocks, width // blocks, 3 * lanes)),
            out((places, rows, width)),
            out((2, width), f32),
            out((heads, span), f32),
        ],
        [
            pltpu.VMEM((width, 3 * lanes), bf16),
            pltpu.VMEM((heads, rows, span), f32),
            pltpu.VMEM((group_rows, lanes), bf16),
            pltpu.VMEM((group_rows, 3 * lanes), bf16),
            pltpu.VMEM((group_rows, 2 * lanes), f32),
            pltpu.VMEM((rows, span), f32),
        ],
        2 * group_rows * width * 7 * lanes,
        group_rows * span * heads,
        scal,
        back_branch,
        out_rows,
        qkv,
        bias,
        token_back,
        first,
        all_tokens,
        full_qkv,
    )
    back_first = sum_to_owner(back_first)
    grad_tokens = (
        norm_back(tokens.astype(f32), back_first, norm_gain[0]) + back_residual
    ).astype(bf16)
    own_grad_qkv = sum_over_dp(grad_qkv, 0)
    both_grads = from_heads(
        jnp.concatenate([own_grad_qkv, own_grad_sqkv], axis=0).astype(bf16)
    ).astype(f32)

    per_distance = distance[:, 1 : window + 1][:, ::-1]
    own_rel = jnp.dot(
        per_distance, lookup, precision=lax.Precision.HIGHEST, preferred_element_type=f32
    ).T
    grad_rel = lax.dynamic_update_slice_in_dim(
        jnp.zeros((bucket_count, head_count), f32), own_rel, here * heads, 1
    )
    small = [
        jnp.stack([first_sums[0], mid_sums[0], state_sums[0]]),
        jnp.stack([first_sums[1], mid_sums[1], state_sums[1]]),
        grad_gate[0],
        grad_rel,
    ]
    packed = sum_over_all(jnp.concatenate([v.reshape(-1, 128) for v in small], axis=0))
    unpacked, start = [], 0
    for v in small:
        count = v.size // 128
        unpacked.append(packed[start : start + count].reshape(v.shape))
        start += count
    return (
        output,
        next_state[None],
        grad_tokens,
        grad_state[None],
        both_grads[:depth],
        own_grad_out,
        both_grads[depth:],
        own_grad_sout,
        own_grad_up,
        own_grad_down,
        unpacked[3],
        unpacked[0],
        unpacked[1],
        unpacked[2],
    )


def solution(mesh):
    rows_spec = P(("dp", "state"), None)
    state_spec = P("dp", "state", None)
    weight_spec = P("dp", "state")
    return jax.shard_map(
        per_device,
        mesh=mesh,
        in_specs=(
            rows_spec,
            state_spec,
            rows_spec,
            state_spec,
            P("dp"),
            P(),
            weight_spec,
            weight_spec,
            weight_spec,
            weight_spec,
            weight_spec,
            P("state", "dp"),
            P(),
            P(),
            P(),
            P(),
        ),
        out_specs=(
            rows_spec,
            state_spec,
            rows_spec,
            state_spec,
            weight_spec,
            weight_spec,
            weight_spec,
            weight_spec,
            weight_spec,
            P("state", "dp"),
            P(),
            P(),
            P(),
            P(),
        ),
        check_vma=False,
    )
```

```python
import functools

import jax
import jax.numpy as jnp
from jax import lax
from jax.experimental import pallas as pl
from jax.experimental.pallas import tpu as pltpu
from jax.sharding import PartitionSpec as P

epsilon = 1e-05
masked_value = -1e30
f32 = jnp.float32
bf16 = jnp.bfloat16

PLACES = (0, 2, 1, 3)
DP_STEPS = (2, 4, 1)
DP_PLACES = (0, 2, 4, 6, 1, 3, 5, 7)


def dot(left, right):
    return lax.dot_general(left, right, (((1,), (0,)), ((), ())), preferred_element_type=f32)


def dot_rt(left, right):
    return lax.dot_general(left, right, (((1,), (1,)), ((), ())), preferred_element_type=f32)


def dot_lt(left, right):
    return lax.dot_general(left, right, (((0,), (0,)), ((), ())), preferred_element_type=f32)


def where_from(sender, place):
    return PLACES.index(PLACES[sender] ^ PLACES[place])


def normalized(values):
    centre = jnp.mean(values, axis=-1, keepdims=True)
    centred = values - centre
    spread = jnp.mean(centred * centred, axis=-1, keepdims=True)
    inverse = lax.rsqrt(spread + epsilon)
    return centred * inverse, inverse


def normed_back(back, hat, inverse, gain):
    grown = back * gain
    return inverse * (
        grown
        - jnp.mean(grown, axis=-1, keepdims=True)
        - hat * jnp.mean(grown * hat, axis=-1, keepdims=True)
    )


def place_of(scal, q):
    return scal[0] ^ PLACES[q]


def aligned(start, size):
    return pl.ds(pl.multiple_of(start, size), size)


def block_at(scal, q):
    return scal[2 + q]


def position_of(scal, block, blocks):
    return scal[2 + blocks + block]


def rows_in_order(scal, target, source):
    blocks, depth = source.shape[0], source.shape[1]
    for q in range(blocks):
        target[aligned(block_at(scal, q) * depth, depth), :] = source[q]


def columns_in_order(scal, target, source):
    blocks, depth = source.shape[0], source.shape[2]
    for q in range(blocks):
        target[:, aligned(block_at(scal, q) * depth, depth)] = source[q]


def put_rows(scal, target, start, value):
    blocks, depth = target.shape[0], target.shape[1]
    rows = value.shape[0]
    if depth >= rows:
        target[position_of(scal, start // depth, blocks), aligned(start % depth, rows), :] = value
    else:
        for i in range(rows // depth):
            position = position_of(scal, start // depth + i, blocks)
            target[position] = value[i * depth : (i + 1) * depth]


def put_columns(scal, target, start, value):
    blocks, depth = target.shape[0], target.shape[2]
    columns = value.shape[1]
    if depth >= columns:
        target[position_of(scal, start // depth, blocks), :, aligned(start % depth, columns)] = value
    else:
        for i in range(columns // depth):
            position = position_of(scal, start // depth + i, blocks)
            target[position] = value[:, i * depth : (i + 1) * depth]


def call(body, name, outs, scratch, flops, exps, *args):
    sizes = sum(a.size * a.dtype.itemsize for a in args) + sum(
        a.size * a.dtype.itemsize for a in outs
    )
    in_specs = [pl.BlockSpec(memory_space=pltpu.SMEM)] + [
        pl.BlockSpec(memory_space=pltpu.VMEM) for _ in args[1:]
    ]
    return pl.pallas_call(
        body,
        out_shape=outs,
        in_specs=in_specs,
        out_specs=[pl.BlockSpec(memory_space=pltpu.VMEM) for _ in outs],
        scratch_shapes=scratch,
        compiler_params=pltpu.CompilerParams(vmem_limit_bytes=56 << 20),
        cost_estimate=pl.CostEstimate(flops=flops, bytes_accessed=sizes, transcendentals=exps),
        name=name,
    )(*args)


def out(shape, kind=bf16):
    return jax.ShapeDtypeStruct(shape, kind)


def by_distance(scores):
    rows, span = scores.shape
    row_at = lax.broadcasted_iota(jnp.int32, scores.shape, 0)
    step = 1
    while step < rows:
        scores = jnp.where(row_at & step != 0, pltpu.roll(scores, span - step, 1), scores)
        step *= 2
    return scores


def bias_blocks(tb, bias):
    heads, rows, span = tb.shape
    for h in range(heads):
        row = jnp.broadcast_to(bias[h], (rows, span))
        tb[h] = pltpu.roll(row, 0, 1, stride=1, stride_axis=0)


def window_probs(scal, query, keys, tb_block, last, scale):
    rows, span = tb_block.shape
    count = keys.shape[0]
    scores = dot_rt(query, keys) * scale + tb_block[:, span - count :]
    if last:
        row_at = lax.broadcasted_iota(jnp.int32, scores.shape, 0)
        col_at = lax.broadcasted_iota(jnp.int32, scores.shape, 1)
        ahead = col_at - (count - rows)
        live = (ahead < scal[1] - last) | (ahead == row_at)
        scores = jnp.where(live, scores, masked_value)
    top = jnp.max(scores, axis=-1, keepdims=True)
    grown = jnp.exp(scores - top)
    return grown * (1.0 / jnp.sum(grown, axis=-1, keepdims=True))


def state_probs(scal, query, state_keys, keys, scale):
    own = dot_rt(query, state_keys) * scale
    token = dot_rt(query, keys) * scale
    col_at = lax.broadcasted_iota(jnp.int32, token.shape, 1)
    token = jnp.where(col_at < scal[1], token, masked_value)
    top = jnp.maximum(
        jnp.max(own, axis=-1, keepdims=True), jnp.max(token, axis=-1, keepdims=True)
    )
    own = jnp.exp(own - top)
    token = jnp.exp(token - top)
    total = jnp.sum(own, axis=-1, keepdims=True) + jnp.sum(token, axis=-1, keepdims=True)
    inverse = 1.0 / total
    return own * inverse, token * inverse


def head_cols(block, h, heads, head_dim):
    start = (block * heads + h) * head_dim
    return slice(start, start + head_dim)


def token_forward(head_dim, scal, tokens, gain, shift, w_qkv, bias, first, qkv, mixed, w_nat, tb):
    places, rows, width = tokens.shape
    heads = bias.shape[0]
    span = bias.shape[1]
    scale = head_dim ** (-0.5)
    rows_in_order(scal, w_nat, w_qkv)
    bias_blocks(tb, [bias[h : h + 1, :] for h in range(heads)])
    for q in range(places):
        hat, _ = normalized(tokens[q].astype(f32))
        normed = (hat * gain[...] + shift[...]).astype(bf16)
        at = aligned(place_of(scal, q) * rows, rows)
        first[at, :] = normed
        qkv[at, :] = dot(normed, w_nat[...]).astype(bf16)
    for c in range(places):
        count = min(span, (c + 1) * rows)
        low, high = (c + 1) * rows - count, (c + 1) * rows
        last = c * rows if c == places - 1 else 0
        parts = []
        for h in range(heads):
            probs = window_probs(
                scal,
                qkv[c * rows : high, head_cols(0, h, heads, head_dim)],
                qkv[low:high, head_cols(1, h, heads, head_dim)],
                tb[h],
                last,
                scale,
            )
            parts.append(
                dot(probs.astype(bf16), qkv[low:high, head_cols(2, h, heads, head_dim)])
            )
        mixed[c] = jnp.concatenate(parts, axis=1).astype(bf16)


def state_forward(
    head_dim, scal, state, gain, shift, w_sqkv, qkv, normed_out, sqkv, read, w_nat
):
    places, rows, width = state.shape
    heads = qkv.shape[1] // (3 * head_dim)
    scale = head_dim ** (-0.5)
    rows_in_order(scal, w_nat, w_sqkv)
    for q in range(places):
        hat, _ = normalized(state[q].astype(f32))
        normed = (hat * gain[...] + shift[...]).astype(bf16)
        normed_out[q * rows : (q + 1) * rows, :] = normed
        sqkv[q * rows : (q + 1) * rows, :] = dot(normed, w_nat[...]).astype(bf16)
    for q in range(places):
        parts = []
        for h in range(heads):
            own, token = state_probs(
                scal,
                sqkv[q * rows : (q + 1) * rows, head_cols(0, h, heads, head_dim)],
                sqkv[:, head_cols(1, h, heads, head_dim)],
                qkv[:, head_cols(1, h, heads, head_dim)],
                scale,
            )
            parts.append(
                dot(own.astype(bf16), sqkv[:, head_cols(2, h, heads, head_dim)])
                + dot(token.astype(bf16), qkv[:, head_cols(2, h, heads, head_dim)])
            )
        read[q] = jnp.concatenate(parts, axis=1).astype(bf16)


def assembled(scal, target, parts):
    for p, part in enumerate(parts):
        blocks, depth, columns = part.shape
        at = aligned(place_of(scal, p) * columns, columns)
        for q in range(blocks):
            target[aligned(block_at(scal, q) * depth, depth), at] = part[q]


def state_backward(
    head_dim,
    scal,
    state_own,
    state_cot,
    gate_bias,
    state,
    read0,
    read1,
    read2,
    read3,
    out0,
    out1,
    out2,
    out3,
    sqkv,
    qkv,
    normed,
    w_sqkv,
    next_state,
    grad_gate,
    grad_sout,
    token_back,
    grad_sqkv,
    back_norm,
    grad_norm,
    w_nat,
    w_out,
    back_update,
    back_read,
    back_sqkv,
    own_sum,
):
    places, rows, width = state_cot.shape
    reads = (read0, read1, read2, read3)
    heads = qkv.shape[1] // (3 * head_dim)
    lanes = heads * head_dim
    scale = head_dim ** (-0.5)
    rows_in_order(scal, w_nat, w_sqkv)
    assembled(scal, w_out, (out0, out1, out2, out3))
    gate = jax.nn.sigmoid(gate_bias[...])
    update = None
    for p in range(places):
        term = dot(reads[p][p], w_out[aligned(place_of(scal, p) * lanes, lanes), :])
        update = term if update is None else update + term
    held = state_own[...].astype(f32)
    cot = state_cot[0].astype(f32)
    next_state[...] = (gate * held + (1.0 - gate) * update).astype(bf16)
    grad_gate[...] = jnp.sum(cot * (held - update), axis=0, keepdims=True) * (gate * (1.0 - gate))
    for q in range(places):
        back_update[q * rows : (q + 1) * rows, :] = (
            (1.0 - gate) * state_cot[q].astype(f32)
        ).astype(bf16)
    own_columns = back_update[:, aligned(scal[0] * lanes, lanes)]
    for p in range(places):
        stack = jnp.concatenate([reads[p][where_from(p, q)] for q in range(places)], axis=0)
        put_rows(
            scal, grad_sout, place_of(scal, p) * lanes, dot_lt(stack, own_columns).astype(bf16)
        )
    back_read[...] = dot_rt(
        back_update[...], w_out[aligned(scal[0] * lanes, lanes), :]
    ).astype(bf16)
    for h in range(heads):
        key_at, value_at = head_cols(1, h, heads, head_dim), head_cols(2, h, heads, head_dim)
        query_at, read_at = head_cols(0, h, heads, head_dim), slice(h * head_dim, (h + 1) * head_dim)
        for q in range(places):
            at = slice(q * rows, (q + 1) * rows)
            query, back = sqkv[at, query_at], back_read[at, read_at]
            own, token = state_probs(scal, query, sqkv[:, key_at], qkv[:, key_at], scale)
            back_own = dot_rt(back, sqkv[:, value_at])
            back_token = dot_rt(back, qkv[:, value_at])
            row_dot = jnp.sum(own * back_own, axis=-1, keepdims=True) + jnp.sum(
                token * back_token, axis=-1, keepdims=True
            )
            own_raw = (own * (back_own - row_dot) * scale).astype(bf16)
            token_raw = (token * (back_token - row_dot) * scale).astype(bf16)
            back_sqkv[at, query_at] = (
                dot(own_raw, sqkv[:, key_at]) + dot(token_raw, qkv[:, key_at])
            ).astype(bf16)
            terms = (
                (own_sum, key_at, dot_lt(own_raw, query)),
                (own_sum, value_at, dot_lt(own.astype(bf16), back)),
                (token_back, key_at, dot_lt(token_raw, query)),
                (token_back, value_at, dot_lt(token.astype(bf16), back)),
            )
            for target, columns, term in terms:
                columns = slice(columns.start - lanes, columns.stop - lanes)
                if q == 0:
                    target[:, columns] = term
                else:
                    target[:, columns] += term
    back_sqkv[:, lanes:] = own_sum[...].astype(bf16)
    for start in range(0, width, 256):
        put_rows(
            scal,
            grad_sqkv,
            start,
            dot_lt(normed[:, start : start + 256], back_sqkv[...]).astype(bf16),
        )
    gain_sum, shift_sum = None, None
    for q in range(places):
        back = dot_rt(back_sqkv[q * rows : (q + 1) * rows, :], w_nat[...])
        back_norm[q] = back.astype(bf16)
        hat, _ = normalized(state[q].astype(f32))
        gain_term = jnp.sum(back * hat, axis=0, keepdims=True)
        shift_term = jnp.sum(back, axis=0, keepdims=True)
        gain_sum = gain_term if q == 0 else gain_sum + gain_term
        shift_sum = shift_term if q == 0 else shift_sum + shift_term
    grad_norm[0:1, :] = gain_sum
    grad_norm[1:2, :] = shift_sum


def ffn_up(
    scal,
    tokens,
    mixed0,
    mixed1,
    mixed2,
    mixed3,
    out0,
    out1,
    out2,
    out3,
    gain,
    shift,
    w_up,
    cot,
    residual,
    second,
    hidden,
    slope,
    out_rows,
    grad_down,
    w_out,
    w_nat,
):
    places, rows, width = tokens.shape
    mixed = (mixed0, mixed1, mixed2, mixed3)
    lanes = mixed0.shape[2]
    assembled(scal, w_out, (out0, out1, out2, out3))
    out_rows[...] = w_out[aligned(scal[0] * lanes, lanes), :]
    rows_in_order(scal, w_nat, w_up)
    for q in range(places):
        total = tokens[q].astype(f32)
        for p in range(places):
            total += dot(
                mixed[p][place_of(scal, q)], w_out[aligned(place_of(scal, p) * lanes, lanes), :]
            )
        residual[q] = total
        hat, _ = normalized(total)
        normed = (hat * gain[...] + shift[...]).astype(bf16)
        at = slice(q * rows, (q + 1) * rows)
        second[at, :] = normed
        inner = dot(normed, w_nat[...])
        root = 0.7978845608028654
        square = inner * inner
        bend = jnp.tanh(root * inner * (1.0 + 0.044715 * square))
        half = 0.5 * (1.0 + bend)
        hidden[at, :] = (inner * half).astype(bf16)
        slope[at, :] = (
            half + (0.5 * root) * inner * (1.0 - bend * bend) * (1.0 + (3 * 0.044715) * square)
        ).astype(bf16)
    for start in range(0, width, 256):
        columns = jnp.concatenate([cot[q, :, start : start + 256] for q in range(places)], axis=0)
        put_columns(scal, grad_down, start, dot_lt(hidden[...], columns).astype(bf16))


def ffn_back(
    scal,
    cot,
    w_down,
    w_up,
    slope,
    residual,
    back_second,
    back_input,
    grad_norm,
    w_nat,
    w_up_nat,
):
    places, rows, width = cot.shape
    columns_in_order(scal, w_nat, w_down)
    rows_in_order(scal, w_up_nat, w_up)
    gain_sum, shift_sum = None, None
    for q in range(places):
        at = slice(q * rows, (q + 1) * rows)
        inner = (dot_rt(cot[q], w_nat[...]) * slope[at, :].astype(f32)).astype(bf16)
        back_input[at, :] = inner
        back = dot_rt(inner, w_up_nat[...])
        back_second[q] = back.astype(bf16)
        hat, _ = normalized(residual[q])
        gain_term = jnp.sum(back * hat, axis=0, keepdims=True)
        shift_term = jnp.sum(back, axis=0, keepdims=True)
        gain_sum = gain_term if q == 0 else gain_sum + gain_term
        shift_sum = shift_term if q == 0 else shift_sum + shift_term
    grad_norm[0:1, :] = gain_sum
    grad_norm[1:2, :] = shift_sum


def ffn_rest(scal, hidden, w_down, second, back_input, partial, grad_up, w_nat):
    places, rows, width = partial.shape
    for start in range(0, width, 256):
        put_rows(
            scal,
            grad_up,
            start,
            dot_lt(second[:, start : start + 256], back_input[...]).astype(bf16),
        )
    columns_in_order(scal, w_nat, w_down)
    for q in range(places):
        partial[q] = dot(hidden[q * rows : (q + 1) * rows, :], w_nat[...]).astype(bf16)


def out_grad(scal, back_branch, mixed0, mixed1, mixed2, mixed3, grad_out):
    places, rows, width = back_branch.shape
    mixed = (mixed0, mixed1, mixed2, mixed3)
    lanes = mixed0.shape[2]
    own_at = aligned(scal[0] * lanes, lanes)
    own_columns = jnp.concatenate([back_branch[q, :, own_at] for q in range(places)], axis=0)
    for p in range(places):
        stack = jnp.concatenate([mixed[p][place_of(scal, q)] for q in range(places)], axis=0)
        put_rows(
            scal, grad_out, place_of(scal, p) * lanes, dot_lt(stack, own_columns).astype(bf16)
        )


def token_backward(
    head_dim,
    scal,
    back_branch,
    out_rows,
    qkv,
    bias,
    token_back,
    first,
    tokens,
    w_qkv,
    grad_qkv,
    back_first,
    grad_norm,
    distance,
    w_nat,
    tb,
    back_mixed,
    back_qkv,
    key_sum,
    band,
):
    places, rows, width = back_branch.shape
    heads, span = bias.shape
    lanes = heads * head_dim
    scale = head_dim ** (-0.5)
    rows_in_order(scal, w_nat, w_qkv)
    bias_blocks(tb, [bias[h : h + 1, :] for h in range(heads)])
    for q in range(places):
        back_mixed[aligned(place_of(scal, q) * rows, rows), :] = dot_rt(
            back_branch[q], out_rows[...]
        ).astype(bf16)
    key_sum[...] = token_back[...]
    for h in range(heads):
        key_at, value_at = head_cols(1, h, heads, head_dim), head_cols(2, h, heads, head_dim)
        query_at, read_at = head_cols(0, h, heads, head_dim), slice(h * head_dim, (h + 1) * head_dim)
        for c in reversed(range(places)):
            count = min(span, (c + 1) * rows)
            low, high = (c + 1) * rows - count, (c + 1) * rows
            last = c * rows if c == places - 1 else 0
            query, back = qkv[c * rows : high, query_at], back_mixed[c * rows : high, read_at]
            keys = qkv[low:high, key_at]
            probs = window_probs(scal, query, keys, tb[h], last, scale)
            back_probs = dot_rt(back, qkv[low:high, value_at])
            row_dot = jnp.sum(probs * back_probs, axis=-1, keepdims=True)
            back_scores = probs * (back_probs - row_dot)
            if c == places - 1:
                band[...] = back_scores
            else:
                band[:, span - count :] += back_scores
            raw = (back_scores * scale).astype(bf16)
            back_qkv[c * rows : high, query_at] = dot(raw, keys).astype(bf16)
            key_to = slice(key_at.start - lanes, key_at.stop - lanes)
            value_to = slice(value_at.start - lanes, value_at.stop - lanes)
            key_sum[low:high, key_to] += dot_lt(raw, query)
            key_sum[low:high, value_to] += dot_lt(probs.astype(bf16), back)
        distance[h : h + 1, :] = jnp.sum(by_distance(band[...]), axis=0, keepdims=True)
    back_qkv[:, lanes:] = key_sum[...].astype(bf16)
    for start in range(0, width, 256):
        put_rows(
            scal,
            grad_qkv,
            start,
            dot_lt(first[:, start : start + 256], back_qkv[...]).astype(bf16),
        )
    gain_sum, shift_sum = None, None
    for q in range(places):
        back = dot_rt(back_qkv[aligned(place_of(scal, q) * rows, rows), :], w_nat[...])
        back_first[q] = back.astype(bf16)
        hat, _ = normalized(tokens[q].astype(f32))
        gain_term = jnp.sum(back * hat, axis=0, keepdims=True)
        shift_term = jnp.sum(back, axis=0, keepdims=True)
        gain_sum = gain_term if q == 0 else gain_sum + gain_term
        shift_sum = shift_term if q == 0 else shift_sum + shift_term
    grad_norm[0:1, :] = gain_sum
    grad_norm[1:2, :] = shift_sum


def flip_low(i):
    return i + 1 - 2 * (i % 2)


class Mover:
    def __init__(self, send, recv):
        self.send, self.recv, self.sends, self.recvs = send, recv, 0, 0

    def send_slot(self):
        self.sends += 1
        return self.sends - 1

    def recv_slot(self):
        self.recvs += 1
        return self.recvs - 1

    def copy(self, source, target, device, send_slot, recv_slot):
        return pltpu.make_async_remote_copy(
            src_ref=source,
            dst_ref=target,
            send_sem=self.send.at[send_slot],
            recv_sem=self.recv.at[recv_slot],
            device_id=device,
            device_id_type=pl.DeviceIdType.MESH,
        )

    def __call__(self, source, target, device):
        return self.copy(source, target, device, self.send_slot(), self.recv_slot())


class Links:
    def __init__(self):
        self.d, self.s = lax.axis_index("dp"), lax.axis_index("state")
        z, y = self.d // 2, self.d % 2
        self.over_z = [2 * (z + 1 - 2 * (z % 2)) + y, 2 * ((z + 2) % 4) + y, 2 * (3 - z) + y]
        self.over_y = flip_low(self.d)
        self.core, self.x = flip_low(self.s), (self.s + 2) % 4
        self.to_core, self.to_x = (self.d, self.core), (self.d, self.x)
        self.to_y = (self.over_y, self.s)
        self.to_z = [(other, self.s) for other in self.over_z]
        self.in_middle = (z == 1) | (z == 2)
        self.far_middle = 2 * (2 - z // 2) + y
        self.far_end = 2 * (3 - 3 * (z // 2)) + y
        self.to_far, self.to_far_end = (self.far_middle, self.s), (self.far_end, self.s)
        self.z, self.z_rest = z, [i // 2 for i in (self.over_z[0], self.far_middle, self.far_end)]

    def greet(self):
        barrier = pltpu.get_barrier_semaphore()
        partners = [self.to_core, self.to_x, self.to_y, *self.to_z]
        for partner in partners:
            pl.semaphore_signal(
                barrier, inc=1, device_id=partner, device_id_type=pl.DeviceIdType.MESH
            )
        pl.semaphore_wait(barrier, len(partners))


class GroupGather:
    def __init__(self, mover, links, whole, at, source=None):
        self.links, self.parts = links, [links.s, links.core, links.x, flip_low(links.x)]
        own = whole.at[at(links.s)]
        source = own if source is None else source
        across = whole.at[at(links.x)]
        self.over_x = mover(source, own, links.to_x)
        self.beside = mover(source, own, links.to_core)
        self.passed = mover(across, across, links.to_core)

    def start(self):
        self.over_x.start()
        self.beside.start()

    def forward(self):
        self.over_x.wait_recv()
        self.passed.start()

    def finish(self):
        self.beside.wait_recv()
        self.passed.wait_recv()

    def sent(self):
        for copy in (self.over_x, self.beside, self.passed):
            copy.wait_send()


class WeightGather:
    def __init__(self, mover, links, whole, at, source):
        own = whole.at[at(links.d)]
        self.links = links
        near, far = mover.send_slot(), mover.send_slot()
        slots = [mover.recv_slot() for _ in range(3)]
        self.near = mover.copy(source, own, links.to_z[0], near, slots[0])
        self.far = [mover.copy(source, own, links.to_far, far, slots[k]) for k in (1, 2)]
        self.own_y = mover(source, own, links.to_y)
        self.passed, self.relayed = [], [None]
        for k, other in enumerate((links.over_z[0], links.far_middle, links.far_end)):
            block = whole.at[at(other)]
            self.passed.append(mover(block, block, links.to_y))
            if k:
                self.relayed.append(
                    mover.copy(block, block, links.to_z[0], mover.send_slot(), slots[k])
                )

    def start_z(self):
        self.near.start()

        @pl.when(self.links.in_middle)
        def _():
            self.far[0].start()

        @pl.when(jnp.logical_not(self.links.in_middle))
        def _():
            self.far[1].start()

    def start_y(self):
        self.own_y.start()

    def forward(self, k):
        if k == 0:
            self.near.wait_recv()
        else:
            self.relayed[k].wait_recv()

            @pl.when(self.links.in_middle)
            def _():
                self.relayed[k].start()

        self.passed[k].start()

    def finish(self):
        self.own_y.wait_recv()
        for copy in self.passed:
            copy.wait_recv()

    def sent(self):
        for copy in (self.near, self.far[0], self.own_y, *self.passed):
            copy.wait_send()

        @pl.when(self.links.in_middle)
        def _():
            for copy in self.relayed[1:]:
                copy.wait_send()


class PairGather:
    def __init__(self, mover, links, whole, at, pair, source):
        own = whole.at[at(links.d)]
        self.links = links
        self.own_y = mover(source, own, links.to_y)
        both = whole.at[pair(links.z)]
        near, far = mover.send_slot(), mover.send_slot()
        slots = [mover.recv_slot() for _ in range(3)]
        self.near = mover.copy(both, both, links.to_z[0], near, slots[0])
        self.far = [mover.copy(both, both, links.to_far, far, slots[k]) for k in (1, 2)]
        self.relayed = [None]
        for k in (1, 2):
            other = whole.at[pair(links.z_rest[k])]
            self.relayed.append(
                mover.copy(other, other, links.to_z[0], mover.send_slot(), slots[k])
            )

    def start_y(self):
        self.own_y.start()

    def start_z(self):
        self.own_y.wait_recv()
        self.near.start()

        @pl.when(self.links.in_middle)
        def _():
            self.far[0].start()

        @pl.when(jnp.logical_not(self.links.in_middle))
        def _():
            self.far[1].start()

    def forward(self, k):
        if k == 0:
            self.near.wait_recv()
        else:
            self.relayed[k].wait_recv()

            @pl.when(self.links.in_middle)
            def _():
                self.relayed[k].start()

    def sent(self):
        for copy in (self.own_y, self.near, self.far[0]):
            copy.wait_send()

        @pl.when(self.links.in_middle)
        def _():
            for copy in self.relayed[1:]:
                copy.wait_send()


class GroupSum:
    def __init__(self, mover, links, partial, at, beside, across):
        self.partial, self.at, self.links = partial, at, links
        self.from_core, self.from_x = beside, across
        diagonal = flip_low(links.x)
        self.far = mover(partial.at[at(diagonal)], beside.at[1], links.to_core)
        self.near = mover(partial.at[at(links.core)], beside.at[0], links.to_core)
        self.over = mover(partial.at[at(links.x)], across, links.to_x)

    def start(self):
        self.far.start()
        self.near.start()

    def keep(self):
        self.near.wait_recv()
        pair = self.partial[self.at(self.links.s)].astype(f32) + self.from_core[0].astype(f32)
        self.from_core[0] = pair.astype(bf16)

    def finish_kept(self):
        self.over.wait_recv()
        return self.from_core[0].astype(f32) + self.from_x[...].astype(f32)

    def middle(self):
        self.far.wait_recv()
        place = self.at(self.links.x)
        total = self.partial[place].astype(f32) + self.from_core[1].astype(f32)
        self.partial[place] = total.astype(bf16)
        self.over.start()

    def finish(self):
        self.near.wait_recv()
        pair = self.partial[self.at(self.links.s)].astype(f32) + self.from_core[0].astype(f32)
        self.over.wait_recv()
        return pair + self.from_x[...].astype(f32)

    def sent(self):
        for copy in (self.far, self.near, self.over):
            copy.wait_send()


class BlockSum:
    def __init__(self, mover, links, partial, from_core, from_x, summed, start, half):
        core = links.s % 2

        def half_at(i):
            return (pl.ds(pl.multiple_of(start + i * half, half), half), slice(None))

        self.partial, self.summed, self.mine = partial, summed, half_at(core)
        self.from_core, self.from_x = from_core, from_x
        self.beside = mover(partial.at[half_at(1 - core)], from_core, links.to_core)
        self.over = mover(partial.at[self.mine], from_x, links.to_x)
        self.back = mover(summed.at[self.mine], summed.at[self.mine], links.to_core)

    def start(self):
        self.beside.start()

    def middle(self):
        self.beside.wait_recv()
        pair = self.partial[self.mine].astype(f32) + self.from_core[...].astype(f32)
        self.partial[self.mine] = pair.astype(bf16)
        self.over.start()

    def total(self):
        self.over.wait_recv()
        return self.partial[self.mine].astype(f32) + self.from_x[...].astype(f32)

    def share(self, value):
        self.summed[self.mine] = value.astype(bf16)
        self.back.start()

    def finish(self):
        self.back.wait_recv()

    def sent(self):
        for copy in (self.beside, self.over, self.back):
            copy.wait_send()


class LineSum:
    def __init__(self, mover, links, grads, places, from_z):
        self.links, self.grads, self.places, self.from_z = links, grads, places, from_z
        sends, slots = [mover.send_slot() for _ in range(3)], [mover.recv_slot() for _ in range(4)]
        blocks = [grads.at[place] for place in places]
        self.to_near = [
            mover.copy(blocks[k], from_z.at[k], links.to_z[0], sends[k], slots[k]) for k in range(3)
        ]
        self.onward = [None] + [
            mover.copy(blocks[k], from_z.at[3], device, sends[k], slots[3])
            for k, device in ((1, links.to_far), (2, links.to_far_end))
        ]

    def send_z(self, k):
        if k == 0:
            self.to_near[0].start()
        else:

            @pl.when(jnp.logical_not(self.links.in_middle))
            def _():
                self.to_near[k].start()

    def combine(self, k):
        @pl.when(self.links.in_middle)
        def _():
            self.to_near[k].wait_recv()
            total = self.grads[self.places[k]].astype(f32) + self.from_z[k].astype(f32)
            self.grads[self.places[k]] = total.astype(bf16)
            self.onward[k].start()

    def arrived_z(self):
        self.to_near[0].wait_recv()
        near = self.from_z[0].astype(f32)
        self.onward[1].wait_recv()
        return near + self.from_z[3].astype(f32)

    def sent(self):
        for copy in self.to_near:
            copy.wait_send()


class WeightSum(LineSum):
    def __init__(self, mover, links, grads, at, from_y, from_z):
        others = [links.over_z[0], links.far_middle, links.far_end]
        super().__init__(mover, links, grads, [at(i) for i in others], from_z)
        self.own, self.from_y = at(links.d), from_y
        self.over_y = [
            mover(grads.at[at(flip_low(i))], from_y.at[k], links.to_y)
            for k, i in enumerate([links.d, *others])
        ]

    def start(self):
        for k in (2, 3, 1, 0):
            self.over_y[k].start()

    def forward(self, *order):
        for k in order:
            self.over_y[k + 1].wait_recv()
            place = self.places[k]
            total = self.grads[place].astype(f32) + self.from_y[k + 1].astype(f32)
            self.grads[place] = total.astype(bf16)
            self.send_z(k)

    def finish(self):
        self.over_y[0].wait_recv()
        total = self.grads[self.own].astype(f32) + self.from_y[0].astype(f32)
        return total + self.arrived_z()

    def sent(self):
        super().sent()
        for copy in self.over_y:
            copy.wait_send()


class PairSum(LineSum):
    def __init__(self, mover, links, grads, at, pair, from_y, from_z):
        super().__init__(mover, links, grads, [pair(i) for i in links.z_rest], from_z)
        self.own_pair, self.own, self.from_y = pair(links.z), at(links.d), from_y
        self.over_y = mover(grads.at[at(links.over_y)], from_y, links.to_y)

    def start(self):
        for k in (1, 2, 0):
            self.send_z(k)

    def middle(self):
        total = self.grads[self.own_pair].astype(f32) + self.arrived_z()
        self.grads[self.own_pair] = total.astype(bf16)
        self.over_y.start()

    def finish(self):
        self.over_y.wait_recv()
        return self.grads[self.own].astype(f32) + self.from_y[...].astype(f32)

    def sent(self):
        super().sent()
        self.over_y.wait_send()


class SmallSum:
    def __init__(self, mover, links, value, arrived):
        self.value, self.arrived = value, arrived
        partners = [links.to_core, links.to_x, links.to_z[0], links.to_z[1], links.to_y]
        self.copies = [mover(value.at[k], arrived.at[k], to) for k, to in enumerate(partners)]

    def start(self):
        self.copies[0].start()

    def step(self, k):
        self.copies[k].wait_recv()
        self.value[k + 1] = self.value[k] + self.arrived[k]
        if k + 1 < len(self.copies):
            self.copies[k + 1].start()

    def sent(self):
        for copy in self.copies:
            copy.wait_send()


LAYER_COPIES = 192


def layer(
    head_dim,
    length,
    tokens,
    state,
    cot,
    state_cot,
    w_qkv,
    w_out,
    w_sqkv,
    w_sout,
    w_up,
    w_down,
    buckets,
    rel_table,
    gains,
    shifts,
    gate_bias,
    output,
    next_state,
    grad_tokens,
    grad_state,
    grad_qkv,
    grad_out,
    grad_sqkv,
    grad_sout,
    grad_up,
    grad_down,
    grad_rel,
    grad_norm,
    send_sem,
    recv_sem,
    local_sem,
    slab,
    qkv_nat,
    sqkv_nat,
    out_nat,
    sout_nat,
    up_nat,
    down_nat,
    tok_all,
    cot_all,
    state_all,
    mixed,
    read_all,
    hid,
    first,
    qkv,
    second,
    sqkv,
    back_read,
    back_sqkv,
    own_sum,
    key_sum,
    res_own,
    hat_half,
    inverse_half,
    tb,
    band,
    out_rows,
    state_grads,
    down_grads,
    y_state,
    y_down,
    y_up,
    y_out,
    y_sout,
    z_state,
    z_down,
    z_up,
    z_out,
    z_sout,
    beside_rows,
    across_rows,
    beside_ffn,
    across_ffn,
    small,
    small_in,
    distance,
    landed,
    credit,
    by_bucket,
):
    rows, width = tokens.shape
    state_rows = state.shape[0]
    heads, _, span = tb.shape
    lanes = heads * head_dim
    depth = w_qkv.shape[0]
    inner_width = up_nat.shape[1]
    all_states = 4 * state_rows
    group_rows = 4 * rows
    scale = head_dim ** (-0.5)
    links = Links()
    s, d = links.s, links.d
    mover = Mover(send_sem, recv_sem)
    back_qkv, back_second, back_input = sqkv_nat, out_nat, sout_nat
    ffn_partial, back_first, back_branch = up_nat, down_nat, cot_all
    slope, up_grads = state_all, state_all
    back_state, ship = down_grads, slab
    hidden, token_grads = hid, hid

    def block(i, size):
        if isinstance(i, int):
            return slice(i * size, (i + 1) * size)
        return pl.ds(pl.multiple_of(i * size, size), size)

    def own_rows(size):
        return lambda i: (block(i, size), slice(None))

    def own_lanes(size):
        return lambda i: (slice(None), block(i, size))

    def cot_rows(i):
        if isinstance(i, int):
            start = all_states + i * state_rows
            return (slice(start, start + state_rows), slice(None))
        return (pl.ds(pl.multiple_of(all_states + i * state_rows, state_rows), state_rows), slice(None))

    own_columns = block(s, lanes)

    def own_out(i):
        return (block(i, depth), own_columns)

    def pair_out(i):
        return (block(i, 2 * depth), own_columns)

    def pair_last(i):
        return (block(i, 2 * depth), slice(3 * lanes, 4 * lanes))

    def last_lanes(i):
        return (block(i, depth), slice(3 * lanes, 4 * lanes))

    def first_lanes(i):
        return (block(i, depth), slice(0, 3 * lanes))

    to_slab = []
    for k, shard in enumerate((w_qkv, w_sqkv)):
        core_slot = 1 - links.core % 2 + links.core // 2
        x_slot = 2 - 2 * (links.x // 2)
        to_slab.append(
            (
                mover(
                    shard.at[:, block(2 - 2 * (s % 2), lanes)],
                    slab.at[k, :, block(x_slot, lanes)],
                    links.to_x,
                ),
                mover(
                    shard.at[:, lanes : 2 * lanes],
                    slab.at[k, :, block(core_slot, lanes)],
                    links.to_core,
                ),
            )
        )
    get_tokens = GroupGather(mover, links, tok_all, own_rows(rows), tokens)
    get_state = GroupGather(mover, links, state_all, own_rows(state_rows), state)
    get_scot = GroupGather(mover, links, state_all, cot_rows, state_cot)
    get_cot = GroupGather(mover, links, cot_all, own_rows(rows), cot)
    dp_sout = PairGather(mover, links, sout_nat, own_out, pair_out, w_sout)
    dp_out = PairGather(mover, links, out_nat, own_out, pair_out, w_out)
    dp_qkv = WeightGather(mover, links, qkv_nat, own_rows(depth), slab.at[0])
    dp_sqkv = WeightGather(mover, links, sqkv_nat, own_rows(depth), slab.at[1])
    dp_up = WeightGather(mover, links, up_nat, own_rows(depth), w_up)
    dp_down = WeightGather(mover, links, down_nat, own_lanes(depth), w_down)
    get_sout = GroupGather(mover, links, sout_nat, own_lanes(lanes))
    get_out = GroupGather(mover, links, out_nat, own_lanes(lanes))
    get_mixed = GroupGather(mover, links, mixed, own_lanes(lanes))
    get_read = GroupGather(mover, links, read_all, own_lanes(lanes))
    sum_state = GroupSum(
        mover,
        links,
        back_state,
        own_rows(state_rows),
        beside_ffn.at[:, 0:state_rows, :],
        across_ffn.at[0:state_rows, :],
    )
    half = rows // 2
    block_sums = [
        BlockSum(
            mover,
            links,
            back_second,
            beside_rows.at[i // 2, i % 2 * half : (i % 2 + 1) * half, :],
            across_rows.at[i // 2, i % 2 * half : (i % 2 + 1) * half, :],
            back_branch,
            i * rows,
            half,
        )
        for i in range(4)
    ]
    sum_ffn = GroupSum(mover, links, ffn_partial, own_rows(rows), beside_ffn, across_ffn)
    sum_first = GroupSum(
        mover, links, back_first, own_rows(rows), beside_rows, across_rows.at[0]
    )
    dp_state = WeightSum(mover, links, state_grads, first_lanes, y_state, z_state)
    dp_grad_sout = PairSum(mover, links, state_grads, last_lanes, pair_last, y_sout, z_sout)
    dp_grad_down = WeightSum(mover, links, down_grads, own_lanes(depth), y_down, z_down)
    dp_grad_up = WeightSum(mover, links, up_grads, own_rows(depth), y_up, z_up)
    dp_grad_out = PairSum(mover, links, token_grads, last_lanes, pair_last, y_out, z_out)
    dp_grad_qkv = WeightSum(mover, links, token_grads, first_lanes, y_state, z_state)
    sum_small = SmallSum(mover, links, small, small_in)
    to_owner = [
        (
            mover(
                ship.at[k, :, block(2 - 2 * (s // 2), lanes)],
                landed.at[k, :, block(2 - 2 * (s % 2), lanes)],
                links.to_x,
            ),
            mover(
                ship.at[k, :, block(1 - s % 2 + s // 2, lanes)],
                landed.at[k, :, lanes : 2 * lanes],
                links.to_core,
            ),
        )
        for k in range(2)
    ]
    assert max(mover.sends, mover.recvs) <= LAYER_COPIES

    local = []
    for source, target in (
        (w_qkv.at[:, block(2 * (s % 2), lanes)], slab.at[0, :, block((s + 1) // 2, lanes)]),
        (w_sqkv.at[:, block(2 * (s % 2), lanes)], slab.at[1, :, block((s + 1) // 2, lanes)]),
        (tokens, tok_all.at[block(s, rows), :]),
        (state, state_all.at[block(s, state_rows), :]),
        (state_cot, state_all.at[cot_rows(s)]),
        (cot, cot_all.at[block(s, rows), :]),
        (w_up, up_nat.at[block(d, depth), :]),
        (w_down, down_nat.at[:, block(d, depth)]),
        (w_out, out_nat.at[block(d, depth), own_columns]),
        (w_sout, sout_nat.at[block(d, depth), own_columns]),
    ):
        local.append(pltpu.make_async_copy(source, target, local_sem.at[len(local)]))

    links.greet()
    for over_x, beside in to_slab:
        over_x.start()
        beside.start()
    dp_sout.start_y()
    dp_out.start_y()
    get_tokens.start()
    for copy in local:
        copy.start()
    small[0] = jnp.zeros(small.shape[1:], f32)
    key_sum[...] = jnp.zeros_like(key_sum)
    own_sum[...] = jnp.zeros_like(own_sum)
    for k, gather in enumerate((dp_qkv, dp_sqkv)):
        for copy in (*to_slab[k],):
            copy.wait_recv()
        local[k].wait()
        if k == 0:
            gather.start_z()
        gather.start_y()
    get_state.start()
    get_scot.start()
    get_cot.start()
    qkv_nat[block(d, depth), :] = slab[0]
    sqkv_nat[block(d, depth), :] = slab[1]
    for copy in local[2:]:
        copy.wait()

    def token_norm(i):
        at = block(i, rows)
        hat, _ = normalized(tok_all[at, :].astype(f32))
        first[at, :] = (hat * gains[0:1, :] + shifts[0:1, :]).astype(bf16)

    token_norm(s)
    onehot = jnp.where(
        lax.broadcasted_iota(jnp.int32, (rel_table.shape[1], buckets.shape[1]), 0) == buckets[...],
        1.0,
        0.0,
    )
    turned = jnp.where(
        lax.broadcasted_iota(jnp.int32, (span, buckets.shape[1]), 0)
        + lax.broadcasted_iota(jnp.int32, (span, buckets.shape[1]), 1)
        == buckets.shape[1],
        1.0,
        0.0,
    )
    by_bucket[...] = dot_rt(turned.astype(bf16), onehot.astype(bf16))
    bias = lax.dot_general(
        rel_table[...],
        by_bucket[...],
        (((1,), (1,)), ((), ())),
        precision=lax.Precision.HIGHEST,
        preferred_element_type=f32,
    )
    column = lax.broadcasted_iota(jnp.int32, bias.shape, 1)
    distance[...] = jnp.where((column > 0) & (column <= span - rows), bias, masked_value)
    bias_blocks(tb, [distance[pl.ds(s * heads + h, 1), :] for h in range(heads)])
    distance[...] = jnp.zeros_like(distance)
    get_tokens.beside.wait_recv()
    token_norm(links.core)
    dp_qkv.forward(0)
    dp_sout.start_z()
    dp_qkv.forward(1)
    dp_sqkv.start_z()
    dp_up.start_y()
    get_tokens.forward()
    token_norm(links.x)
    dp_qkv.forward(2)
    for k in range(3):
        dp_sout.forward(k)
    get_sout.start()
    dp_out.start_z()
    dp_up.start_z()
    get_tokens.passed.wait_recv()
    token_norm(flip_low(links.x))
    get_state.forward()
    dp_sqkv.forward(0)
    dp_qkv.finish()
    get_scot.forward()

    def token_qkv(i):
        at = block(i, rows)
        qkv[at, :] = dot(first[at, :], qkv_nat[...]).astype(bf16)

    for i in range(4):
        token_qkv(i)
    for c in range(4):
        count = min(span, (c + 1) * rows)
        low, high = (c + 1) * rows - count, (c + 1) * rows
        last = c * rows if c == 3 else 0
        parts = []
        for h in range(heads):
            probs = window_probs(
                (0, length[0]),
                qkv[c * rows : high, head_cols(0, h, heads, head_dim)],
                qkv[low:high, head_cols(1, h, heads, head_dim)],
                tb[h],
                last,
                scale,
            )
            parts.append(
                dot(probs.astype(bf16), qkv[low:high, head_cols(2, h, heads, head_dim)])
            )
        mixed[c * rows : high, own_columns] = jnp.concatenate(parts, axis=1).astype(bf16)
        if c == 1:
            dp_sqkv.forward(1)
        elif c == 2:
            dp_sqkv.forward(2)
            dp_down.start_z()
    get_mixed.start()
    dp_out.forward(0)
    get_cot.forward()

    get_state.finish()

    def state_norms(i):
        at = block(i, state_rows)
        hat, _ = normalized(state_all[at, :].astype(f32))
        hid[at, :] = (hat * gains[2:3, :] + shifts[2:3, :]).astype(bf16)

    for i in range(4):
        state_norms(i)
    dp_sqkv.finish()
    state_norm, back_update = slice(0, all_states), slice(all_states, 2 * all_states)
    sqkv[...] = dot(hid[state_norm, :], sqkv_nat[...]).astype(bf16)
    dp_out.forward(1)
    dp_out.forward(2)
    get_out.start()
    dp_up.forward(0)

    def state_read(i):
        at = block(i, state_rows)
        parts = []
        for h in range(heads):
            own, token = state_probs(
                (0, length[0]),
                sqkv[at, head_cols(0, h, heads, head_dim)],
                sqkv[:, head_cols(1, h, heads, head_dim)],
                qkv[:, head_cols(1, h, heads, head_dim)],
                scale,
            )
            parts.append(
                dot(own.astype(bf16), sqkv[:, head_cols(2, h, heads, head_dim)])
                + dot(token.astype(bf16), qkv[:, head_cols(2, h, heads, head_dim)])
            )
        read_all[at, own_columns] = jnp.concatenate(parts, axis=1).astype(bf16)

    for i in range(4):
        state_read(i)
        if i == 1:
            dp_up.forward(1)
    get_read.start()
    dp_up.forward(2)
    dp_down.start_y()
    dp_down.forward(0)
    get_sout.forward()

    gate = jax.nn.sigmoid(gate_bias[...])
    get_scot.finish()

    def updates(i):
        hid[cot_rows(i)] = ((1.0 - gate) * state_all[cot_rows(i)].astype(f32)).astype(bf16)

    for i in range(4):
        updates(i)
    get_sout.finish()
    back_read[...] = dot_rt(hid[back_update, :], sout_nat[block(s, lanes), :]).astype(bf16)

    def state_back(h):
        key_at, value_at = head_cols(1, h, heads, head_dim), head_cols(2, h, heads, head_dim)
        query_at, read_at = head_cols(0, h, heads, head_dim), head_cols(0, h, heads, head_dim)

        def one(i):
            at = block(i, state_rows)
            query, back = sqkv[at, query_at], back_read[at, read_at]
            own, token = state_probs(
                (0, length[0]), query, sqkv[:, key_at], qkv[:, key_at], scale
            )
            back_own = dot_rt(back, sqkv[:, value_at])
            back_token = dot_rt(back, qkv[:, value_at])
            row_dot = jnp.sum(own * back_own, axis=-1, keepdims=True) + jnp.sum(
                token * back_token, axis=-1, keepdims=True
            )
            own_raw = (own * (back_own - row_dot) * scale).astype(bf16)
            token_raw = (token * (back_token - row_dot) * scale).astype(bf16)
            back_sqkv[at, query_at] = (
                dot(own_raw, sqkv[:, key_at]) + dot(token_raw, qkv[:, key_at])
            ).astype(bf16)
            key_to = slice(key_at.start - lanes, key_at.stop - lanes)
            value_to = slice(value_at.start - lanes, value_at.stop - lanes)
            own_sum[:, key_to] += dot_lt(own_raw, query)
            own_sum[:, value_to] += dot_lt(own.astype(bf16), back)
            key_sum[:, key_to] += dot_lt(token_raw, query)
            key_sum[:, value_to] += dot_lt(token.astype(bf16), back)

        for i in range(4):
            one(i)

    for h in range(heads):
        state_back(h)
        if h == 0:
            dp_down.forward(1)
    back_sqkv[:, lanes:] = own_sum[...].astype(bf16)

    back_state[0:all_states, :] = dot_rt(back_sqkv[...], sqkv_nat[...]).astype(bf16)
    sum_state.start()
    dp_down.forward(2)
    get_mixed.forward()

    for start in range(0, width, 256):
        at = slice(start, start + 256)
        state_grads[at, 0 : 3 * lanes] = dot_lt(hid[state_norm, at], back_sqkv[...]).astype(bf16)
    sum_state.middle()
    sum_state.keep()
    get_out.forward()
    get_read.forward()

    get_read.finish()
    update = dot(read_all[block(s, state_rows), :], sout_nat[...])
    held = state_all[block(s, state_rows), :].astype(f32)
    own_cot = state_all[cot_rows(s)].astype(f32)
    next_state[...] = (gate * held + (1.0 - gate) * update).astype(bf16)
    small[0, 6:7, :] = jnp.sum(own_cot * (held - update), axis=0, keepdims=True) * (
        gate * (1.0 - gate)
    )
    state_grads[:, 3 * lanes : 4 * lanes] = dot_lt(
        read_all[...], hid[back_update, own_columns]
    ).astype(bf16)

    get_read.sent()
    own_state, own_scot = slice(0, state_rows), slice(state_rows, 2 * state_rows)
    again = [
        pltpu.make_async_copy(source, read_all.at[place, :], local_sem.at[k])
        for k, (source, place) in enumerate(((state, own_state), (state_cot, own_scot)))
    ]
    for copy in again:
        copy.start()
    dp_grad_sout.start()

    get_mixed.finish()
    get_out.finish()
    dp_up.finish()
    get_cot.finish()
    for gather in (get_state, get_scot, get_sout, dp_sout, get_out, dp_out, dp_sqkv):
        gather.sent()
    out_rows[...] = out_nat[block(s, lanes), :]
    dp_state.start()

    def ffn_rows(i):
        at = block(i, rows)
        total = tok_all[at, :].astype(f32) + dot(mixed[at, :], out_nat[...])

        @pl.when(i == s)
        def _():
            res_own[...] = total

        hat, inverse = normalized(total)
        normed = (hat * gains[1:2, :] + shifts[1:2, :]).astype(bf16)
        second[at, :] = normed
        own_half = block(i, half)
        upper = s % 2 == 0
        hat_half[own_half, :] = jnp.where(upper, hat[:half], hat[half:]).astype(bf16)
        inverse_half[own_half, :] = jnp.broadcast_to(
            jnp.where(upper, inverse[:half], inverse[half:]), (half, 128)
        )
        inner = dot(normed, up_nat[...])
        root = 0.7978845608028654
        square = inner * inner
        bend = jnp.tanh(inner * (root + (root * 0.044715) * square))
        open_part = 0.5 + 0.5 * bend
        hidden[at, :] = (inner * open_part).astype(bf16)
        slope[at, :] = (
            open_part
            + (inner - inner * bend * bend) * (0.5 * root + (1.5 * root * 0.044715) * square)
        ).astype(bf16)

    for i in range(4):
        ffn_rows(i)

    sum_state.sent()

    def down_columns(i):
        at = block(i, 256)
        down_grads[:, at] = dot_lt(hidden[...], cot_all[:, at]).astype(bf16)

    for i in range(width // 256):
        down_columns(i)
    dp_grad_down.start()
    get_cot.sent()
    for copy in again:
        copy.wait()
    hat_state, inverse_state = normalized(read_all[own_state, :].astype(f32))
    back_own_state = sum_state.finish_kept()
    small[0, 2:3, :] = jnp.sum(back_own_state * hat_state, axis=0, keepdims=True)
    small[0, 5:6, :] = jnp.sum(back_own_state, axis=0, keepdims=True)
    grad_state[...] = (
        gate * read_all[own_scot, :].astype(f32)
        + normed_back(back_own_state, hat_state, inverse_state, gains[2:3, :])
    ).astype(bf16)
    dp_down.finish()

    def ffn_back_rows(i):
        at = block(i, rows)
        inner = (dot_rt(cot_all[at, :], down_nat[...]) * slope[at, :].astype(f32)).astype(bf16)
        back_input[at, :] = inner
        back_second[at, :] = dot_rt(inner, up_nat[...]).astype(bf16)
        block_sums[i].start()

    def up_columns(i):
        at = block(i, 256)
        up_grads[at, :] = dot_lt(second[:, at], back_input[...]).astype(bf16)

    def ffn_out_rows(i):
        at = block(i, rows)
        ffn_partial[at, :] = dot(hidden[at, :], down_nat[...]).astype(bf16)

    def norm_rows(i):
        back = block_sums[i].total()
        at = block(i, half)
        hat = hat_half[at, :].astype(f32)
        small[0, 1:2, :] += 0.5 * jnp.sum(back * hat, axis=0, keepdims=True)
        small[0, 4:5, :] += 0.5 * jnp.sum(back, axis=0, keepdims=True)
        kept_cot = cot_all[block_sums[i].mine].astype(f32)
        block_sums[i].share(
            kept_cot + normed_back(back, hat, inverse_half[at, 0:1], gains[1:2, :])
        )

    def window_back(c):
        block_sums[c].finish()
        count = min(span, (c + 1) * rows)
        low, high = (c + 1) * rows - count, (c + 1) * rows
        last = c * rows if c == 3 else 0
        at = block(c, rows)
        back_mixed = dot_rt(back_branch[at, :], out_rows[...]).astype(bf16)
        for h in range(heads):
            key_at, value_at = head_cols(1, h, heads, head_dim), head_cols(2, h, heads, head_dim)
            query_at = head_cols(0, h, heads, head_dim)
            query, back = qkv[at, query_at], back_mixed[:, query_at]
            keys = qkv[low:high, key_at]
            probs = window_probs((0, length[0]), query, keys, tb[h], last, scale)
            back_probs = dot_rt(back, qkv[low:high, value_at])
            row_dot = jnp.sum(probs * back_probs, axis=-1, keepdims=True)
            back_scores = probs * (back_probs - row_dot)
            if c == 0:
                band[h] = jnp.zeros(band.shape[1:], f32)
            band[h, :, span - count :] += back_scores
            raw = (back_scores * scale).astype(bf16)
            back_qkv[at, query_at] = dot(raw, keys).astype(bf16)
            key_to = slice(key_at.start - lanes, key_at.stop - lanes)
            value_to = slice(value_at.start - lanes, value_at.stop - lanes)
            key_sum[low:high, key_to] += dot_lt(raw, query)
            key_sum[low:high, value_to] += dot_lt(probs.astype(bf16), back)

    ffn_back_rows(0)
    ffn_back_rows(1)
    block_sums[0].middle()
    ffn_back_rows(2)
    block_sums[1].middle()
    ffn_back_rows(3)
    block_sums[2].middle()
    for k in (1, 2):
        dp_grad_sout.combine(k)
    block_sums[3].middle()
    dp_state.forward(1)
    for i in range(width // 256):
        up_columns(i)
    dp_grad_sout.middle()
    dp_grad_up.start()
    dp_up.sent()
    dp_state.forward(2)
    for i in range(4):
        ffn_out_rows(i)
    sum_ffn.start()
    dp_down.sent()
    norm_rows(0)
    dp_state.forward(0)
    norm_rows(1)
    window_back(0)
    dp_state.combine(1)
    dp_state.combine(2)
    sum_ffn.middle()
    norm_rows(2)
    window_back(1)
    dp_grad_down.forward(1)
    norm_rows(3)
    window_back(2)
    dp_grad_down.forward(2)
    state_total = dp_state.finish()
    for partner in (links.to_y, *links.to_z):
        pl.semaphore_signal(credit, inc=1, device_id=partner, device_id_type=pl.DeviceIdType.MESH)
    dp_qkv.sent()
    ship[1] = state_total.astype(bf16)
    grad_sqkv[:, block(2 * (s % 2), lanes)] = ship[1, :, block((s + 1) // 2, lanes)]
    for copy in to_owner[1]:
        copy.start()
    window_back(3)
    dp_grad_down.forward(0)
    back_qkv[:, lanes:] = key_sum[...].astype(bf16)
    small[0, 0:1, :] = jnp.zeros((1, width), f32)
    small[0, 3:4, :] = jnp.zeros((1, width), f32)

    def qkv_grads(i):
        at = block(i, 256)
        token_grads[at, 0 : 3 * lanes] = dot_lt(first[:, at], back_qkv[...]).astype(bf16)

    def first_partial(i):
        at = block(i, rows)
        back = dot_rt(back_qkv[at, :], qkv_nat[...])
        back_first[at, :] = back.astype(bf16)
        hat, _ = normalized(tok_all[at, :].astype(f32))
        small[0, 0:1, :] += jnp.sum(back * hat, axis=0, keepdims=True)
        small[0, 3:4, :] += jnp.sum(back, axis=0, keepdims=True)

    for i in range(width // 256):
        qkv_grads(i)
    pl.semaphore_wait(credit, 4)
    dp_grad_qkv.start()
    token_grads[:, 3 * lanes : 4 * lanes] = dot_lt(
        mixed[...], back_branch[:, own_columns]
    ).astype(bf16)
    dp_grad_out.start()
    dp_grad_down.combine(1)
    for i in range(4):
        first_partial(i)
    sum_first.start()
    dp_grad_down.combine(2)
    for h in range(heads):
        distance[pl.ds(s * heads + h, 1), :] = jnp.sum(by_distance(band[h]), axis=0, keepdims=True)
    small[0, 8:16, 0 : by_bucket.shape[1]] = lax.dot_general(
        distance[...],
        by_bucket[...],
        (((1,), (0,)), ((), ())),
        precision=lax.Precision.HIGHEST,
        preferred_element_type=f32,
    )
    output[...] = (res_own[...] + sum_ffn.finish()).astype(bf16)
    sum_small.start()
    sum_first.middle()
    for k in (1, 2):
        dp_grad_out.combine(k)
    dp_grad_up.forward(1)
    sum_small.step(0)
    grad_down[...] = dp_grad_down.finish().astype(bf16)
    dp_grad_out.middle()
    dp_grad_up.forward(2)
    dp_grad_up.combine(1)
    dp_grad_up.forward(0)
    dp_grad_up.combine(2)
    hat_first, inverse_first = normalized(tok_all[block(s, rows), :].astype(f32))
    back_own_first = sum_first.finish()
    grad_tokens[...] = (
        back_branch[block(s, rows), :].astype(f32)
        + normed_back(back_own_first, hat_first, inverse_first, gains[0:1, :])
    ).astype(bf16)
    sum_small.step(1)
    dp_grad_qkv.forward(1)
    grad_sout[...] = dp_grad_sout.finish().astype(bf16)
    dp_grad_qkv.forward(2)
    grad_up[...] = dp_grad_up.finish().astype(bf16)
    sum_small.step(2)
    dp_grad_qkv.forward(0)
    dp_grad_qkv.combine(1)
    sum_small.step(3)
    dp_grad_qkv.combine(2)
    grad_out[...] = dp_grad_out.finish().astype(bf16)
    sum_small.step(4)
    grad_norm[...] = small[5, 0:8, :]
    grad_rel[...] = small[5, 8:16, 0:128]
    ship[0] = dp_grad_qkv.finish().astype(bf16)
    for copy in to_owner[0]:
        copy.start()
    grad_qkv[:, block(2 * (s % 2), lanes)] = ship[0, :, block((s + 1) // 2, lanes)]
    for k, grads in ((1, grad_sqkv), (0, grad_qkv)):
        for copy in to_owner[k]:
            copy.wait_recv()
        grads[:, lanes : 2 * lanes] = landed[k, :, lanes : 2 * lanes]
        x_at = block(2 - 2 * (s % 2), lanes)
        grads[:, x_at] = landed[k, :, x_at]
    for over_x, beside in (*to_slab, *to_owner):
        over_x.wait_send()
        beside.wait_send()
    for used in (
        get_tokens,
        get_mixed,
        *block_sums,
        sum_ffn,
        sum_first,
        dp_state,
        dp_grad_sout,
        dp_grad_down,
        dp_grad_up,
        dp_grad_out,
        dp_grad_qkv,
        sum_small,
    ):
        used.sent()


def settle(
    output,
    next_state,
    grad_tokens,
    grad_state,
    grad_qkv,
    grad_out,
    grad_sqkv,
    grad_sout,
    grad_up,
    grad_down,
    grad_rel,
    grad_norm,
    *results,
):
    for result, value in zip(results, (output, next_state, grad_tokens, grad_state)):
        if len(result.shape) == 3:
            result[0] = value[...]
        else:
            result[...] = value[...]
    grads = (grad_qkv, grad_out, grad_sqkv, grad_sout, grad_up, grad_down)
    for result, value in zip(results[4:], grads):
        result[...] = value[...].astype(f32)
    rel, gain, shift, gate = results[10:]
    rel[...] = grad_rel[:, 0 : rel.shape[1]]
    gain[...] = grad_norm[0:3, :]
    shift[...] = grad_norm[3:6, :]
    gate[...] = grad_norm[6, :]


def norm_back(values, back, gain):
    hat, inverse = normalized(values)
    return normed_back(back, hat, inverse, gain)


def per_device(
    tokens,
    state_in,
    cotangent,
    state_cotangent,
    seq_len,
    bucket_table,
    w_qkv,
    w_out,
    w_sqkv,
    w_sout,
    w_up,
    w_down,
    rel_table,
    norm_gain,
    norm_shift,
    gate_bias,
):
    rows, width = tokens.shape
    bucket_count, head_count = rel_table.shape
    window = bucket_table.shape[0]
    state_rows = state_in.shape[1]
    places = lax.axis_size("state")
    assert places == len(PLACES)
    dp_count = lax.axis_size("dp")
    here, dp_here = lax.axis_index("state"), lax.axis_index("dp")
    head_dim = width // head_count
    heads = head_count // places
    lanes = heads * head_dim
    span = window + rows
    group_rows = rows * places
    all_states = state_rows * places
    inner_width = w_up.shape[1]
    hops = dp_count == len(DP_PLACES)
    blocks = dp_count if hops else 1

    def swap(value, axis, bit):
        count = lax.axis_size(axis)
        return lax.ppermute(value, axis, [(i, i ^ bit) for i in range(count)])

    def from_group(value):
        pair = jnp.stack([value, swap(value, "state", 2)])
        return jnp.concatenate([pair, swap(pair, "state", 1)], axis=0)

    def list_from_group(value):
        across = swap(value, "state", 2)
        return [value, across, swap(value, "state", 1), swap(across, "state", 1)]

    def sum_to_owner(partial):
        half = partial.shape[0] // 2
        pair = partial[:half].astype(f32) + swap(partial[half:], "state", 1).astype(f32)
        return pair[0] + swap(pair[1].astype(bf16), "state", 2).astype(f32)

    def from_dp(block, axis):
        if not hops:
            return lax.all_gather(block, "dp", axis=axis, tiled=True)[None]
        gathered = block[None]
        for bit in DP_STEPS:
            gathered = jnp.concatenate([gathered, swap(gathered, "dp", bit)], axis=0)
        return gathered

    def sum_over_dp(partial, axis):
        if not hops:
            return lax.psum_scatter(partial[0], "dp", scatter_dimension=axis, tiled=True).astype(f32)
        for bit in reversed(DP_STEPS):
            half = partial.shape[0] // 2
            arrived = swap(partial[half:], "dp", bit)
            total = partial[:half].astype(f32) + arrived.astype(f32)
            partial = total.astype(bf16)
        return total[0]

    def sum_over_all(vector):
        if not hops:
            return lax.psum(vector, ("dp", "state"))
        for axis, bit in (("state", 1), ("state", 2), ("dp", 1), ("dp", 2), ("dp", 4)):
            vector = vector + swap(vector, axis, bit)
        return vector

    even = here % 2 == 0

    def pick(*by_place):
        value = by_place[-1]
        for i in reversed(range(places - 1)):
            value = jnp.where(here == i, by_place[i], value)
        return value

    def to_heads(shard):
        left, middle, right = (shard[:, i * lanes : (i + 1) * lanes] for i in range(3))
        own = jnp.where(even, left, right)
        across = swap(jnp.where(even, right, left), "state", 2)
        beside = swap(middle, "state", 1)
        query = pick(own, beside, across, across)
        keys = pick(beside, own, own, beside)
        values = pick(across, across, beside, own)
        return jnp.concatenate([query, keys, values], axis=1)

    def from_heads(grads):
        query, keys, values = (grads[:, i * lanes : (i + 1) * lanes] for i in range(3))
        own = pick(query, keys, keys, values)
        beside = swap(pick(keys, query, values, keys), "state", 1)
        across = swap(pick(values, values, query, query), "state", 2)
        return jnp.concatenate(
            [jnp.where(even, own, across), beside, jnp.where(even, across, own)], axis=1
        )

    if hops:
        block_list = dp_here ^ jnp.array(DP_PLACES, jnp.int32)
        position_list = jnp.array(
            [DP_PLACES.index(i) for i in range(dp_count)], jnp.int32
        )[dp_here ^ jnp.arange(dp_count)]
    else:
        block_list = position_list = jnp.zeros((1,), jnp.int32)
    scal = jnp.concatenate(
        [here[None].astype(jnp.int32), seq_len.astype(jnp.int32), block_list, position_list]
    ).astype(jnp.int32)

    gains = [norm_gain[i : i + 1] for i in range(3)]
    shifts = [norm_shift[i : i + 1] for i in range(3)]

    depth = w_qkv.shape[0]
    if hops:
        whole = pl.BlockSpec(memory_space=pltpu.VMEM)
        anywhere = pl.BlockSpec(memory_space=pl.ANY)
        vmem = lambda shape, kind=bf16: pltpu.VMEM(shape, kind)
        square = vmem((width, width))
        summed = pl.pallas_call(
            functools.partial(layer, head_dim),
            out_shape=[
                out((rows, width)),
                out((state_rows, width)),
                out((rows, width)),
                out((state_rows, width)),
                out((depth, 3 * lanes)),
                out((depth, lanes)),
                out((depth, 3 * lanes)),
                out((depth, lanes)),
                out((depth, inner_width)),
                out((inner_width, depth)),
                out((head_count, 128), f32),
                out((8, width), f32),
            ],
            in_specs=[pl.BlockSpec(memory_space=pltpu.SMEM)] + [anywhere] * 10 + [whole] * 5,
            out_specs=[whole] * 12,
            scratch_shapes=[
                pltpu.SemaphoreType.DMA((LAYER_COPIES,)),
                pltpu.SemaphoreType.DMA((LAYER_COPIES,)),
                pltpu.SemaphoreType.DMA((16,)),
                vmem((2, depth, 3 * lanes)),
                vmem((width, 3 * lanes)),
                vmem((width, 3 * lanes)),
                square,
                square,
                vmem((width, inner_width)),
                vmem((inner_width, width)),
                vmem((group_rows, width)),
                vmem((group_rows, width)),
                vmem((2 * all_states, width)),
                vmem((group_rows, width)),
                vmem((all_states, width)),
                vmem((2 * all_states, width)),
                vmem((group_rows, width)),
                vmem((group_rows, 3 * lanes)),
                vmem((group_rows, width)),
                vmem((all_states, 3 * lanes)),
                vmem((all_states, lanes)),
                vmem((all_states, 3 * lanes)),
                vmem((all_states, 2 * lanes), f32),
                vmem((group_rows, 2 * lanes), f32),
                vmem((rows, width), f32),
                vmem((group_rows // 2, width)),
                vmem((group_rows // 2, 128), f32),
                vmem((heads, rows, span), f32),
                vmem((heads, rows, span), f32),
                vmem((lanes, width)),
                square,
                vmem((inner_width, width)),
                vmem((4, depth, 3 * lanes)),
                vmem((4, inner_width, depth)),
                vmem((4, depth, inner_width)),
                vmem((depth, lanes)),
                vmem((depth, lanes)),
                vmem((4, depth, 3 * lanes)),
                vmem((4, inner_width, depth)),
                vmem((4, depth, inner_width)),
                vmem((4, 2 * depth, lanes)),
                vmem((4, 2 * depth, lanes)),
                vmem((2, rows, width)),
                vmem((2, rows, width)),
                vmem((2, rows, width)),
                vmem((rows, width)),
                vmem((6, 16, width), f32),
                vmem((5, 16, width), f32),
                vmem((8, span), f32),
                vmem((2, depth, 3 * lanes)),
                pltpu.SemaphoreType.REGULAR,
                vmem((span, bucket_count), f32),
            ],
            compiler_params=pltpu.CompilerParams(
                collective_id=0, has_side_effects=True, vmem_limit_bytes=64 << 20
            ),
            name="layer",
        )(
            seq_len,
            tokens,
            state_in[0],
            cotangent,
            state_cotangent[0],
            w_qkv,
            w_out,
            w_sqkv,
            w_sout,
            w_up,
            w_down,
            bucket_table[None],
            rel_table.T,
            norm_gain,
            norm_shift,
            gate_bias[None],
        )
        results = pl.pallas_call(
            settle,
            out_shape=[
                out((rows, width)),
                out((1, state_rows, width)),
                out((rows, width)),
                out((1, state_rows, width)),
                out((depth, 3 * lanes), f32),
                out((depth, lanes), f32),
                out((depth, 3 * lanes), f32),
                out((depth, lanes), f32),
                out((depth, inner_width), f32),
                out((inner_width, depth), f32),
                out((head_count, bucket_count), f32),
                out((3, width), f32),
                out((3, width), f32),
                out((width,), f32),
            ],
            in_specs=[whole] * 12,
            out_specs=[whole] * 14,
            compiler_params=pltpu.CompilerParams(vmem_limit_bytes=60 << 20),
            name="settle",
        )(*summed)
        return (*results[:10], results[10].T, *results[11:])

    lookup = (bucket_table[:, None] == jnp.arange(bucket_count)[None, :]).astype(f32)
    own_table = lax.dynamic_slice_in_dim(rel_table, here * heads, heads, 1)
    bias_rows = jnp.dot(
        own_table.T, lookup.T, precision=lax.Precision.HIGHEST, preferred_element_type=f32
    )
    bias = jnp.concatenate(
        [
            jnp.full((heads, 1), masked_value, f32),
            bias_rows[:, ::-1],
            jnp.full((heads, span - window - 1), masked_value, f32),
        ],
        axis=1,
    )
    both = to_heads(jnp.concatenate([w_qkv, w_sqkv], axis=0))
    full_qkv = from_dp(both[:depth], 0)
    all_tokens = from_group(tokens)
    full_sqkv = from_dp(both[depth:], 0)
    all_state = from_group(state_in[0])
    all_cot = from_group(cotangent)
    all_state_cot = from_group(state_cotangent[0])
    outs_pair = from_dp(jnp.concatenate([w_out, w_sout], axis=1), 0)
    half = outs_pair.shape[2] // 2
    full_sout = list_from_group(outs_pair[:, :, half:])
    full_out = list_from_group(outs_pair[:, :, :half])
    full_up = from_dp(w_up, 0)
    full_down = from_dp(w_down, 1)

    first, qkv, mixed = call(
        functools.partial(token_forward, head_dim),
        "token_forward",
        [out((group_rows, width)), out((group_rows, 3 * lanes)), out((places, rows, lanes))],
        [pltpu.VMEM((width, 3 * lanes), bf16), pltpu.VMEM((heads, rows, span), f32)],
        2 * group_rows * width * 3 * lanes,
        group_rows * span * heads,
        scal,
        all_tokens,
        gains[0],
        shifts[0],
        full_qkv,
        bias,
    )
    mixed_parts = list_from_group(mixed)

    state_norm, sqkv, read = call(
        functools.partial(state_forward, head_dim),
        "state_forward",
        [
            out((all_states, width)),
            out((all_states, 3 * lanes)),
            out((places, state_rows, lanes)),
        ],
        [pltpu.VMEM((width, 3 * lanes), bf16)],
        2 * all_states * width * 3 * lanes,
        all_states * (all_states + group_rows) * heads,
        scal,
        all_state,
        gains[2],
        shifts[2],
        full_sqkv,
        qkv,
    )
    read_parts = list_from_group(read)

    next_state, grad_gate, grad_sout, token_back, grad_sqkv, back_state_norm, state_sums = call(
        functools.partial(state_backward, head_dim),
        "state_backward",
        [
            out((state_rows, width)),
            out((1, width), f32),
            out((blocks, width // blocks, lanes)),
            out((group_rows, 2 * lanes), f32),
            out((blocks, width // blocks, 3 * lanes)),
            out((places, state_rows, width)),
            out((2, width), f32),
        ],
        [
            pltpu.VMEM((width, 3 * lanes), bf16),
            pltpu.VMEM((width, width), bf16),
            pltpu.VMEM((all_states, width), bf16),
            pltpu.VMEM((all_states, lanes), bf16),
            pltpu.VMEM((all_states, 3 * lanes), bf16),
            pltpu.VMEM((all_states, 2 * lanes), f32),
        ],
        4 * all_states * width * 4 * lanes,
        all_states * (all_states + group_rows) * heads,
        scal,
        state_in[0],
        all_state_cot,
        gate_bias[None],
        all_state,
        *read_parts,
        *full_sout,
        sqkv,
        qkv,
        state_norm,
        full_sqkv,
    )
    residual, second, hidden, slope, out_rows, grad_down = call(
        ffn_up,
        "ffn_up",
        [
            out((places, rows, width), f32),
            out((group_rows, width)),
            out((group_rows, inner_width)),
            out((group_rows, inner_width)),
            out((lanes, width)),
            out((blocks, inner_width, width // blocks)),
        ],
        [pltpu.VMEM((width, width), bf16), pltpu.VMEM((width, inner_width), bf16)],
        2 * group_rows * width * (width + 2 * inner_width),
        group_rows * inner_width,
        scal,
        all_tokens,
        *mixed_parts,
        *full_out,
        gains[1],
        shifts[1],
        full_up,
        all_cot,
    )

    back_second, back_input, mid_sums = call(
        ffn_back,
        "ffn_back",
        [
            out((places, rows, width)),
            out((group_rows, inner_width)),
            out((2, width), f32),
        ],
        [pltpu.VMEM((inner_width, width), bf16), pltpu.VMEM((width, inner_width), bf16)],
        4 * group_rows * width * inner_width,
        0,
        scal,
        all_cot,
        full_down,
        full_up,
        slope,
        residual,
    )
    residual_own = residual[0]
    own_grad_sout = sum_over_dp(grad_sout, 0)
    own_grad_sqkv = sum_over_dp(grad_sqkv, 0)
    back_state = sum_to_owner(back_state_norm)
    gate_open = jax.nn.sigmoid(gate_bias)
    grad_state = (
        gate_open * state_cotangent[0].astype(f32)
        + norm_back(state_in[0].astype(f32), back_state, norm_gain[2])
    ).astype(bf16)

    own_grad_down = sum_over_dp(grad_down, 1)
    back_second = sum_to_owner(back_second)
    back_residual = cotangent.astype(f32) + norm_back(residual_own, back_second, norm_gain[1])
    back_branch = from_group(back_residual.astype(bf16))

    ffn_partial, grad_up = call(
        ffn_rest,
        "ffn_rest",
        [out((places, rows, width)), out((blocks, width // blocks, inner_width))],
        [pltpu.VMEM((inner_width, width), bf16)],
        4 * group_rows * width * inner_width,
        0,
        scal,
        hidden,
        full_down,
        second,
        back_input,
    )
    own_grad_up = sum_over_dp(grad_up, 0)
    output = (residual_own + sum_to_owner(ffn_partial)).astype(bf16)

    (grad_out,) = call(
        out_grad,
        "out_grad",
        [out((blocks, width // blocks, lanes))],
        [],
        2 * group_rows * width * lanes,
        0,
        scal,
        back_branch,
        *mixed_parts,
    )
    own_grad_out = sum_over_dp(grad_out, 0)

    grad_qkv, back_first, first_sums, distance = call(
        functools.partial(token_backward, head_dim),
        "token_backward",
        [
            out((blocks, width // blocks, 3 * lanes)),
            out((places, rows, width)),
            out((2, width), f32),
            out((heads, span), f32),
        ],
        [
            pltpu.VMEM((width, 3 * lanes), bf16),
            pltpu.VMEM((heads, rows, span), f32),
            pltpu.VMEM((group_rows, lanes), bf16),
            pltpu.VMEM((group_rows, 3 * lanes), bf16),
            pltpu.VMEM((group_rows, 2 * lanes), f32),
            pltpu.VMEM((rows, span), f32),
        ],
        2 * group_rows * width * 7 * lanes,
        group_rows * span * heads,
        scal,
        back_branch,
        out_rows,
        qkv,
        bias,
        token_back,
        first,
        all_tokens,
        full_qkv,
    )
    back_first = sum_to_owner(back_first)
    grad_tokens = (
        norm_back(tokens.astype(f32), back_first, norm_gain[0]) + back_residual
    ).astype(bf16)
    own_grad_qkv = sum_over_dp(grad_qkv, 0)
    both_grads = from_heads(
        jnp.concatenate([own_grad_qkv, own_grad_sqkv], axis=0).astype(bf16)
    ).astype(f32)

    per_distance = distance[:, 1 : window + 1][:, ::-1]
    own_rel = jnp.dot(
        per_distance, lookup, precision=lax.Precision.HIGHEST, preferred_element_type=f32
    ).T
    grad_rel = lax.dynamic_update_slice_in_dim(
        jnp.zeros((bucket_count, head_count), f32), own_rel, here * heads, 1
    )
    small = [
        jnp.stack([first_sums[0], mid_sums[0], state_sums[0]]),
        jnp.stack([first_sums[1], mid_sums[1], state_sums[1]]),
        grad_gate[0],
        grad_rel,
    ]
    packed = sum_over_all(jnp.concatenate([v.reshape(-1, 128) for v in small], axis=0))
    unpacked, start = [], 0
    for v in small:
        count = v.size // 128
        unpacked.append(packed[start : start + count].reshape(v.shape))
        start += count
    return (
        output,
        next_state[None],
        grad_tokens,
        grad_state[None],
        both_grads[:depth],
        own_grad_out,
        both_grads[depth:],
        own_grad_sout,
        own_grad_up,
        own_grad_down,
        unpacked[3],
        unpacked[0],
        unpacked[1],
        unpacked[2],
    )


def solution(mesh):
    rows_spec = P(("dp", "state"), None)
    state_spec = P("dp", "state", None)
    weight_spec = P("dp", "state")
    return jax.shard_map(
        per_device,
        mesh=mesh,
        in_specs=(
            rows_spec,
            state_spec,
            rows_spec,
            state_spec,
            P("dp"),
            P(),
            weight_spec,
            weight_spec,
            weight_spec,
            weight_spec,
            weight_spec,
            P("state", "dp"),
            P(),
            P(),
            P(),
            P(),
        ),
        out_specs=(
            rows_spec,
            state_spec,
            rows_spec,
            state_spec,
            weight_spec,
            weight_spec,
            weight_spec,
            weight_spec,
            weight_spec,
            P("state", "dp"),
            P(),
            P(),
            P(),
            P(),
        ),
        check_vma=False,
    )
```

```python
import functools

import jax
import jax.numpy as jnp
from jax import lax
from jax.experimental import pallas as pl
from jax.experimental.pallas import tpu as pltpu
from jax.sharding import PartitionSpec as P

epsilon = 1e-05
masked_value = -1e30
f32 = jnp.float32
bf16 = jnp.bfloat16

PLACES = (0, 2, 1, 3)
DP_STEPS = (2, 4, 1)
DP_PLACES = (0, 2, 4, 6, 1, 3, 5, 7)


def dot(left, right):
    return lax.dot_general(left, right, (((1,), (0,)), ((), ())), preferred_element_type=f32)


def dot_rt(left, right):
    return lax.dot_general(left, right, (((1,), (1,)), ((), ())), preferred_element_type=f32)


def dot_lt(left, right):
    return lax.dot_general(left, right, (((0,), (0,)), ((), ())), preferred_element_type=f32)


def where_from(sender, place):
    return PLACES.index(PLACES[sender] ^ PLACES[place])


def normalized(values):
    centre = jnp.mean(values, axis=-1, keepdims=True)
    centred = values - centre
    spread = jnp.mean(centred * centred, axis=-1, keepdims=True)
    inverse = lax.rsqrt(spread + epsilon)
    return centred * inverse, inverse


def normed_back(back, hat, inverse, gain):
    grown = back * gain
    return inverse * (
        grown
        - jnp.mean(grown, axis=-1, keepdims=True)
        - hat * jnp.mean(grown * hat, axis=-1, keepdims=True)
    )


def place_of(scal, q):
    return scal[0] ^ PLACES[q]


def aligned(start, size):
    return pl.ds(pl.multiple_of(start, size), size)


def block_at(scal, q):
    return scal[2 + q]


def position_of(scal, block, blocks):
    return scal[2 + blocks + block]


def rows_in_order(scal, target, source):
    blocks, depth = source.shape[0], source.shape[1]
    for q in range(blocks):
        target[aligned(block_at(scal, q) * depth, depth), :] = source[q]


def columns_in_order(scal, target, source):
    blocks, depth = source.shape[0], source.shape[2]
    for q in range(blocks):
        target[:, aligned(block_at(scal, q) * depth, depth)] = source[q]


def put_rows(scal, target, start, value):
    blocks, depth = target.shape[0], target.shape[1]
    rows = value.shape[0]
    if depth >= rows:
        target[position_of(scal, start // depth, blocks), aligned(start % depth, rows), :] = value
    else:
        for i in range(rows // depth):
            position = position_of(scal, start // depth + i, blocks)
            target[position] = value[i * depth : (i + 1) * depth]


def put_columns(scal, target, start, value):
    blocks, depth = target.shape[0], target.shape[2]
    columns = value.shape[1]
    if depth >= columns:
        target[position_of(scal, start // depth, blocks), :, aligned(start % depth, columns)] = value
    else:
        for i in range(columns // depth):
            position = position_of(scal, start // depth + i, blocks)
            target[position] = value[:, i * depth : (i + 1) * depth]


def call(body, name, outs, scratch, flops, exps, *args):
    sizes = sum(a.size * a.dtype.itemsize for a in args) + sum(
        a.size * a.dtype.itemsize for a in outs
    )
    in_specs = [pl.BlockSpec(memory_space=pltpu.SMEM)] + [
        pl.BlockSpec(memory_space=pltpu.VMEM) for _ in args[1:]
    ]
    return pl.pallas_call(
        body,
        out_shape=outs,
        in_specs=in_specs,
        out_specs=[pl.BlockSpec(memory_space=pltpu.VMEM) for _ in outs],
        scratch_shapes=scratch,
        compiler_params=pltpu.CompilerParams(vmem_limit_bytes=56 << 20),
        cost_estimate=pl.CostEstimate(flops=flops, bytes_accessed=sizes, transcendentals=exps),
        name=name,
    )(*args)


def out(shape, kind=bf16):
    return jax.ShapeDtypeStruct(shape, kind)


def by_distance(scores):
    rows, span = scores.shape
    row_at = lax.broadcasted_iota(jnp.int32, scores.shape, 0)
    step = 1
    while step < rows:
        scores = jnp.where(row_at & step != 0, pltpu.roll(scores, span - step, 1), scores)
        step *= 2
    return scores


def bias_blocks(tb, bias):
    heads, rows, span = tb.shape
    for h in range(heads):
        row = jnp.broadcast_to(bias[h], (rows, span))
        tb[h] = pltpu.roll(row, 0, 1, stride=1, stride_axis=0)


def window_probs(scal, query, keys, tb_block, last, scale):
    rows, span = tb_block.shape
    count = keys.shape[0]
    scores = dot_rt(query, keys) * scale + tb_block[:, span - count :]
    if last:
        row_at = lax.broadcasted_iota(jnp.int32, scores.shape, 0)
        col_at = lax.broadcasted_iota(jnp.int32, scores.shape, 1)
        ahead = col_at - (count - rows)
        live = (ahead < scal[1] - last) | (ahead == row_at)
        scores = jnp.where(live, scores, masked_value)
    top = jnp.max(scores, axis=-1, keepdims=True)
    grown = jnp.exp(scores - top)
    return grown * (1.0 / jnp.sum(grown, axis=-1, keepdims=True))


def state_probs(scal, query, state_keys, keys, scale):
    own = dot_rt(query, state_keys) * scale
    token = dot_rt(query, keys) * scale
    col_at = lax.broadcasted_iota(jnp.int32, token.shape, 1)
    token = jnp.where(col_at < scal[1], token, masked_value)
    top = jnp.maximum(
        jnp.max(own, axis=-1, keepdims=True), jnp.max(token, axis=-1, keepdims=True)
    )
    own = jnp.exp(own - top)
    token = jnp.exp(token - top)
    total = jnp.sum(own, axis=-1, keepdims=True) + jnp.sum(token, axis=-1, keepdims=True)
    inverse = 1.0 / total
    return own * inverse, token * inverse


def head_cols(block, h, heads, head_dim):
    start = (block * heads + h) * head_dim
    return slice(start, start + head_dim)


def token_forward(head_dim, scal, tokens, gain, shift, w_qkv, bias, first, qkv, mixed, w_nat, tb):
    places, rows, width = tokens.shape
    heads = bias.shape[0]
    span = bias.shape[1]
    scale = head_dim ** (-0.5)
    rows_in_order(scal, w_nat, w_qkv)
    bias_blocks(tb, [bias[h : h + 1, :] for h in range(heads)])
    for q in range(places):
        hat, _ = normalized(tokens[q].astype(f32))
        normed = (hat * gain[...] + shift[...]).astype(bf16)
        at = aligned(place_of(scal, q) * rows, rows)
        first[at, :] = normed
        qkv[at, :] = dot(normed, w_nat[...]).astype(bf16)
    for c in range(places):
        count = min(span, (c + 1) * rows)
        low, high = (c + 1) * rows - count, (c + 1) * rows
        last = c * rows if c == places - 1 else 0
        parts = []
        for h in range(heads):
            probs = window_probs(
                scal,
                qkv[c * rows : high, head_cols(0, h, heads, head_dim)],
                qkv[low:high, head_cols(1, h, heads, head_dim)],
                tb[h],
                last,
                scale,
            )
            parts.append(
                dot(probs.astype(bf16), qkv[low:high, head_cols(2, h, heads, head_dim)])
            )
        mixed[c] = jnp.concatenate(parts, axis=1).astype(bf16)


def state_forward(
    head_dim, scal, state, gain, shift, w_sqkv, qkv, normed_out, sqkv, read, w_nat
):
    places, rows, width = state.shape
    heads = qkv.shape[1] // (3 * head_dim)
    scale = head_dim ** (-0.5)
    rows_in_order(scal, w_nat, w_sqkv)
    for q in range(places):
        hat, _ = normalized(state[q].astype(f32))
        normed = (hat * gain[...] + shift[...]).astype(bf16)
        normed_out[q * rows : (q + 1) * rows, :] = normed
        sqkv[q * rows : (q + 1) * rows, :] = dot(normed, w_nat[...]).astype(bf16)
    for q in range(places):
        parts = []
        for h in range(heads):
            own, token = state_probs(
                scal,
                sqkv[q * rows : (q + 1) * rows, head_cols(0, h, heads, head_dim)],
                sqkv[:, head_cols(1, h, heads, head_dim)],
                qkv[:, head_cols(1, h, heads, head_dim)],
                scale,
            )
            parts.append(
                dot(own.astype(bf16), sqkv[:, head_cols(2, h, heads, head_dim)])
                + dot(token.astype(bf16), qkv[:, head_cols(2, h, heads, head_dim)])
            )
        read[q] = jnp.concatenate(parts, axis=1).astype(bf16)


def assembled(scal, target, parts):
    for p, part in enumerate(parts):
        blocks, depth, columns = part.shape
        at = aligned(place_of(scal, p) * columns, columns)
        for q in range(blocks):
            target[aligned(block_at(scal, q) * depth, depth), at] = part[q]


def state_backward(
    head_dim,
    scal,
    state_own,
    state_cot,
    gate_bias,
    state,
    read0,
    read1,
    read2,
    read3,
    out0,
    out1,
    out2,
    out3,
    sqkv,
    qkv,
    normed,
    w_sqkv,
    next_state,
    grad_gate,
    grad_sout,
    token_back,
    grad_sqkv,
    back_norm,
    grad_norm,
    w_nat,
    w_out,
    back_update,
    back_read,
    back_sqkv,
    own_sum,
):
    places, rows, width = state_cot.shape
    reads = (read0, read1, read2, read3)
    heads = qkv.shape[1] // (3 * head_dim)
    lanes = heads * head_dim
    scale = head_dim ** (-0.5)
    rows_in_order(scal, w_nat, w_sqkv)
    assembled(scal, w_out, (out0, out1, out2, out3))
    gate = jax.nn.sigmoid(gate_bias[...])
    update = None
    for p in range(places):
        term = dot(reads[p][p], w_out[aligned(place_of(scal, p) * lanes, lanes), :])
        update = term if update is None else update + term
    held = state_own[...].astype(f32)
    cot = state_cot[0].astype(f32)
    next_state[...] = (gate * held + (1.0 - gate) * update).astype(bf16)
    grad_gate[...] = jnp.sum(cot * (held - update), axis=0, keepdims=True) * (gate * (1.0 - gate))
    for q in range(places):
        back_update[q * rows : (q + 1) * rows, :] = (
            (1.0 - gate) * state_cot[q].astype(f32)
        ).astype(bf16)
    own_columns = back_update[:, aligned(scal[0] * lanes, lanes)]
    for p in range(places):
        stack = jnp.concatenate([reads[p][where_from(p, q)] for q in range(places)], axis=0)
        put_rows(
            scal, grad_sout, place_of(scal, p) * lanes, dot_lt(stack, own_columns).astype(bf16)
        )
    back_read[...] = dot_rt(
        back_update[...], w_out[aligned(scal[0] * lanes, lanes), :]
    ).astype(bf16)
    for h in range(heads):
        key_at, value_at = head_cols(1, h, heads, head_dim), head_cols(2, h, heads, head_dim)
        query_at, read_at = head_cols(0, h, heads, head_dim), slice(h * head_dim, (h + 1) * head_dim)
        for q in range(places):
            at = slice(q * rows, (q + 1) * rows)
            query, back = sqkv[at, query_at], back_read[at, read_at]
            own, token = state_probs(scal, query, sqkv[:, key_at], qkv[:, key_at], scale)
            back_own = dot_rt(back, sqkv[:, value_at])
            back_token = dot_rt(back, qkv[:, value_at])
            row_dot = jnp.sum(own * back_own, axis=-1, keepdims=True) + jnp.sum(
                token * back_token, axis=-1, keepdims=True
            )
            own_raw = (own * (back_own - row_dot) * scale).astype(bf16)
            token_raw = (token * (back_token - row_dot) * scale).astype(bf16)
            back_sqkv[at, query_at] = (
                dot(own_raw, sqkv[:, key_at]) + dot(token_raw, qkv[:, key_at])
            ).astype(bf16)
            terms = (
                (own_sum, key_at, dot_lt(own_raw, query)),
                (own_sum, value_at, dot_lt(own.astype(bf16), back)),
                (token_back, key_at, dot_lt(token_raw, query)),
                (token_back, value_at, dot_lt(token.astype(bf16), back)),
            )
            for target, columns, term in terms:
                columns = slice(columns.start - lanes, columns.stop - lanes)
                if q == 0:
                    target[:, columns] = term
                else:
                    target[:, columns] += term
    back_sqkv[:, lanes:] = own_sum[...].astype(bf16)
    for start in range(0, width, 256):
        put_rows(
            scal,
            grad_sqkv,
            start,
            dot_lt(normed[:, start : start + 256], back_sqkv[...]).astype(bf16),
        )
    gain_sum, shift_sum = None, None
    for q in range(places):
        back = dot_rt(back_sqkv[q * rows : (q + 1) * rows, :], w_nat[...])
        back_norm[q] = back.astype(bf16)
        hat, _ = normalized(state[q].astype(f32))
        gain_term = jnp.sum(back * hat, axis=0, keepdims=True)
        shift_term = jnp.sum(back, axis=0, keepdims=True)
        gain_sum = gain_term if q == 0 else gain_sum + gain_term
        shift_sum = shift_term if q == 0 else shift_sum + shift_term
    grad_norm[0:1, :] = gain_sum
    grad_norm[1:2, :] = shift_sum


def ffn_up(
    scal,
    tokens,
    mixed0,
    mixed1,
    mixed2,
    mixed3,
    out0,
    out1,
    out2,
    out3,
    gain,
    shift,
    w_up,
    cot,
    residual,
    second,
    hidden,
    slope,
    out_rows,
    grad_down,
    w_out,
    w_nat,
):
    places, rows, width = tokens.shape
    mixed = (mixed0, mixed1, mixed2, mixed3)
    lanes = mixed0.shape[2]
    assembled(scal, w_out, (out0, out1, out2, out3))
    out_rows[...] = w_out[aligned(scal[0] * lanes, lanes), :]
    rows_in_order(scal, w_nat, w_up)
    for q in range(places):
        total = tokens[q].astype(f32)
        for p in range(places):
            total += dot(
                mixed[p][place_of(scal, q)], w_out[aligned(place_of(scal, p) * lanes, lanes), :]
            )
        residual[q] = total
        hat, _ = normalized(total)
        normed = (hat * gain[...] + shift[...]).astype(bf16)
        at = slice(q * rows, (q + 1) * rows)
        second[at, :] = normed
        inner = dot(normed, w_nat[...])
        root = 0.7978845608028654
        square = inner * inner
        bend = jnp.tanh(root * inner * (1.0 + 0.044715 * square))
        half = 0.5 * (1.0 + bend)
        hidden[at, :] = (inner * half).astype(bf16)
        slope[at, :] = (
            half + (0.5 * root) * inner * (1.0 - bend * bend) * (1.0 + (3 * 0.044715) * square)
        ).astype(bf16)
    for start in range(0, width, 256):
        columns = jnp.concatenate([cot[q, :, start : start + 256] for q in range(places)], axis=0)
        put_columns(scal, grad_down, start, dot_lt(hidden[...], columns).astype(bf16))


def ffn_back(
    scal,
    cot,
    w_down,
    w_up,
    slope,
    residual,
    back_second,
    back_input,
    grad_norm,
    w_nat,
    w_up_nat,
):
    places, rows, width = cot.shape
    columns_in_order(scal, w_nat, w_down)
    rows_in_order(scal, w_up_nat, w_up)
    gain_sum, shift_sum = None, None
    for q in range(places):
        at = slice(q * rows, (q + 1) * rows)
        inner = (dot_rt(cot[q], w_nat[...]) * slope[at, :].astype(f32)).astype(bf16)
        back_input[at, :] = inner
        back = dot_rt(inner, w_up_nat[...])
        back_second[q] = back.astype(bf16)
        hat, _ = normalized(residual[q])
        gain_term = jnp.sum(back * hat, axis=0, keepdims=True)
        shift_term = jnp.sum(back, axis=0, keepdims=True)
        gain_sum = gain_term if q == 0 else gain_sum + gain_term
        shift_sum = shift_term if q == 0 else shift_sum + shift_term
    grad_norm[0:1, :] = gain_sum
    grad_norm[1:2, :] = shift_sum


def ffn_rest(scal, hidden, w_down, second, back_input, partial, grad_up, w_nat):
    places, rows, width = partial.shape
    for start in range(0, width, 256):
        put_rows(
            scal,
            grad_up,
            start,
            dot_lt(second[:, start : start + 256], back_input[...]).astype(bf16),
        )
    columns_in_order(scal, w_nat, w_down)
    for q in range(places):
        partial[q] = dot(hidden[q * rows : (q + 1) * rows, :], w_nat[...]).astype(bf16)


def out_grad(scal, back_branch, mixed0, mixed1, mixed2, mixed3, grad_out):
    places, rows, width = back_branch.shape
    mixed = (mixed0, mixed1, mixed2, mixed3)
    lanes = mixed0.shape[2]
    own_at = aligned(scal[0] * lanes, lanes)
    own_columns = jnp.concatenate([back_branch[q, :, own_at] for q in range(places)], axis=0)
    for p in range(places):
        stack = jnp.concatenate([mixed[p][place_of(scal, q)] for q in range(places)], axis=0)
        put_rows(
            scal, grad_out, place_of(scal, p) * lanes, dot_lt(stack, own_columns).astype(bf16)
        )


def token_backward(
    head_dim,
    scal,
    back_branch,
    out_rows,
    qkv,
    bias,
    token_back,
    first,
    tokens,
    w_qkv,
    grad_qkv,
    back_first,
    grad_norm,
    distance,
    w_nat,
    tb,
    back_mixed,
    back_qkv,
    key_sum,
    band,
):
    places, rows, width = back_branch.shape
    heads, span = bias.shape
    lanes = heads * head_dim
    scale = head_dim ** (-0.5)
    rows_in_order(scal, w_nat, w_qkv)
    bias_blocks(tb, [bias[h : h + 1, :] for h in range(heads)])
    for q in range(places):
        back_mixed[aligned(place_of(scal, q) * rows, rows), :] = dot_rt(
            back_branch[q], out_rows[...]
        ).astype(bf16)
    key_sum[...] = token_back[...]
    for h in range(heads):
        key_at, value_at = head_cols(1, h, heads, head_dim), head_cols(2, h, heads, head_dim)
        query_at, read_at = head_cols(0, h, heads, head_dim), slice(h * head_dim, (h + 1) * head_dim)
        for c in reversed(range(places)):
            count = min(span, (c + 1) * rows)
            low, high = (c + 1) * rows - count, (c + 1) * rows
            last = c * rows if c == places - 1 else 0
            query, back = qkv[c * rows : high, query_at], back_mixed[c * rows : high, read_at]
            keys = qkv[low:high, key_at]
            probs = window_probs(scal, query, keys, tb[h], last, scale)
            back_probs = dot_rt(back, qkv[low:high, value_at])
            row_dot = jnp.sum(probs * back_probs, axis=-1, keepdims=True)
            back_scores = probs * (back_probs - row_dot)
            if c == places - 1:
                band[...] = back_scores
            else:
                band[:, span - count :] += back_scores
            raw = (back_scores * scale).astype(bf16)
            back_qkv[c * rows : high, query_at] = dot(raw, keys).astype(bf16)
            key_to = slice(key_at.start - lanes, key_at.stop - lanes)
            value_to = slice(value_at.start - lanes, value_at.stop - lanes)
            key_sum[low:high, key_to] += dot_lt(raw, query)
            key_sum[low:high, value_to] += dot_lt(probs.astype(bf16), back)
        distance[h : h + 1, :] = jnp.sum(by_distance(band[...]), axis=0, keepdims=True)
    back_qkv[:, lanes:] = key_sum[...].astype(bf16)
    for start in range(0, width, 256):
        put_rows(
            scal,
            grad_qkv,
            start,
            dot_lt(first[:, start : start + 256], back_qkv[...]).astype(bf16),
        )
    gain_sum, shift_sum = None, None
    for q in range(places):
        back = dot_rt(back_qkv[aligned(place_of(scal, q) * rows, rows), :], w_nat[...])
        back_first[q] = back.astype(bf16)
        hat, _ = normalized(tokens[q].astype(f32))
        gain_term = jnp.sum(back * hat, axis=0, keepdims=True)
        shift_term = jnp.sum(back, axis=0, keepdims=True)
        gain_sum = gain_term if q == 0 else gain_sum + gain_term
        shift_sum = shift_term if q == 0 else shift_sum + shift_term
    grad_norm[0:1, :] = gain_sum
    grad_norm[1:2, :] = shift_sum


def flip_low(i):
    return i + 1 - 2 * (i % 2)


class Mover:
    def __init__(self, send, recv):
        self.send, self.recv, self.sends, self.recvs = send, recv, 0, 0

    def send_slot(self):
        self.sends += 1
        return self.sends - 1

    def recv_slot(self):
        self.recvs += 1
        return self.recvs - 1

    def copy(self, source, target, device, send_slot, recv_slot):
        return pltpu.make_async_remote_copy(
            src_ref=source,
            dst_ref=target,
            send_sem=self.send.at[send_slot],
            recv_sem=self.recv.at[recv_slot],
            device_id=device,
            device_id_type=pl.DeviceIdType.MESH,
        )

    def __call__(self, source, target, device):
        return self.copy(source, target, device, self.send_slot(), self.recv_slot())


class Links:
    def __init__(self):
        self.d, self.s = lax.axis_index("dp"), lax.axis_index("state")
        z, y = self.d // 2, self.d % 2
        self.over_z = [2 * (z + 1 - 2 * (z % 2)) + y, 2 * ((z + 2) % 4) + y, 2 * (3 - z) + y]
        self.over_y = flip_low(self.d)
        self.core, self.x = flip_low(self.s), (self.s + 2) % 4
        self.to_core, self.to_x = (self.d, self.core), (self.d, self.x)
        self.to_y = (self.over_y, self.s)
        self.to_z = [(other, self.s) for other in self.over_z]
        self.in_middle = (z == 1) | (z == 2)
        self.far_middle = 2 * (2 - z // 2) + y
        self.far_end = 2 * (3 - 3 * (z // 2)) + y
        self.to_far, self.to_far_end = (self.far_middle, self.s), (self.far_end, self.s)
        self.z, self.z_rest = z, [i // 2 for i in (self.over_z[0], self.far_middle, self.far_end)]

    def greet(self):
        barrier = pltpu.get_barrier_semaphore()
        partners = [self.to_core, self.to_x, self.to_y, *self.to_z]
        for partner in partners:
            pl.semaphore_signal(
                barrier, inc=1, device_id=partner, device_id_type=pl.DeviceIdType.MESH
            )
        pl.semaphore_wait(barrier, len(partners))


class GroupGather:
    def __init__(self, mover, links, whole, at, source=None):
        self.links, self.parts = links, [links.s, links.core, links.x, flip_low(links.x)]
        own = whole.at[at(links.s)]
        source = own if source is None else source
        across = whole.at[at(links.x)]
        self.over_x = mover(source, own, links.to_x)
        self.beside = mover(source, own, links.to_core)
        self.passed = mover(across, across, links.to_core)

    def start(self):
        self.over_x.start()
        self.beside.start()

    def forward(self):
        self.over_x.wait_recv()
        self.passed.start()

    def finish(self):
        self.beside.wait_recv()
        self.passed.wait_recv()

    def sent(self):
        for copy in (self.over_x, self.beside, self.passed):
            copy.wait_send()


class WeightGather:
    def __init__(self, mover, links, whole, at, source):
        own = whole.at[at(links.d)]
        self.links = links
        near, far = mover.send_slot(), mover.send_slot()
        slots = [mover.recv_slot() for _ in range(3)]
        self.near = mover.copy(source, own, links.to_z[0], near, slots[0])
        self.far = [mover.copy(source, own, links.to_far, far, slots[k]) for k in (1, 2)]
        self.own_y = mover(source, own, links.to_y)
        self.passed, self.relayed = [], [None]
        for k, other in enumerate((links.over_z[0], links.far_middle, links.far_end)):
            block = whole.at[at(other)]
            self.passed.append(mover(block, block, links.to_y))
            if k:
                self.relayed.append(
                    mover.copy(block, block, links.to_z[0], mover.send_slot(), slots[k])
                )

    def start_z(self):
        self.near.start()

        @pl.when(self.links.in_middle)
        def _():
            self.far[0].start()

        @pl.when(jnp.logical_not(self.links.in_middle))
        def _():
            self.far[1].start()

    def start_y(self):
        self.own_y.start()

    def pass_on(self, k):
        if k == 0:
            self.near.wait_recv()
        else:
            self.relayed[k].wait_recv()
        self.passed[k].start()

    def pass_middle(self, *ks):
        @pl.when(self.links.in_middle)
        def _():
            for k in ks:
                if k:
                    self.relayed[k].wait_recv()
                    self.relayed[k].start()
                    self.passed[k].start()
                else:
                    self.pass_on(0)

    def pass_end(self, *ks):
        @pl.when(jnp.logical_not(self.links.in_middle))
        def _():
            for k in ks:
                self.pass_on(k)

    def finish(self):
        self.own_y.wait_recv()
        for copy in self.passed:
            copy.wait_recv()

    def sent(self):
        for copy in (self.near, self.far[0], self.own_y, *self.passed):
            copy.wait_send()

        @pl.when(self.links.in_middle)
        def _():
            for copy in self.relayed[1:]:
                copy.wait_send()


class PairGather:
    def __init__(self, mover, links, whole, at, pair, source):
        own = whole.at[at(links.d)]
        self.links = links
        self.own_y = mover(source, own, links.to_y)
        both = whole.at[pair(links.z)]
        near, far = mover.send_slot(), mover.send_slot()
        slots = [mover.recv_slot() for _ in range(3)]
        self.near = mover.copy(both, both, links.to_z[0], near, slots[0])
        self.far = [mover.copy(both, both, links.to_far, far, slots[k]) for k in (1, 2)]
        self.relayed = [None]
        for k in (1, 2):
            other = whole.at[pair(links.z_rest[k])]
            self.relayed.append(
                mover.copy(other, other, links.to_z[0], mover.send_slot(), slots[k])
            )

    def start_y(self):
        self.own_y.start()

    def start_z(self):
        self.own_y.wait_recv()
        self.near.start()

        @pl.when(self.links.in_middle)
        def _():
            self.far[0].start()

        @pl.when(jnp.logical_not(self.links.in_middle))
        def _():
            self.far[1].start()

    def pass_middle(self, *ks):
        @pl.when(self.links.in_middle)
        def _():
            for k in ks:
                if k:
                    self.relayed[k].wait_recv()
                    self.relayed[k].start()
                else:
                    self.near.wait_recv()

    def pass_end(self, *ks):
        @pl.when(jnp.logical_not(self.links.in_middle))
        def _():
            for k in ks:
                if k:
                    self.relayed[k].wait_recv()
                else:
                    self.near.wait_recv()

    def sent(self):
        for copy in (self.own_y, self.near, self.far[0]):
            copy.wait_send()

        @pl.when(self.links.in_middle)
        def _():
            for copy in self.relayed[1:]:
                copy.wait_send()


class GroupSum:
    def __init__(self, mover, links, partial, at, beside, across):
        self.partial, self.at, self.links = partial, at, links
        self.from_core, self.from_x = beside, across
        diagonal = flip_low(links.x)
        self.far = mover(partial.at[at(diagonal)], beside.at[1], links.to_core)
        self.near = mover(partial.at[at(links.core)], beside.at[0], links.to_core)
        self.over = mover(partial.at[at(links.x)], across, links.to_x)

    def start(self):
        self.far.start()
        self.near.start()

    def keep(self):
        self.near.wait_recv()
        pair = self.partial[self.at(self.links.s)].astype(f32) + self.from_core[0].astype(f32)
        self.from_core[0] = pair.astype(bf16)

    def finish_kept(self):
        self.over.wait_recv()
        return self.from_core[0].astype(f32) + self.from_x[...].astype(f32)

    def middle(self):
        self.far.wait_recv()
        place = self.at(self.links.x)
        total = self.partial[place].astype(f32) + self.from_core[1].astype(f32)
        self.partial[place] = total.astype(bf16)
        self.over.start()

    def finish(self):
        self.near.wait_recv()
        pair = self.partial[self.at(self.links.s)].astype(f32) + self.from_core[0].astype(f32)
        self.over.wait_recv()
        return pair + self.from_x[...].astype(f32)

    def sent(self):
        for copy in (self.far, self.near, self.over):
            copy.wait_send()


class BlockSum:
    def __init__(self, mover, links, partial, from_core, from_x, summed, start, half):
        core = links.s % 2

        def half_at(i):
            return (pl.ds(pl.multiple_of(start + i * half, half), half), slice(None))

        self.partial, self.summed, self.mine = partial, summed, half_at(core)
        self.from_core, self.from_x = from_core, from_x
        self.beside = mover(partial.at[half_at(1 - core)], from_core, links.to_core)
        self.over = mover(partial.at[self.mine], from_x, links.to_x)
        self.back = mover(summed.at[self.mine], summed.at[self.mine], links.to_core)

    def start(self):
        self.beside.start()

    def middle(self):
        self.beside.wait_recv()
        pair = self.partial[self.mine].astype(f32) + self.from_core[...].astype(f32)
        self.partial[self.mine] = pair.astype(bf16)
        self.over.start()

    def total(self):
        self.over.wait_recv()
        return self.partial[self.mine].astype(f32) + self.from_x[...].astype(f32)

    def share(self, value):
        self.summed[self.mine] = value.astype(bf16)
        self.back.start()

    def finish(self):
        self.back.wait_recv()

    def sent(self):
        for copy in (self.beside, self.over, self.back):
            copy.wait_send()


class LineSum:
    def __init__(self, mover, links, grads, places, from_z):
        self.links, self.grads, self.places, self.from_z = links, grads, places, from_z
        sends, slots = [mover.send_slot() for _ in range(3)], [mover.recv_slot() for _ in range(4)]
        blocks = [grads.at[place] for place in places]
        self.to_near = [
            mover.copy(blocks[k], from_z.at[k], links.to_z[0], sends[k], slots[k]) for k in range(3)
        ]
        self.onward = [None] + [
            mover.copy(blocks[k], from_z.at[3], device, sends[k], slots[3])
            for k, device in ((1, links.to_far), (2, links.to_far_end))
        ]

    def send_z(self, k):
        if k == 0:
            self.to_near[0].start()
        else:

            @pl.when(jnp.logical_not(self.links.in_middle))
            def _():
                self.to_near[k].start()

    def combine(self, k):
        @pl.when(self.links.in_middle)
        def _():
            self.to_near[k].wait_recv()
            total = self.grads[self.places[k]].astype(f32) + self.from_z[k].astype(f32)
            self.grads[self.places[k]] = total.astype(bf16)
            self.onward[k].start()

    def arrived_z(self):
        self.to_near[0].wait_recv()
        near = self.from_z[0].astype(f32)
        self.onward[1].wait_recv()
        return near + self.from_z[3].astype(f32)

    def sent(self):
        for copy in self.to_near:
            copy.wait_send()


class WeightSum(LineSum):
    def __init__(self, mover, links, grads, at, from_y, from_z):
        others = [links.over_z[0], links.far_middle, links.far_end]
        super().__init__(mover, links, grads, [at(i) for i in others], from_z)
        self.own, self.from_y = at(links.d), from_y
        self.over_y = [
            mover(grads.at[at(flip_low(i))], from_y.at[k], links.to_y)
            for k, i in enumerate([links.d, *others])
        ]

    def start(self):
        for k in (2, 3, 1, 0):
            self.over_y[k].start()

    def forward(self, *order):
        for k in order:
            self.over_y[k + 1].wait_recv()
            place = self.places[k]
            total = self.grads[place].astype(f32) + self.from_y[k + 1].astype(f32)
            self.grads[place] = total.astype(bf16)
            self.send_z(k)

    def finish(self):
        self.over_y[0].wait_recv()
        total = self.grads[self.own].astype(f32) + self.from_y[0].astype(f32)
        return total + self.arrived_z()

    def sent(self):
        super().sent()
        for copy in self.over_y:
            copy.wait_send()


class PairSum(LineSum):
    def __init__(self, mover, links, grads, at, pair, from_y, from_z):
        super().__init__(mover, links, grads, [pair(i) for i in links.z_rest], from_z)
        self.own_pair, self.own, self.from_y = pair(links.z), at(links.d), from_y
        self.over_y = mover(grads.at[at(links.over_y)], from_y, links.to_y)

    def start(self):
        for k in (1, 2, 0):
            self.send_z(k)

    def middle(self):
        total = self.grads[self.own_pair].astype(f32) + self.arrived_z()
        self.grads[self.own_pair] = total.astype(bf16)
        self.over_y.start()

    def finish(self):
        self.over_y.wait_recv()
        return self.grads[self.own].astype(f32) + self.from_y[...].astype(f32)

    def sent(self):
        super().sent()
        self.over_y.wait_send()


class SmallSum:
    def __init__(self, mover, links, value, arrived):
        self.value, self.arrived = value, arrived
        partners = [links.to_core, links.to_x, links.to_z[0], links.to_z[1], links.to_y]
        self.copies = [mover(value.at[k], arrived.at[k], to) for k, to in enumerate(partners)]

    def start(self):
        self.copies[0].start()

    def step(self, k):
        self.copies[k].wait_recv()
        self.value[k + 1] = self.value[k] + self.arrived[k]
        if k + 1 < len(self.copies):
            self.copies[k + 1].start()

    def sent(self):
        for copy in self.copies:
            copy.wait_send()


LAYER_COPIES = 192


def layer(
    head_dim,
    length,
    tokens,
    state,
    cot,
    state_cot,
    w_qkv,
    w_out,
    w_sqkv,
    w_sout,
    w_up,
    w_down,
    buckets,
    rel_table,
    gains,
    shifts,
    gate_bias,
    output,
    next_state,
    grad_tokens,
    grad_state,
    grad_qkv,
    grad_out,
    grad_sqkv,
    grad_sout,
    grad_up,
    grad_down,
    grad_rel,
    grad_norm,
    send_sem,
    recv_sem,
    local_sem,
    slab,
    qkv_nat,
    sqkv_nat,
    out_nat,
    sout_nat,
    up_nat,
    down_nat,
    tok_all,
    cot_all,
    state_all,
    mixed,
    read_all,
    hid,
    first,
    qkv,
    second,
    sqkv,
    back_read,
    back_sqkv,
    own_sum,
    key_sum,
    res_own,
    hat_half,
    inverse_half,
    tb,
    band,
    out_rows,
    state_grads,
    down_grads,
    y_state,
    y_down,
    y_up,
    y_out,
    y_sout,
    z_state,
    z_down,
    z_up,
    z_out,
    z_sout,
    beside_rows,
    across_rows,
    beside_ffn,
    across_ffn,
    small,
    small_in,
    distance,
    landed,
    credit,
    by_bucket,
):
    rows, width = tokens.shape
    state_rows = state.shape[0]
    heads, _, span = tb.shape
    lanes = heads * head_dim
    depth = w_qkv.shape[0]
    inner_width = up_nat.shape[1]
    all_states = 4 * state_rows
    group_rows = 4 * rows
    scale = head_dim ** (-0.5)
    links = Links()
    s, d = links.s, links.d
    mover = Mover(send_sem, recv_sem)
    back_qkv, back_second, back_input = sqkv_nat, out_nat, sout_nat
    ffn_partial, back_first, back_branch = up_nat, down_nat, cot_all
    slope, up_grads = state_all, state_all
    back_state, ship = down_grads, slab
    hidden, token_grads = hid, hid

    def block(i, size):
        if isinstance(i, int):
            return slice(i * size, (i + 1) * size)
        return pl.ds(pl.multiple_of(i * size, size), size)

    def own_rows(size):
        return lambda i: (block(i, size), slice(None))

    def own_lanes(size):
        return lambda i: (slice(None), block(i, size))

    def cot_rows(i):
        if isinstance(i, int):
            start = all_states + i * state_rows
            return (slice(start, start + state_rows), slice(None))
        return (pl.ds(pl.multiple_of(all_states + i * state_rows, state_rows), state_rows), slice(None))

    own_columns = block(s, lanes)

    def own_out(i):
        return (block(i, depth), own_columns)

    def pair_out(i):
        return (block(i, 2 * depth), own_columns)

    def pair_last(i):
        return (block(i, 2 * depth), slice(3 * lanes, 4 * lanes))

    def last_lanes(i):
        return (block(i, depth), slice(3 * lanes, 4 * lanes))

    def first_lanes(i):
        return (block(i, depth), slice(0, 3 * lanes))

    to_slab = []
    for k, shard in enumerate((w_qkv, w_sqkv)):
        core_slot = 1 - links.core % 2 + links.core // 2
        x_slot = 2 - 2 * (links.x // 2)
        to_slab.append(
            (
                mover(
                    shard.at[:, block(2 - 2 * (s % 2), lanes)],
                    slab.at[k, :, block(x_slot, lanes)],
                    links.to_x,
                ),
                mover(
                    shard.at[:, lanes : 2 * lanes],
                    slab.at[k, :, block(core_slot, lanes)],
                    links.to_core,
                ),
            )
        )
    get_tokens = GroupGather(mover, links, tok_all, own_rows(rows), tokens)
    get_state = GroupGather(mover, links, state_all, own_rows(state_rows), state)
    get_scot = GroupGather(mover, links, state_all, cot_rows, state_cot)
    get_cot = GroupGather(mover, links, cot_all, own_rows(rows), cot)
    dp_sout = PairGather(mover, links, sout_nat, own_out, pair_out, w_sout)
    dp_out = PairGather(mover, links, out_nat, own_out, pair_out, w_out)
    dp_qkv = WeightGather(mover, links, qkv_nat, own_rows(depth), slab.at[0])
    dp_sqkv = WeightGather(mover, links, sqkv_nat, own_rows(depth), slab.at[1])
    dp_up = WeightGather(mover, links, up_nat, own_rows(depth), w_up)
    dp_down = WeightGather(mover, links, down_nat, own_lanes(depth), w_down)
    get_sout = GroupGather(mover, links, sout_nat, own_lanes(lanes))
    get_out = [
        GroupGather(mover, links, out_nat, lambda i, at=at: (at, block(i, lanes)))
        for at in (slice(0, width // 2), slice(width // 2, width))
    ]
    get_mixed = GroupGather(mover, links, mixed, own_lanes(lanes))
    get_read = GroupGather(mover, links, read_all, own_lanes(lanes))
    sum_state = GroupSum(
        mover,
        links,
        back_state,
        own_rows(state_rows),
        beside_ffn.at[:, 0:state_rows, :],
        across_ffn.at[0:state_rows, :],
    )
    half = rows // 2
    block_sums = [
        BlockSum(
            mover,
            links,
            back_second,
            beside_rows.at[i // 2, i % 2 * half : (i % 2 + 1) * half, :],
            across_rows.at[i // 2, i % 2 * half : (i % 2 + 1) * half, :],
            back_branch,
            i * rows,
            half,
        )
        for i in range(4)
    ]
    sum_ffn = GroupSum(mover, links, ffn_partial, own_rows(rows), beside_ffn, across_ffn)
    sum_first = GroupSum(
        mover, links, back_first, own_rows(rows), beside_rows, across_rows.at[0]
    )
    dp_state = WeightSum(mover, links, state_grads, first_lanes, y_state, z_state)
    dp_grad_sout = PairSum(mover, links, state_grads, last_lanes, pair_last, y_sout, z_sout)
    dp_grad_down = WeightSum(mover, links, down_grads, own_lanes(depth), y_down, z_down)
    up_cut = inner_width * 3 // 4
    dp_grad_up, dp_grad_up_last = [
        WeightSum(
            mover,
            links,
            up_grads,
            lambda i, at=at: (block(i, depth), at),
            y_up.at[:, :, at],
            z_up.at[:, :, at],
        )
        for at in (slice(0, up_cut), slice(up_cut, inner_width))
    ]
    dp_grad_out = PairSum(mover, links, token_grads, last_lanes, pair_last, y_out, z_out)
    dp_grad_qkv = WeightSum(mover, links, token_grads, first_lanes, y_state, z_state)
    sum_small = SmallSum(mover, links, small, small_in)
    to_owner = [
        (
            mover(
                ship.at[k, :, block(2 - 2 * (s // 2), lanes)],
                landed.at[k, :, block(2 - 2 * (s % 2), lanes)],
                links.to_x,
            ),
            mover(
                ship.at[k, :, block(1 - s % 2 + s // 2, lanes)],
                landed.at[k, :, lanes : 2 * lanes],
                links.to_core,
            ),
        )
        for k in range(2)
    ]
    assert max(mover.sends, mover.recvs) <= LAYER_COPIES

    local = []
    for source, target in (
        (w_qkv.at[:, block(2 * (s % 2), lanes)], slab.at[0, :, block((s + 1) // 2, lanes)]),
        (w_sqkv.at[:, block(2 * (s % 2), lanes)], slab.at[1, :, block((s + 1) // 2, lanes)]),
        (tokens, tok_all.at[block(s, rows), :]),
        (state, state_all.at[block(s, state_rows), :]),
        (state_cot, state_all.at[cot_rows(s)]),
        (cot, cot_all.at[block(s, rows), :]),
        (w_up, up_nat.at[block(d, depth), :]),
        (w_down, down_nat.at[:, block(d, depth)]),
        (w_out, out_nat.at[block(d, depth), own_columns]),
        (w_sout, sout_nat.at[block(d, depth), own_columns]),
    ):
        local.append(pltpu.make_async_copy(source, target, local_sem.at[len(local)]))

    links.greet()
    for over_x, beside in to_slab:
        over_x.start()
        beside.start()
    dp_sout.start_y()
    dp_out.start_y()
    get_tokens.start()
    for copy in local:
        copy.start()
    small[0] = jnp.zeros(small.shape[1:], f32)
    key_sum[...] = jnp.zeros_like(key_sum)
    own_sum[...] = jnp.zeros_like(own_sum)
    for k, gather in enumerate((dp_qkv, dp_sqkv)):
        for copy in (*to_slab[k],):
            copy.wait_recv()
        local[k].wait()
        if k == 0:
            gather.start_z()
            gather.start_y()
    get_state.start()
    get_scot.start()
    get_cot.start()
    qkv_nat[block(d, depth), :] = slab[0]
    sqkv_nat[block(d, depth), :] = slab[1]
    for copy in local[2:]:
        copy.wait()

    def token_norm(i):
        at = block(i, rows)
        hat, _ = normalized(tok_all[at, :].astype(f32))
        first[at, :] = (hat * gains[0:1, :] + shifts[0:1, :]).astype(bf16)

    token_norm(s)
    onehot = jnp.where(
        lax.broadcasted_iota(jnp.int32, (rel_table.shape[1], buckets.shape[1]), 0) == buckets[...],
        1.0,
        0.0,
    )
    turned = jnp.where(
        lax.broadcasted_iota(jnp.int32, (span, buckets.shape[1]), 0)
        + lax.broadcasted_iota(jnp.int32, (span, buckets.shape[1]), 1)
        == buckets.shape[1],
        1.0,
        0.0,
    )
    by_bucket[...] = dot_rt(turned.astype(bf16), onehot.astype(bf16))
    bias = lax.dot_general(
        rel_table[...],
        by_bucket[...],
        (((1,), (1,)), ((), ())),
        precision=lax.Precision.HIGHEST,
        preferred_element_type=f32,
    )
    column = lax.broadcasted_iota(jnp.int32, bias.shape, 1)
    distance[...] = jnp.where((column > 0) & (column <= span - rows), bias, masked_value)
    bias_blocks(tb, [distance[pl.ds(s * heads + h, 1), :] for h in range(heads)])
    distance[...] = jnp.zeros_like(distance)
    get_tokens.beside.wait_recv()
    token_norm(links.core)
    dp_qkv.pass_on(0)
    dp_sout.start_z()
    dp_qkv.pass_middle(1)
    dp_sqkv.start_z()
    dp_qkv.pass_middle(2)
    dp_qkv.pass_end(1)
    dp_sqkv.start_y()
    get_tokens.forward()
    token_norm(links.x)
    dp_qkv.pass_end(2)
    dp_up.start_y()
    dp_sout.pass_middle(0, 1, 2)
    dp_sout.pass_end(0, 1, 2)
    get_sout.start()
    dp_out.start_z()
    dp_up.start_z()
    get_tokens.passed.wait_recv()
    token_norm(flip_low(links.x))
    get_state.forward()
    dp_sqkv.pass_on(0)
    dp_sqkv.pass_middle(1)
    dp_qkv.finish()
    get_scot.forward()

    def token_qkv(i):
        at = block(i, rows)
        qkv[at, :] = dot(first[at, :], qkv_nat[...]).astype(bf16)

    for i in range(4):
        token_qkv(i)
    for c in range(4):
        count = min(span, (c + 1) * rows)
        low, high = (c + 1) * rows - count, (c + 1) * rows
        last = c * rows if c == 3 else 0
        parts = []
        for h in range(heads):
            probs = window_probs(
                (0, length[0]),
                qkv[c * rows : high, head_cols(0, h, heads, head_dim)],
                qkv[low:high, head_cols(1, h, heads, head_dim)],
                tb[h],
                last,
                scale,
            )
            parts.append(
                dot(probs.astype(bf16), qkv[low:high, head_cols(2, h, heads, head_dim)])
            )
        mixed[c * rows : high, own_columns] = jnp.concatenate(parts, axis=1).astype(bf16)
        if c == 0:
            dp_sqkv.pass_middle(2)
        elif c == 1:
            dp_sqkv.pass_end(1)
            dp_out.pass_middle(0, 1)
        elif c == 2:
            dp_sqkv.pass_end(2)
            dp_down.start_z()
            dp_down.start_y()
    get_mixed.start()
    dp_out.pass_middle(2)
    dp_out.pass_end(0)
    get_cot.forward()

    get_state.finish()

    def state_norms(i):
        at = block(i, state_rows)
        hat, _ = normalized(state_all[at, :].astype(f32))
        hid[at, :] = (hat * gains[2:3, :] + shifts[2:3, :]).astype(bf16)

    for i in range(4):
        state_norms(i)
    dp_sqkv.finish()
    state_norm, back_update = slice(0, all_states), slice(all_states, 2 * all_states)
    sqkv[...] = dot(hid[state_norm, :], sqkv_nat[...]).astype(bf16)
    dp_up.pass_middle(0, 1)
    dp_out.pass_end(1, 2)
    get_out[0].start()
    dp_up.pass_end(0)

    def state_read(i):
        at = block(i, state_rows)
        parts = []
        for h in range(heads):
            own, token = state_probs(
                (0, length[0]),
                sqkv[at, head_cols(0, h, heads, head_dim)],
                sqkv[:, head_cols(1, h, heads, head_dim)],
                qkv[:, head_cols(1, h, heads, head_dim)],
                scale,
            )
            parts.append(
                dot(own.astype(bf16), sqkv[:, head_cols(2, h, heads, head_dim)])
                + dot(token.astype(bf16), qkv[:, head_cols(2, h, heads, head_dim)])
            )
        read_all[at, own_columns] = jnp.concatenate(parts, axis=1).astype(bf16)

    for i in range(4):
        state_read(i)
        if i == 1:
            dp_up.pass_middle(2)
            dp_up.pass_end(1)
    get_read.start()
    get_out[1].start()
    dp_down.pass_middle(0, 1)
    dp_up.pass_end(2)
    get_sout.forward()

    gate = jax.nn.sigmoid(gate_bias[...])
    get_scot.finish()

    def updates(i):
        hid[cot_rows(i)] = ((1.0 - gate) * state_all[cot_rows(i)].astype(f32)).astype(bf16)

    for i in range(4):
        updates(i)
    get_sout.finish()
    back_read[...] = dot_rt(hid[back_update, :], sout_nat[block(s, lanes), :]).astype(bf16)

    def state_back(h):
        key_at, value_at = head_cols(1, h, heads, head_dim), head_cols(2, h, heads, head_dim)
        query_at, read_at = head_cols(0, h, heads, head_dim), head_cols(0, h, heads, head_dim)

        def one(i):
            at = block(i, state_rows)
            query, back = sqkv[at, query_at], back_read[at, read_at]
            own, token = state_probs(
                (0, length[0]), query, sqkv[:, key_at], qkv[:, key_at], scale
            )
            back_own = dot_rt(back, sqkv[:, value_at])
            back_token = dot_rt(back, qkv[:, value_at])
            row_dot = jnp.sum(own * back_own, axis=-1, keepdims=True) + jnp.sum(
                token * back_token, axis=-1, keepdims=True
            )
            own_raw = (own * (back_own - row_dot) * scale).astype(bf16)
            token_raw = (token * (back_token - row_dot) * scale).astype(bf16)
            back_sqkv[at, query_at] = (
                dot(own_raw, sqkv[:, key_at]) + dot(token_raw, qkv[:, key_at])
            ).astype(bf16)
            key_to = slice(key_at.start - lanes, key_at.stop - lanes)
            value_to = slice(value_at.start - lanes, value_at.stop - lanes)
            own_sum[:, key_to] += dot_lt(own_raw, query)
            own_sum[:, value_to] += dot_lt(own.astype(bf16), back)
            key_sum[:, key_to] += dot_lt(token_raw, query)
            key_sum[:, value_to] += dot_lt(token.astype(bf16), back)

        for i in range(4):
            one(i)

    for h in range(heads):
        state_back(h)
        if h == 0:
            dp_down.pass_middle(2)
            dp_down.pass_end(0, 1)
            get_mixed.forward()
            get_out[0].forward()
    back_sqkv[:, lanes:] = own_sum[...].astype(bf16)

    back_state[0:all_states, :] = dot_rt(back_sqkv[...], sqkv_nat[...]).astype(bf16)
    sum_state.start()
    dp_down.pass_end(2)
    get_read.forward()

    for start in range(0, width, 256):
        at = slice(start, start + 256)
        state_grads[at, 0 : 3 * lanes] = dot_lt(hid[state_norm, at], back_sqkv[...]).astype(bf16)
    sum_state.middle()
    sum_state.keep()
    get_out[1].forward()

    get_read.finish()
    update = dot(read_all[block(s, state_rows), :], sout_nat[...])
    held = state_all[block(s, state_rows), :].astype(f32)
    own_cot = state_all[cot_rows(s)].astype(f32)
    next_state[...] = (gate * held + (1.0 - gate) * update).astype(bf16)
    small[0, 6:7, :] = jnp.sum(own_cot * (held - update), axis=0, keepdims=True) * (
        gate * (1.0 - gate)
    )
    state_grads[:, 3 * lanes : 4 * lanes] = dot_lt(
        read_all[...], hid[back_update, own_columns]
    ).astype(bf16)

    get_read.sent()
    own_state, own_scot = slice(0, state_rows), slice(state_rows, 2 * state_rows)
    again = [
        pltpu.make_async_copy(source, read_all.at[place, :], local_sem.at[k])
        for k, (source, place) in enumerate(((state, own_state), (state_cot, own_scot)))
    ]
    for copy in again:
        copy.start()
    dp_grad_sout.start()

    get_mixed.finish()
    for gather in get_out:
        gather.finish()
    dp_up.finish()
    get_cot.finish()
    for gather in (get_state, get_scot, get_sout, dp_sout, *get_out, dp_out, dp_sqkv):
        gather.sent()
    out_rows[...] = out_nat[block(s, lanes), :]
    dp_state.start()

    def ffn_rows(i):
        at = block(i, rows)
        total = tok_all[at, :].astype(f32) + dot(mixed[at, :], out_nat[...])

        @pl.when(i == s)
        def _():
            res_own[...] = total

        hat, inverse = normalized(total)
        normed = (hat * gains[1:2, :] + shifts[1:2, :]).astype(bf16)
        second[at, :] = normed
        own_half = block(i, half)
        upper = s % 2 == 0
        hat_half[own_half, :] = jnp.where(upper, hat[:half], hat[half:]).astype(bf16)
        inverse_half[own_half, :] = jnp.broadcast_to(
            jnp.where(upper, inverse[:half], inverse[half:]), (half, 128)
        )
        inner = dot(normed, up_nat[...])
        root = 0.7978845608028654
        square = inner * inner
        bend = jnp.tanh(inner * (root + (root * 0.044715) * square))
        open_part = 0.5 + 0.5 * bend
        hidden[at, :] = (inner * open_part).astype(bf16)
        slope[at, :] = (
            open_part
            + (inner - inner * bend * bend) * (0.5 * root + (1.5 * root * 0.044715) * square)
        ).astype(bf16)

    for i in range(4):
        ffn_rows(i)

    sum_state.sent()

    def down_columns(i):
        at = block(i, 256)
        down_grads[:, at] = dot_lt(hidden[...], cot_all[:, at]).astype(bf16)

    for i in range(width // 256):
        down_columns(i)
    dp_grad_down.start()
    get_cot.sent()
    for copy in again:
        copy.wait()
    hat_state, inverse_state = normalized(read_all[own_state, :].astype(f32))
    back_own_state = sum_state.finish_kept()
    small[0, 2:3, :] = jnp.sum(back_own_state * hat_state, axis=0, keepdims=True)
    small[0, 5:6, :] = jnp.sum(back_own_state, axis=0, keepdims=True)
    grad_state[...] = (
        gate * read_all[own_scot, :].astype(f32)
        + normed_back(back_own_state, hat_state, inverse_state, gains[2:3, :])
    ).astype(bf16)
    dp_down.finish()

    def ffn_back_rows(i):
        at = block(i, rows)
        inner = (dot_rt(cot_all[at, :], down_nat[...]) * slope[at, :].astype(f32)).astype(bf16)
        back_input[at, :] = inner
        back_second[at, :] = dot_rt(inner, up_nat[...]).astype(bf16)
        block_sums[i].start()

    def up_columns(i):
        at = block(i, 256)
        up_grads[at, :] = dot_lt(second[:, at], back_input[...]).astype(bf16)

    def ffn_out_rows(i):
        at = block(i, rows)
        ffn_partial[at, :] = dot(hidden[at, :], down_nat[...]).astype(bf16)

    def norm_rows(i):
        back = block_sums[i].total()
        at = block(i, half)
        hat = hat_half[at, :].astype(f32)
        small[0, 1:2, :] += 0.5 * jnp.sum(back * hat, axis=0, keepdims=True)
        small[0, 4:5, :] += 0.5 * jnp.sum(back, axis=0, keepdims=True)
        kept_cot = cot_all[block_sums[i].mine].astype(f32)
        block_sums[i].share(
            kept_cot + normed_back(back, hat, inverse_half[at, 0:1], gains[1:2, :])
        )

    def window_back(c):
        block_sums[c].finish()
        count = min(span, (c + 1) * rows)
        low, high = (c + 1) * rows - count, (c + 1) * rows
        last = c * rows if c == 3 else 0
        at = block(c, rows)
        back_mixed = dot_rt(back_branch[at, :], out_rows[...]).astype(bf16)
        for h in range(heads):
            key_at, value_at = head_cols(1, h, heads, head_dim), head_cols(2, h, heads, head_dim)
            query_at = head_cols(0, h, heads, head_dim)
            query, back = qkv[at, query_at], back_mixed[:, query_at]
            keys = qkv[low:high, key_at]
            probs = window_probs((0, length[0]), query, keys, tb[h], last, scale)
            back_probs = dot_rt(back, qkv[low:high, value_at])
            row_dot = jnp.sum(probs * back_probs, axis=-1, keepdims=True)
            back_scores = probs * (back_probs - row_dot)
            if c == 0:
                band[h] = jnp.zeros(band.shape[1:], f32)
            band[h, :, span - count :] += back_scores
            raw = (back_scores * scale).astype(bf16)
            back_qkv[at, query_at] = dot(raw, keys).astype(bf16)
            key_to = slice(key_at.start - lanes, key_at.stop - lanes)
            value_to = slice(value_at.start - lanes, value_at.stop - lanes)
            key_sum[low:high, key_to] += dot_lt(raw, query)
            key_sum[low:high, value_to] += dot_lt(probs.astype(bf16), back)

    ffn_back_rows(0)
    ffn_back_rows(1)
    block_sums[0].middle()
    ffn_back_rows(2)
    block_sums[1].middle()
    ffn_back_rows(3)
    block_sums[2].middle()
    for k in (1, 2):
        dp_grad_sout.combine(k)
    block_sums[3].middle()
    dp_state.forward(1)
    for i in range(width // 256):
        up_columns(i)
    dp_grad_sout.middle()
    dp_grad_up.start()
    dp_up.sent()
    dp_state.forward(2)
    for i in range(4):
        ffn_out_rows(i)
    sum_ffn.start()
    dp_down.sent()
    norm_rows(0)
    dp_state.forward(0)
    norm_rows(1)
    window_back(0)
    dp_state.combine(1)
    dp_state.combine(2)
    sum_ffn.middle()
    norm_rows(2)
    window_back(1)
    dp_grad_down.forward(1)
    norm_rows(3)
    window_back(2)
    dp_grad_down.forward(2)
    state_total = dp_state.finish()
    for partner in (links.to_y, *links.to_z):
        pl.semaphore_signal(credit, inc=1, device_id=partner, device_id_type=pl.DeviceIdType.MESH)
    dp_qkv.sent()
    ship[1] = state_total.astype(bf16)
    grad_sqkv[:, block(2 * (s % 2), lanes)] = ship[1, :, block((s + 1) // 2, lanes)]
    for copy in to_owner[1]:
        copy.start()
    window_back(3)
    dp_grad_down.forward(0)
    back_qkv[:, lanes:] = key_sum[...].astype(bf16)
    small[0, 0:1, :] = jnp.zeros((1, width), f32)
    small[0, 3:4, :] = jnp.zeros((1, width), f32)

    def qkv_grads(i):
        at = block(i, 256)
        token_grads[at, 0 : 3 * lanes] = dot_lt(first[:, at], back_qkv[...]).astype(bf16)

    def first_partial(i):
        at = block(i, rows)
        back = dot_rt(back_qkv[at, :], qkv_nat[...])
        back_first[at, :] = back.astype(bf16)
        hat, _ = normalized(tok_all[at, :].astype(f32))
        small[0, 0:1, :] += jnp.sum(back * hat, axis=0, keepdims=True)
        small[0, 3:4, :] += jnp.sum(back, axis=0, keepdims=True)

    for i in range(width // 256):
        qkv_grads(i)
    pl.semaphore_wait(credit, 4)
    dp_grad_qkv.start()
    dp_grad_up_last.start()
    token_grads[:, 3 * lanes : 4 * lanes] = dot_lt(
        mixed[...], back_branch[:, own_columns]
    ).astype(bf16)
    dp_grad_out.start()
    dp_grad_down.combine(1)
    for h in range(heads):
        distance[pl.ds(s * heads + h, 1), :] = jnp.sum(by_distance(band[h]), axis=0, keepdims=True)
    small[0, 8:16, 0 : by_bucket.shape[1]] = lax.dot_general(
        distance[...],
        by_bucket[...],
        (((1,), (0,)), ((), ())),
        precision=lax.Precision.HIGHEST,
        preferred_element_type=f32,
    )
    for i in range(4):
        first_partial(i)
    sum_small.start()
    sum_first.start()
    dp_grad_down.combine(2)
    output[...] = (res_own[...] + sum_ffn.finish()).astype(bf16)
    sum_small.step(0)
    sum_first.middle()
    for k in (1, 2):
        dp_grad_out.combine(k)
    dp_grad_up.forward(1)
    grad_down[...] = dp_grad_down.finish().astype(bf16)
    sum_small.step(1)
    dp_grad_out.middle()
    dp_grad_up.forward(2)
    dp_grad_up.combine(1)
    dp_grad_up.forward(0)
    dp_grad_up.combine(2)
    hat_first, inverse_first = normalized(tok_all[block(s, rows), :].astype(f32))
    back_own_first = sum_first.finish()
    grad_tokens[...] = (
        back_branch[block(s, rows), :].astype(f32)
        + normed_back(back_own_first, hat_first, inverse_first, gains[0:1, :])
    ).astype(bf16)
    sum_small.step(2)
    dp_grad_qkv.forward(1)
    grad_sout[...] = dp_grad_sout.finish().astype(bf16)
    dp_grad_qkv.forward(2)
    grad_up[:, 0:up_cut] = dp_grad_up.finish().astype(bf16)
    dp_grad_qkv.combine(1)
    dp_grad_qkv.forward(0)
    sum_small.step(3)
    dp_grad_up_last.forward(1)
    dp_grad_qkv.combine(2)
    dp_grad_up_last.forward(2)
    dp_grad_up_last.forward(0)
    dp_grad_up_last.combine(1)
    dp_grad_up_last.combine(2)
    grad_out[...] = dp_grad_out.finish().astype(bf16)
    ship[0] = dp_grad_qkv.finish().astype(bf16)
    for copy in to_owner[0]:
        copy.start()
    grad_qkv[:, block(2 * (s % 2), lanes)] = ship[0, :, block((s + 1) // 2, lanes)]
    sum_small.step(4)
    grad_norm[...] = small[5, 0:8, :]
    grad_rel[...] = small[5, 8:16, 0:128]
    grad_up[:, up_cut:] = dp_grad_up_last.finish().astype(bf16)
    for k, grads in ((1, grad_sqkv), (0, grad_qkv)):
        for copy in to_owner[k]:
            copy.wait_recv()
        grads[:, lanes : 2 * lanes] = landed[k, :, lanes : 2 * lanes]
        x_at = block(2 - 2 * (s % 2), lanes)
        grads[:, x_at] = landed[k, :, x_at]
    for over_x, beside in (*to_slab, *to_owner):
        over_x.wait_send()
        beside.wait_send()
    for used in (
        get_tokens,
        get_mixed,
        *block_sums,
        sum_ffn,
        sum_first,
        dp_state,
        dp_grad_sout,
        dp_grad_down,
        dp_grad_up,
        dp_grad_up_last,
        dp_grad_out,
        dp_grad_qkv,
        sum_small,
    ):
        used.sent()


def settle(
    output,
    next_state,
    grad_tokens,
    grad_state,
    grad_qkv,
    grad_out,
    grad_sqkv,
    grad_sout,
    grad_up,
    grad_down,
    grad_rel,
    grad_norm,
    *results,
):
    for result, value in zip(results, (output, next_state, grad_tokens, grad_state)):
        if len(result.shape) == 3:
            result[0] = value[...]
        else:
            result[...] = value[...]
    grads = (grad_qkv, grad_out, grad_sqkv, grad_sout, grad_up, grad_down)
    for result, value in zip(results[4:], grads):
        result[...] = value[...].astype(f32)
    rel, gain, shift, gate = results[10:]
    rel[...] = grad_rel[:, 0 : rel.shape[1]]
    gain[...] = grad_norm[0:3, :]
    shift[...] = grad_norm[3:6, :]
    gate[...] = grad_norm[6, :]


def norm_back(values, back, gain):
    hat, inverse = normalized(values)
    return normed_back(back, hat, inverse, gain)


def per_device(
    tokens,
    state_in,
    cotangent,
    state_cotangent,
    seq_len,
    bucket_table,
    w_qkv,
    w_out,
    w_sqkv,
    w_sout,
    w_up,
    w_down,
    rel_table,
    norm_gain,
    norm_shift,
    gate_bias,
):
    rows, width = tokens.shape
    bucket_count, head_count = rel_table.shape
    window = bucket_table.shape[0]
    state_rows = state_in.shape[1]
    places = lax.axis_size("state")
    assert places == len(PLACES)
    dp_count = lax.axis_size("dp")
    here, dp_here = lax.axis_index("state"), lax.axis_index("dp")
    head_dim = width // head_count
    heads = head_count // places
    lanes = heads * head_dim
    span = window + rows
    group_rows = rows * places
    all_states = state_rows * places
    inner_width = w_up.shape[1]
    hops = dp_count == len(DP_PLACES)
    blocks = dp_count if hops else 1

    def swap(value, axis, bit):
        count = lax.axis_size(axis)
        return lax.ppermute(value, axis, [(i, i ^ bit) for i in range(count)])

    def from_group(value):
        pair = jnp.stack([value, swap(value, "state", 2)])
        return jnp.concatenate([pair, swap(pair, "state", 1)], axis=0)

    def list_from_group(value):
        across = swap(value, "state", 2)
        return [value, across, swap(value, "state", 1), swap(across, "state", 1)]

    def sum_to_owner(partial):
        half = partial.shape[0] // 2
        pair = partial[:half].astype(f32) + swap(partial[half:], "state", 1).astype(f32)
        return pair[0] + swap(pair[1].astype(bf16), "state", 2).astype(f32)

    def from_dp(block, axis):
        if not hops:
            return lax.all_gather(block, "dp", axis=axis, tiled=True)[None]
        gathered = block[None]
        for bit in DP_STEPS:
            gathered = jnp.concatenate([gathered, swap(gathered, "dp", bit)], axis=0)
        return gathered

    def sum_over_dp(partial, axis):
        if not hops:
            return lax.psum_scatter(partial[0], "dp", scatter_dimension=axis, tiled=True).astype(f32)
        for bit in reversed(DP_STEPS):
            half = partial.shape[0] // 2
            arrived = swap(partial[half:], "dp", bit)
            total = partial[:half].astype(f32) + arrived.astype(f32)
            partial = total.astype(bf16)
        return total[0]

    def sum_over_all(vector):
        if not hops:
            return lax.psum(vector, ("dp", "state"))
        for axis, bit in (("state", 1), ("state", 2), ("dp", 1), ("dp", 2), ("dp", 4)):
            vector = vector + swap(vector, axis, bit)
        return vector

    even = here % 2 == 0

    def pick(*by_place):
        value = by_place[-1]
        for i in reversed(range(places - 1)):
            value = jnp.where(here == i, by_place[i], value)
        return value

    def to_heads(shard):
        left, middle, right = (shard[:, i * lanes : (i + 1) * lanes] for i in range(3))
        own = jnp.where(even, left, right)
        across = swap(jnp.where(even, right, left), "state", 2)
        beside = swap(middle, "state", 1)
        query = pick(own, beside, across, across)
        keys = pick(beside, own, own, beside)
        values = pick(across, across, beside, own)
        return jnp.concatenate([query, keys, values], axis=1)

    def from_heads(grads):
        query, keys, values = (grads[:, i * lanes : (i + 1) * lanes] for i in range(3))
        own = pick(query, keys, keys, values)
        beside = swap(pick(keys, query, values, keys), "state", 1)
        across = swap(pick(values, values, query, query), "state", 2)
        return jnp.concatenate(
            [jnp.where(even, own, across), beside, jnp.where(even, across, own)], axis=1
        )

    if hops:
        block_list = dp_here ^ jnp.array(DP_PLACES, jnp.int32)
        position_list = jnp.array(
            [DP_PLACES.index(i) for i in range(dp_count)], jnp.int32
        )[dp_here ^ jnp.arange(dp_count)]
    else:
        block_list = position_list = jnp.zeros((1,), jnp.int32)
    scal = jnp.concatenate(
        [here[None].astype(jnp.int32), seq_len.astype(jnp.int32), block_list, position_list]
    ).astype(jnp.int32)

    gains = [norm_gain[i : i + 1] for i in range(3)]
    shifts = [norm_shift[i : i + 1] for i in range(3)]

    depth = w_qkv.shape[0]
    if hops:
        whole = pl.BlockSpec(memory_space=pltpu.VMEM)
        anywhere = pl.BlockSpec(memory_space=pl.ANY)
        vmem = lambda shape, kind=bf16: pltpu.VMEM(shape, kind)
        square = vmem((width, width))
        summed = pl.pallas_call(
            functools.partial(layer, head_dim),
            out_shape=[
                out((rows, width)),
                out((state_rows, width)),
                out((rows, width)),
                out((state_rows, width)),
                out((depth, 3 * lanes)),
                out((depth, lanes)),
                out((depth, 3 * lanes)),
                out((depth, lanes)),
                out((depth, inner_width)),
                out((inner_width, depth)),
                out((head_count, 128), f32),
                out((8, width), f32),
            ],
            in_specs=[pl.BlockSpec(memory_space=pltpu.SMEM)] + [anywhere] * 10 + [whole] * 5,
            out_specs=[whole] * 12,
            scratch_shapes=[
                pltpu.SemaphoreType.DMA((LAYER_COPIES,)),
                pltpu.SemaphoreType.DMA((LAYER_COPIES,)),
                pltpu.SemaphoreType.DMA((16,)),
                vmem((2, depth, 3 * lanes)),
                vmem((width, 3 * lanes)),
                vmem((width, 3 * lanes)),
                square,
                square,
                vmem((width, inner_width)),
                vmem((inner_width, width)),
                vmem((group_rows, width)),
                vmem((group_rows, width)),
                vmem((2 * all_states, width)),
                vmem((group_rows, width)),
                vmem((all_states, width)),
                vmem((2 * all_states, width)),
                vmem((group_rows, width)),
                vmem((group_rows, 3 * lanes)),
                vmem((group_rows, width)),
                vmem((all_states, 3 * lanes)),
                vmem((all_states, lanes)),
                vmem((all_states, 3 * lanes)),
                vmem((all_states, 2 * lanes), f32),
                vmem((group_rows, 2 * lanes), f32),
                vmem((rows, width), f32),
                vmem((group_rows // 2, width)),
                vmem((group_rows // 2, 128), f32),
                vmem((heads, rows, span), f32),
                vmem((heads, rows, span), f32),
                vmem((lanes, width)),
                square,
                vmem((inner_width, width)),
                vmem((4, depth, 3 * lanes)),
                vmem((4, inner_width, depth)),
                vmem((4, depth, inner_width)),
                vmem((depth, lanes)),
                vmem((depth, lanes)),
                vmem((4, depth, 3 * lanes)),
                vmem((4, inner_width, depth)),
                vmem((4, depth, inner_width)),
                vmem((4, 2 * depth, lanes)),
                vmem((4, 2 * depth, lanes)),
                vmem((2, rows, width)),
                vmem((2, rows, width)),
                vmem((2, rows, width)),
                vmem((rows, width)),
                vmem((6, 16, width), f32),
                vmem((5, 16, width), f32),
                vmem((8, span), f32),
                vmem((2, depth, 3 * lanes)),
                pltpu.SemaphoreType.REGULAR,
                vmem((span, bucket_count), f32),
            ],
            compiler_params=pltpu.CompilerParams(
                collective_id=0, has_side_effects=True, vmem_limit_bytes=64 << 20
            ),
            name="layer",
        )(
            seq_len,
            tokens,
            state_in[0],
            cotangent,
            state_cotangent[0],
            w_qkv,
            w_out,
            w_sqkv,
            w_sout,
            w_up,
            w_down,
            bucket_table[None],
            rel_table.T,
            norm_gain,
            norm_shift,
            gate_bias[None],
        )
        results = pl.pallas_call(
            settle,
            out_shape=[
                out((rows, width)),
                out((1, state_rows, width)),
                out((rows, width)),
                out((1, state_rows, width)),
                out((depth, 3 * lanes), f32),
                out((depth, lanes), f32),
                out((depth, 3 * lanes), f32),
                out((depth, lanes), f32),
                out((depth, inner_width), f32),
                out((inner_width, depth), f32),
                out((head_count, bucket_count), f32),
                out((3, width), f32),
                out((3, width), f32),
                out((width,), f32),
            ],
            in_specs=[whole] * 12,
            out_specs=[whole] * 14,
            compiler_params=pltpu.CompilerParams(vmem_limit_bytes=60 << 20),
            name="settle",
        )(*summed)
        return (*results[:10], results[10].T, *results[11:])

    lookup = (bucket_table[:, None] == jnp.arange(bucket_count)[None, :]).astype(f32)
    own_table = lax.dynamic_slice_in_dim(rel_table, here * heads, heads, 1)
    bias_rows = jnp.dot(
        own_table.T, lookup.T, precision=lax.Precision.HIGHEST, preferred_element_type=f32
    )
    bias = jnp.concatenate(
        [
            jnp.full((heads, 1), masked_value, f32),
            bias_rows[:, ::-1],
            jnp.full((heads, span - window - 1), masked_value, f32),
        ],
        axis=1,
    )
    both = to_heads(jnp.concatenate([w_qkv, w_sqkv], axis=0))
    full_qkv = from_dp(both[:depth], 0)
    all_tokens = from_group(tokens)
    full_sqkv = from_dp(both[depth:], 0)
    all_state = from_group(state_in[0])
    all_cot = from_group(cotangent)
    all_state_cot = from_group(state_cotangent[0])
    outs_pair = from_dp(jnp.concatenate([w_out, w_sout], axis=1), 0)
    half = outs_pair.shape[2] // 2
    full_sout = list_from_group(outs_pair[:, :, half:])
    full_out = list_from_group(outs_pair[:, :, :half])
    full_up = from_dp(w_up, 0)
    full_down = from_dp(w_down, 1)

    first, qkv, mixed = call(
        functools.partial(token_forward, head_dim),
        "token_forward",
        [out((group_rows, width)), out((group_rows, 3 * lanes)), out((places, rows, lanes))],
        [pltpu.VMEM((width, 3 * lanes), bf16), pltpu.VMEM((heads, rows, span), f32)],
        2 * group_rows * width * 3 * lanes,
        group_rows * span * heads,
        scal,
        all_tokens,
        gains[0],
        shifts[0],
        full_qkv,
        bias,
    )
    mixed_parts = list_from_group(mixed)

    state_norm, sqkv, read = call(
        functools.partial(state_forward, head_dim),
        "state_forward",
        [
            out((all_states, width)),
            out((all_states, 3 * lanes)),
            out((places, state_rows, lanes)),
        ],
        [pltpu.VMEM((width, 3 * lanes), bf16)],
        2 * all_states * width * 3 * lanes,
        all_states * (all_states + group_rows) * heads,
        scal,
        all_state,
        gains[2],
        shifts[2],
        full_sqkv,
        qkv,
    )
    read_parts = list_from_group(read)

    next_state, grad_gate, grad_sout, token_back, grad_sqkv, back_state_norm, state_sums = call(
        functools.partial(state_backward, head_dim),
        "state_backward",
        [
            out((state_rows, width)),
            out((1, width), f32),
            out((blocks, width // blocks, lanes)),
            out((group_rows, 2 * lanes), f32),
            out((blocks, width // blocks, 3 * lanes)),
            out((places, state_rows, width)),
            out((2, width), f32),
        ],
        [
            pltpu.VMEM((width, 3 * lanes), bf16),
            pltpu.VMEM((width, width), bf16),
            pltpu.VMEM((all_states, width), bf16),
            pltpu.VMEM((all_states, lanes), bf16),
            pltpu.VMEM((all_states, 3 * lanes), bf16),
            pltpu.VMEM((all_states, 2 * lanes), f32),
        ],
        4 * all_states * width * 4 * lanes,
        all_states * (all_states + group_rows) * heads,
        scal,
        state_in[0],
        all_state_cot,
        gate_bias[None],
        all_state,
        *read_parts,
        *full_sout,
        sqkv,
        qkv,
        state_norm,
        full_sqkv,
    )
    residual, second, hidden, slope, out_rows, grad_down = call(
        ffn_up,
        "ffn_up",
        [
            out((places, rows, width), f32),
            out((group_rows, width)),
            out((group_rows, inner_width)),
            out((group_rows, inner_width)),
            out((lanes, width)),
            out((blocks, inner_width, width // blocks)),
        ],
        [pltpu.VMEM((width, width), bf16), pltpu.VMEM((width, inner_width), bf16)],
        2 * group_rows * width * (width + 2 * inner_width),
        group_rows * inner_width,
        scal,
        all_tokens,
        *mixed_parts,
        *full_out,
        gains[1],
        shifts[1],
        full_up,
        all_cot,
    )

    back_second, back_input, mid_sums = call(
        ffn_back,
        "ffn_back",
        [
            out((places, rows, width)),
            out((group_rows, inner_width)),
            out((2, width), f32),
        ],
        [pltpu.VMEM((inner_width, width), bf16), pltpu.VMEM((width, inner_width), bf16)],
        4 * group_rows * width * inner_width,
        0,
        scal,
        all_cot,
        full_down,
        full_up,
        slope,
        residual,
    )
    residual_own = residual[0]
    own_grad_sout = sum_over_dp(grad_sout, 0)
    own_grad_sqkv = sum_over_dp(grad_sqkv, 0)
    back_state = sum_to_owner(back_state_norm)
    gate_open = jax.nn.sigmoid(gate_bias)
    grad_state = (
        gate_open * state_cotangent[0].astype(f32)
        + norm_back(state_in[0].astype(f32), back_state, norm_gain[2])
    ).astype(bf16)

    own_grad_down = sum_over_dp(grad_down, 1)
    back_second = sum_to_owner(back_second)
    back_residual = cotangent.astype(f32) + norm_back(residual_own, back_second, norm_gain[1])
    back_branch = from_group(back_residual.astype(bf16))

    ffn_partial, grad_up = call(
        ffn_rest,
        "ffn_rest",
        [out((places, rows, width)), out((blocks, width // blocks, inner_width))],
        [pltpu.VMEM((inner_width, width), bf16)],
        4 * group_rows * width * inner_width,
        0,
        scal,
        hidden,
        full_down,
        second,
        back_input,
    )
    own_grad_up = sum_over_dp(grad_up, 0)
    output = (residual_own + sum_to_owner(ffn_partial)).astype(bf16)

    (grad_out,) = call(
        out_grad,
        "out_grad",
        [out((blocks, width // blocks, lanes))],
        [],
        2 * group_rows * width * lanes,
        0,
        scal,
        back_branch,
        *mixed_parts,
    )
    own_grad_out = sum_over_dp(grad_out, 0)

    grad_qkv, back_first, first_sums, distance = call(
        functools.partial(token_backward, head_dim),
        "token_backward",
        [
            out((blocks, width // blocks, 3 * lanes)),
            out((places, rows, width)),
            out((2, width), f32),
            out((heads, span), f32),
        ],
        [
            pltpu.VMEM((width, 3 * lanes), bf16),
            pltpu.VMEM((heads, rows, span), f32),
            pltpu.VMEM((group_rows, lanes), bf16),
            pltpu.VMEM((group_rows, 3 * lanes), bf16),
            pltpu.VMEM((group_rows, 2 * lanes), f32),
            pltpu.VMEM((rows, span), f32),
        ],
        2 * group_rows * width * 7 * lanes,
        group_rows * span * heads,
        scal,
        back_branch,
        out_rows,
        qkv,
        bias,
        token_back,
        first,
        all_tokens,
        full_qkv,
    )
    back_first = sum_to_owner(back_first)
    grad_tokens = (
        norm_back(tokens.astype(f32), back_first, norm_gain[0]) + back_residual
    ).astype(bf16)
    own_grad_qkv = sum_over_dp(grad_qkv, 0)
    both_grads = from_heads(
        jnp.concatenate([own_grad_qkv, own_grad_sqkv], axis=0).astype(bf16)
    ).astype(f32)

    per_distance = distance[:, 1 : window + 1][:, ::-1]
    own_rel = jnp.dot(
        per_distance, lookup, precision=lax.Precision.HIGHEST, preferred_element_type=f32
    ).T
    grad_rel = lax.dynamic_update_slice_in_dim(
        jnp.zeros((bucket_count, head_count), f32), own_rel, here * heads, 1
    )
    small = [
        jnp.stack([first_sums[0], mid_sums[0], state_sums[0]]),
        jnp.stack([first_sums[1], mid_sums[1], state_sums[1]]),
        grad_gate[0],
        grad_rel,
    ]
    packed = sum_over_all(jnp.concatenate([v.reshape(-1, 128) for v in small], axis=0))
    unpacked, start = [], 0
    for v in small:
        count = v.size // 128
        unpacked.append(packed[start : start + count].reshape(v.shape))
        start += count
    return (
        output,
        next_state[None],
        grad_tokens,
        grad_state[None],
        both_grads[:depth],
        own_grad_out,
        both_grads[depth:],
        own_grad_sout,
        own_grad_up,
        own_grad_down,
        unpacked[3],
        unpacked[0],
        unpacked[1],
        unpacked[2],
    )


def solution(mesh):
    rows_spec = P(("dp", "state"), None)
    state_spec = P("dp", "state", None)
    weight_spec = P("dp", "state")
    return jax.shard_map(
        per_device,
        mesh=mesh,
        in_specs=(
            rows_spec,
            state_spec,
            rows_spec,
            state_spec,
            P("dp"),
            P(),
            weight_spec,
            weight_spec,
            weight_spec,
            weight_spec,
            weight_spec,
            P("state", "dp"),
            P(),
            P(),
            P(),
            P(),
        ),
        out_specs=(
            rows_spec,
            state_spec,
            rows_spec,
            state_spec,
            weight_spec,
            weight_spec,
            weight_spec,
            weight_spec,
            weight_spec,
            P("state", "dp"),
            P(),
            P(),
            P(),
            P(),
        ),
        check_vma=False,
    )
```

```python
import functools

import jax
import jax.numpy as jnp
from jax import lax
from jax.experimental import pallas as pl
from jax.experimental.pallas import tpu as pltpu
from jax.sharding import PartitionSpec as P

epsilon = 1e-05
masked_value = -1e30
f32 = jnp.float32
bf16 = jnp.bfloat16

PLACES = (0, 2, 1, 3)
DP_STEPS = (2, 4, 1)
DP_PLACES = (0, 2, 4, 6, 1, 3, 5, 7)


def dot(left, right):
    return lax.dot_general(left, right, (((1,), (0,)), ((), ())), preferred_element_type=f32)


def dot_rt(left, right):
    return lax.dot_general(left, right, (((1,), (1,)), ((), ())), preferred_element_type=f32)


def dot_lt(left, right):
    return lax.dot_general(left, right, (((0,), (0,)), ((), ())), preferred_element_type=f32)


def where_from(sender, place):
    return PLACES.index(PLACES[sender] ^ PLACES[place])


def normalized(values):
    centre = jnp.mean(values, axis=-1, keepdims=True)
    centred = values - centre
    spread = jnp.mean(centred * centred, axis=-1, keepdims=True)
    inverse = lax.rsqrt(spread + epsilon)
    return centred * inverse, inverse


def normed_back(back, hat, inverse, gain):
    grown = back * gain
    return inverse * (
        grown
        - jnp.mean(grown, axis=-1, keepdims=True)
        - hat * jnp.mean(grown * hat, axis=-1, keepdims=True)
    )


def place_of(scal, q):
    return scal[0] ^ PLACES[q]


def aligned(start, size):
    return pl.ds(pl.multiple_of(start, size), size)


def block_at(scal, q):
    return scal[2 + q]


def position_of(scal, block, blocks):
    return scal[2 + blocks + block]


def rows_in_order(scal, target, source):
    blocks, depth = source.shape[0], source.shape[1]
    for q in range(blocks):
        target[aligned(block_at(scal, q) * depth, depth), :] = source[q]


def columns_in_order(scal, target, source):
    blocks, depth = source.shape[0], source.shape[2]
    for q in range(blocks):
        target[:, aligned(block_at(scal, q) * depth, depth)] = source[q]


def put_rows(scal, target, start, value):
    blocks, depth = target.shape[0], target.shape[1]
    rows = value.shape[0]
    if depth >= rows:
        target[position_of(scal, start // depth, blocks), aligned(start % depth, rows), :] = value
    else:
        for i in range(rows // depth):
            position = position_of(scal, start // depth + i, blocks)
            target[position] = value[i * depth : (i + 1) * depth]


def put_columns(scal, target, start, value):
    blocks, depth = target.shape[0], target.shape[2]
    columns = value.shape[1]
    if depth >= columns:
        target[position_of(scal, start // depth, blocks), :, aligned(start % depth, columns)] = value
    else:
        for i in range(columns // depth):
            position = position_of(scal, start // depth + i, blocks)
            target[position] = value[:, i * depth : (i + 1) * depth]


def call(body, name, outs, scratch, flops, exps, *args):
    sizes = sum(a.size * a.dtype.itemsize for a in args) + sum(
        a.size * a.dtype.itemsize for a in outs
    )
    in_specs = [pl.BlockSpec(memory_space=pltpu.SMEM)] + [
        pl.BlockSpec(memory_space=pltpu.VMEM) for _ in args[1:]
    ]
    return pl.pallas_call(
        body,
        out_shape=outs,
        in_specs=in_specs,
        out_specs=[pl.BlockSpec(memory_space=pltpu.VMEM) for _ in outs],
        scratch_shapes=scratch,
        compiler_params=pltpu.CompilerParams(vmem_limit_bytes=56 << 20),
        cost_estimate=pl.CostEstimate(flops=flops, bytes_accessed=sizes, transcendentals=exps),
        name=name,
    )(*args)


def out(shape, kind=bf16):
    return jax.ShapeDtypeStruct(shape, kind)


def by_distance(scores):
    rows, span = scores.shape
    row_at = lax.broadcasted_iota(jnp.int32, scores.shape, 0)
    step = 1
    while step < rows:
        scores = jnp.where(row_at & step != 0, pltpu.roll(scores, span - step, 1), scores)
        step *= 2
    return scores


def bias_blocks(tb, bias):
    heads, rows, span = tb.shape
    for h in range(heads):
        row = jnp.broadcast_to(bias[h], (rows, span))
        tb[h] = pltpu.roll(row, 0, 1, stride=1, stride_axis=0)


def window_probs(scal, query, keys, tb_block, last, scale):
    rows, span = tb_block.shape
    count = keys.shape[0]
    scores = dot_rt(query, keys) * scale + tb_block[:, span - count :]
    if last:
        row_at = lax.broadcasted_iota(jnp.int32, scores.shape, 0)
        col_at = lax.broadcasted_iota(jnp.int32, scores.shape, 1)
        ahead = col_at - (count - rows)
        live = (ahead < scal[1] - last) | (ahead == row_at)
        scores = jnp.where(live, scores, masked_value)
    top = jnp.max(scores, axis=-1, keepdims=True)
    grown = jnp.exp(scores - top)
    return grown * (1.0 / jnp.sum(grown, axis=-1, keepdims=True))


def state_probs(scal, query, state_keys, keys, scale):
    own = dot_rt(query, state_keys) * scale
    token = dot_rt(query, keys) * scale
    col_at = lax.broadcasted_iota(jnp.int32, token.shape, 1)
    token = jnp.where(col_at < scal[1], token, masked_value)
    top = jnp.maximum(
        jnp.max(own, axis=-1, keepdims=True), jnp.max(token, axis=-1, keepdims=True)
    )
    own = jnp.exp(own - top)
    token = jnp.exp(token - top)
    total = jnp.sum(own, axis=-1, keepdims=True) + jnp.sum(token, axis=-1, keepdims=True)
    inverse = 1.0 / total
    return own * inverse, token * inverse


def head_cols(block, h, heads, head_dim):
    start = (block * heads + h) * head_dim
    return slice(start, start + head_dim)


def token_forward(head_dim, scal, tokens, gain, shift, w_qkv, bias, first, qkv, mixed, w_nat, tb):
    places, rows, width = tokens.shape
    heads = bias.shape[0]
    span = bias.shape[1]
    scale = head_dim ** (-0.5)
    rows_in_order(scal, w_nat, w_qkv)
    bias_blocks(tb, [bias[h : h + 1, :] for h in range(heads)])
    for q in range(places):
        hat, _ = normalized(tokens[q].astype(f32))
        normed = (hat * gain[...] + shift[...]).astype(bf16)
        at = aligned(place_of(scal, q) * rows, rows)
        first[at, :] = normed
        qkv[at, :] = dot(normed, w_nat[...]).astype(bf16)
    for c in range(places):
        count = min(span, (c + 1) * rows)
        low, high = (c + 1) * rows - count, (c + 1) * rows
        last = c * rows if c == places - 1 else 0
        parts = []
        for h in range(heads):
            probs = window_probs(
                scal,
                qkv[c * rows : high, head_cols(0, h, heads, head_dim)],
                qkv[low:high, head_cols(1, h, heads, head_dim)],
                tb[h],
                last,
                scale,
            )
            parts.append(
                dot(probs.astype(bf16), qkv[low:high, head_cols(2, h, heads, head_dim)])
            )
        mixed[c] = jnp.concatenate(parts, axis=1).astype(bf16)


def state_forward(
    head_dim, scal, state, gain, shift, w_sqkv, qkv, normed_out, sqkv, read, w_nat
):
    places, rows, width = state.shape
    heads = qkv.shape[1] // (3 * head_dim)
    scale = head_dim ** (-0.5)
    rows_in_order(scal, w_nat, w_sqkv)
    for q in range(places):
        hat, _ = normalized(state[q].astype(f32))
        normed = (hat * gain[...] + shift[...]).astype(bf16)
        normed_out[q * rows : (q + 1) * rows, :] = normed
        sqkv[q * rows : (q + 1) * rows, :] = dot(normed, w_nat[...]).astype(bf16)
    for q in range(places):
        parts = []
        for h in range(heads):
            own, token = state_probs(
                scal,
                sqkv[q * rows : (q + 1) * rows, head_cols(0, h, heads, head_dim)],
                sqkv[:, head_cols(1, h, heads, head_dim)],
                qkv[:, head_cols(1, h, heads, head_dim)],
                scale,
            )
            parts.append(
                dot(own.astype(bf16), sqkv[:, head_cols(2, h, heads, head_dim)])
                + dot(token.astype(bf16), qkv[:, head_cols(2, h, heads, head_dim)])
            )
        read[q] = jnp.concatenate(parts, axis=1).astype(bf16)


def assembled(scal, target, parts):
    for p, part in enumerate(parts):
        blocks, depth, columns = part.shape
        at = aligned(place_of(scal, p) * columns, columns)
        for q in range(blocks):
            target[aligned(block_at(scal, q) * depth, depth), at] = part[q]


def state_backward(
    head_dim,
    scal,
    state_own,
    state_cot,
    gate_bias,
    state,
    read0,
    read1,
    read2,
    read3,
    out0,
    out1,
    out2,
    out3,
    sqkv,
    qkv,
    normed,
    w_sqkv,
    next_state,
    grad_gate,
    grad_sout,
    token_back,
    grad_sqkv,
    back_norm,
    grad_norm,
    w_nat,
    w_out,
    back_update,
    back_read,
    back_sqkv,
    own_sum,
):
    places, rows, width = state_cot.shape
    reads = (read0, read1, read2, read3)
    heads = qkv.shape[1] // (3 * head_dim)
    lanes = heads * head_dim
    scale = head_dim ** (-0.5)
    rows_in_order(scal, w_nat, w_sqkv)
    assembled(scal, w_out, (out0, out1, out2, out3))
    gate = jax.nn.sigmoid(gate_bias[...])
    update = None
    for p in range(places):
        term = dot(reads[p][p], w_out[aligned(place_of(scal, p) * lanes, lanes), :])
        update = term if update is None else update + term
    held = state_own[...].astype(f32)
    cot = state_cot[0].astype(f32)
    next_state[...] = (gate * held + (1.0 - gate) * update).astype(bf16)
    grad_gate[...] = jnp.sum(cot * (held - update), axis=0, keepdims=True) * (gate * (1.0 - gate))
    for q in range(places):
        back_update[q * rows : (q + 1) * rows, :] = (
            (1.0 - gate) * state_cot[q].astype(f32)
        ).astype(bf16)
    own_columns = back_update[:, aligned(scal[0] * lanes, lanes)]
    for p in range(places):
        stack = jnp.concatenate([reads[p][where_from(p, q)] for q in range(places)], axis=0)
        put_rows(
            scal, grad_sout, place_of(scal, p) * lanes, dot_lt(stack, own_columns).astype(bf16)
        )
    back_read[...] = dot_rt(
        back_update[...], w_out[aligned(scal[0] * lanes, lanes), :]
    ).astype(bf16)
    for h in range(heads):
        key_at, value_at = head_cols(1, h, heads, head_dim), head_cols(2, h, heads, head_dim)
        query_at, read_at = head_cols(0, h, heads, head_dim), slice(h * head_dim, (h + 1) * head_dim)
        for q in range(places):
            at = slice(q * rows, (q + 1) * rows)
            query, back = sqkv[at, query_at], back_read[at, read_at]
            own, token = state_probs(scal, query, sqkv[:, key_at], qkv[:, key_at], scale)
            back_own = dot_rt(back, sqkv[:, value_at])
            back_token = dot_rt(back, qkv[:, value_at])
            row_dot = jnp.sum(own * back_own, axis=-1, keepdims=True) + jnp.sum(
                token * back_token, axis=-1, keepdims=True
            )
            own_raw = (own * (back_own - row_dot) * scale).astype(bf16)
            token_raw = (token * (back_token - row_dot) * scale).astype(bf16)
            back_sqkv[at, query_at] = (
                dot(own_raw, sqkv[:, key_at]) + dot(token_raw, qkv[:, key_at])
            ).astype(bf16)
            terms = (
                (own_sum, key_at, dot_lt(own_raw, query)),
                (own_sum, value_at, dot_lt(own.astype(bf16), back)),
                (token_back, key_at, dot_lt(token_raw, query)),
                (token_back, value_at, dot_lt(token.astype(bf16), back)),
            )
            for target, columns, term in terms:
                columns = slice(columns.start - lanes, columns.stop - lanes)
                if q == 0:
                    target[:, columns] = term
                else:
                    target[:, columns] += term
    back_sqkv[:, lanes:] = own_sum[...].astype(bf16)
    for start in range(0, width, 256):
        put_rows(
            scal,
            grad_sqkv,
            start,
            dot_lt(normed[:, start : start + 256], back_sqkv[...]).astype(bf16),
        )
    gain_sum, shift_sum = None, None
    for q in range(places):
        back = dot_rt(back_sqkv[q * rows : (q + 1) * rows, :], w_nat[...])
        back_norm[q] = back.astype(bf16)
        hat, _ = normalized(state[q].astype(f32))
        gain_term = jnp.sum(back * hat, axis=0, keepdims=True)
        shift_term = jnp.sum(back, axis=0, keepdims=True)
        gain_sum = gain_term if q == 0 else gain_sum + gain_term
        shift_sum = shift_term if q == 0 else shift_sum + shift_term
    grad_norm[0:1, :] = gain_sum
    grad_norm[1:2, :] = shift_sum


def ffn_up(
    scal,
    tokens,
    mixed0,
    mixed1,
    mixed2,
    mixed3,
    out0,
    out1,
    out2,
    out3,
    gain,
    shift,
    w_up,
    cot,
    residual,
    second,
    hidden,
    slope,
    out_rows,
    grad_down,
    w_out,
    w_nat,
):
    places, rows, width = tokens.shape
    mixed = (mixed0, mixed1, mixed2, mixed3)
    lanes = mixed0.shape[2]
    assembled(scal, w_out, (out0, out1, out2, out3))
    out_rows[...] = w_out[aligned(scal[0] * lanes, lanes), :]
    rows_in_order(scal, w_nat, w_up)
    for q in range(places):
        total = tokens[q].astype(f32)
        for p in range(places):
            total += dot(
                mixed[p][place_of(scal, q)], w_out[aligned(place_of(scal, p) * lanes, lanes), :]
            )
        residual[q] = total
        hat, _ = normalized(total)
        normed = (hat * gain[...] + shift[...]).astype(bf16)
        at = slice(q * rows, (q + 1) * rows)
        second[at, :] = normed
        inner = dot(normed, w_nat[...])
        root = 0.7978845608028654
        square = inner * inner
        bend = jnp.tanh(root * inner * (1.0 + 0.044715 * square))
        half = 0.5 * (1.0 + bend)
        hidden[at, :] = (inner * half).astype(bf16)
        slope[at, :] = (
            half + (0.5 * root) * inner * (1.0 - bend * bend) * (1.0 + (3 * 0.044715) * square)
        ).astype(bf16)
    for start in range(0, width, 256):
        columns = jnp.concatenate([cot[q, :, start : start + 256] for q in range(places)], axis=0)
        put_columns(scal, grad_down, start, dot_lt(hidden[...], columns).astype(bf16))


def ffn_back(
    scal,
    cot,
    w_down,
    w_up,
    slope,
    residual,
    back_second,
    back_input,
    grad_norm,
    w_nat,
    w_up_nat,
):
    places, rows, width = cot.shape
    columns_in_order(scal, w_nat, w_down)
    rows_in_order(scal, w_up_nat, w_up)
    gain_sum, shift_sum = None, None
    for q in range(places):
        at = slice(q * rows, (q + 1) * rows)
        inner = (dot_rt(cot[q], w_nat[...]) * slope[at, :].astype(f32)).astype(bf16)
        back_input[at, :] = inner
        back = dot_rt(inner, w_up_nat[...])
        back_second[q] = back.astype(bf16)
        hat, _ = normalized(residual[q])
        gain_term = jnp.sum(back * hat, axis=0, keepdims=True)
        shift_term = jnp.sum(back, axis=0, keepdims=True)
        gain_sum = gain_term if q == 0 else gain_sum + gain_term
        shift_sum = shift_term if q == 0 else shift_sum + shift_term
    grad_norm[0:1, :] = gain_sum
    grad_norm[1:2, :] = shift_sum


def ffn_rest(scal, hidden, w_down, second, back_input, partial, grad_up, w_nat):
    places, rows, width = partial.shape
    for start in range(0, width, 256):
        put_rows(
            scal,
            grad_up,
            start,
            dot_lt(second[:, start : start + 256], back_input[...]).astype(bf16),
        )
    columns_in_order(scal, w_nat, w_down)
    for q in range(places):
        partial[q] = dot(hidden[q * rows : (q + 1) * rows, :], w_nat[...]).astype(bf16)


def out_grad(scal, back_branch, mixed0, mixed1, mixed2, mixed3, grad_out):
    places, rows, width = back_branch.shape
    mixed = (mixed0, mixed1, mixed2, mixed3)
    lanes = mixed0.shape[2]
    own_at = aligned(scal[0] * lanes, lanes)
    own_columns = jnp.concatenate([back_branch[q, :, own_at] for q in range(places)], axis=0)
    for p in range(places):
        stack = jnp.concatenate([mixed[p][place_of(scal, q)] for q in range(places)], axis=0)
        put_rows(
            scal, grad_out, place_of(scal, p) * lanes, dot_lt(stack, own_columns).astype(bf16)
        )


def token_backward(
    head_dim,
    scal,
    back_branch,
    out_rows,
    qkv,
    bias,
    token_back,
    first,
    tokens,
    w_qkv,
    grad_qkv,
    back_first,
    grad_norm,
    distance,
    w_nat,
    tb,
    back_mixed,
    back_qkv,
    key_sum,
    band,
):
    places, rows, width = back_branch.shape
    heads, span = bias.shape
    lanes = heads * head_dim
    scale = head_dim ** (-0.5)
    rows_in_order(scal, w_nat, w_qkv)
    bias_blocks(tb, [bias[h : h + 1, :] for h in range(heads)])
    for q in range(places):
        back_mixed[aligned(place_of(scal, q) * rows, rows), :] = dot_rt(
            back_branch[q], out_rows[...]
        ).astype(bf16)
    key_sum[...] = token_back[...]
    for h in range(heads):
        key_at, value_at = head_cols(1, h, heads, head_dim), head_cols(2, h, heads, head_dim)
        query_at, read_at = head_cols(0, h, heads, head_dim), slice(h * head_dim, (h + 1) * head_dim)
        for c in reversed(range(places)):
            count = min(span, (c + 1) * rows)
            low, high = (c + 1) * rows - count, (c + 1) * rows
            last = c * rows if c == places - 1 else 0
            query, back = qkv[c * rows : high, query_at], back_mixed[c * rows : high, read_at]
            keys = qkv[low:high, key_at]
            probs = window_probs(scal, query, keys, tb[h], last, scale)
            back_probs = dot_rt(back, qkv[low:high, value_at])
            row_dot = jnp.sum(probs * back_probs, axis=-1, keepdims=True)
            back_scores = probs * (back_probs - row_dot)
            if c == places - 1:
                band[...] = back_scores
            else:
                band[:, span - count :] += back_scores
            raw = (back_scores * scale).astype(bf16)
            back_qkv[c * rows : high, query_at] = dot(raw, keys).astype(bf16)
            key_to = slice(key_at.start - lanes, key_at.stop - lanes)
            value_to = slice(value_at.start - lanes, value_at.stop - lanes)
            key_sum[low:high, key_to] += dot_lt(raw, query)
            key_sum[low:high, value_to] += dot_lt(probs.astype(bf16), back)
        distance[h : h + 1, :] = jnp.sum(by_distance(band[...]), axis=0, keepdims=True)
    back_qkv[:, lanes:] = key_sum[...].astype(bf16)
    for start in range(0, width, 256):
        put_rows(
            scal,
            grad_qkv,
            start,
            dot_lt(first[:, start : start + 256], back_qkv[...]).astype(bf16),
        )
    gain_sum, shift_sum = None, None
    for q in range(places):
        back = dot_rt(back_qkv[aligned(place_of(scal, q) * rows, rows), :], w_nat[...])
        back_first[q] = back.astype(bf16)
        hat, _ = normalized(tokens[q].astype(f32))
        gain_term = jnp.sum(back * hat, axis=0, keepdims=True)
        shift_term = jnp.sum(back, axis=0, keepdims=True)
        gain_sum = gain_term if q == 0 else gain_sum + gain_term
        shift_sum = shift_term if q == 0 else shift_sum + shift_term
    grad_norm[0:1, :] = gain_sum
    grad_norm[1:2, :] = shift_sum


def flip_low(i):
    return i + 1 - 2 * (i % 2)


class Mover:
    def __init__(self, send, recv):
        self.send, self.recv, self.sends, self.recvs = send, recv, 0, 0

    def send_slot(self):
        self.sends += 1
        return self.sends - 1

    def recv_slot(self):
        self.recvs += 1
        return self.recvs - 1

    def copy(self, source, target, device, send_slot, recv_slot):
        return pltpu.make_async_remote_copy(
            src_ref=source,
            dst_ref=target,
            send_sem=self.send.at[send_slot],
            recv_sem=self.recv.at[recv_slot],
            device_id=device,
            device_id_type=pl.DeviceIdType.MESH,
        )

    def __call__(self, source, target, device):
        return self.copy(source, target, device, self.send_slot(), self.recv_slot())


class Links:
    def __init__(self):
        self.d, self.s = lax.axis_index("dp"), lax.axis_index("state")
        z, y = self.d // 2, self.d % 2
        self.over_z = [2 * (z + 1 - 2 * (z % 2)) + y, 2 * ((z + 2) % 4) + y, 2 * (3 - z) + y]
        self.over_y = flip_low(self.d)
        self.core, self.x = flip_low(self.s), (self.s + 2) % 4
        self.to_core, self.to_x = (self.d, self.core), (self.d, self.x)
        self.to_y = (self.over_y, self.s)
        self.to_z = [(other, self.s) for other in self.over_z]
        self.in_middle = (z == 1) | (z == 2)
        self.far_middle = 2 * (2 - z // 2) + y
        self.far_end = 2 * (3 - 3 * (z // 2)) + y
        self.to_far, self.to_far_end = (self.far_middle, self.s), (self.far_end, self.s)
        self.z, self.z_rest = z, [i // 2 for i in (self.over_z[0], self.far_middle, self.far_end)]

    def greet(self):
        barrier = pltpu.get_barrier_semaphore()
        partners = [self.to_core, self.to_x, self.to_y, *self.to_z]
        for partner in partners:
            pl.semaphore_signal(
                barrier, inc=1, device_id=partner, device_id_type=pl.DeviceIdType.MESH
            )
        pl.semaphore_wait(barrier, len(partners))


class GroupGather:
    def __init__(self, mover, links, whole, at, source=None):
        self.links, self.parts = links, [links.s, links.core, links.x, flip_low(links.x)]
        own = whole.at[at(links.s)]
        source = own if source is None else source
        across = whole.at[at(links.x)]
        self.over_x = mover(source, own, links.to_x)
        self.beside = mover(source, own, links.to_core)
        self.passed = mover(across, across, links.to_core)

    def start(self):
        self.over_x.start()
        self.beside.start()

    def forward(self):
        self.over_x.wait_recv()
        self.passed.start()

    def finish(self):
        self.beside.wait_recv()
        self.passed.wait_recv()

    def sent(self):
        for copy in (self.over_x, self.beside, self.passed):
            copy.wait_send()


class WeightGather:
    def __init__(self, mover, links, whole, at, source):
        own = whole.at[at(links.d)]
        self.links = links
        near, far = mover.send_slot(), mover.send_slot()
        slots = [mover.recv_slot() for _ in range(3)]
        self.near = mover.copy(source, own, links.to_z[0], near, slots[0])
        self.far = [mover.copy(source, own, links.to_far, far, slots[k]) for k in (1, 2)]
        self.own_y = mover(source, own, links.to_y)
        self.passed, self.relayed = [], [None]
        for k, other in enumerate((links.over_z[0], links.far_middle, links.far_end)):
            block = whole.at[at(other)]
            self.passed.append(mover(block, block, links.to_y))
            if k:
                self.relayed.append(
                    mover.copy(block, block, links.to_z[0], mover.send_slot(), slots[k])
                )

    def start_z(self):
        self.near.start()

        @pl.when(self.links.in_middle)
        def _():
            self.far[0].start()

        @pl.when(jnp.logical_not(self.links.in_middle))
        def _():
            self.far[1].start()

    def start_y(self):
        self.own_y.start()

    def pass_on(self, k):
        if k == 0:
            self.near.wait_recv()
        else:
            self.relayed[k].wait_recv()
        self.passed[k].start()

    def pass_middle(self, *ks):
        @pl.when(self.links.in_middle)
        def _():
            for k in ks:
                if k:
                    self.relayed[k].wait_recv()
                    self.relayed[k].start()
                    self.passed[k].start()
                else:
                    self.pass_on(0)

    def pass_end(self, *ks):
        @pl.when(jnp.logical_not(self.links.in_middle))
        def _():
            for k in ks:
                self.pass_on(k)

    def finish(self):
        self.own_y.wait_recv()
        for copy in self.passed:
            copy.wait_recv()

    def sent(self):
        for copy in (self.near, self.far[0], self.own_y, *self.passed):
            copy.wait_send()

        @pl.when(self.links.in_middle)
        def _():
            for copy in self.relayed[1:]:
                copy.wait_send()


class PairGather:
    def __init__(self, mover, links, whole, at, pair, source):
        own = whole.at[at(links.d)]
        self.links = links
        self.own_y = mover(source, own, links.to_y)
        both = whole.at[pair(links.z)]
        near, far = mover.send_slot(), mover.send_slot()
        slots = [mover.recv_slot() for _ in range(3)]
        self.near = mover.copy(both, both, links.to_z[0], near, slots[0])
        self.far = [mover.copy(both, both, links.to_far, far, slots[k]) for k in (1, 2)]
        self.relayed = [None]
        for k in (1, 2):
            other = whole.at[pair(links.z_rest[k])]
            self.relayed.append(
                mover.copy(other, other, links.to_z[0], mover.send_slot(), slots[k])
            )

    def start_y(self):
        self.own_y.start()

    def start_z(self):
        self.own_y.wait_recv()
        self.near.start()

        @pl.when(self.links.in_middle)
        def _():
            self.far[0].start()

        @pl.when(jnp.logical_not(self.links.in_middle))
        def _():
            self.far[1].start()

    def pass_middle(self, *ks):
        @pl.when(self.links.in_middle)
        def _():
            for k in ks:
                if k:
                    self.relayed[k].wait_recv()
                    self.relayed[k].start()
                else:
                    self.near.wait_recv()

    def pass_end(self, *ks):
        @pl.when(jnp.logical_not(self.links.in_middle))
        def _():
            for k in ks:
                if k:
                    self.relayed[k].wait_recv()
                else:
                    self.near.wait_recv()

    def sent(self):
        for copy in (self.own_y, self.near, self.far[0]):
            copy.wait_send()

        @pl.when(self.links.in_middle)
        def _():
            for copy in self.relayed[1:]:
                copy.wait_send()


class GroupSum:
    def __init__(self, mover, links, partial, at, beside, across):
        self.partial, self.at, self.links = partial, at, links
        self.from_core, self.from_x = beside, across
        diagonal = flip_low(links.x)
        self.far = mover(partial.at[at(diagonal)], beside.at[1], links.to_core)
        self.near = mover(partial.at[at(links.core)], beside.at[0], links.to_core)
        self.over = mover(partial.at[at(links.x)], across, links.to_x)

    def start(self):
        self.far.start()
        self.near.start()

    def keep(self):
        self.near.wait_recv()
        pair = self.partial[self.at(self.links.s)].astype(f32) + self.from_core[0].astype(f32)
        self.from_core[0] = pair.astype(bf16)

    def finish_kept(self):
        self.over.wait_recv()
        return self.from_core[0].astype(f32) + self.from_x[...].astype(f32)

    def middle(self):
        self.far.wait_recv()
        place = self.at(self.links.x)
        total = self.partial[place].astype(f32) + self.from_core[1].astype(f32)
        self.partial[place] = total.astype(bf16)
        self.over.start()

    def finish(self):
        self.near.wait_recv()
        pair = self.partial[self.at(self.links.s)].astype(f32) + self.from_core[0].astype(f32)
        self.over.wait_recv()
        return pair + self.from_x[...].astype(f32)

    def sent(self):
        for copy in (self.far, self.near, self.over):
            copy.wait_send()


class BlockSum:
    def __init__(self, mover, links, partial, from_core, from_x, summed, start, half):
        core = links.s % 2

        def half_at(i):
            return (pl.ds(pl.multiple_of(start + i * half, half), half), slice(None))

        self.partial, self.summed, self.mine = partial, summed, half_at(core)
        self.from_core, self.from_x = from_core, from_x
        self.beside = mover(partial.at[half_at(1 - core)], from_core, links.to_core)
        self.over = mover(partial.at[self.mine], from_x, links.to_x)
        self.back = mover(summed.at[self.mine], summed.at[self.mine], links.to_core)

    def start(self):
        self.beside.start()

    def middle(self):
        self.beside.wait_recv()
        pair = self.partial[self.mine].astype(f32) + self.from_core[...].astype(f32)
        self.partial[self.mine] = pair.astype(bf16)
        self.over.start()

    def total(self):
        self.over.wait_recv()
        return self.partial[self.mine].astype(f32) + self.from_x[...].astype(f32)

    def share(self, value):
        self.summed[self.mine] = value.astype(bf16)
        self.back.start()

    def finish(self):
        self.back.wait_recv()

    def sent(self):
        for copy in (self.beside, self.over, self.back):
            copy.wait_send()


class LineSum:
    def __init__(self, mover, links, grads, places, from_z):
        self.links, self.grads, self.places, self.from_z = links, grads, places, from_z
        sends, slots = [mover.send_slot() for _ in range(3)], [mover.recv_slot() for _ in range(4)]
        blocks = [grads.at[place] for place in places]
        self.to_near = [
            mover.copy(blocks[k], from_z.at[k], links.to_z[0], sends[k], slots[k]) for k in range(3)
        ]
        self.onward = [None] + [
            mover.copy(blocks[k], from_z.at[3], device, sends[k], slots[3])
            for k, device in ((1, links.to_far), (2, links.to_far_end))
        ]

    def send_z(self, k):
        if k == 0:
            self.to_near[0].start()
        else:

            @pl.when(jnp.logical_not(self.links.in_middle))
            def _():
                self.to_near[k].start()

    def combine(self, k):
        @pl.when(self.links.in_middle)
        def _():
            self.to_near[k].wait_recv()
            total = self.grads[self.places[k]].astype(f32) + self.from_z[k].astype(f32)
            self.grads[self.places[k]] = total.astype(bf16)
            self.onward[k].start()

    def arrived_z(self):
        self.to_near[0].wait_recv()
        near = self.from_z[0].astype(f32)
        self.onward[1].wait_recv()
        return near + self.from_z[3].astype(f32)

    def sent(self):
        for copy in self.to_near:
            copy.wait_send()


class WeightSum(LineSum):
    def __init__(self, mover, links, grads, at, from_y, from_z):
        others = [links.over_z[0], links.far_middle, links.far_end]
        super().__init__(mover, links, grads, [at(i) for i in others], from_z)
        self.own, self.from_y = at(links.d), from_y
        self.over_y = [
            mover(grads.at[at(flip_low(i))], from_y.at[k], links.to_y)
            for k, i in enumerate([links.d, *others])
        ]

    def start(self):
        for k in (2, 3, 1, 0):
            self.over_y[k].start()

    def forward(self, *order):
        for k in order:
            self.over_y[k + 1].wait_recv()
            place = self.places[k]
            total = self.grads[place].astype(f32) + self.from_y[k + 1].astype(f32)
            self.grads[place] = total.astype(bf16)
            self.send_z(k)

    def finish(self):
        self.over_y[0].wait_recv()
        total = self.grads[self.own].astype(f32) + self.from_y[0].astype(f32)
        return total + self.arrived_z()

    def sent(self):
        super().sent()
        for copy in self.over_y:
            copy.wait_send()


class PairSum(LineSum):
    def __init__(self, mover, links, grads, at, pair, from_y, from_z):
        super().__init__(mover, links, grads, [pair(i) for i in links.z_rest], from_z)
        self.own_pair, self.own, self.from_y = pair(links.z), at(links.d), from_y
        self.over_y = mover(grads.at[at(links.over_y)], from_y, links.to_y)

    def start(self):
        for k in (1, 2, 0):
            self.send_z(k)

    def middle(self):
        total = self.grads[self.own_pair].astype(f32) + self.arrived_z()
        self.grads[self.own_pair] = total.astype(bf16)
        self.over_y.start()

    def finish(self):
        self.over_y.wait_recv()
        return self.grads[self.own].astype(f32) + self.from_y[...].astype(f32)

    def sent(self):
        super().sent()
        self.over_y.wait_send()


class SmallSum:
    def __init__(self, mover, links, value, arrived):
        self.value, self.arrived = value, arrived
        partners = [links.to_core, links.to_x, links.to_z[0], links.to_z[1], links.to_y]
        self.copies = [mover(value.at[k], arrived.at[k], to) for k, to in enumerate(partners)]

    def start(self):
        self.copies[0].start()

    def step(self, k):
        self.copies[k].wait_recv()
        self.value[k + 1] = self.value[k] + self.arrived[k]
        if k + 1 < len(self.copies):
            self.copies[k + 1].start()

    def sent(self):
        for copy in self.copies:
            copy.wait_send()


LAYER_COPIES = 157


def layer(
    head_dim,
    length,
    tokens,
    state,
    cot,
    state_cot,
    w_qkv,
    w_out,
    w_sqkv,
    w_sout,
    w_up,
    w_down,
    buckets,
    rel_table,
    gains,
    shifts,
    gate_bias,
    home_output,
    home_next_state,
    home_grad_tokens,
    home_grad_state,
    home_grad_qkv,
    home_grad_out,
    home_grad_sqkv,
    home_grad_sout,
    home_grad_up,
    home_grad_down,
    home_grad_rel,
    home_grad_norm,
    send_sem,
    recv_sem,
    local_sem,
    slab,
    qkv_nat,
    sqkv_nat,
    out_nat,
    sout_nat,
    up_nat,
    down_nat,
    tok_all,
    cot_all,
    state_all,
    mixed,
    read_all,
    hid,
    first,
    qkv,
    second,
    sqkv,
    back_read,
    back_sqkv,
    own_sum,
    key_sum,
    res_own,
    hat_half,
    inverse_half,
    tb,
    band,
    out_rows,
    state_grads,
    down_grads,
    y_state,
    y_down,
    y_up,
    y_out,
    y_sout,
    z_state,
    z_down,
    z_up,
    z_out,
    z_sout,
    beside_rows,
    across_rows,
    beside_ffn,
    across_ffn,
    small,
    small_in,
    distance,
    landed,
    credit,
    by_bucket,
    home_sem,
    output,
    next_state,
    grad_tokens,
    grad_state,
    grad_qkv,
    grad_out,
    grad_sqkv,
    grad_sout,
    grad_up,
    grad_down,
    grad_rel,
    grad_norm,
):
    rows, width = tokens.shape
    state_rows = state.shape[0]
    heads, _, span = tb.shape
    lanes = heads * head_dim
    depth = w_qkv.shape[0]
    inner_width = up_nat.shape[1]
    all_states = 4 * state_rows
    group_rows = 4 * rows
    scale = head_dim ** (-0.5)
    links = Links()
    s, d = links.s, links.d
    mover = Mover(send_sem, recv_sem)
    back_qkv, back_second, back_input = sqkv_nat, out_nat, sout_nat
    ffn_partial, back_first, back_branch = up_nat, down_nat, cot_all
    slope, up_grads = state_all, state_all
    back_state, ship = down_grads, slab
    hidden, token_grads = hid, hid

    def block(i, size):
        if isinstance(i, int):
            return slice(i * size, (i + 1) * size)
        return pl.ds(pl.multiple_of(i * size, size), size)

    def own_rows(size):
        return lambda i: (block(i, size), slice(None))

    def own_lanes(size):
        return lambda i: (slice(None), block(i, size))

    def cot_rows(i):
        if isinstance(i, int):
            start = all_states + i * state_rows
            return (slice(start, start + state_rows), slice(None))
        return (pl.ds(pl.multiple_of(all_states + i * state_rows, state_rows), state_rows), slice(None))

    own_columns = block(s, lanes)

    def own_out(i):
        return (block(i, depth), own_columns)

    def pair_last(i):
        return (block(i, 2 * depth), slice(3 * lanes, 4 * lanes))

    def last_lanes(i):
        return (block(i, depth), slice(3 * lanes, 4 * lanes))

    def first_lanes(i):
        return (block(i, depth), slice(0, 3 * lanes))

    to_slab = []
    for k, shard in enumerate((w_qkv, w_sqkv)):
        core_slot = 1 - links.core % 2 + links.core // 2
        x_slot = 2 - 2 * (links.x // 2)
        to_slab.append(
            (
                mover(
                    shard.at[:, block(2 - 2 * (s % 2), lanes)],
                    slab.at[k, :, block(x_slot, lanes)],
                    links.to_x,
                ),
                mover(
                    shard.at[:, lanes : 2 * lanes],
                    slab.at[k, :, block(core_slot, lanes)],
                    links.to_core,
                ),
            )
        )
    get_tokens = GroupGather(mover, links, tok_all, own_rows(rows), tokens)
    get_state = GroupGather(mover, links, state_all, own_rows(state_rows), state)
    get_scot = GroupGather(mover, links, state_all, cot_rows, state_cot)
    get_cot = GroupGather(mover, links, cot_all, own_rows(rows), cot)
    dp_sout = WeightGather(mover, links, sout_nat, own_out, w_sout)
    dp_out = WeightGather(mover, links, out_nat, own_out, w_out)
    dp_qkv = WeightGather(mover, links, qkv_nat, own_rows(depth), slab.at[0])
    dp_sqkv = WeightGather(mover, links, sqkv_nat, own_rows(depth), slab.at[1])
    dp_up = WeightGather(mover, links, up_nat, own_rows(depth), w_up)
    top, bottom = slice(0, inner_width // 2), slice(inner_width // 2, inner_width)
    dp_down = WeightGather(
        mover, links, down_nat, lambda i: (top, block(i, depth)), w_down.at[top, :]
    )
    dp_pair = PairGather(
        mover,
        links,
        down_nat,
        lambda i: (bottom, block(i, depth)),
        lambda i: (bottom, block(i, 2 * depth)),
        w_down.at[bottom, :],
    )
    get_sout = GroupGather(mover, links, sout_nat, own_lanes(lanes))
    get_out = [
        GroupGather(mover, links, out_nat, lambda i, at=at: (at, block(i, lanes)))
        for at in (slice(0, width // 2), slice(width // 2, width))
    ]
    get_mixed = GroupGather(mover, links, mixed, own_lanes(lanes))
    get_read = GroupGather(mover, links, read_all, own_lanes(lanes))
    sum_state = GroupSum(
        mover,
        links,
        back_state,
        own_rows(state_rows),
        beside_ffn.at[:, 0:state_rows, :],
        across_ffn.at[0:state_rows, :],
    )
    half = rows // 2
    block_sums = [
        BlockSum(
            mover,
            links,
            back_second,
            beside_rows.at[i // 2, i % 2 * half : (i % 2 + 1) * half, :],
            across_rows.at[i // 2, i % 2 * half : (i % 2 + 1) * half, :],
            back_branch,
            i * rows,
            half,
        )
        for i in range(4)
    ]
    sum_ffn = GroupSum(mover, links, ffn_partial, own_rows(rows), beside_ffn, across_ffn)
    sum_first = GroupSum(
        mover, links, back_first, own_rows(rows), beside_rows, across_rows.at[0]
    )
    dp_state = WeightSum(mover, links, state_grads, first_lanes, y_state, z_state)
    dp_grad_sout = PairSum(mover, links, state_grads, last_lanes, pair_last, y_sout, z_sout)
    dp_grad_down = WeightSum(mover, links, down_grads, own_lanes(depth), y_down, z_down)
    up_cut = inner_width * 3 // 4
    dp_grad_up, dp_grad_up_last = [
        WeightSum(
            mover,
            links,
            up_grads,
            lambda i, at=at: (block(i, depth), at),
            y_up.at[:, :, at],
            z_up.at[:, :, at],
        )
        for at in (slice(0, up_cut), slice(up_cut, inner_width))
    ]
    dp_grad_out = PairSum(mover, links, token_grads, last_lanes, pair_last, y_out, z_out)
    dp_grad_qkv = WeightSum(mover, links, token_grads, first_lanes, y_state, z_state)
    sum_small = SmallSum(mover, links, small, small_in)
    to_owner = [
        (
            mover(
                ship.at[k, :, block(2 - 2 * (s // 2), lanes)],
                landed.at[k, :, block(2 - 2 * (s % 2), lanes)],
                links.to_x,
            ),
            mover(
                ship.at[k, :, block(1 - s % 2 + s // 2, lanes)],
                landed.at[k, :, lanes : 2 * lanes],
                links.to_core,
            ),
        )
        for k in range(2)
    ]
    assert max(mover.sends, mover.recvs) == LAYER_COPIES
    leaving = []

    def send_home(staged, home):
        copy = pltpu.make_async_copy(staged, home, home_sem.at[len(leaving)])
        leaving.append(copy)
        copy.start()


    local = []
    for source, target in (
        (w_qkv.at[:, block(2 * (s % 2), lanes)], slab.at[0, :, block((s + 1) // 2, lanes)]),
        (w_sqkv.at[:, block(2 * (s % 2), lanes)], slab.at[1, :, block((s + 1) // 2, lanes)]),
        (tokens, tok_all.at[block(s, rows), :]),
        (state, state_all.at[block(s, state_rows), :]),
        (state_cot, state_all.at[cot_rows(s)]),
        (cot, cot_all.at[block(s, rows), :]),
        (w_up, up_nat.at[block(d, depth), :]),
        (w_down, down_nat.at[:, block(d, depth)]),
        (w_out, out_nat.at[block(d, depth), own_columns]),
        (w_sout, sout_nat.at[block(d, depth), own_columns]),
    ):
        local.append(pltpu.make_async_copy(source, target, local_sem.at[len(local)]))

    links.greet()
    for over_x, beside in to_slab:
        over_x.start()
        beside.start()
    dp_sout.start_y()
    dp_out.start_y()
    get_tokens.start()
    for copy in local:
        copy.start()
    small[0] = jnp.zeros(small.shape[1:], f32)
    key_sum[...] = jnp.zeros_like(key_sum)
    own_sum[...] = jnp.zeros_like(own_sum)
    for k, gather in enumerate((dp_qkv, dp_sqkv)):
        for copy in (*to_slab[k],):
            copy.wait_recv()
        local[k].wait()
        if k == 0:
            gather.start_z()
            gather.start_y()
    get_state.start()
    qkv_nat[block(d, depth), :] = slab[0]
    sqkv_nat[block(d, depth), :] = slab[1]
    for copy in local[2:]:
        copy.wait()

    def token_norm(i):
        at = block(i, rows)
        hat, _ = normalized(tok_all[at, :].astype(f32))
        first[at, :] = (hat * gains[0:1, :] + shifts[0:1, :]).astype(bf16)

    token_norm(s)
    onehot = jnp.where(
        lax.broadcasted_iota(jnp.int32, (rel_table.shape[1], buckets.shape[1]), 0) == buckets[...],
        1.0,
        0.0,
    )
    turned = jnp.where(
        lax.broadcasted_iota(jnp.int32, (span, buckets.shape[1]), 0)
        + lax.broadcasted_iota(jnp.int32, (span, buckets.shape[1]), 1)
        == buckets.shape[1],
        1.0,
        0.0,
    )
    by_bucket[...] = dot_rt(turned.astype(bf16), onehot.astype(bf16))
    bias = lax.dot_general(
        rel_table[...],
        by_bucket[...],
        (((1,), (1,)), ((), ())),
        precision=lax.Precision.HIGHEST,
        preferred_element_type=f32,
    )
    column = lax.broadcasted_iota(jnp.int32, bias.shape, 1)
    distance[...] = jnp.where((column > 0) & (column <= span - rows), bias, masked_value)
    bias_blocks(tb, [distance[pl.ds(s * heads + h, 1), :] for h in range(heads)])
    distance[...] = jnp.zeros_like(distance)
    get_tokens.beside.wait_recv()
    token_norm(links.core)
    dp_qkv.pass_on(0)
    dp_qkv.pass_middle(1, 2)
    dp_sout.start_z()
    dp_qkv.pass_end(1)
    get_tokens.forward()
    get_scot.start()
    dp_sqkv.start_z()
    token_norm(links.x)
    dp_sout.pass_on(0)
    dp_sout.pass_middle(1, 2)
    dp_qkv.pass_end(2)
    dp_sqkv.start_y()
    dp_sout.pass_end(1, 2)
    get_tokens.passed.wait_recv()
    token_norm(flip_low(links.x))
    get_state.forward()
    get_cot.start()
    dp_sqkv.pass_on(0)
    dp_sqkv.pass_middle(1)
    dp_out.start_z()
    dp_pair.start_y()
    dp_qkv.finish()
    dp_sqkv.pass_middle(2)

    def token_qkv(i):
        at = block(i, rows)
        qkv[at, :] = dot(first[at, :], qkv_nat[...]).astype(bf16)

    for i in range(4):
        token_qkv(i)
    for c in range(4):
        count = min(span, (c + 1) * rows)
        low, high = (c + 1) * rows - count, (c + 1) * rows
        last = c * rows if c == 3 else 0
        parts = []
        for h in range(heads):
            probs = window_probs(
                (0, length[0]),
                qkv[c * rows : high, head_cols(0, h, heads, head_dim)],
                qkv[low:high, head_cols(1, h, heads, head_dim)],
                tb[h],
                last,
                scale,
            )
            parts.append(
                dot(probs.astype(bf16), qkv[low:high, head_cols(2, h, heads, head_dim)])
            )
        mixed[c * rows : high, own_columns] = jnp.concatenate(parts, axis=1).astype(bf16)
        if c == 0:
            dp_sout.finish()
            get_sout.start()
            dp_up.start_z()
        elif c == 1:
            dp_sqkv.pass_end(1)
            dp_out.pass_on(0)
            dp_down.start_z()
        elif c == 2:
            dp_sqkv.pass_end(2)
            dp_out.pass_middle(1, 2)
    get_mixed.start()
    dp_out.pass_end(1)
    dp_up.start_y()
    get_scot.forward()

    get_state.finish()

    def state_norms(i):
        at = block(i, state_rows)
        hat, _ = normalized(state_all[at, :].astype(f32))
        hid[at, :] = (hat * gains[2:3, :] + shifts[2:3, :]).astype(bf16)

    for i in range(4):
        state_norms(i)
    dp_sqkv.finish()
    state_norm, back_update = slice(0, all_states), slice(all_states, 2 * all_states)
    sqkv[...] = dot(hid[state_norm, :], sqkv_nat[...]).astype(bf16)
    dp_out.pass_end(2)
    dp_up.pass_on(0)
    dp_up.pass_middle(1)
    dp_pair.start_z()
    dp_down.start_y()

    def state_read(i):
        at = block(i, state_rows)
        parts = []
        for h in range(heads):
            own, token = state_probs(
                (0, length[0]),
                sqkv[at, head_cols(0, h, heads, head_dim)],
                sqkv[:, head_cols(1, h, heads, head_dim)],
                qkv[:, head_cols(1, h, heads, head_dim)],
                scale,
            )
            parts.append(
                dot(own.astype(bf16), sqkv[:, head_cols(2, h, heads, head_dim)])
                + dot(token.astype(bf16), qkv[:, head_cols(2, h, heads, head_dim)])
            )
        read_all[at, own_columns] = jnp.concatenate(parts, axis=1).astype(bf16)

    for i in range(4):
        state_read(i)
        if i == 0:
            dp_out.finish()
            get_out[0].start()
        elif i == 1:
            dp_up.pass_middle(2)
            dp_up.pass_end(1)
    get_read.start()
    get_out[1].start()
    dp_down.pass_on(0)
    dp_down.pass_middle(1)
    dp_up.pass_end(2)
    get_cot.forward()
    get_sout.forward()

    gate = jax.nn.sigmoid(gate_bias[...])
    get_scot.finish()

    def updates(i):
        hid[cot_rows(i)] = ((1.0 - gate) * state_all[cot_rows(i)].astype(f32)).astype(bf16)

    for i in range(4):
        updates(i)
    get_sout.finish()
    back_read[...] = dot_rt(hid[back_update, :], sout_nat[block(s, lanes), :]).astype(bf16)

    def state_back(h):
        key_at, value_at = head_cols(1, h, heads, head_dim), head_cols(2, h, heads, head_dim)
        query_at, read_at = head_cols(0, h, heads, head_dim), head_cols(0, h, heads, head_dim)

        def one(i):
            at = block(i, state_rows)
            query, back = sqkv[at, query_at], back_read[at, read_at]
            own, token = state_probs(
                (0, length[0]), query, sqkv[:, key_at], qkv[:, key_at], scale
            )
            back_own = dot_rt(back, sqkv[:, value_at])
            back_token = dot_rt(back, qkv[:, value_at])
            row_dot = jnp.sum(own * back_own, axis=-1, keepdims=True) + jnp.sum(
                token * back_token, axis=-1, keepdims=True
            )
            own_raw = (own * (back_own - row_dot) * scale).astype(bf16)
            token_raw = (token * (back_token - row_dot) * scale).astype(bf16)
            back_sqkv[at, query_at] = (
                dot(own_raw, sqkv[:, key_at]) + dot(token_raw, qkv[:, key_at])
            ).astype(bf16)
            key_to = slice(key_at.start - lanes, key_at.stop - lanes)
            value_to = slice(value_at.start - lanes, value_at.stop - lanes)
            own_sum[:, key_to] += dot_lt(own_raw, query)
            own_sum[:, value_to] += dot_lt(own.astype(bf16), back)
            key_sum[:, key_to] += dot_lt(token_raw, query)
            key_sum[:, value_to] += dot_lt(token.astype(bf16), back)

        for i in range(4):
            one(i)

    for h in range(heads):
        state_back(h)
        if h == 0:
            dp_down.pass_middle(2)
            dp_down.pass_end(1)
            dp_pair.pass_middle(0, 1)
            get_mixed.forward()
            get_out[0].forward()
    back_sqkv[:, lanes:] = own_sum[...].astype(bf16)

    back_state[0:all_states, :] = dot_rt(back_sqkv[...], sqkv_nat[...]).astype(bf16)
    sum_state.start()
    dp_down.pass_end(2)
    dp_pair.pass_middle(2)
    get_read.forward()

    for start in range(0, width, 256):
        at = slice(start, start + 256)
        state_grads[at, 0 : 3 * lanes] = dot_lt(hid[state_norm, at], back_sqkv[...]).astype(bf16)
    sum_state.middle()
    sum_state.keep()
    get_out[1].forward()

    get_read.finish()
    update = dot(read_all[block(s, state_rows), :], sout_nat[...])
    held = state_all[block(s, state_rows), :].astype(f32)
    own_cot = state_all[cot_rows(s)].astype(f32)
    next_state[...] = (gate * held + (1.0 - gate) * update).astype(bf16)
    send_home(next_state, home_next_state)
    small[0, 6:7, :] = jnp.sum(own_cot * (held - update), axis=0, keepdims=True) * (
        gate * (1.0 - gate)
    )
    state_grads[:, 3 * lanes : 4 * lanes] = dot_lt(
        read_all[...], hid[back_update, own_columns]
    ).astype(bf16)

    get_read.sent()
    own_state, own_scot = slice(0, state_rows), slice(state_rows, 2 * state_rows)
    again = [
        pltpu.make_async_copy(source, read_all.at[place, :], local_sem.at[k])
        for k, (source, place) in enumerate(((state, own_state), (state_cot, own_scot)))
    ]
    for copy in again:
        copy.start()
    dp_grad_sout.start()

    get_mixed.finish()
    for gather in get_out:
        gather.finish()
    dp_up.finish()
    get_cot.finish()
    for gather in (get_state, get_scot, get_sout, dp_sout, *get_out, dp_out, dp_sqkv):
        gather.sent()
    out_rows[...] = out_nat[block(s, lanes), :]
    dp_state.start()

    def ffn_rows(i):
        at = block(i, rows)
        total = tok_all[at, :].astype(f32) + dot(mixed[at, :], out_nat[...])

        @pl.when(i == s)
        def _():
            res_own[...] = total

        hat, inverse = normalized(total)
        normed = (hat * gains[1:2, :] + shifts[1:2, :]).astype(bf16)
        second[at, :] = normed
        own_half = block(i, half)
        upper = s % 2 == 0
        hat_half[own_half, :] = jnp.where(upper, hat[:half], hat[half:]).astype(bf16)
        inverse_half[own_half, :] = jnp.broadcast_to(
            jnp.where(upper, inverse[:half], inverse[half:]), (half, 128)
        )
        inner = dot(normed, up_nat[...])
        root = 0.7978845608028654
        square = inner * inner
        bend = jnp.tanh(inner * (root + (root * 0.044715) * square))
        open_part = 0.5 + 0.5 * bend
        hidden[at, :] = (inner * open_part).astype(bf16)
        slope[at, :] = (
            open_part
            + (inner - inner * bend * bend) * (0.5 * root + (1.5 * root * 0.044715) * square)
        ).astype(bf16)

    for i in range(4):
        ffn_rows(i)

    sum_state.sent()

    def down_columns(i):
        at = block(i, 256)
        down_grads[:, at] = dot_lt(hidden[...], cot_all[:, at]).astype(bf16)

    for i in range(width // 256):
        down_columns(i)
    dp_grad_down.start()
    get_cot.sent()
    for copy in again:
        copy.wait()
    hat_state, inverse_state = normalized(read_all[own_state, :].astype(f32))
    back_own_state = sum_state.finish_kept()
    small[0, 2:3, :] = jnp.sum(back_own_state * hat_state, axis=0, keepdims=True)
    small[0, 5:6, :] = jnp.sum(back_own_state, axis=0, keepdims=True)
    grad_state[...] = (
        gate * read_all[own_scot, :].astype(f32)
        + normed_back(back_own_state, hat_state, inverse_state, gains[2:3, :])
    ).astype(bf16)
    send_home(grad_state, home_grad_state)
    dp_down.finish()
    dp_pair.pass_end(0, 1, 2)

    def ffn_back_rows(i):
        at = block(i, rows)
        inner = (dot_rt(cot_all[at, :], down_nat[...]) * slope[at, :].astype(f32)).astype(bf16)
        back_input[at, :] = inner
        back_second[at, :] = dot_rt(inner, up_nat[...]).astype(bf16)
        block_sums[i].start()

    def up_columns(i):
        at = block(i, 256)
        up_grads[at, :] = dot_lt(second[:, at], back_input[...]).astype(bf16)

    def ffn_out_rows(i):
        at = block(i, rows)
        ffn_partial[at, :] = dot(hidden[at, :], down_nat[...]).astype(bf16)

    def norm_rows(i):
        back = block_sums[i].total()
        at = block(i, half)
        hat = hat_half[at, :].astype(f32)
        small[0, 1:2, :] += 0.5 * jnp.sum(back * hat, axis=0, keepdims=True)
        small[0, 4:5, :] += 0.5 * jnp.sum(back, axis=0, keepdims=True)
        kept_cot = cot_all[block_sums[i].mine].astype(f32)
        block_sums[i].share(
            kept_cot + normed_back(back, hat, inverse_half[at, 0:1], gains[1:2, :])
        )

    def window_back(c):
        block_sums[c].finish()
        count = min(span, (c + 1) * rows)
        low, high = (c + 1) * rows - count, (c + 1) * rows
        last = c * rows if c == 3 else 0
        at = block(c, rows)
        back_mixed = dot_rt(back_branch[at, :], out_rows[...]).astype(bf16)
        for h in range(heads):
            key_at, value_at = head_cols(1, h, heads, head_dim), head_cols(2, h, heads, head_dim)
            query_at = head_cols(0, h, heads, head_dim)
            query, back = qkv[at, query_at], back_mixed[:, query_at]
            keys = qkv[low:high, key_at]
            probs = window_probs((0, length[0]), query, keys, tb[h], last, scale)
            back_probs = dot_rt(back, qkv[low:high, value_at])
            row_dot = jnp.sum(probs * back_probs, axis=-1, keepdims=True)
            back_scores = probs * (back_probs - row_dot)
            if c == 0:
                band[h] = jnp.zeros(band.shape[1:], f32)
            band[h, :, span - count :] += back_scores
            raw = (back_scores * scale).astype(bf16)
            back_qkv[at, query_at] = dot(raw, keys).astype(bf16)
            key_to = slice(key_at.start - lanes, key_at.stop - lanes)
            value_to = slice(value_at.start - lanes, value_at.stop - lanes)
            key_sum[low:high, key_to] += dot_lt(raw, query)
            key_sum[low:high, value_to] += dot_lt(probs.astype(bf16), back)

    ffn_back_rows(0)
    ffn_back_rows(1)
    block_sums[0].middle()
    ffn_back_rows(2)
    block_sums[1].middle()
    ffn_back_rows(3)
    block_sums[2].middle()
    for k in (1, 2):
        dp_grad_sout.combine(k)
    block_sums[3].middle()
    dp_state.forward(1)
    for i in range(width // 256):
        up_columns(i)
    dp_grad_sout.middle()
    dp_grad_up.start()
    dp_up.sent()
    dp_state.forward(2)
    for i in range(4):
        ffn_out_rows(i)
    sum_ffn.start()
    dp_down.sent()
    dp_pair.sent()
    norm_rows(0)
    dp_state.forward(0)
    norm_rows(1)
    window_back(0)
    dp_state.combine(1)
    dp_state.combine(2)
    sum_ffn.middle()
    norm_rows(2)
    window_back(1)
    dp_grad_down.forward(1)
    norm_rows(3)
    window_back(2)
    dp_grad_down.forward(2)
    state_total = dp_state.finish()
    for partner in (links.to_y, *links.to_z):
        pl.semaphore_signal(credit, inc=1, device_id=partner, device_id_type=pl.DeviceIdType.MESH)
    dp_qkv.sent()
    ship[1] = state_total.astype(bf16)
    grad_sqkv[:, block(2 * (s % 2), lanes)] = ship[1, :, block((s + 1) // 2, lanes)]
    for copy in to_owner[1]:
        copy.start()
    window_back(3)
    dp_grad_down.forward(0)
    back_qkv[:, lanes:] = key_sum[...].astype(bf16)
    small[0, 0:1, :] = jnp.zeros((1, width), f32)
    small[0, 3:4, :] = jnp.zeros((1, width), f32)

    def qkv_grads(i):
        at = block(i, 256)
        token_grads[at, 0 : 3 * lanes] = dot_lt(first[:, at], back_qkv[...]).astype(bf16)

    def first_partial(i):
        at = block(i, rows)
        back = dot_rt(back_qkv[at, :], qkv_nat[...])
        back_first[at, :] = back.astype(bf16)
        hat, _ = normalized(tok_all[at, :].astype(f32))
        small[0, 0:1, :] += jnp.sum(back * hat, axis=0, keepdims=True)
        small[0, 3:4, :] += jnp.sum(back, axis=0, keepdims=True)

    def land(k, grads):
        for copy in to_owner[k]:
            copy.wait_recv()
        grads[:, lanes : 2 * lanes] = landed[k, :, lanes : 2 * lanes]
        x_at = block(2 - 2 * (s % 2), lanes)
        grads[:, x_at] = landed[k, :, x_at]

    for i in range(width // 256):
        qkv_grads(i)
    pl.semaphore_wait(credit, 4)
    dp_grad_qkv.start()
    dp_grad_up_last.start()
    token_grads[:, 3 * lanes : 4 * lanes] = dot_lt(
        mixed[...], back_branch[:, own_columns]
    ).astype(bf16)
    dp_grad_out.start()
    dp_grad_down.combine(1)
    for h in range(heads):
        distance[pl.ds(s * heads + h, 1), :] = jnp.sum(by_distance(band[h]), axis=0, keepdims=True)
    small[0, 8:16, 0 : by_bucket.shape[1]] = lax.dot_general(
        distance[...],
        by_bucket[...],
        (((1,), (0,)), ((), ())),
        precision=lax.Precision.HIGHEST,
        preferred_element_type=f32,
    )
    for i in range(4):
        first_partial(i)
    sum_small.start()
    sum_first.start()
    dp_grad_down.combine(2)
    output[...] = (res_own[...] + sum_ffn.finish()).astype(bf16)
    send_home(output, home_output)
    sum_small.step(0)
    sum_first.middle()
    for k in (1, 2):
        dp_grad_out.combine(k)
    dp_grad_up.forward(1)
    grad_down[...] = dp_grad_down.finish().astype(bf16)
    send_home(grad_down, home_grad_down)
    sum_small.step(1)
    dp_grad_out.middle()
    dp_grad_up.forward(2)
    dp_grad_up.combine(1)
    dp_grad_up.forward(0)
    dp_grad_up.combine(2)
    hat_first, inverse_first = normalized(tok_all[block(s, rows), :].astype(f32))
    back_own_first = sum_first.finish()
    grad_tokens[...] = (
        back_branch[block(s, rows), :].astype(f32)
        + normed_back(back_own_first, hat_first, inverse_first, gains[0:1, :])
    ).astype(bf16)
    send_home(grad_tokens, home_grad_tokens)
    sum_small.step(2)
    dp_grad_qkv.forward(1)
    grad_sout[...] = dp_grad_sout.finish().astype(bf16)
    send_home(grad_sout, home_grad_sout)
    dp_grad_qkv.forward(2)
    grad_up[:, 0:up_cut] = dp_grad_up.finish().astype(bf16)
    send_home(grad_up.at[:, 0:up_cut], home_grad_up.at[:, 0:up_cut])
    land(1, grad_sqkv)
    send_home(grad_sqkv, home_grad_sqkv)
    dp_grad_qkv.combine(1)
    dp_grad_qkv.forward(0)
    sum_small.step(3)
    dp_grad_up_last.forward(1)
    dp_grad_qkv.combine(2)
    dp_grad_up_last.forward(2)
    dp_grad_up_last.forward(0)
    dp_grad_up_last.combine(1)
    dp_grad_up_last.combine(2)
    grad_out[...] = dp_grad_out.finish().astype(bf16)
    send_home(grad_out, home_grad_out)
    ship[0] = dp_grad_qkv.finish().astype(bf16)
    for copy in to_owner[0]:
        copy.start()
    grad_qkv[:, block(2 * (s % 2), lanes)] = ship[0, :, block((s + 1) // 2, lanes)]
    sum_small.step(4)
    grad_norm[...] = small[5, 0:8, :]
    grad_rel[...] = small[5, 8:16, 0:128]
    send_home(grad_norm, home_grad_norm)
    send_home(grad_rel, home_grad_rel)
    grad_up[:, up_cut:] = dp_grad_up_last.finish().astype(bf16)
    send_home(grad_up.at[:, up_cut:], home_grad_up.at[:, up_cut:])
    land(0, grad_qkv)
    send_home(grad_qkv, home_grad_qkv)
    for over_x, beside in (*to_slab, *to_owner):
        over_x.wait_send()
        beside.wait_send()
    for used in (
        get_tokens,
        get_mixed,
        *block_sums,
        sum_ffn,
        sum_first,
        dp_state,
        dp_grad_sout,
        dp_grad_down,
        dp_grad_up,
        dp_grad_up_last,
        dp_grad_out,
        dp_grad_qkv,
        sum_small,
    ):
        used.sent()
    for copy in leaving:
        copy.wait()


def settle(*refs):
    values, results, rest = refs[:12], refs[12:26], refs[26:]
    held, widened, (read_sem, write_sem) = rest[:10], rest[10:16], rest[16:]
    reads = [pltpu.make_async_copy(values[k], held[k], read_sem.at[k]) for k in range(10)]
    for copy in reads:
        copy.start()
    writes = []
    for k in range(10):
        reads[k].wait()
        target = results[k].at[0] if len(results[k].shape) == 3 else results[k]
        ready = held[k]
        if k >= 4:
            ready = widened[k - 4]
            ready[...] = held[k][...].astype(f32)
        writes.append(pltpu.make_async_copy(ready, target, write_sem.at[k]))
        writes[-1].start()
    rel, gain, shift, gate = results[10:]
    grad_rel, grad_norm = values[10:]
    rel[...] = grad_rel[:, 0 : rel.shape[1]]
    gain[...] = grad_norm[0:3, :]
    shift[...] = grad_norm[3:6, :]
    gate[...] = grad_norm[6, :]
    for copy in writes:
        copy.wait()


def norm_back(values, back, gain):
    hat, inverse = normalized(values)
    return normed_back(back, hat, inverse, gain)


def per_device(
    tokens,
    state_in,
    cotangent,
    state_cotangent,
    seq_len,
    bucket_table,
    w_qkv,
    w_out,
    w_sqkv,
    w_sout,
    w_up,
    w_down,
    rel_table,
    norm_gain,
    norm_shift,
    gate_bias,
):
    rows, width = tokens.shape
    bucket_count, head_count = rel_table.shape
    window = bucket_table.shape[0]
    state_rows = state_in.shape[1]
    places = lax.axis_size("state")
    assert places == len(PLACES)
    dp_count = lax.axis_size("dp")
    here, dp_here = lax.axis_index("state"), lax.axis_index("dp")
    head_dim = width // head_count
    heads = head_count // places
    lanes = heads * head_dim
    span = window + rows
    group_rows = rows * places
    all_states = state_rows * places
    inner_width = w_up.shape[1]
    hops = dp_count == len(DP_PLACES)
    blocks = dp_count if hops else 1

    def swap(value, axis, bit):
        count = lax.axis_size(axis)
        return lax.ppermute(value, axis, [(i, i ^ bit) for i in range(count)])

    def from_group(value):
        pair = jnp.stack([value, swap(value, "state", 2)])
        return jnp.concatenate([pair, swap(pair, "state", 1)], axis=0)

    def list_from_group(value):
        across = swap(value, "state", 2)
        return [value, across, swap(value, "state", 1), swap(across, "state", 1)]

    def sum_to_owner(partial):
        half = partial.shape[0] // 2
        pair = partial[:half].astype(f32) + swap(partial[half:], "state", 1).astype(f32)
        return pair[0] + swap(pair[1].astype(bf16), "state", 2).astype(f32)

    def from_dp(block, axis):
        if not hops:
            return lax.all_gather(block, "dp", axis=axis, tiled=True)[None]
        gathered = block[None]
        for bit in DP_STEPS:
            gathered = jnp.concatenate([gathered, swap(gathered, "dp", bit)], axis=0)
        return gathered

    def sum_over_dp(partial, axis):
        if not hops:
            return lax.psum_scatter(partial[0], "dp", scatter_dimension=axis, tiled=True).astype(f32)
        for bit in reversed(DP_STEPS):
            half = partial.shape[0] // 2
            arrived = swap(partial[half:], "dp", bit)
            total = partial[:half].astype(f32) + arrived.astype(f32)
            partial = total.astype(bf16)
        return total[0]

    def sum_over_all(vector):
        if not hops:
            return lax.psum(vector, ("dp", "state"))
        for axis, bit in (("state", 1), ("state", 2), ("dp", 1), ("dp", 2), ("dp", 4)):
            vector = vector + swap(vector, axis, bit)
        return vector

    even = here % 2 == 0

    def pick(*by_place):
        value = by_place[-1]
        for i in reversed(range(places - 1)):
            value = jnp.where(here == i, by_place[i], value)
        return value

    def to_heads(shard):
        left, middle, right = (shard[:, i * lanes : (i + 1) * lanes] for i in range(3))
        own = jnp.where(even, left, right)
        across = swap(jnp.where(even, right, left), "state", 2)
        beside = swap(middle, "state", 1)
        query = pick(own, beside, across, across)
        keys = pick(beside, own, own, beside)
        values = pick(across, across, beside, own)
        return jnp.concatenate([query, keys, values], axis=1)

    def from_heads(grads):
        query, keys, values = (grads[:, i * lanes : (i + 1) * lanes] for i in range(3))
        own = pick(query, keys, keys, values)
        beside = swap(pick(keys, query, values, keys), "state", 1)
        across = swap(pick(values, values, query, query), "state", 2)
        return jnp.concatenate(
            [jnp.where(even, own, across), beside, jnp.where(even, across, own)], axis=1
        )

    if hops:
        block_list = dp_here ^ jnp.array(DP_PLACES, jnp.int32)
        position_list = jnp.array(
            [DP_PLACES.index(i) for i in range(dp_count)], jnp.int32
        )[dp_here ^ jnp.arange(dp_count)]
    else:
        block_list = position_list = jnp.zeros((1,), jnp.int32)
    scal = jnp.concatenate(
        [here[None].astype(jnp.int32), seq_len.astype(jnp.int32), block_list, position_list]
    ).astype(jnp.int32)

    gains = [norm_gain[i : i + 1] for i in range(3)]
    shifts = [norm_shift[i : i + 1] for i in range(3)]

    depth = w_qkv.shape[0]
    if hops:
        whole = pl.BlockSpec(memory_space=pltpu.VMEM)
        anywhere = pl.BlockSpec(memory_space=pl.ANY)
        vmem = lambda shape, kind=bf16: pltpu.VMEM(shape, kind)
        square = vmem((width, width))
        grad_blocks = lambda kind: [
            vmem(shape, kind)
            for shape in (
                (depth, 3 * lanes),
                (depth, lanes),
                (depth, 3 * lanes),
                (depth, lanes),
                (depth, inner_width),
                (inner_width, depth),
            )
        ]
        summed = pl.pallas_call(
            functools.partial(layer, head_dim),
            out_shape=[
                out((rows, width)),
                out((state_rows, width)),
                out((rows, width)),
                out((state_rows, width)),
                out((depth, 3 * lanes)),
                out((depth, lanes)),
                out((depth, 3 * lanes)),
                out((depth, lanes)),
                out((depth, inner_width)),
                out((inner_width, depth)),
                out((head_count, 128), f32),
                out((8, width), f32),
            ],
            in_specs=[pl.BlockSpec(memory_space=pltpu.SMEM)] + [anywhere] * 10 + [whole] * 5,
            out_specs=[anywhere] * 12,
            scratch_shapes=[
                pltpu.SemaphoreType.DMA((LAYER_COPIES,)),
                pltpu.SemaphoreType.DMA((LAYER_COPIES,)),
                pltpu.SemaphoreType.DMA((16,)),
                vmem((2, depth, 3 * lanes)),
                vmem((width, 3 * lanes)),
                vmem((width, 3 * lanes)),
                square,
                square,
                vmem((width, inner_width)),
                vmem((inner_width, width)),
                vmem((group_rows, width)),
                vmem((group_rows, width)),
                vmem((2 * all_states, width)),
                vmem((group_rows, width)),
                vmem((all_states, width)),
                vmem((2 * all_states, width)),
                vmem((group_rows, width)),
                vmem((group_rows, 3 * lanes)),
                vmem((group_rows, width)),
                vmem((all_states, 3 * lanes)),
                vmem((all_states, lanes)),
                vmem((all_states, 3 * lanes)),
                vmem((all_states, 2 * lanes), f32),
                vmem((group_rows, 2 * lanes), f32),
                vmem((rows, width), f32),
                vmem((group_rows // 2, width)),
                vmem((group_rows // 2, 128), f32),
                vmem((heads, rows, span), f32),
                vmem((heads, rows, span), f32),
                vmem((lanes, width)),
                square,
                vmem((inner_width, width)),
                vmem((4, depth, 3 * lanes)),
                vmem((4, inner_width, depth)),
                vmem((4, depth, inner_width)),
                vmem((depth, lanes)),
                vmem((depth, lanes)),
                vmem((4, depth, 3 * lanes)),
                vmem((4, inner_width, depth)),
                vmem((4, depth, inner_width)),
                vmem((4, 2 * depth, lanes)),
                vmem((4, 2 * depth, lanes)),
                vmem((2, rows, width)),
                vmem((2, rows, width)),
                vmem((2, rows, width)),
                vmem((rows, width)),
                vmem((6, 16, width), f32),
                vmem((5, 16, width), f32),
                vmem((8, span), f32),
                vmem((2, depth, 3 * lanes)),
                pltpu.SemaphoreType.REGULAR,
                vmem((span, bucket_count), f32),
                pltpu.SemaphoreType.DMA((16,)),
                vmem((rows, width)),
                vmem((state_rows, width)),
                vmem((rows, width)),
                vmem((state_rows, width)),
                *grad_blocks(bf16),
                vmem((head_count, 128), f32),
                vmem((8, width), f32),
            ],
            compiler_params=pltpu.CompilerParams(
                collective_id=0, has_side_effects=True, vmem_limit_bytes=64 << 20
            ),
            name="layer",
        )(
            seq_len,
            tokens,
            state_in[0],
            cotangent,
            state_cotangent[0],
            w_qkv,
            w_out,
            w_sqkv,
            w_sout,
            w_up,
            w_down,
            bucket_table[None],
            rel_table.T,
            norm_gain,
            norm_shift,
            gate_bias[None],
        )
        results = pl.pallas_call(
            settle,
            out_shape=[
                out((rows, width)),
                out((1, state_rows, width)),
                out((rows, width)),
                out((1, state_rows, width)),
                out((depth, 3 * lanes), f32),
                out((depth, lanes), f32),
                out((depth, 3 * lanes), f32),
                out((depth, lanes), f32),
                out((depth, inner_width), f32),
                out((inner_width, depth), f32),
                out((head_count, bucket_count), f32),
                out((3, width), f32),
                out((3, width), f32),
                out((width,), f32),
            ],
            in_specs=[anywhere] * 10 + [whole] * 2,
            out_specs=[anywhere] * 10 + [whole] * 4,
            scratch_shapes=[
                vmem((rows, width)),
                vmem((state_rows, width)),
                vmem((rows, width)),
                vmem((state_rows, width)),
                *grad_blocks(bf16),
                *grad_blocks(f32),
                pltpu.SemaphoreType.DMA((10,)),
                pltpu.SemaphoreType.DMA((10,)),
            ],
            compiler_params=pltpu.CompilerParams(vmem_limit_bytes=60 << 20),
            name="settle",
        )(*summed)
        return (*results[:10], results[10].T, *results[11:])

    lookup = (bucket_table[:, None] == jnp.arange(bucket_count)[None, :]).astype(f32)
    own_table = lax.dynamic_slice_in_dim(rel_table, here * heads, heads, 1)
    bias_rows = jnp.dot(
        own_table.T, lookup.T, precision=lax.Precision.HIGHEST, preferred_element_type=f32
    )
    bias = jnp.concatenate(
        [
            jnp.full((heads, 1), masked_value, f32),
            bias_rows[:, ::-1],
            jnp.full((heads, span - window - 1), masked_value, f32),
        ],
        axis=1,
    )
    both = to_heads(jnp.concatenate([w_qkv, w_sqkv], axis=0))
    full_qkv = from_dp(both[:depth], 0)
    all_tokens = from_group(tokens)
    full_sqkv = from_dp(both[depth:], 0)
    all_state = from_group(state_in[0])
    all_cot = from_group(cotangent)
    all_state_cot = from_group(state_cotangent[0])
    outs_pair = from_dp(jnp.concatenate([w_out, w_sout], axis=1), 0)
    half = outs_pair.shape[2] // 2
    full_sout = list_from_group(outs_pair[:, :, half:])
    full_out = list_from_group(outs_pair[:, :, :half])
    full_up = from_dp(w_up, 0)
    full_down = from_dp(w_down, 1)

    first, qkv, mixed = call(
        functools.partial(token_forward, head_dim),
        "token_forward",
        [out((group_rows, width)), out((group_rows, 3 * lanes)), out((places, rows, lanes))],
        [pltpu.VMEM((width, 3 * lanes), bf16), pltpu.VMEM((heads, rows, span), f32)],
        2 * group_rows * width * 3 * lanes,
        group_rows * span * heads,
        scal,
        all_tokens,
        gains[0],
        shifts[0],
        full_qkv,
        bias,
    )
    mixed_parts = list_from_group(mixed)

    state_norm, sqkv, read = call(
        functools.partial(state_forward, head_dim),
        "state_forward",
        [
            out((all_states, width)),
            out((all_states, 3 * lanes)),
            out((places, state_rows, lanes)),
        ],
        [pltpu.VMEM((width, 3 * lanes), bf16)],
        2 * all_states * width * 3 * lanes,
        all_states * (all_states + group_rows) * heads,
        scal,
        all_state,
        gains[2],
        shifts[2],
        full_sqkv,
        qkv,
    )
    read_parts = list_from_group(read)

    next_state, grad_gate, grad_sout, token_back, grad_sqkv, back_state_norm, state_sums = call(
        functools.partial(state_backward, head_dim),
        "state_backward",
        [
            out((state_rows, width)),
            out((1, width), f32),
            out((blocks, width // blocks, lanes)),
            out((group_rows, 2 * lanes), f32),
            out((blocks, width // blocks, 3 * lanes)),
            out((places, state_rows, width)),
            out((2, width), f32),
        ],
        [
            pltpu.VMEM((width, 3 * lanes), bf16),
            pltpu.VMEM((width, width), bf16),
            pltpu.VMEM((all_states, width), bf16),
            pltpu.VMEM((all_states, lanes), bf16),
            pltpu.VMEM((all_states, 3 * lanes), bf16),
            pltpu.VMEM((all_states, 2 * lanes), f32),
        ],
        4 * all_states * width * 4 * lanes,
        all_states * (all_states + group_rows) * heads,
        scal,
        state_in[0],
        all_state_cot,
        gate_bias[None],
        all_state,
        *read_parts,
        *full_sout,
        sqkv,
        qkv,
        state_norm,
        full_sqkv,
    )
    residual, second, hidden, slope, out_rows, grad_down = call(
        ffn_up,
        "ffn_up",
        [
            out((places, rows, width), f32),
            out((group_rows, width)),
            out((group_rows, inner_width)),
            out((group_rows, inner_width)),
            out((lanes, width)),
            out((blocks, inner_width, width // blocks)),
        ],
        [pltpu.VMEM((width, width), bf16), pltpu.VMEM((width, inner_width), bf16)],
        2 * group_rows * width * (width + 2 * inner_width),
        group_rows * inner_width,
        scal,
        all_tokens,
        *mixed_parts,
        *full_out,
        gains[1],
        shifts[1],
        full_up,
        all_cot,
    )

    back_second, back_input, mid_sums = call(
        ffn_back,
        "ffn_back",
        [
            out((places, rows, width)),
            out((group_rows, inner_width)),
            out((2, width), f32),
        ],
        [pltpu.VMEM((inner_width, width), bf16), pltpu.VMEM((width, inner_width), bf16)],
        4 * group_rows * width * inner_width,
        0,
        scal,
        all_cot,
        full_down,
        full_up,
        slope,
        residual,
    )
    residual_own = residual[0]
    own_grad_sout = sum_over_dp(grad_sout, 0)
    own_grad_sqkv = sum_over_dp(grad_sqkv, 0)
    back_state = sum_to_owner(back_state_norm)
    gate_open = jax.nn.sigmoid(gate_bias)
    grad_state = (
        gate_open * state_cotangent[0].astype(f32)
        + norm_back(state_in[0].astype(f32), back_state, norm_gain[2])
    ).astype(bf16)

    own_grad_down = sum_over_dp(grad_down, 1)
    back_second = sum_to_owner(back_second)
    back_residual = cotangent.astype(f32) + norm_back(residual_own, back_second, norm_gain[1])
    back_branch = from_group(back_residual.astype(bf16))

    ffn_partial, grad_up = call(
        ffn_rest,
        "ffn_rest",
        [out((places, rows, width)), out((blocks, width // blocks, inner_width))],
        [pltpu.VMEM((inner_width, width), bf16)],
        4 * group_rows * width * inner_width,
        0,
        scal,
        hidden,
        full_down,
        second,
        back_input,
    )
    own_grad_up = sum_over_dp(grad_up, 0)
    output = (residual_own + sum_to_owner(ffn_partial)).astype(bf16)

    (grad_out,) = call(
        out_grad,
        "out_grad",
        [out((blocks, width // blocks, lanes))],
        [],
        2 * group_rows * width * lanes,
        0,
        scal,
        back_branch,
        *mixed_parts,
    )
    own_grad_out = sum_over_dp(grad_out, 0)

    grad_qkv, back_first, first_sums, distance = call(
        functools.partial(token_backward, head_dim),
        "token_backward",
        [
            out((blocks, width // blocks, 3 * lanes)),
            out((places, rows, width)),
            out((2, width), f32),
            out((heads, span), f32),
        ],
        [
            pltpu.VMEM((width, 3 * lanes), bf16),
            pltpu.VMEM((heads, rows, span), f32),
            pltpu.VMEM((group_rows, lanes), bf16),
            pltpu.VMEM((group_rows, 3 * lanes), bf16),
            pltpu.VMEM((group_rows, 2 * lanes), f32),
            pltpu.VMEM((rows, span), f32),
        ],
        2 * group_rows * width * 7 * lanes,
        group_rows * span * heads,
        scal,
        back_branch,
        out_rows,
        qkv,
        bias,
        token_back,
        first,
        all_tokens,
        full_qkv,
    )
    back_first = sum_to_owner(back_first)
    grad_tokens = (
        norm_back(tokens.astype(f32), back_first, norm_gain[0]) + back_residual
    ).astype(bf16)
    own_grad_qkv = sum_over_dp(grad_qkv, 0)
    both_grads = from_heads(
        jnp.concatenate([own_grad_qkv, own_grad_sqkv], axis=0).astype(bf16)
    ).astype(f32)

    per_distance = distance[:, 1 : window + 1][:, ::-1]
    own_rel = jnp.dot(
        per_distance, lookup, precision=lax.Precision.HIGHEST, preferred_element_type=f32
    ).T
    grad_rel = lax.dynamic_update_slice_in_dim(
        jnp.zeros((bucket_count, head_count), f32), own_rel, here * heads, 1
    )
    small = [
        jnp.stack([first_sums[0], mid_sums[0], state_sums[0]]),
        jnp.stack([first_sums[1], mid_sums[1], state_sums[1]]),
        grad_gate[0],
        grad_rel,
    ]
    packed = sum_over_all(jnp.concatenate([v.reshape(-1, 128) for v in small], axis=0))
    unpacked, start = [], 0
    for v in small:
        count = v.size // 128
        unpacked.append(packed[start : start + count].reshape(v.shape))
        start += count
    return (
        output,
        next_state[None],
        grad_tokens,
        grad_state[None],
        both_grads[:depth],
        own_grad_out,
        both_grads[depth:],
        own_grad_sout,
        own_grad_up,
        own_grad_down,
        unpacked[3],
        unpacked[0],
        unpacked[1],
        unpacked[2],
    )


def solution(mesh):
    rows_spec = P(("dp", "state"), None)
    state_spec = P("dp", "state", None)
    weight_spec = P("dp", "state")
    return jax.shard_map(
        per_device,
        mesh=mesh,
        in_specs=(
            rows_spec,
            state_spec,
            rows_spec,
            state_spec,
            P("dp"),
            P(),
            weight_spec,
            weight_spec,
            weight_spec,
            weight_spec,
            weight_spec,
            P("state", "dp"),
            P(),
            P(),
            P(),
            P(),
        ),
        out_specs=(
            rows_spec,
            state_spec,
            rows_spec,
            state_spec,
            weight_spec,
            weight_spec,
            weight_spec,
            weight_spec,
            weight_spec,
            P("state", "dp"),
            P(),
            P(),
            P(),
            P(),
        ),
        check_vma=False,
    )
```

```python
import functools

import jax
import jax.numpy as jnp
from jax import lax
from jax.experimental import pallas as pl
from jax.experimental.pallas import tpu as pltpu
from jax.sharding import PartitionSpec as P

epsilon = 1e-05
masked_value = -1e30
f32 = jnp.float32
bf16 = jnp.bfloat16

PLACES = (0, 2, 1, 3)
DP_STEPS = (2, 4, 1)
DP_PLACES = (0, 2, 4, 6, 1, 3, 5, 7)


def dot(left, right):
    return lax.dot_general(left, right, (((1,), (0,)), ((), ())), preferred_element_type=f32)


def dot_rt(left, right):
    return lax.dot_general(left, right, (((1,), (1,)), ((), ())), preferred_element_type=f32)


def dot_lt(left, right):
    return lax.dot_general(left, right, (((0,), (0,)), ((), ())), preferred_element_type=f32)


def where_from(sender, place):
    return PLACES.index(PLACES[sender] ^ PLACES[place])


def normalized(values):
    centre = jnp.mean(values, axis=-1, keepdims=True)
    centred = values - centre
    spread = jnp.mean(centred * centred, axis=-1, keepdims=True)
    inverse = lax.rsqrt(spread + epsilon)
    return centred * inverse, inverse


def normed_back(back, hat, inverse, gain):
    grown = back * gain
    return inverse * (
        grown
        - jnp.mean(grown, axis=-1, keepdims=True)
        - hat * jnp.mean(grown * hat, axis=-1, keepdims=True)
    )


def place_of(scal, q):
    return scal[0] ^ PLACES[q]


def aligned(start, size):
    return pl.ds(pl.multiple_of(start, size), size)


def block_at(scal, q):
    return scal[2 + q]


def position_of(scal, block, blocks):
    return scal[2 + blocks + block]


def rows_in_order(scal, target, source):
    blocks, depth = source.shape[0], source.shape[1]
    for q in range(blocks):
        target[aligned(block_at(scal, q) * depth, depth), :] = source[q]


def columns_in_order(scal, target, source):
    blocks, depth = source.shape[0], source.shape[2]
    for q in range(blocks):
        target[:, aligned(block_at(scal, q) * depth, depth)] = source[q]


def put_rows(scal, target, start, value):
    blocks, depth = target.shape[0], target.shape[1]
    rows = value.shape[0]
    if depth >= rows:
        target[position_of(scal, start // depth, blocks), aligned(start % depth, rows), :] = value
    else:
        for i in range(rows // depth):
            position = position_of(scal, start // depth + i, blocks)
            target[position] = value[i * depth : (i + 1) * depth]


def put_columns(scal, target, start, value):
    blocks, depth = target.shape[0], target.shape[2]
    columns = value.shape[1]
    if depth >= columns:
        target[position_of(scal, start // depth, blocks), :, aligned(start % depth, columns)] = value
    else:
        for i in range(columns // depth):
            position = position_of(scal, start // depth + i, blocks)
            target[position] = value[:, i * depth : (i + 1) * depth]


def call(body, name, outs, scratch, flops, exps, *args):
    sizes = sum(a.size * a.dtype.itemsize for a in args) + sum(
        a.size * a.dtype.itemsize for a in outs
    )
    in_specs = [pl.BlockSpec(memory_space=pltpu.SMEM)] + [
        pl.BlockSpec(memory_space=pltpu.VMEM) for _ in args[1:]
    ]
    return pl.pallas_call(
        body,
        out_shape=outs,
        in_specs=in_specs,
        out_specs=[pl.BlockSpec(memory_space=pltpu.VMEM) for _ in outs],
        scratch_shapes=scratch,
        compiler_params=pltpu.CompilerParams(vmem_limit_bytes=56 << 20),
        cost_estimate=pl.CostEstimate(flops=flops, bytes_accessed=sizes, transcendentals=exps),
        name=name,
    )(*args)


def out(shape, kind=bf16):
    return jax.ShapeDtypeStruct(shape, kind)


def by_distance(scores):
    rows, span = scores.shape
    row_at = lax.broadcasted_iota(jnp.int32, scores.shape, 0)
    step = 1
    while step < rows:
        scores = jnp.where(row_at & step != 0, pltpu.roll(scores, span - step, 1), scores)
        step *= 2
    return scores


def bias_blocks(tb, bias):
    heads, rows, span = tb.shape
    for h in range(heads):
        row = jnp.broadcast_to(bias[h], (rows, span))
        tb[h] = pltpu.roll(row, 0, 1, stride=1, stride_axis=0)


def window_probs(scal, query, keys, tb_block, last, scale):
    rows, span = tb_block.shape
    count = keys.shape[0]
    scores = dot_rt(query, keys) * scale + tb_block[:, span - count :]
    if last:
        row_at = lax.broadcasted_iota(jnp.int32, scores.shape, 0)
        col_at = lax.broadcasted_iota(jnp.int32, scores.shape, 1)
        ahead = col_at - (count - rows)
        live = (ahead < scal[1] - last) | (ahead == row_at)
        scores = jnp.where(live, scores, masked_value)
    top = jnp.max(scores, axis=-1, keepdims=True)
    grown = jnp.exp(scores - top)
    return grown * (1.0 / jnp.sum(grown, axis=-1, keepdims=True))


def state_probs(scal, query, state_keys, keys, scale):
    own = dot_rt(query, state_keys) * scale
    token = dot_rt(query, keys) * scale
    col_at = lax.broadcasted_iota(jnp.int32, token.shape, 1)
    token = jnp.where(col_at < scal[1], token, masked_value)
    top = jnp.maximum(
        jnp.max(own, axis=-1, keepdims=True), jnp.max(token, axis=-1, keepdims=True)
    )
    own = jnp.exp(own - top)
    token = jnp.exp(token - top)
    total = jnp.sum(own, axis=-1, keepdims=True) + jnp.sum(token, axis=-1, keepdims=True)
    inverse = 1.0 / total
    return own * inverse, token * inverse


def head_cols(block, h, heads, head_dim):
    start = (block * heads + h) * head_dim
    return slice(start, start + head_dim)


def token_forward(head_dim, scal, tokens, gain, shift, w_qkv, bias, first, qkv, mixed, w_nat, tb):
    places, rows, width = tokens.shape
    heads = bias.shape[0]
    span = bias.shape[1]
    scale = head_dim ** (-0.5)
    rows_in_order(scal, w_nat, w_qkv)
    bias_blocks(tb, [bias[h : h + 1, :] for h in range(heads)])
    for q in range(places):
        hat, _ = normalized(tokens[q].astype(f32))
        normed = (hat * gain[...] + shift[...]).astype(bf16)
        at = aligned(place_of(scal, q) * rows, rows)
        first[at, :] = normed
        qkv[at, :] = dot(normed, w_nat[...]).astype(bf16)
    for c in range(places):
        count = min(span, (c + 1) * rows)
        low, high = (c + 1) * rows - count, (c + 1) * rows
        last = c * rows if c == places - 1 else 0
        parts = []
        for h in range(heads):
            probs = window_probs(
                scal,
                qkv[c * rows : high, head_cols(0, h, heads, head_dim)],
                qkv[low:high, head_cols(1, h, heads, head_dim)],
                tb[h],
                last,
                scale,
            )
            parts.append(
                dot(probs.astype(bf16), qkv[low:high, head_cols(2, h, heads, head_dim)])
            )
        mixed[c] = jnp.concatenate(parts, axis=1).astype(bf16)


def state_forward(
    head_dim, scal, state, gain, shift, w_sqkv, qkv, normed_out, sqkv, read, w_nat
):
    places, rows, width = state.shape
    heads = qkv.shape[1] // (3 * head_dim)
    scale = head_dim ** (-0.5)
    rows_in_order(scal, w_nat, w_sqkv)
    for q in range(places):
        hat, _ = normalized(state[q].astype(f32))
        normed = (hat * gain[...] + shift[...]).astype(bf16)
        normed_out[q * rows : (q + 1) * rows, :] = normed
        sqkv[q * rows : (q + 1) * rows, :] = dot(normed, w_nat[...]).astype(bf16)
    for q in range(places):
        parts = []
        for h in range(heads):
            own, token = state_probs(
                scal,
                sqkv[q * rows : (q + 1) * rows, head_cols(0, h, heads, head_dim)],
                sqkv[:, head_cols(1, h, heads, head_dim)],
                qkv[:, head_cols(1, h, heads, head_dim)],
                scale,
            )
            parts.append(
                dot(own.astype(bf16), sqkv[:, head_cols(2, h, heads, head_dim)])
                + dot(token.astype(bf16), qkv[:, head_cols(2, h, heads, head_dim)])
            )
        read[q] = jnp.concatenate(parts, axis=1).astype(bf16)


def assembled(scal, target, parts):
    for p, part in enumerate(parts):
        blocks, depth, columns = part.shape
        at = aligned(place_of(scal, p) * columns, columns)
        for q in range(blocks):
            target[aligned(block_at(scal, q) * depth, depth), at] = part[q]


def state_backward(
    head_dim,
    scal,
    state_own,
    state_cot,
    gate_bias,
    state,
    read0,
    read1,
    read2,
    read3,
    out0,
    out1,
    out2,
    out3,
    sqkv,
    qkv,
    normed,
    w_sqkv,
    next_state,
    grad_gate,
    grad_sout,
    token_back,
    grad_sqkv,
    back_norm,
    grad_norm,
    w_nat,
    w_out,
    back_update,
    back_read,
    back_sqkv,
    own_sum,
):
    places, rows, width = state_cot.shape
    reads = (read0, read1, read2, read3)
    heads = qkv.shape[1] // (3 * head_dim)
    lanes = heads * head_dim
    scale = head_dim ** (-0.5)
    rows_in_order(scal, w_nat, w_sqkv)
    assembled(scal, w_out, (out0, out1, out2, out3))
    gate = jax.nn.sigmoid(gate_bias[...])
    update = None
    for p in range(places):
        term = dot(reads[p][p], w_out[aligned(place_of(scal, p) * lanes, lanes), :])
        update = term if update is None else update + term
    held = state_own[...].astype(f32)
    cot = state_cot[0].astype(f32)
    next_state[...] = (gate * held + (1.0 - gate) * update).astype(bf16)
    grad_gate[...] = jnp.sum(cot * (held - update), axis=0, keepdims=True) * (gate * (1.0 - gate))
    for q in range(places):
        back_update[q * rows : (q + 1) * rows, :] = (
            (1.0 - gate) * state_cot[q].astype(f32)
        ).astype(bf16)
    own_columns = back_update[:, aligned(scal[0] * lanes, lanes)]
    for p in range(places):
        stack = jnp.concatenate([reads[p][where_from(p, q)] for q in range(places)], axis=0)
        put_rows(
            scal, grad_sout, place_of(scal, p) * lanes, dot_lt(stack, own_columns).astype(bf16)
        )
    back_read[...] = dot_rt(
        back_update[...], w_out[aligned(scal[0] * lanes, lanes), :]
    ).astype(bf16)
    for h in range(heads):
        key_at, value_at = head_cols(1, h, heads, head_dim), head_cols(2, h, heads, head_dim)
        query_at, read_at = head_cols(0, h, heads, head_dim), slice(h * head_dim, (h + 1) * head_dim)
        for q in range(places):
            at = slice(q * rows, (q + 1) * rows)
            query, back = sqkv[at, query_at], back_read[at, read_at]
            own, token = state_probs(scal, query, sqkv[:, key_at], qkv[:, key_at], scale)
            back_own = dot_rt(back, sqkv[:, value_at])
            back_token = dot_rt(back, qkv[:, value_at])
            row_dot = jnp.sum(own * back_own, axis=-1, keepdims=True) + jnp.sum(
                token * back_token, axis=-1, keepdims=True
            )
            own_raw = (own * (back_own - row_dot) * scale).astype(bf16)
            token_raw = (token * (back_token - row_dot) * scale).astype(bf16)
            back_sqkv[at, query_at] = (
                dot(own_raw, sqkv[:, key_at]) + dot(token_raw, qkv[:, key_at])
            ).astype(bf16)
            terms = (
                (own_sum, key_at, dot_lt(own_raw, query)),
                (own_sum, value_at, dot_lt(own.astype(bf16), back)),
                (token_back, key_at, dot_lt(token_raw, query)),
                (token_back, value_at, dot_lt(token.astype(bf16), back)),
            )
            for target, columns, term in terms:
                columns = slice(columns.start - lanes, columns.stop - lanes)
                if q == 0:
                    target[:, columns] = term
                else:
                    target[:, columns] += term
    back_sqkv[:, lanes:] = own_sum[...].astype(bf16)
    for start in range(0, width, 256):
        put_rows(
            scal,
            grad_sqkv,
            start,
            dot_lt(normed[:, start : start + 256], back_sqkv[...]).astype(bf16),
        )
    gain_sum, shift_sum = None, None
    for q in range(places):
        back = dot_rt(back_sqkv[q * rows : (q + 1) * rows, :], w_nat[...])
        back_norm[q] = back.astype(bf16)
        hat, _ = normalized(state[q].astype(f32))
        gain_term = jnp.sum(back * hat, axis=0, keepdims=True)
        shift_term = jnp.sum(back, axis=0, keepdims=True)
        gain_sum = gain_term if q == 0 else gain_sum + gain_term
        shift_sum = shift_term if q == 0 else shift_sum + shift_term
    grad_norm[0:1, :] = gain_sum
    grad_norm[1:2, :] = shift_sum


def ffn_up(
    scal,
    tokens,
    mixed0,
    mixed1,
    mixed2,
    mixed3,
    out0,
    out1,
    out2,
    out3,
    gain,
    shift,
    w_up,
    cot,
    residual,
    second,
    hidden,
    slope,
    out_rows,
    grad_down,
    w_out,
    w_nat,
):
    places, rows, width = tokens.shape
    mixed = (mixed0, mixed1, mixed2, mixed3)
    lanes = mixed0.shape[2]
    assembled(scal, w_out, (out0, out1, out2, out3))
    out_rows[...] = w_out[aligned(scal[0] * lanes, lanes), :]
    rows_in_order(scal, w_nat, w_up)
    for q in range(places):
        total = tokens[q].astype(f32)
        for p in range(places):
            total += dot(
                mixed[p][place_of(scal, q)], w_out[aligned(place_of(scal, p) * lanes, lanes), :]
            )
        residual[q] = total
        hat, _ = normalized(total)
        normed = (hat * gain[...] + shift[...]).astype(bf16)
        at = slice(q * rows, (q + 1) * rows)
        second[at, :] = normed
        inner = dot(normed, w_nat[...])
        root = 0.7978845608028654
        square = inner * inner
        bend = jnp.tanh(root * inner * (1.0 + 0.044715 * square))
        half = 0.5 * (1.0 + bend)
        hidden[at, :] = (inner * half).astype(bf16)
        slope[at, :] = (
            half + (0.5 * root) * inner * (1.0 - bend * bend) * (1.0 + (3 * 0.044715) * square)
        ).astype(bf16)
    for start in range(0, width, 256):
        columns = jnp.concatenate([cot[q, :, start : start + 256] for q in range(places)], axis=0)
        put_columns(scal, grad_down, start, dot_lt(hidden[...], columns).astype(bf16))


def ffn_back(
    scal,
    cot,
    w_down,
    w_up,
    slope,
    residual,
    back_second,
    back_input,
    grad_norm,
    w_nat,
    w_up_nat,
):
    places, rows, width = cot.shape
    columns_in_order(scal, w_nat, w_down)
    rows_in_order(scal, w_up_nat, w_up)
    gain_sum, shift_sum = None, None
    for q in range(places):
        at = slice(q * rows, (q + 1) * rows)
        inner = (dot_rt(cot[q], w_nat[...]) * slope[at, :].astype(f32)).astype(bf16)
        back_input[at, :] = inner
        back = dot_rt(inner, w_up_nat[...])
        back_second[q] = back.astype(bf16)
        hat, _ = normalized(residual[q])
        gain_term = jnp.sum(back * hat, axis=0, keepdims=True)
        shift_term = jnp.sum(back, axis=0, keepdims=True)
        gain_sum = gain_term if q == 0 else gain_sum + gain_term
        shift_sum = shift_term if q == 0 else shift_sum + shift_term
    grad_norm[0:1, :] = gain_sum
    grad_norm[1:2, :] = shift_sum


def ffn_rest(scal, hidden, w_down, second, back_input, partial, grad_up, w_nat):
    places, rows, width = partial.shape
    for start in range(0, width, 256):
        put_rows(
            scal,
            grad_up,
            start,
            dot_lt(second[:, start : start + 256], back_input[...]).astype(bf16),
        )
    columns_in_order(scal, w_nat, w_down)
    for q in range(places):
        partial[q] = dot(hidden[q * rows : (q + 1) * rows, :], w_nat[...]).astype(bf16)


def out_grad(scal, back_branch, mixed0, mixed1, mixed2, mixed3, grad_out):
    places, rows, width = back_branch.shape
    mixed = (mixed0, mixed1, mixed2, mixed3)
    lanes = mixed0.shape[2]
    own_at = aligned(scal[0] * lanes, lanes)
    own_columns = jnp.concatenate([back_branch[q, :, own_at] for q in range(places)], axis=0)
    for p in range(places):
        stack = jnp.concatenate([mixed[p][place_of(scal, q)] for q in range(places)], axis=0)
        put_rows(
            scal, grad_out, place_of(scal, p) * lanes, dot_lt(stack, own_columns).astype(bf16)
        )


def token_backward(
    head_dim,
    scal,
    back_branch,
    out_rows,
    qkv,
    bias,
    token_back,
    first,
    tokens,
    w_qkv,
    grad_qkv,
    back_first,
    grad_norm,
    distance,
    w_nat,
    tb,
    back_mixed,
    back_qkv,
    key_sum,
    band,
):
    places, rows, width = back_branch.shape
    heads, span = bias.shape
    lanes = heads * head_dim
    scale = head_dim ** (-0.5)
    rows_in_order(scal, w_nat, w_qkv)
    bias_blocks(tb, [bias[h : h + 1, :] for h in range(heads)])
    for q in range(places):
        back_mixed[aligned(place_of(scal, q) * rows, rows), :] = dot_rt(
            back_branch[q], out_rows[...]
        ).astype(bf16)
    key_sum[...] = token_back[...]
    for h in range(heads):
        key_at, value_at = head_cols(1, h, heads, head_dim), head_cols(2, h, heads, head_dim)
        query_at, read_at = head_cols(0, h, heads, head_dim), slice(h * head_dim, (h + 1) * head_dim)
        for c in reversed(range(places)):
            count = min(span, (c + 1) * rows)
            low, high = (c + 1) * rows - count, (c + 1) * rows
            last = c * rows if c == places - 1 else 0
            query, back = qkv[c * rows : high, query_at], back_mixed[c * rows : high, read_at]
            keys = qkv[low:high, key_at]
            probs = window_probs(scal, query, keys, tb[h], last, scale)
            back_probs = dot_rt(back, qkv[low:high, value_at])
            row_dot = jnp.sum(probs * back_probs, axis=-1, keepdims=True)
            back_scores = probs * (back_probs - row_dot)
            if c == places - 1:
                band[...] = back_scores
            else:
                band[:, span - count :] += back_scores
            raw = (back_scores * scale).astype(bf16)
            back_qkv[c * rows : high, query_at] = dot(raw, keys).astype(bf16)
            key_to = slice(key_at.start - lanes, key_at.stop - lanes)
            value_to = slice(value_at.start - lanes, value_at.stop - lanes)
            key_sum[low:high, key_to] += dot_lt(raw, query)
            key_sum[low:high, value_to] += dot_lt(probs.astype(bf16), back)
        distance[h : h + 1, :] = jnp.sum(by_distance(band[...]), axis=0, keepdims=True)
    back_qkv[:, lanes:] = key_sum[...].astype(bf16)
    for start in range(0, width, 256):
        put_rows(
            scal,
            grad_qkv,
            start,
            dot_lt(first[:, start : start + 256], back_qkv[...]).astype(bf16),
        )
    gain_sum, shift_sum = None, None
    for q in range(places):
        back = dot_rt(back_qkv[aligned(place_of(scal, q) * rows, rows), :], w_nat[...])
        back_first[q] = back.astype(bf16)
        hat, _ = normalized(tokens[q].astype(f32))
        gain_term = jnp.sum(back * hat, axis=0, keepdims=True)
        shift_term = jnp.sum(back, axis=0, keepdims=True)
        gain_sum = gain_term if q == 0 else gain_sum + gain_term
        shift_sum = shift_term if q == 0 else shift_sum + shift_term
    grad_norm[0:1, :] = gain_sum
    grad_norm[1:2, :] = shift_sum


def flip_low(i):
    return i + 1 - 2 * (i % 2)


class Mover:
    def __init__(self, send, recv):
        self.send, self.recv, self.sends, self.recvs = send, recv, 0, 0

    def send_slot(self):
        self.sends += 1
        return self.sends - 1

    def recv_slot(self):
        self.recvs += 1
        return self.recvs - 1

    def copy(self, source, target, device, send_slot, recv_slot):
        return pltpu.make_async_remote_copy(
            src_ref=source,
            dst_ref=target,
            send_sem=self.send.at[send_slot],
            recv_sem=self.recv.at[recv_slot],
            device_id=device,
            device_id_type=pl.DeviceIdType.MESH,
        )

    def __call__(self, source, target, device):
        return self.copy(source, target, device, self.send_slot(), self.recv_slot())


class Links:
    def __init__(self):
        self.d, self.s = lax.axis_index("dp"), lax.axis_index("state")
        z, y = self.d // 2, self.d % 2
        self.over_z = [2 * (z + 1 - 2 * (z % 2)) + y, 2 * ((z + 2) % 4) + y, 2 * (3 - z) + y]
        self.over_y = flip_low(self.d)
        self.core, self.x = flip_low(self.s), (self.s + 2) % 4
        self.to_core, self.to_x = (self.d, self.core), (self.d, self.x)
        self.to_y = (self.over_y, self.s)
        self.to_z = [(other, self.s) for other in self.over_z]
        self.in_middle = (z == 1) | (z == 2)
        self.far_middle = 2 * (2 - z // 2) + y
        self.far_end = 2 * (3 - 3 * (z // 2)) + y
        self.to_far, self.to_far_end = (self.far_middle, self.s), (self.far_end, self.s)
        self.z, self.z_rest = z, [i // 2 for i in (self.over_z[0], self.far_middle, self.far_end)]

    def greet(self):
        barrier = pltpu.get_barrier_semaphore()
        partners = [self.to_core, self.to_x, self.to_y, *self.to_z]
        for partner in partners:
            pl.semaphore_signal(
                barrier, inc=1, device_id=partner, device_id_type=pl.DeviceIdType.MESH
            )
        pl.semaphore_wait(barrier, len(partners))


class GroupGather:
    def __init__(self, mover, links, whole, at, source=None):
        self.links, self.parts = links, [links.s, links.core, links.x, flip_low(links.x)]
        own = whole.at[at(links.s)]
        source = own if source is None else source
        across = whole.at[at(links.x)]
        self.over_x = mover(source, own, links.to_x)
        self.beside = mover(source, own, links.to_core)
        self.passed = mover(across, across, links.to_core)

    def start(self):
        self.over_x.start()
        self.beside.start()

    def forward(self):
        self.over_x.wait_recv()
        self.passed.start()

    def finish(self):
        self.beside.wait_recv()
        self.passed.wait_recv()

    def sent(self):
        for copy in (self.over_x, self.beside, self.passed):
            copy.wait_send()


class WeightGather:
    def __init__(self, mover, links, whole, at, source):
        own = whole.at[at(links.d)]
        self.links = links
        near, far = mover.send_slot(), mover.send_slot()
        slots = [mover.recv_slot() for _ in range(3)]
        self.near = mover.copy(source, own, links.to_z[0], near, slots[0])
        self.far = [mover.copy(source, own, links.to_far, far, slots[k]) for k in (1, 2)]
        self.own_y = mover(source, own, links.to_y)
        self.passed, self.relayed = [], [None]
        for k, other in enumerate((links.over_z[0], links.far_middle, links.far_end)):
            block = whole.at[at(other)]
            self.passed.append(mover(block, block, links.to_y))
            if k:
                self.relayed.append(
                    mover.copy(block, block, links.to_z[0], mover.send_slot(), slots[k])
                )

    def start_z(self):
        self.near.start()

        @pl.when(self.links.in_middle)
        def _():
            self.far[0].start()

        @pl.when(jnp.logical_not(self.links.in_middle))
        def _():
            self.far[1].start()

    def start_y(self):
        self.own_y.start()

    def pass_on(self, k):
        if k == 0:
            self.near.wait_recv()
        else:
            self.relayed[k].wait_recv()
        self.passed[k].start()

    def pass_middle(self, *ks):
        @pl.when(self.links.in_middle)
        def _():
            for k in ks:
                if k:
                    self.relayed[k].wait_recv()
                    self.relayed[k].start()
                    self.passed[k].start()
                else:
                    self.pass_on(0)

    def pass_end(self, *ks):
        @pl.when(jnp.logical_not(self.links.in_middle))
        def _():
            for k in ks:
                self.pass_on(k)

    def finish(self):
        self.own_y.wait_recv()
        for copy in self.passed:
            copy.wait_recv()

    def sent(self):
        for copy in (self.near, self.far[0], self.own_y, *self.passed):
            copy.wait_send()

        @pl.when(self.links.in_middle)
        def _():
            for copy in self.relayed[1:]:
                copy.wait_send()


class PairGather:
    def __init__(self, mover, links, whole, at, pair, source):
        own = whole.at[at(links.d)]
        self.links = links
        self.own_y = mover(source, own, links.to_y)
        both = whole.at[pair(links.z)]
        near, far = mover.send_slot(), mover.send_slot()
        slots = [mover.recv_slot() for _ in range(3)]
        self.near = mover.copy(both, both, links.to_z[0], near, slots[0])
        self.far = [mover.copy(both, both, links.to_far, far, slots[k]) for k in (1, 2)]
        self.relayed = [None]
        for k in (1, 2):
            other = whole.at[pair(links.z_rest[k])]
            self.relayed.append(
                mover.copy(other, other, links.to_z[0], mover.send_slot(), slots[k])
            )

    def start_y(self):
        self.own_y.start()

    def start_z(self):
        self.own_y.wait_recv()
        self.near.start()

        @pl.when(self.links.in_middle)
        def _():
            self.far[0].start()

        @pl.when(jnp.logical_not(self.links.in_middle))
        def _():
            self.far[1].start()

    def pass_middle(self, *ks):
        @pl.when(self.links.in_middle)
        def _():
            for k in ks:
                if k:
                    self.relayed[k].wait_recv()
                    self.relayed[k].start()
                else:
                    self.near.wait_recv()

    def pass_end(self, *ks):
        @pl.when(jnp.logical_not(self.links.in_middle))
        def _():
            for k in ks:
                if k:
                    self.relayed[k].wait_recv()
                else:
                    self.near.wait_recv()

    def sent(self):
        for copy in (self.own_y, self.near, self.far[0]):
            copy.wait_send()

        @pl.when(self.links.in_middle)
        def _():
            for copy in self.relayed[1:]:
                copy.wait_send()


class GroupSum:
    def __init__(self, mover, links, partial, at, beside, across):
        self.partial, self.at, self.links = partial, at, links
        self.from_core, self.from_x = beside, across
        diagonal = flip_low(links.x)
        self.far = mover(partial.at[at(diagonal)], beside.at[1], links.to_core)
        self.near = mover(partial.at[at(links.core)], beside.at[0], links.to_core)
        self.over = mover(partial.at[at(links.x)], across, links.to_x)

    def start(self):
        self.far.start()
        self.near.start()

    def keep(self):
        self.near.wait_recv()
        pair = self.partial[self.at(self.links.s)].astype(f32) + self.from_core[0].astype(f32)
        self.from_core[0] = pair.astype(bf16)

    def finish_kept(self):
        self.over.wait_recv()
        return self.from_core[0].astype(f32) + self.from_x[...].astype(f32)

    def middle(self):
        self.far.wait_recv()
        place = self.at(self.links.x)
        total = self.partial[place].astype(f32) + self.from_core[1].astype(f32)
        self.partial[place] = total.astype(bf16)
        self.over.start()

    def finish(self):
        self.near.wait_recv()
        pair = self.partial[self.at(self.links.s)].astype(f32) + self.from_core[0].astype(f32)
        self.over.wait_recv()
        return pair + self.from_x[...].astype(f32)

    def sent(self):
        for copy in (self.far, self.near, self.over):
            copy.wait_send()


class BlockSum:
    def __init__(self, mover, links, partial, from_core, from_x, summed, start, half):
        core = links.s % 2

        def half_at(i):
            return (pl.ds(pl.multiple_of(start + i * half, half), half), slice(None))

        self.partial, self.summed, self.mine = partial, summed, half_at(core)
        self.from_core, self.from_x = from_core, from_x
        self.beside = mover(partial.at[half_at(1 - core)], from_core, links.to_core)
        self.over = mover(partial.at[self.mine], from_x, links.to_x)
        self.back = mover(summed.at[self.mine], summed.at[self.mine], links.to_core)

    def start(self):
        self.beside.start()

    def middle(self):
        self.beside.wait_recv()
        pair = self.partial[self.mine].astype(f32) + self.from_core[...].astype(f32)
        self.partial[self.mine] = pair.astype(bf16)
        self.over.start()

    def total(self):
        self.over.wait_recv()
        return self.partial[self.mine].astype(f32) + self.from_x[...].astype(f32)

    def share(self, value):
        self.summed[self.mine] = value.astype(bf16)
        self.back.start()

    def finish(self):
        self.back.wait_recv()

    def sent(self):
        for copy in (self.beside, self.over, self.back):
            copy.wait_send()


class LineSum:
    def __init__(self, mover, links, grads, places, from_z):
        self.links, self.grads, self.places, self.from_z = links, grads, places, from_z
        sends, slots = [mover.send_slot() for _ in range(3)], [mover.recv_slot() for _ in range(4)]
        blocks = [grads.at[place] for place in places]
        self.to_near = [
            mover.copy(blocks[k], from_z.at[k], links.to_z[0], sends[k], slots[k]) for k in range(3)
        ]
        self.onward = [None] + [
            mover.copy(blocks[k], from_z.at[3], device, sends[k], slots[3])
            for k, device in ((1, links.to_far), (2, links.to_far_end))
        ]

    def send_z(self, k):
        if k == 0:
            self.to_near[0].start()
        else:

            @pl.when(jnp.logical_not(self.links.in_middle))
            def _():
                self.to_near[k].start()

    def combine(self, k):
        @pl.when(self.links.in_middle)
        def _():
            self.to_near[k].wait_recv()
            total = self.grads[self.places[k]].astype(f32) + self.from_z[k].astype(f32)
            self.grads[self.places[k]] = total.astype(bf16)
            self.onward[k].start()

    def arrived_z(self):
        self.to_near[0].wait_recv()
        near = self.from_z[0].astype(f32)
        self.onward[1].wait_recv()
        return near + self.from_z[3].astype(f32)

    def sent(self):
        for copy in self.to_near:
            copy.wait_send()


class WeightSum(LineSum):
    def __init__(self, mover, links, grads, at, from_y, from_z):
        others = [links.over_z[0], links.far_middle, links.far_end]
        super().__init__(mover, links, grads, [at(i) for i in others], from_z)
        self.own, self.from_y = at(links.d), from_y
        self.over_y = [
            mover(grads.at[at(flip_low(i))], from_y.at[k], links.to_y)
            for k, i in enumerate([links.d, *others])
        ]

    def start(self):
        for k in (2, 3, 1, 0):
            self.over_y[k].start()

    def forward(self, *order):
        for k in order:
            self.over_y[k + 1].wait_recv()
            place = self.places[k]
            total = self.grads[place].astype(f32) + self.from_y[k + 1].astype(f32)
            self.grads[place] = total.astype(bf16)
            self.send_z(k)

    def finish(self):
        self.over_y[0].wait_recv()
        total = self.grads[self.own].astype(f32) + self.from_y[0].astype(f32)
        return total + self.arrived_z()

    def sent(self):
        super().sent()
        for copy in self.over_y:
            copy.wait_send()


class PairSum(LineSum):
    def __init__(self, mover, links, grads, at, pair, from_y, from_z):
        super().__init__(mover, links, grads, [pair(i) for i in links.z_rest], from_z)
        self.own_pair, self.own, self.from_y = pair(links.z), at(links.d), from_y
        self.over_y = mover(grads.at[at(links.over_y)], from_y, links.to_y)

    def start(self):
        for k in (1, 2, 0):
            self.send_z(k)

    def middle(self):
        total = self.grads[self.own_pair].astype(f32) + self.arrived_z()
        self.grads[self.own_pair] = total.astype(bf16)
        self.over_y.start()

    def finish(self):
        self.over_y.wait_recv()
        return self.grads[self.own].astype(f32) + self.from_y[...].astype(f32)

    def sent(self):
        super().sent()
        self.over_y.wait_send()


class SmallSum:
    def __init__(self, mover, links, value, arrived):
        self.value, self.arrived = value, arrived
        partners = [links.to_core, links.to_x, links.to_z[0], links.to_z[1], links.to_y]
        self.copies = [mover(value.at[k], arrived.at[k], to) for k, to in enumerate(partners)]

    def start(self):
        self.copies[0].start()

    def step(self, k):
        self.copies[k].wait_recv()
        self.value[k + 1] = self.value[k] + self.arrived[k]
        if k + 1 < len(self.copies):
            self.copies[k + 1].start()

    def sent(self):
        for copy in self.copies:
            copy.wait_send()


LAYER_COPIES = 160


def layer(
    head_dim,
    length,
    tokens,
    state,
    cot,
    state_cot,
    w_qkv,
    w_out,
    w_sqkv,
    w_sout,
    w_up,
    w_down,
    buckets,
    rel_table,
    gains,
    shifts,
    gate_bias,
    home_output,
    home_next_state,
    home_grad_tokens,
    home_grad_state,
    home_grad_qkv,
    home_grad_out,
    home_grad_sqkv,
    home_grad_sout,
    home_grad_up,
    home_grad_down,
    home_grad_rel,
    home_grad_norm,
    send_sem,
    recv_sem,
    local_sem,
    slab,
    qkv_nat,
    sqkv_nat,
    out_nat,
    sout_nat,
    up_nat,
    down_nat,
    tok_all,
    cot_all,
    state_all,
    mixed,
    read_all,
    hid,
    first,
    qkv,
    second,
    sqkv,
    back_read,
    back_sqkv,
    own_sum,
    key_sum,
    res_own,
    hat_half,
    inverse_half,
    tb,
    band,
    out_rows,
    state_grads,
    down_grads,
    y_state,
    y_down,
    y_up,
    y_out,
    y_sout,
    z_state,
    z_down,
    z_up,
    z_out,
    z_sout,
    beside_rows,
    across_rows,
    beside_ffn,
    across_ffn,
    small,
    small_in,
    distance,
    landed,
    credit,
    by_bucket,
    home_sem,
    output,
    next_state,
    grad_tokens,
    grad_state,
    grad_qkv,
    grad_out,
    grad_sqkv,
    grad_sout,
    grad_up,
    grad_down,
    grad_rel,
    grad_norm,
):
    rows, width = tokens.shape
    state_rows = state.shape[0]
    heads, _, span = tb.shape
    lanes = heads * head_dim
    depth = w_qkv.shape[0]
    inner_width = up_nat.shape[1]
    all_states = 4 * state_rows
    group_rows = 4 * rows
    scale = head_dim ** (-0.5)
    links = Links()
    s, d = links.s, links.d
    mover = Mover(send_sem, recv_sem)
    back_qkv, back_second, back_input = sqkv_nat, out_nat, sout_nat
    ffn_partial, back_first, back_branch = up_nat, down_nat, cot_all
    slope, up_grads = state_all, state_all
    back_state, ship = down_grads, slab
    hidden, token_grads = hid, hid

    def block(i, size):
        if isinstance(i, int):
            return slice(i * size, (i + 1) * size)
        return pl.ds(pl.multiple_of(i * size, size), size)

    def own_rows(size):
        return lambda i: (block(i, size), slice(None))

    def own_lanes(size):
        return lambda i: (slice(None), block(i, size))

    def cot_rows(i):
        if isinstance(i, int):
            start = all_states + i * state_rows
            return (slice(start, start + state_rows), slice(None))
        return (pl.ds(pl.multiple_of(all_states + i * state_rows, state_rows), state_rows), slice(None))

    own_columns = block(s, lanes)

    def own_out(i):
        return (block(i, depth), own_columns)

    def pair_last(i):
        return (block(i, 2 * depth), slice(3 * lanes, 4 * lanes))

    def last_lanes(i):
        return (block(i, depth), slice(3 * lanes, 4 * lanes))

    def first_lanes(i):
        return (block(i, depth), slice(0, 3 * lanes))

    to_slab = []
    for k, shard in enumerate((w_qkv, w_sqkv)):
        core_slot = 1 - links.core % 2 + links.core // 2
        x_slot = 2 - 2 * (links.x // 2)
        to_slab.append(
            (
                mover(
                    shard.at[:, block(2 - 2 * (s % 2), lanes)],
                    slab.at[k, :, block(x_slot, lanes)],
                    links.to_x,
                ),
                mover(
                    shard.at[:, lanes : 2 * lanes],
                    slab.at[k, :, block(core_slot, lanes)],
                    links.to_core,
                ),
            )
        )
    get_tokens = GroupGather(mover, links, tok_all, own_rows(rows), tokens)
    get_state = GroupGather(mover, links, state_all, own_rows(state_rows), state)
    get_scot = GroupGather(mover, links, state_all, cot_rows, state_cot)
    get_cot = GroupGather(mover, links, cot_all, own_rows(rows), cot)
    dp_sout = WeightGather(mover, links, sout_nat, own_out, w_sout)
    dp_out = WeightGather(mover, links, out_nat, own_out, w_out)
    dp_qkv = WeightGather(mover, links, qkv_nat, own_rows(depth), slab.at[0])
    dp_sqkv = WeightGather(mover, links, sqkv_nat, own_rows(depth), slab.at[1])
    dp_up = WeightGather(mover, links, up_nat, own_rows(depth), w_up)
    top, bottom = slice(0, inner_width // 2), slice(inner_width // 2, inner_width)
    dp_down = WeightGather(
        mover, links, down_nat, lambda i: (top, block(i, depth)), w_down.at[top, :]
    )
    dp_pair = PairGather(
        mover,
        links,
        down_nat,
        lambda i: (bottom, block(i, depth)),
        lambda i: (bottom, block(i, 2 * depth)),
        w_down.at[bottom, :],
    )
    get_sout = GroupGather(mover, links, sout_nat, own_lanes(lanes))
    get_out = [
        GroupGather(mover, links, out_nat, lambda i, at=at: (at, block(i, lanes)))
        for at in (slice(0, width // 2), slice(width // 2, width))
    ]
    get_mixed = GroupGather(mover, links, mixed, own_lanes(lanes))
    get_read = GroupGather(mover, links, read_all, own_lanes(lanes))
    sum_state = GroupSum(
        mover,
        links,
        back_state,
        own_rows(state_rows),
        beside_ffn.at[:, 0:state_rows, :],
        across_ffn.at[0:state_rows, :],
    )
    half = rows // 2
    block_sums = [
        BlockSum(
            mover,
            links,
            back_second,
            beside_rows.at[i // 2, i % 2 * half : (i % 2 + 1) * half, :],
            across_rows.at[i // 2, i % 2 * half : (i % 2 + 1) * half, :],
            back_branch,
            i * rows,
            half,
        )
        for i in range(4)
    ]
    sum_ffn = GroupSum(mover, links, ffn_partial, own_rows(rows), beside_ffn, across_ffn)
    sum_first = GroupSum(
        mover, links, back_first, own_rows(rows), beside_rows, across_rows.at[0]
    )
    dp_state = WeightSum(mover, links, state_grads, first_lanes, y_state, z_state)
    dp_grad_sout = PairSum(mover, links, state_grads, last_lanes, pair_last, y_sout, z_sout)
    dp_grad_down = WeightSum(mover, links, down_grads, own_lanes(depth), y_down, z_down)
    up_cut = inner_width * 3 // 4
    dp_grad_up, dp_grad_up_last = [
        WeightSum(
            mover,
            links,
            up_grads,
            lambda i, at=at: (block(i, depth), at),
            y_up.at[:, :, at],
            z_up.at[:, :, at],
        )
        for at in (slice(0, up_cut), slice(up_cut, inner_width))
    ]
    dp_grad_out = WeightSum(mover, links, token_grads, last_lanes, y_out, z_out)
    dp_grad_qkv = WeightSum(mover, links, token_grads, first_lanes, y_state, z_state)
    sum_small = SmallSum(mover, links, small, small_in)
    to_owner = [
        (
            mover(
                ship.at[k, :, block(2 - 2 * (s // 2), lanes)],
                landed.at[k, :, block(2 - 2 * (s % 2), lanes)],
                links.to_x,
            ),
            mover(
                ship.at[k, :, block(1 - s % 2 + s // 2, lanes)],
                landed.at[k, :, lanes : 2 * lanes],
                links.to_core,
            ),
        )
        for k in range(2)
    ]
    assert max(mover.sends, mover.recvs) == LAYER_COPIES
    leaving = []

    def send_home(staged, home):
        copy = pltpu.make_async_copy(staged, home, home_sem.at[len(leaving)])
        leaving.append(copy)
        copy.start()


    local = []
    for source, target in (
        (w_qkv.at[:, block(2 * (s % 2), lanes)], slab.at[0, :, block((s + 1) // 2, lanes)]),
        (w_sqkv.at[:, block(2 * (s % 2), lanes)], slab.at[1, :, block((s + 1) // 2, lanes)]),
        (tokens, tok_all.at[block(s, rows), :]),
        (state, state_all.at[block(s, state_rows), :]),
        (state_cot, state_all.at[cot_rows(s)]),
        (cot, cot_all.at[block(s, rows), :]),
        (w_up, up_nat.at[block(d, depth), :]),
        (w_down, down_nat.at[:, block(d, depth)]),
        (w_out, out_nat.at[block(d, depth), own_columns]),
        (w_sout, sout_nat.at[block(d, depth), own_columns]),
    ):
        local.append(pltpu.make_async_copy(source, target, local_sem.at[len(local)]))

    links.greet()
    for over_x, beside in to_slab:
        over_x.start()
        beside.start()
    dp_sout.start_y()
    dp_out.start_y()
    get_tokens.start()
    for copy in local:
        copy.start()
    small[0] = jnp.zeros(small.shape[1:], f32)
    key_sum[...] = jnp.zeros_like(key_sum)
    own_sum[...] = jnp.zeros_like(own_sum)
    for k, gather in enumerate((dp_qkv, dp_sqkv)):
        for copy in (*to_slab[k],):
            copy.wait_recv()
        local[k].wait()
        if k == 0:
            gather.start_z()
            gather.start_y()
    get_state.start()
    qkv_nat[block(d, depth), :] = slab[0]
    sqkv_nat[block(d, depth), :] = slab[1]
    for copy in local[2:]:
        copy.wait()

    def token_norm(i):
        at = block(i, rows)
        hat, _ = normalized(tok_all[at, :].astype(f32))
        first[at, :] = (hat * gains[0:1, :] + shifts[0:1, :]).astype(bf16)

    token_norm(s)
    onehot = jnp.where(
        lax.broadcasted_iota(jnp.int32, (rel_table.shape[1], buckets.shape[1]), 0) == buckets[...],
        1.0,
        0.0,
    )
    turned = jnp.where(
        lax.broadcasted_iota(jnp.int32, (span, buckets.shape[1]), 0)
        + lax.broadcasted_iota(jnp.int32, (span, buckets.shape[1]), 1)
        == buckets.shape[1],
        1.0,
        0.0,
    )
    by_bucket[...] = dot_rt(turned.astype(bf16), onehot.astype(bf16))
    bias = lax.dot_general(
        rel_table[...],
        by_bucket[...],
        (((1,), (1,)), ((), ())),
        precision=lax.Precision.HIGHEST,
        preferred_element_type=f32,
    )
    column = lax.broadcasted_iota(jnp.int32, bias.shape, 1)
    distance[...] = jnp.where((column > 0) & (column <= span - rows), bias, masked_value)
    bias_blocks(tb, [distance[pl.ds(s * heads + h, 1), :] for h in range(heads)])
    distance[...] = jnp.zeros_like(distance)
    get_tokens.beside.wait_recv()
    token_norm(links.core)
    dp_qkv.pass_on(0)
    dp_qkv.pass_middle(1, 2)
    dp_sout.start_z()
    dp_qkv.pass_end(1)
    get_tokens.forward()
    get_scot.start()
    dp_sqkv.start_z()
    token_norm(links.x)
    dp_sout.pass_on(0)
    dp_sout.pass_middle(1, 2)
    dp_qkv.pass_end(2)
    dp_sqkv.start_y()
    dp_sout.pass_end(1, 2)
    get_tokens.passed.wait_recv()
    token_norm(flip_low(links.x))
    get_state.forward()
    get_cot.start()
    dp_sqkv.pass_on(0)
    dp_sqkv.pass_middle(1)
    dp_out.start_z()
    dp_pair.start_y()
    dp_qkv.finish()
    dp_sqkv.pass_middle(2)

    def token_qkv(i):
        at = block(i, rows)
        qkv[at, :] = dot(first[at, :], qkv_nat[...]).astype(bf16)

    for i in range(4):
        token_qkv(i)
    for c in range(4):
        count = min(span, (c + 1) * rows)
        low, high = (c + 1) * rows - count, (c + 1) * rows
        last = c * rows if c == 3 else 0
        parts = []
        for h in range(heads):
            probs = window_probs(
                (0, length[0]),
                qkv[c * rows : high, head_cols(0, h, heads, head_dim)],
                qkv[low:high, head_cols(1, h, heads, head_dim)],
                tb[h],
                last,
                scale,
            )
            parts.append(
                dot(probs.astype(bf16), qkv[low:high, head_cols(2, h, heads, head_dim)])
            )
        mixed[c * rows : high, own_columns] = jnp.concatenate(parts, axis=1).astype(bf16)
        if c == 0:
            dp_sout.finish()
            get_sout.start()
            dp_up.start_z()
        elif c == 1:
            dp_sqkv.pass_end(1)
            dp_out.pass_on(0)
            dp_down.start_z()
        elif c == 2:
            dp_sqkv.pass_end(2)
            dp_out.pass_middle(1, 2)
    get_mixed.start()
    dp_out.pass_end(1)
    dp_up.start_y()
    get_scot.forward()

    get_state.finish()

    def state_norms(i):
        at = block(i, state_rows)
        hat, _ = normalized(state_all[at, :].astype(f32))
        hid[at, :] = (hat * gains[2:3, :] + shifts[2:3, :]).astype(bf16)

    for i in range(4):
        state_norms(i)
    dp_sqkv.finish()
    state_norm, back_update = slice(0, all_states), slice(all_states, 2 * all_states)
    sqkv[...] = dot(hid[state_norm, :], sqkv_nat[...]).astype(bf16)
    dp_out.pass_end(2)
    dp_up.pass_on(0)
    dp_up.pass_middle(1)
    dp_pair.start_z()
    dp_down.start_y()

    def state_read(i):
        at = block(i, state_rows)
        parts = []
        for h in range(heads):
            own, token = state_probs(
                (0, length[0]),
                sqkv[at, head_cols(0, h, heads, head_dim)],
                sqkv[:, head_cols(1, h, heads, head_dim)],
                qkv[:, head_cols(1, h, heads, head_dim)],
                scale,
            )
            parts.append(
                dot(own.astype(bf16), sqkv[:, head_cols(2, h, heads, head_dim)])
                + dot(token.astype(bf16), qkv[:, head_cols(2, h, heads, head_dim)])
            )
        read_all[at, own_columns] = jnp.concatenate(parts, axis=1).astype(bf16)

    for i in range(4):
        state_read(i)
        if i == 0:
            dp_out.finish()
            get_out[0].start()
        elif i == 1:
            dp_up.pass_middle(2)
            dp_up.pass_end(1)
    get_read.start()
    get_out[1].start()
    dp_down.pass_on(0)
    dp_down.pass_middle(1)
    dp_up.pass_end(2)
    get_cot.forward()
    get_sout.forward()

    gate = jax.nn.sigmoid(gate_bias[...])
    get_scot.finish()

    def updates(i):
        hid[cot_rows(i)] = ((1.0 - gate) * state_all[cot_rows(i)].astype(f32)).astype(bf16)

    for i in range(4):
        updates(i)
    get_sout.finish()
    back_read[...] = dot_rt(hid[back_update, :], sout_nat[block(s, lanes), :]).astype(bf16)

    def state_back(h):
        key_at, value_at = head_cols(1, h, heads, head_dim), head_cols(2, h, heads, head_dim)
        query_at, read_at = head_cols(0, h, heads, head_dim), head_cols(0, h, heads, head_dim)

        def one(i):
            at = block(i, state_rows)
            query, back = sqkv[at, query_at], back_read[at, read_at]
            own, token = state_probs(
                (0, length[0]), query, sqkv[:, key_at], qkv[:, key_at], scale
            )
            back_own = dot_rt(back, sqkv[:, value_at])
            back_token = dot_rt(back, qkv[:, value_at])
            row_dot = jnp.sum(own * back_own, axis=-1, keepdims=True) + jnp.sum(
                token * back_token, axis=-1, keepdims=True
            )
            own_raw = (own * (back_own - row_dot) * scale).astype(bf16)
            token_raw = (token * (back_token - row_dot) * scale).astype(bf16)
            back_sqkv[at, query_at] = (
                dot(own_raw, sqkv[:, key_at]) + dot(token_raw, qkv[:, key_at])
            ).astype(bf16)
            key_to = slice(key_at.start - lanes, key_at.stop - lanes)
            value_to = slice(value_at.start - lanes, value_at.stop - lanes)
            own_sum[:, key_to] += dot_lt(own_raw, query)
            own_sum[:, value_to] += dot_lt(own.astype(bf16), back)
            key_sum[:, key_to] += dot_lt(token_raw, query)
            key_sum[:, value_to] += dot_lt(token.astype(bf16), back)

        for i in range(4):
            one(i)

    for h in range(heads):
        state_back(h)
        if h == 0:
            dp_down.pass_middle(2)
            dp_down.pass_end(1)
            dp_pair.pass_middle(0, 1)
            get_mixed.forward()
            get_out[0].forward()
    back_sqkv[:, lanes:] = own_sum[...].astype(bf16)

    back_state[0:all_states, :] = dot_rt(back_sqkv[...], sqkv_nat[...]).astype(bf16)
    sum_state.start()
    dp_down.pass_end(2)
    dp_pair.pass_middle(2)
    get_read.forward()

    for start in range(0, width, 256):
        at = slice(start, start + 256)
        state_grads[at, 0 : 3 * lanes] = dot_lt(hid[state_norm, at], back_sqkv[...]).astype(bf16)
    sum_state.middle()
    sum_state.keep()
    get_out[1].forward()

    get_read.finish()
    update = dot(read_all[block(s, state_rows), :], sout_nat[...])
    held = state_all[block(s, state_rows), :].astype(f32)
    own_cot = state_all[cot_rows(s)].astype(f32)
    next_state[...] = (gate * held + (1.0 - gate) * update).astype(bf16)
    send_home(next_state, home_next_state)
    small[0, 6:7, :] = jnp.sum(own_cot * (held - update), axis=0, keepdims=True) * (
        gate * (1.0 - gate)
    )
    state_grads[:, 3 * lanes : 4 * lanes] = dot_lt(
        read_all[...], hid[back_update, own_columns]
    ).astype(bf16)

    get_read.sent()
    own_state, own_scot = slice(0, state_rows), slice(state_rows, 2 * state_rows)
    again = [
        pltpu.make_async_copy(source, read_all.at[place, :], local_sem.at[k])
        for k, (source, place) in enumerate(((state, own_state), (state_cot, own_scot)))
    ]
    for copy in again:
        copy.start()
    dp_grad_sout.start()

    get_mixed.finish()
    for gather in get_out:
        gather.finish()
    dp_up.finish()
    get_cot.finish()
    for gather in (get_state, get_scot, get_sout, dp_sout, *get_out, dp_out, dp_sqkv):
        gather.sent()
    out_rows[...] = out_nat[block(s, lanes), :]
    dp_state.start()

    def ffn_rows(i):
        at = block(i, rows)
        total = tok_all[at, :].astype(f32) + dot(mixed[at, :], out_nat[...])

        @pl.when(i == s)
        def _():
            res_own[...] = total

        hat, inverse = normalized(total)
        normed = (hat * gains[1:2, :] + shifts[1:2, :]).astype(bf16)
        second[at, :] = normed
        own_half = block(i, half)
        upper = s % 2 == 0
        hat_half[own_half, :] = jnp.where(upper, hat[:half], hat[half:]).astype(bf16)
        inverse_half[own_half, :] = jnp.broadcast_to(
            jnp.where(upper, inverse[:half], inverse[half:]), (half, 128)
        )
        inner = dot(normed, up_nat[...])
        root = 0.7978845608028654
        square = inner * inner
        bend = jnp.tanh(inner * (root + (root * 0.044715) * square))
        open_part = 0.5 + 0.5 * bend
        hidden[at, :] = (inner * open_part).astype(bf16)
        slope[at, :] = (
            open_part
            + (inner - inner * bend * bend) * (0.5 * root + (1.5 * root * 0.044715) * square)
        ).astype(bf16)

    for i in range(4):
        ffn_rows(i)

    sum_state.sent()

    def down_columns(i):
        at = block(i, 256)
        down_grads[:, at] = dot_lt(hidden[...], cot_all[:, at]).astype(bf16)

    for i in range(width // 256):
        down_columns(i)
    dp_grad_down.start()
    get_cot.sent()
    for copy in again:
        copy.wait()
    hat_state, inverse_state = normalized(read_all[own_state, :].astype(f32))
    back_own_state = sum_state.finish_kept()
    small[0, 2:3, :] = jnp.sum(back_own_state * hat_state, axis=0, keepdims=True)
    small[0, 5:6, :] = jnp.sum(back_own_state, axis=0, keepdims=True)
    grad_state[...] = (
        gate * read_all[own_scot, :].astype(f32)
        + normed_back(back_own_state, hat_state, inverse_state, gains[2:3, :])
    ).astype(bf16)
    send_home(grad_state, home_grad_state)
    dp_down.finish()
    dp_pair.pass_end(0, 1, 2)

    def ffn_back_rows(i):
        at = block(i, rows)
        inner = (dot_rt(cot_all[at, :], down_nat[...]) * slope[at, :].astype(f32)).astype(bf16)
        back_input[at, :] = inner
        back_second[at, :] = dot_rt(inner, up_nat[...]).astype(bf16)
        block_sums[i].start()

    def up_columns(i):
        at = block(i, 256)
        up_grads[at, :] = dot_lt(second[:, at], back_input[...]).astype(bf16)

    def ffn_out_rows(i):
        at = block(i, rows)
        ffn_partial[at, :] = dot(hidden[at, :], down_nat[...]).astype(bf16)

    def norm_rows(i):
        back = block_sums[i].total()
        at = block(i, half)
        hat = hat_half[at, :].astype(f32)
        small[0, 1:2, :] += 0.5 * jnp.sum(back * hat, axis=0, keepdims=True)
        small[0, 4:5, :] += 0.5 * jnp.sum(back, axis=0, keepdims=True)
        kept_cot = cot_all[block_sums[i].mine].astype(f32)
        block_sums[i].share(
            kept_cot + normed_back(back, hat, inverse_half[at, 0:1], gains[1:2, :])
        )

    def window_back(c):
        block_sums[c].finish()
        count = min(span, (c + 1) * rows)
        low, high = (c + 1) * rows - count, (c + 1) * rows
        last = c * rows if c == 3 else 0
        at = block(c, rows)
        back_mixed = dot_rt(back_branch[at, :], out_rows[...]).astype(bf16)
        for h in range(heads):
            key_at, value_at = head_cols(1, h, heads, head_dim), head_cols(2, h, heads, head_dim)
            query_at = head_cols(0, h, heads, head_dim)
            query, back = qkv[at, query_at], back_mixed[:, query_at]
            keys = qkv[low:high, key_at]
            probs = window_probs((0, length[0]), query, keys, tb[h], last, scale)
            back_probs = dot_rt(back, qkv[low:high, value_at])
            row_dot = jnp.sum(probs * back_probs, axis=-1, keepdims=True)
            back_scores = probs * (back_probs - row_dot)
            if c == 0:
                band[h] = jnp.zeros(band.shape[1:], f32)
            band[h, :, span - count :] += back_scores
            raw = (back_scores * scale).astype(bf16)
            back_qkv[at, query_at] = dot(raw, keys).astype(bf16)
            key_to = slice(key_at.start - lanes, key_at.stop - lanes)
            value_to = slice(value_at.start - lanes, value_at.stop - lanes)
            key_sum[low:high, key_to] += dot_lt(raw, query)
            key_sum[low:high, value_to] += dot_lt(probs.astype(bf16), back)

    ffn_back_rows(0)
    ffn_back_rows(1)
    block_sums[0].middle()
    ffn_back_rows(2)
    block_sums[1].middle()
    ffn_back_rows(3)
    block_sums[2].middle()
    for k in (1, 2):
        dp_grad_sout.combine(k)
    block_sums[3].middle()
    dp_state.forward(1)
    for i in range(width // 256):
        up_columns(i)
    dp_grad_sout.middle()
    dp_grad_up.start()
    dp_up.sent()
    dp_state.forward(2)
    for i in range(4):
        ffn_out_rows(i)
    sum_ffn.start()
    dp_down.sent()
    dp_pair.sent()
    norm_rows(0)
    dp_state.forward(0)
    norm_rows(1)
    window_back(0)
    dp_state.combine(1)
    dp_state.combine(2)
    sum_ffn.middle()
    norm_rows(2)
    window_back(1)
    dp_grad_down.forward(1)
    norm_rows(3)
    window_back(2)
    dp_grad_down.forward(2)
    state_total = dp_state.finish()
    for partner in (links.to_y, *links.to_z):
        pl.semaphore_signal(credit, inc=1, device_id=partner, device_id_type=pl.DeviceIdType.MESH)
    dp_qkv.sent()
    ship[1] = state_total.astype(bf16)
    grad_sqkv[:, block(2 * (s % 2), lanes)] = ship[1, :, block((s + 1) // 2, lanes)]
    for copy in to_owner[1]:
        copy.start()
    window_back(3)
    dp_grad_down.forward(0)
    back_qkv[:, lanes:] = key_sum[...].astype(bf16)
    small[0, 0:1, :] = jnp.zeros((1, width), f32)
    small[0, 3:4, :] = jnp.zeros((1, width), f32)

    def qkv_grads(i):
        at = block(i, 256)
        token_grads[at, 0 : 3 * lanes] = dot_lt(first[:, at], back_qkv[...]).astype(bf16)

    def first_partial(i):
        at = block(i, rows)
        back = dot_rt(back_qkv[at, :], qkv_nat[...])
        back_first[at, :] = back.astype(bf16)
        hat, _ = normalized(tok_all[at, :].astype(f32))
        small[0, 0:1, :] += jnp.sum(back * hat, axis=0, keepdims=True)
        small[0, 3:4, :] += jnp.sum(back, axis=0, keepdims=True)

    def land(k, grads):
        for copy in to_owner[k]:
            copy.wait_recv()
        grads[:, lanes : 2 * lanes] = landed[k, :, lanes : 2 * lanes]
        x_at = block(2 - 2 * (s % 2), lanes)
        grads[:, x_at] = landed[k, :, x_at]

    token_grads[:, 3 * lanes : 4 * lanes] = dot_lt(
        mixed[...], back_branch[:, own_columns]
    ).astype(bf16)
    dp_grad_out.start()
    for i in range(width // 256):
        qkv_grads(i)
    pl.semaphore_wait(credit, 4)
    dp_grad_qkv.start()
    dp_grad_up_last.start()
    dp_grad_up.forward(1)
    dp_grad_down.combine(1)
    for h in range(heads):
        distance[pl.ds(s * heads + h, 1), :] = jnp.sum(by_distance(band[h]), axis=0, keepdims=True)
    small[0, 8:16, 0 : by_bucket.shape[1]] = lax.dot_general(
        distance[...],
        by_bucket[...],
        (((1,), (0,)), ((), ())),
        precision=lax.Precision.HIGHEST,
        preferred_element_type=f32,
    )
    dp_grad_up.forward(2)
    for i in range(4):
        first_partial(i)
    sum_small.start()
    sum_first.start()
    dp_grad_down.combine(2)
    dp_grad_up.forward(0)
    output[...] = (res_own[...] + sum_ffn.finish()).astype(bf16)
    send_home(output, home_output)
    sum_small.step(0)
    sum_first.middle()
    grad_down[...] = dp_grad_down.finish().astype(bf16)
    send_home(grad_down, home_grad_down)
    dp_grad_up.combine(1)
    sum_small.step(1)
    dp_grad_out.forward(1, 2, 0)
    dp_grad_up.combine(2)
    for k in (1, 2):
        dp_grad_out.combine(k)
    dp_grad_qkv.forward(1)
    dp_grad_qkv.forward(2)
    hat_first, inverse_first = normalized(tok_all[block(s, rows), :].astype(f32))
    back_own_first = sum_first.finish()
    grad_tokens[...] = (
        back_branch[block(s, rows), :].astype(f32)
        + normed_back(back_own_first, hat_first, inverse_first, gains[0:1, :])
    ).astype(bf16)
    send_home(grad_tokens, home_grad_tokens)
    dp_grad_qkv.combine(1)
    dp_grad_qkv.forward(0)
    sum_small.step(2)
    grad_sout[...] = dp_grad_sout.finish().astype(bf16)
    send_home(grad_sout, home_grad_sout)
    dp_grad_qkv.combine(2)
    dp_grad_up_last.forward(1)
    dp_grad_up_last.forward(2)
    grad_up[:, 0:up_cut] = dp_grad_up.finish().astype(bf16)
    send_home(grad_up.at[:, 0:up_cut], home_grad_up.at[:, 0:up_cut])
    dp_grad_up_last.forward(0)
    dp_grad_up_last.combine(1)
    dp_grad_up_last.combine(2)
    land(1, grad_sqkv)
    send_home(grad_sqkv, home_grad_sqkv)
    grad_out[...] = dp_grad_out.finish().astype(bf16)
    send_home(grad_out, home_grad_out)
    ship[0] = dp_grad_qkv.finish().astype(bf16)
    for copy in to_owner[0]:
        copy.start()
    grad_qkv[:, block(2 * (s % 2), lanes)] = ship[0, :, block((s + 1) // 2, lanes)]
    sum_small.step(3)
    sum_small.step(4)
    grad_norm[...] = small[5, 0:8, :]
    grad_rel[...] = small[5, 8:16, 0:128]
    send_home(grad_norm, home_grad_norm)
    send_home(grad_rel, home_grad_rel)
    grad_up[:, up_cut:] = dp_grad_up_last.finish().astype(bf16)
    send_home(grad_up.at[:, up_cut:], home_grad_up.at[:, up_cut:])
    land(0, grad_qkv)
    send_home(grad_qkv, home_grad_qkv)
    for over_x, beside in (*to_slab, *to_owner):
        over_x.wait_send()
        beside.wait_send()
    for used in (
        get_tokens,
        get_mixed,
        *block_sums,
        sum_ffn,
        sum_first,
        dp_state,
        dp_grad_sout,
        dp_grad_down,
        dp_grad_up,
        dp_grad_up_last,
        dp_grad_out,
        dp_grad_qkv,
        sum_small,
    ):
        used.sent()
    for copy in leaving:
        copy.wait()


def settle(*refs):
    values, results, rest = refs[:12], refs[12:26], refs[26:]
    held, widened, (read_sem, write_sem) = rest[:10], rest[10:16], rest[16:]
    reads = [pltpu.make_async_copy(values[k], held[k], read_sem.at[k]) for k in range(10)]
    for copy in reads:
        copy.start()
    writes = []
    for k in range(10):
        reads[k].wait()
        target = results[k].at[0] if len(results[k].shape) == 3 else results[k]
        ready = held[k]
        if k >= 4:
            ready = widened[k - 4]
            ready[...] = held[k][...].astype(f32)
        writes.append(pltpu.make_async_copy(ready, target, write_sem.at[k]))
        writes[-1].start()
    rel, gain, shift, gate = results[10:]
    grad_rel, grad_norm = values[10:]
    rel[...] = grad_rel[:, 0 : rel.shape[1]]
    gain[...] = grad_norm[0:3, :]
    shift[...] = grad_norm[3:6, :]
    gate[...] = grad_norm[6, :]
    for copy in writes:
        copy.wait()


def norm_back(values, back, gain):
    hat, inverse = normalized(values)
    return normed_back(back, hat, inverse, gain)


def per_device(
    tokens,
    state_in,
    cotangent,
    state_cotangent,
    seq_len,
    bucket_table,
    w_qkv,
    w_out,
    w_sqkv,
    w_sout,
    w_up,
    w_down,
    rel_table,
    norm_gain,
    norm_shift,
    gate_bias,
):
    rows, width = tokens.shape
    bucket_count, head_count = rel_table.shape
    window = bucket_table.shape[0]
    state_rows = state_in.shape[1]
    places = lax.axis_size("state")
    assert places == len(PLACES)
    dp_count = lax.axis_size("dp")
    here, dp_here = lax.axis_index("state"), lax.axis_index("dp")
    head_dim = width // head_count
    heads = head_count // places
    lanes = heads * head_dim
    span = window + rows
    group_rows = rows * places
    all_states = state_rows * places
    inner_width = w_up.shape[1]
    hops = dp_count == len(DP_PLACES)
    blocks = dp_count if hops else 1

    def swap(value, axis, bit):
        count = lax.axis_size(axis)
        return lax.ppermute(value, axis, [(i, i ^ bit) for i in range(count)])

    def from_group(value):
        pair = jnp.stack([value, swap(value, "state", 2)])
        return jnp.concatenate([pair, swap(pair, "state", 1)], axis=0)

    def list_from_group(value):
        across = swap(value, "state", 2)
        return [value, across, swap(value, "state", 1), swap(across, "state", 1)]

    def sum_to_owner(partial):
        half = partial.shape[0] // 2
        pair = partial[:half].astype(f32) + swap(partial[half:], "state", 1).astype(f32)
        return pair[0] + swap(pair[1].astype(bf16), "state", 2).astype(f32)

    def from_dp(block, axis):
        if not hops:
            return lax.all_gather(block, "dp", axis=axis, tiled=True)[None]
        gathered = block[None]
        for bit in DP_STEPS:
            gathered = jnp.concatenate([gathered, swap(gathered, "dp", bit)], axis=0)
        return gathered

    def sum_over_dp(partial, axis):
        if not hops:
            return lax.psum_scatter(partial[0], "dp", scatter_dimension=axis, tiled=True).astype(f32)
        for bit in reversed(DP_STEPS):
            half = partial.shape[0] // 2
            arrived = swap(partial[half:], "dp", bit)
            total = partial[:half].astype(f32) + arrived.astype(f32)
            partial = total.astype(bf16)
        return total[0]

    def sum_over_all(vector):
        if not hops:
            return lax.psum(vector, ("dp", "state"))
        for axis, bit in (("state", 1), ("state", 2), ("dp", 1), ("dp", 2), ("dp", 4)):
            vector = vector + swap(vector, axis, bit)
        return vector

    even = here % 2 == 0

    def pick(*by_place):
        value = by_place[-1]
        for i in reversed(range(places - 1)):
            value = jnp.where(here == i, by_place[i], value)
        return value

    def to_heads(shard):
        left, middle, right = (shard[:, i * lanes : (i + 1) * lanes] for i in range(3))
        own = jnp.where(even, left, right)
        across = swap(jnp.where(even, right, left), "state", 2)
        beside = swap(middle, "state", 1)
        query = pick(own, beside, across, across)
        keys = pick(beside, own, own, beside)
        values = pick(across, across, beside, own)
        return jnp.concatenate([query, keys, values], axis=1)

    def from_heads(grads):
        query, keys, values = (grads[:, i * lanes : (i + 1) * lanes] for i in range(3))
        own = pick(query, keys, keys, values)
        beside = swap(pick(keys, query, values, keys), "state", 1)
        across = swap(pick(values, values, query, query), "state", 2)
        return jnp.concatenate(
            [jnp.where(even, own, across), beside, jnp.where(even, across, own)], axis=1
        )

    if hops:
        block_list = dp_here ^ jnp.array(DP_PLACES, jnp.int32)
        position_list = jnp.array(
            [DP_PLACES.index(i) for i in range(dp_count)], jnp.int32
        )[dp_here ^ jnp.arange(dp_count)]
    else:
        block_list = position_list = jnp.zeros((1,), jnp.int32)
    scal = jnp.concatenate(
        [here[None].astype(jnp.int32), seq_len.astype(jnp.int32), block_list, position_list]
    ).astype(jnp.int32)

    gains = [norm_gain[i : i + 1] for i in range(3)]
    shifts = [norm_shift[i : i + 1] for i in range(3)]

    depth = w_qkv.shape[0]
    if hops:
        whole = pl.BlockSpec(memory_space=pltpu.VMEM)
        anywhere = pl.BlockSpec(memory_space=pl.ANY)
        vmem = lambda shape, kind=bf16: pltpu.VMEM(shape, kind)
        square = vmem((width, width))
        grad_blocks = lambda kind: [
            vmem(shape, kind)
            for shape in (
                (depth, 3 * lanes),
                (depth, lanes),
                (depth, 3 * lanes),
                (depth, lanes),
                (depth, inner_width),
                (inner_width, depth),
            )
        ]
        summed = pl.pallas_call(
            functools.partial(layer, head_dim),
            out_shape=[
                out((rows, width)),
                out((state_rows, width)),
                out((rows, width)),
                out((state_rows, width)),
                out((depth, 3 * lanes)),
                out((depth, lanes)),
                out((depth, 3 * lanes)),
                out((depth, lanes)),
                out((depth, inner_width)),
                out((inner_width, depth)),
                out((head_count, 128), f32),
                out((8, width), f32),
            ],
            in_specs=[pl.BlockSpec(memory_space=pltpu.SMEM)] + [anywhere] * 10 + [whole] * 5,
            out_specs=[anywhere] * 12,
            scratch_shapes=[
                pltpu.SemaphoreType.DMA((LAYER_COPIES,)),
                pltpu.SemaphoreType.DMA((LAYER_COPIES,)),
                pltpu.SemaphoreType.DMA((16,)),
                vmem((2, depth, 3 * lanes)),
                vmem((width, 3 * lanes)),
                vmem((width, 3 * lanes)),
                square,
                square,
                vmem((width, inner_width)),
                vmem((inner_width, width)),
                vmem((group_rows, width)),
                vmem((group_rows, width)),
                vmem((2 * all_states, width)),
                vmem((group_rows, width)),
                vmem((all_states, width)),
                vmem((2 * all_states, width)),
                vmem((group_rows, width)),
                vmem((group_rows, 3 * lanes)),
                vmem((group_rows, width)),
                vmem((all_states, 3 * lanes)),
                vmem((all_states, lanes)),
                vmem((all_states, 3 * lanes)),
                vmem((all_states, 2 * lanes), f32),
                vmem((group_rows, 2 * lanes), f32),
                vmem((rows, width), f32),
                vmem((group_rows // 2, width)),
                vmem((group_rows // 2, 128), f32),
                vmem((heads, rows, span), f32),
                vmem((heads, rows, span), f32),
                vmem((lanes, width)),
                square,
                vmem((inner_width, width)),
                vmem((4, depth, 3 * lanes)),
                vmem((4, inner_width, depth)),
                vmem((4, depth, inner_width)),
                vmem((4, depth, lanes)),
                vmem((depth, lanes)),
                vmem((4, depth, 3 * lanes)),
                vmem((4, inner_width, depth)),
                vmem((4, depth, inner_width)),
                vmem((4, depth, lanes)),
                vmem((4, 2 * depth, lanes)),
                vmem((2, rows, width)),
                vmem((2, rows, width)),
                vmem((2, rows, width)),
                vmem((rows, width)),
                vmem((6, 16, width), f32),
                vmem((5, 16, width), f32),
                vmem((8, span), f32),
                vmem((2, depth, 3 * lanes)),
                pltpu.SemaphoreType.REGULAR,
                vmem((span, bucket_count), f32),
                pltpu.SemaphoreType.DMA((16,)),
                vmem((rows, width)),
                vmem((state_rows, width)),
                vmem((rows, width)),
                vmem((state_rows, width)),
                *grad_blocks(bf16),
                vmem((head_count, 128), f32),
                vmem((8, width), f32),
            ],
            compiler_params=pltpu.CompilerParams(
                collective_id=0, has_side_effects=True, vmem_limit_bytes=64 << 20
            ),
            name="layer",
        )(
            seq_len,
            tokens,
            state_in[0],
            cotangent,
            state_cotangent[0],
            w_qkv,
            w_out,
            w_sqkv,
            w_sout,
            w_up,
            w_down,
            bucket_table[None],
            rel_table.T,
            norm_gain,
            norm_shift,
            gate_bias[None],
        )
        results = pl.pallas_call(
            settle,
            out_shape=[
                out((rows, width)),
                out((1, state_rows, width)),
                out((rows, width)),
                out((1, state_rows, width)),
                out((depth, 3 * lanes), f32),
                out((depth, lanes), f32),
                out((depth, 3 * lanes), f32),
                out((depth, lanes), f32),
                out((depth, inner_width), f32),
                out((inner_width, depth), f32),
                out((head_count, bucket_count), f32),
                out((3, width), f32),
                out((3, width), f32),
                out((width,), f32),
            ],
            in_specs=[anywhere] * 10 + [whole] * 2,
            out_specs=[anywhere] * 10 + [whole] * 4,
            scratch_shapes=[
                vmem((rows, width)),
                vmem((state_rows, width)),
                vmem((rows, width)),
                vmem((state_rows, width)),
                *grad_blocks(bf16),
                *grad_blocks(f32),
                pltpu.SemaphoreType.DMA((10,)),
                pltpu.SemaphoreType.DMA((10,)),
            ],
            compiler_params=pltpu.CompilerParams(vmem_limit_bytes=60 << 20),
            name="settle",
        )(*summed)
        return (*results[:10], results[10].T, *results[11:])

    lookup = (bucket_table[:, None] == jnp.arange(bucket_count)[None, :]).astype(f32)
    own_table = lax.dynamic_slice_in_dim(rel_table, here * heads, heads, 1)
    bias_rows = jnp.dot(
        own_table.T, lookup.T, precision=lax.Precision.HIGHEST, preferred_element_type=f32
    )
    bias = jnp.concatenate(
        [
            jnp.full((heads, 1), masked_value, f32),
            bias_rows[:, ::-1],
            jnp.full((heads, span - window - 1), masked_value, f32),
        ],
        axis=1,
    )
    both = to_heads(jnp.concatenate([w_qkv, w_sqkv], axis=0))
    full_qkv = from_dp(both[:depth], 0)
    all_tokens = from_group(tokens)
    full_sqkv = from_dp(both[depth:], 0)
    all_state = from_group(state_in[0])
    all_cot = from_group(cotangent)
    all_state_cot = from_group(state_cotangent[0])
    outs_pair = from_dp(jnp.concatenate([w_out, w_sout], axis=1), 0)
    half = outs_pair.shape[2] // 2
    full_sout = list_from_group(outs_pair[:, :, half:])
    full_out = list_from_group(outs_pair[:, :, :half])
    full_up = from_dp(w_up, 0)
    full_down = from_dp(w_down, 1)

    first, qkv, mixed = call(
        functools.partial(token_forward, head_dim),
        "token_forward",
        [out((group_rows, width)), out((group_rows, 3 * lanes)), out((places, rows, lanes))],
        [pltpu.VMEM((width, 3 * lanes), bf16), pltpu.VMEM((heads, rows, span), f32)],
        2 * group_rows * width * 3 * lanes,
        group_rows * span * heads,
        scal,
        all_tokens,
        gains[0],
        shifts[0],
        full_qkv,
        bias,
    )
    mixed_parts = list_from_group(mixed)

    state_norm, sqkv, read = call(
        functools.partial(state_forward, head_dim),
        "state_forward",
        [
            out((all_states, width)),
            out((all_states, 3 * lanes)),
            out((places, state_rows, lanes)),
        ],
        [pltpu.VMEM((width, 3 * lanes), bf16)],
        2 * all_states * width * 3 * lanes,
        all_states * (all_states + group_rows) * heads,
        scal,
        all_state,
        gains[2],
        shifts[2],
        full_sqkv,
        qkv,
    )
    read_parts = list_from_group(read)

    next_state, grad_gate, grad_sout, token_back, grad_sqkv, back_state_norm, state_sums = call(
        functools.partial(state_backward, head_dim),
        "state_backward",
        [
            out((state_rows, width)),
            out((1, width), f32),
            out((blocks, width // blocks, lanes)),
            out((group_rows, 2 * lanes), f32),
            out((blocks, width // blocks, 3 * lanes)),
            out((places, state_rows, width)),
            out((2, width), f32),
        ],
        [
            pltpu.VMEM((width, 3 * lanes), bf16),
            pltpu.VMEM((width, width), bf16),
            pltpu.VMEM((all_states, width), bf16),
            pltpu.VMEM((all_states, lanes), bf16),
            pltpu.VMEM((all_states, 3 * lanes), bf16),
            pltpu.VMEM((all_states, 2 * lanes), f32),
        ],
        4 * all_states * width * 4 * lanes,
        all_states * (all_states + group_rows) * heads,
        scal,
        state_in[0],
        all_state_cot,
        gate_bias[None],
        all_state,
        *read_parts,
        *full_sout,
        sqkv,
        qkv,
        state_norm,
        full_sqkv,
    )
    residual, second, hidden, slope, out_rows, grad_down = call(
        ffn_up,
        "ffn_up",
        [
            out((places, rows, width), f32),
            out((group_rows, width)),
            out((group_rows, inner_width)),
            out((group_rows, inner_width)),
            out((lanes, width)),
            out((blocks, inner_width, width // blocks)),
        ],
        [pltpu.VMEM((width, width), bf16), pltpu.VMEM((width, inner_width), bf16)],
        2 * group_rows * width * (width + 2 * inner_width),
        group_rows * inner_width,
        scal,
        all_tokens,
        *mixed_parts,
        *full_out,
        gains[1],
        shifts[1],
        full_up,
        all_cot,
    )

    back_second, back_input, mid_sums = call(
        ffn_back,
        "ffn_back",
        [
            out((places, rows, width)),
            out((group_rows, inner_width)),
            out((2, width), f32),
        ],
        [pltpu.VMEM((inner_width, width), bf16), pltpu.VMEM((width, inner_width), bf16)],
        4 * group_rows * width * inner_width,
        0,
        scal,
        all_cot,
        full_down,
        full_up,
        slope,
        residual,
    )
    residual_own = residual[0]
    own_grad_sout = sum_over_dp(grad_sout, 0)
    own_grad_sqkv = sum_over_dp(grad_sqkv, 0)
    back_state = sum_to_owner(back_state_norm)
    gate_open = jax.nn.sigmoid(gate_bias)
    grad_state = (
        gate_open * state_cotangent[0].astype(f32)
        + norm_back(state_in[0].astype(f32), back_state, norm_gain[2])
    ).astype(bf16)

    own_grad_down = sum_over_dp(grad_down, 1)
    back_second = sum_to_owner(back_second)
    back_residual = cotangent.astype(f32) + norm_back(residual_own, back_second, norm_gain[1])
    back_branch = from_group(back_residual.astype(bf16))

    ffn_partial, grad_up = call(
        ffn_rest,
        "ffn_rest",
        [out((places, rows, width)), out((blocks, width // blocks, inner_width))],
        [pltpu.VMEM((inner_width, width), bf16)],
        4 * group_rows * width * inner_width,
        0,
        scal,
        hidden,
        full_down,
        second,
        back_input,
    )
    own_grad_up = sum_over_dp(grad_up, 0)
    output = (residual_own + sum_to_owner(ffn_partial)).astype(bf16)

    (grad_out,) = call(
        out_grad,
        "out_grad",
        [out((blocks, width // blocks, lanes))],
        [],
        2 * group_rows * width * lanes,
        0,
        scal,
        back_branch,
        *mixed_parts,
    )
    own_grad_out = sum_over_dp(grad_out, 0)

    grad_qkv, back_first, first_sums, distance = call(
        functools.partial(token_backward, head_dim),
        "token_backward",
        [
            out((blocks, width // blocks, 3 * lanes)),
            out((places, rows, width)),
            out((2, width), f32),
            out((heads, span), f32),
        ],
        [
            pltpu.VMEM((width, 3 * lanes), bf16),
            pltpu.VMEM((heads, rows, span), f32),
            pltpu.VMEM((group_rows, lanes), bf16),
            pltpu.VMEM((group_rows, 3 * lanes), bf16),
            pltpu.VMEM((group_rows, 2 * lanes), f32),
            pltpu.VMEM((rows, span), f32),
        ],
        2 * group_rows * width * 7 * lanes,
        group_rows * span * heads,
        scal,
        back_branch,
        out_rows,
        qkv,
        bias,
        token_back,
        first,
        all_tokens,
        full_qkv,
    )
    back_first = sum_to_owner(back_first)
    grad_tokens = (
        norm_back(tokens.astype(f32), back_first, norm_gain[0]) + back_residual
    ).astype(bf16)
    own_grad_qkv = sum_over_dp(grad_qkv, 0)
    both_grads = from_heads(
        jnp.concatenate([own_grad_qkv, own_grad_sqkv], axis=0).astype(bf16)
    ).astype(f32)

    per_distance = distance[:, 1 : window + 1][:, ::-1]
    own_rel = jnp.dot(
        per_distance, lookup, precision=lax.Precision.HIGHEST, preferred_element_type=f32
    ).T
    grad_rel = lax.dynamic_update_slice_in_dim(
        jnp.zeros((bucket_count, head_count), f32), own_rel, here * heads, 1
    )
    small = [
        jnp.stack([first_sums[0], mid_sums[0], state_sums[0]]),
        jnp.stack([first_sums[1], mid_sums[1], state_sums[1]]),
        grad_gate[0],
        grad_rel,
    ]
    packed = sum_over_all(jnp.concatenate([v.reshape(-1, 128) for v in small], axis=0))
    unpacked, start = [], 0
    for v in small:
        count = v.size // 128
        unpacked.append(packed[start : start + count].reshape(v.shape))
        start += count
    return (
        output,
        next_state[None],
        grad_tokens,
        grad_state[None],
        both_grads[:depth],
        own_grad_out,
        both_grads[depth:],
        own_grad_sout,
        own_grad_up,
        own_grad_down,
        unpacked[3],
        unpacked[0],
        unpacked[1],
        unpacked[2],
    )


def solution(mesh):
    rows_spec = P(("dp", "state"), None)
    state_spec = P("dp", "state", None)
    weight_spec = P("dp", "state")
    return jax.shard_map(
        per_device,
        mesh=mesh,
        in_specs=(
            rows_spec,
            state_spec,
            rows_spec,
            state_spec,
            P("dp"),
            P(),
            weight_spec,
            weight_spec,
            weight_spec,
            weight_spec,
            weight_spec,
            P("state", "dp"),
            P(),
            P(),
            P(),
            P(),
        ),
        out_specs=(
            rows_spec,
            state_spec,
            rows_spec,
            state_spec,
            weight_spec,
            weight_spec,
            weight_spec,
            weight_spec,
            weight_spec,
            P("state", "dp"),
            P(),
            P(),
            P(),
            P(),
        ),
        check_vma=False,
    )
```

```python
import functools

import jax
import jax.numpy as jnp
from jax import lax
from jax.experimental import pallas as pl
from jax.experimental.pallas import tpu as pltpu
from jax.sharding import PartitionSpec as P

epsilon = 1e-05
masked_value = -1e30
f32 = jnp.float32
bf16 = jnp.bfloat16

PLACES = (0, 2, 1, 3)
DP_STEPS = (2, 4, 1)
DP_PLACES = (0, 2, 4, 6, 1, 3, 5, 7)


def dot(left, right):
    return lax.dot_general(left, right, (((1,), (0,)), ((), ())), preferred_element_type=f32)


def dot_rt(left, right):
    return lax.dot_general(left, right, (((1,), (1,)), ((), ())), preferred_element_type=f32)


def dot_lt(left, right):
    return lax.dot_general(left, right, (((0,), (0,)), ((), ())), preferred_element_type=f32)


def where_from(sender, place):
    return PLACES.index(PLACES[sender] ^ PLACES[place])


def normalized(values):
    centre = jnp.mean(values, axis=-1, keepdims=True)
    centred = values - centre
    spread = jnp.mean(centred * centred, axis=-1, keepdims=True)
    inverse = lax.rsqrt(spread + epsilon)
    return centred * inverse, inverse


def normed_back(back, hat, inverse, gain):
    grown = back * gain
    return inverse * (
        grown
        - jnp.mean(grown, axis=-1, keepdims=True)
        - hat * jnp.mean(grown * hat, axis=-1, keepdims=True)
    )


def place_of(scal, q):
    return scal[0] ^ PLACES[q]


def aligned(start, size):
    return pl.ds(pl.multiple_of(start, size), size)


def block_at(scal, q):
    return scal[2 + q]


def position_of(scal, block, blocks):
    return scal[2 + blocks + block]


def rows_in_order(scal, target, source):
    blocks, depth = source.shape[0], source.shape[1]
    for q in range(blocks):
        target[aligned(block_at(scal, q) * depth, depth), :] = source[q]


def columns_in_order(scal, target, source):
    blocks, depth = source.shape[0], source.shape[2]
    for q in range(blocks):
        target[:, aligned(block_at(scal, q) * depth, depth)] = source[q]


def put_rows(scal, target, start, value):
    blocks, depth = target.shape[0], target.shape[1]
    rows = value.shape[0]
    if depth >= rows:
        target[position_of(scal, start // depth, blocks), aligned(start % depth, rows), :] = value
    else:
        for i in range(rows // depth):
            position = position_of(scal, start // depth + i, blocks)
            target[position] = value[i * depth : (i + 1) * depth]


def put_columns(scal, target, start, value):
    blocks, depth = target.shape[0], target.shape[2]
    columns = value.shape[1]
    if depth >= columns:
        target[position_of(scal, start // depth, blocks), :, aligned(start % depth, columns)] = value
    else:
        for i in range(columns // depth):
            position = position_of(scal, start // depth + i, blocks)
            target[position] = value[:, i * depth : (i + 1) * depth]


def call(body, name, outs, scratch, flops, exps, *args):
    sizes = sum(a.size * a.dtype.itemsize for a in args) + sum(
        a.size * a.dtype.itemsize for a in outs
    )
    in_specs = [pl.BlockSpec(memory_space=pltpu.SMEM)] + [
        pl.BlockSpec(memory_space=pltpu.VMEM) for _ in args[1:]
    ]
    return pl.pallas_call(
        body,
        out_shape=outs,
        in_specs=in_specs,
        out_specs=[pl.BlockSpec(memory_space=pltpu.VMEM) for _ in outs],
        scratch_shapes=scratch,
        compiler_params=pltpu.CompilerParams(vmem_limit_bytes=56 << 20),
        cost_estimate=pl.CostEstimate(flops=flops, bytes_accessed=sizes, transcendentals=exps),
        name=name,
    )(*args)


def out(shape, kind=bf16):
    return jax.ShapeDtypeStruct(shape, kind)


def by_distance(scores):
    rows, span = scores.shape
    row_at = lax.broadcasted_iota(jnp.int32, scores.shape, 0)
    step = 1
    while step < rows:
        scores = jnp.where(row_at & step != 0, pltpu.roll(scores, span - step, 1), scores)
        step *= 2
    return scores


def bias_blocks(tb, bias):
    heads, rows, span = tb.shape
    for h in range(heads):
        row = jnp.broadcast_to(bias[h], (rows, span))
        tb[h] = pltpu.roll(row, 0, 1, stride=1, stride_axis=0)


def window_probs(scal, query, keys, tb_block, last, scale):
    rows, span = tb_block.shape
    count = keys.shape[0]
    scores = dot_rt(query, keys) * scale + tb_block[:, span - count :]
    if last:
        row_at = lax.broadcasted_iota(jnp.int32, scores.shape, 0)
        col_at = lax.broadcasted_iota(jnp.int32, scores.shape, 1)
        ahead = col_at - (count - rows)
        live = (ahead < scal[1] - last) | (ahead == row_at)
        scores = jnp.where(live, scores, masked_value)
    top = jnp.max(scores, axis=-1, keepdims=True)
    grown = jnp.exp(scores - top)
    return grown * (1.0 / jnp.sum(grown, axis=-1, keepdims=True))


def state_probs(scal, query, state_keys, keys, scale):
    own = dot_rt(query, state_keys) * scale
    token = dot_rt(query, keys) * scale
    col_at = lax.broadcasted_iota(jnp.int32, token.shape, 1)
    token = jnp.where(col_at < scal[1], token, masked_value)
    top = jnp.maximum(
        jnp.max(own, axis=-1, keepdims=True), jnp.max(token, axis=-1, keepdims=True)
    )
    own = jnp.exp(own - top)
    token = jnp.exp(token - top)
    total = jnp.sum(own, axis=-1, keepdims=True) + jnp.sum(token, axis=-1, keepdims=True)
    inverse = 1.0 / total
    return own * inverse, token * inverse


def head_cols(block, h, heads, head_dim):
    start = (block * heads + h) * head_dim
    return slice(start, start + head_dim)


def token_forward(head_dim, scal, tokens, gain, shift, w_qkv, bias, first, qkv, mixed, w_nat, tb):
    places, rows, width = tokens.shape
    heads = bias.shape[0]
    span = bias.shape[1]
    scale = head_dim ** (-0.5)
    rows_in_order(scal, w_nat, w_qkv)
    bias_blocks(tb, [bias[h : h + 1, :] for h in range(heads)])
    for q in range(places):
        hat, _ = normalized(tokens[q].astype(f32))
        normed = (hat * gain[...] + shift[...]).astype(bf16)
        at = aligned(place_of(scal, q) * rows, rows)
        first[at, :] = normed
        qkv[at, :] = dot(normed, w_nat[...]).astype(bf16)
    for c in range(places):
        count = min(span, (c + 1) * rows)
        low, high = (c + 1) * rows - count, (c + 1) * rows
        last = c * rows if c == places - 1 else 0
        parts = []
        for h in range(heads):
            probs = window_probs(
                scal,
                qkv[c * rows : high, head_cols(0, h, heads, head_dim)],
                qkv[low:high, head_cols(1, h, heads, head_dim)],
                tb[h],
                last,
                scale,
            )
            parts.append(
                dot(probs.astype(bf16), qkv[low:high, head_cols(2, h, heads, head_dim)])
            )
        mixed[c] = jnp.concatenate(parts, axis=1).astype(bf16)


def state_forward(
    head_dim, scal, state, gain, shift, w_sqkv, qkv, normed_out, sqkv, read, w_nat
):
    places, rows, width = state.shape
    heads = qkv.shape[1] // (3 * head_dim)
    scale = head_dim ** (-0.5)
    rows_in_order(scal, w_nat, w_sqkv)
    for q in range(places):
        hat, _ = normalized(state[q].astype(f32))
        normed = (hat * gain[...] + shift[...]).astype(bf16)
        normed_out[q * rows : (q + 1) * rows, :] = normed
        sqkv[q * rows : (q + 1) * rows, :] = dot(normed, w_nat[...]).astype(bf16)
    for q in range(places):
        parts = []
        for h in range(heads):
            own, token = state_probs(
                scal,
                sqkv[q * rows : (q + 1) * rows, head_cols(0, h, heads, head_dim)],
                sqkv[:, head_cols(1, h, heads, head_dim)],
                qkv[:, head_cols(1, h, heads, head_dim)],
                scale,
            )
            parts.append(
                dot(own.astype(bf16), sqkv[:, head_cols(2, h, heads, head_dim)])
                + dot(token.astype(bf16), qkv[:, head_cols(2, h, heads, head_dim)])
            )
        read[q] = jnp.concatenate(parts, axis=1).astype(bf16)


def assembled(scal, target, parts):
    for p, part in enumerate(parts):
        blocks, depth, columns = part.shape
        at = aligned(place_of(scal, p) * columns, columns)
        for q in range(blocks):
            target[aligned(block_at(scal, q) * depth, depth), at] = part[q]


def state_backward(
    head_dim,
    scal,
    state_own,
    state_cot,
    gate_bias,
    state,
    read0,
    read1,
    read2,
    read3,
    out0,
    out1,
    out2,
    out3,
    sqkv,
    qkv,
    normed,
    w_sqkv,
    next_state,
    grad_gate,
    grad_sout,
    token_back,
    grad_sqkv,
    back_norm,
    grad_norm,
    w_nat,
    w_out,
    back_update,
    back_read,
    back_sqkv,
    own_sum,
):
    places, rows, width = state_cot.shape
    reads = (read0, read1, read2, read3)
    heads = qkv.shape[1] // (3 * head_dim)
    lanes = heads * head_dim
    scale = head_dim ** (-0.5)
    rows_in_order(scal, w_nat, w_sqkv)
    assembled(scal, w_out, (out0, out1, out2, out3))
    gate = jax.nn.sigmoid(gate_bias[...])
    update = None
    for p in range(places):
        term = dot(reads[p][p], w_out[aligned(place_of(scal, p) * lanes, lanes), :])
        update = term if update is None else update + term
    held = state_own[...].astype(f32)
    cot = state_cot[0].astype(f32)
    next_state[...] = (gate * held + (1.0 - gate) * update).astype(bf16)
    grad_gate[...] = jnp.sum(cot * (held - update), axis=0, keepdims=True) * (gate * (1.0 - gate))
    for q in range(places):
        back_update[q * rows : (q + 1) * rows, :] = (
            (1.0 - gate) * state_cot[q].astype(f32)
        ).astype(bf16)
    own_columns = back_update[:, aligned(scal[0] * lanes, lanes)]
    for p in range(places):
        stack = jnp.concatenate([reads[p][where_from(p, q)] for q in range(places)], axis=0)
        put_rows(
            scal, grad_sout, place_of(scal, p) * lanes, dot_lt(stack, own_columns).astype(bf16)
        )
    back_read[...] = dot_rt(
        back_update[...], w_out[aligned(scal[0] * lanes, lanes), :]
    ).astype(bf16)
    for h in range(heads):
        key_at, value_at = head_cols(1, h, heads, head_dim), head_cols(2, h, heads, head_dim)
        query_at, read_at = head_cols(0, h, heads, head_dim), slice(h * head_dim, (h + 1) * head_dim)
        for q in range(places):
            at = slice(q * rows, (q + 1) * rows)
            query, back = sqkv[at, query_at], back_read[at, read_at]
            own, token = state_probs(scal, query, sqkv[:, key_at], qkv[:, key_at], scale)
            back_own = dot_rt(back, sqkv[:, value_at])
            back_token = dot_rt(back, qkv[:, value_at])
            row_dot = jnp.sum(own * back_own, axis=-1, keepdims=True) + jnp.sum(
                token * back_token, axis=-1, keepdims=True
            )
            own_raw = (own * (back_own - row_dot) * scale).astype(bf16)
            token_raw = (token * (back_token - row_dot) * scale).astype(bf16)
            back_sqkv[at, query_at] = (
                dot(own_raw, sqkv[:, key_at]) + dot(token_raw, qkv[:, key_at])
            ).astype(bf16)
            terms = (
                (own_sum, key_at, dot_lt(own_raw, query)),
                (own_sum, value_at, dot_lt(own.astype(bf16), back)),
                (token_back, key_at, dot_lt(token_raw, query)),
                (token_back, value_at, dot_lt(token.astype(bf16), back)),
            )
            for target, columns, term in terms:
                columns = slice(columns.start - lanes, columns.stop - lanes)
                if q == 0:
                    target[:, columns] = term
                else:
                    target[:, columns] += term
    back_sqkv[:, lanes:] = own_sum[...].astype(bf16)
    for start in range(0, width, 256):
        put_rows(
            scal,
            grad_sqkv,
            start,
            dot_lt(normed[:, start : start + 256], back_sqkv[...]).astype(bf16),
        )
    gain_sum, shift_sum = None, None
    for q in range(places):
        back = dot_rt(back_sqkv[q * rows : (q + 1) * rows, :], w_nat[...])
        back_norm[q] = back.astype(bf16)
        hat, _ = normalized(state[q].astype(f32))
        gain_term = jnp.sum(back * hat, axis=0, keepdims=True)
        shift_term = jnp.sum(back, axis=0, keepdims=True)
        gain_sum = gain_term if q == 0 else gain_sum + gain_term
        shift_sum = shift_term if q == 0 else shift_sum + shift_term
    grad_norm[0:1, :] = gain_sum
    grad_norm[1:2, :] = shift_sum


def ffn_up(
    scal,
    tokens,
    mixed0,
    mixed1,
    mixed2,
    mixed3,
    out0,
    out1,
    out2,
    out3,
    gain,
    shift,
    w_up,
    cot,
    residual,
    second,
    hidden,
    slope,
    out_rows,
    grad_down,
    w_out,
    w_nat,
):
    places, rows, width = tokens.shape
    mixed = (mixed0, mixed1, mixed2, mixed3)
    lanes = mixed0.shape[2]
    assembled(scal, w_out, (out0, out1, out2, out3))
    out_rows[...] = w_out[aligned(scal[0] * lanes, lanes), :]
    rows_in_order(scal, w_nat, w_up)
    for q in range(places):
        total = tokens[q].astype(f32)
        for p in range(places):
            total += dot(
                mixed[p][place_of(scal, q)], w_out[aligned(place_of(scal, p) * lanes, lanes), :]
            )
        residual[q] = total
        hat, _ = normalized(total)
        normed = (hat * gain[...] + shift[...]).astype(bf16)
        at = slice(q * rows, (q + 1) * rows)
        second[at, :] = normed
        inner = dot(normed, w_nat[...])
        root = 0.7978845608028654
        square = inner * inner
        bend = jnp.tanh(root * inner * (1.0 + 0.044715 * square))
        half = 0.5 * (1.0 + bend)
        hidden[at, :] = (inner * half).astype(bf16)
        slope[at, :] = (
            half + (0.5 * root) * inner * (1.0 - bend * bend) * (1.0 + (3 * 0.044715) * square)
        ).astype(bf16)
    for start in range(0, width, 256):
        columns = jnp.concatenate([cot[q, :, start : start + 256] for q in range(places)], axis=0)
        put_columns(scal, grad_down, start, dot_lt(hidden[...], columns).astype(bf16))


def ffn_back(
    scal,
    cot,
    w_down,
    w_up,
    slope,
    residual,
    back_second,
    back_input,
    grad_norm,
    w_nat,
    w_up_nat,
):
    places, rows, width = cot.shape
    columns_in_order(scal, w_nat, w_down)
    rows_in_order(scal, w_up_nat, w_up)
    gain_sum, shift_sum = None, None
    for q in range(places):
        at = slice(q * rows, (q + 1) * rows)
        inner = (dot_rt(cot[q], w_nat[...]) * slope[at, :].astype(f32)).astype(bf16)
        back_input[at, :] = inner
        back = dot_rt(inner, w_up_nat[...])
        back_second[q] = back.astype(bf16)
        hat, _ = normalized(residual[q])
        gain_term = jnp.sum(back * hat, axis=0, keepdims=True)
        shift_term = jnp.sum(back, axis=0, keepdims=True)
        gain_sum = gain_term if q == 0 else gain_sum + gain_term
        shift_sum = shift_term if q == 0 else shift_sum + shift_term
    grad_norm[0:1, :] = gain_sum
    grad_norm[1:2, :] = shift_sum


def ffn_rest(scal, hidden, w_down, second, back_input, partial, grad_up, w_nat):
    places, rows, width = partial.shape
    for start in range(0, width, 256):
        put_rows(
            scal,
            grad_up,
            start,
            dot_lt(second[:, start : start + 256], back_input[...]).astype(bf16),
        )
    columns_in_order(scal, w_nat, w_down)
    for q in range(places):
        partial[q] = dot(hidden[q * rows : (q + 1) * rows, :], w_nat[...]).astype(bf16)


def out_grad(scal, back_branch, mixed0, mixed1, mixed2, mixed3, grad_out):
    places, rows, width = back_branch.shape
    mixed = (mixed0, mixed1, mixed2, mixed3)
    lanes = mixed0.shape[2]
    own_at = aligned(scal[0] * lanes, lanes)
    own_columns = jnp.concatenate([back_branch[q, :, own_at] for q in range(places)], axis=0)
    for p in range(places):
        stack = jnp.concatenate([mixed[p][place_of(scal, q)] for q in range(places)], axis=0)
        put_rows(
            scal, grad_out, place_of(scal, p) * lanes, dot_lt(stack, own_columns).astype(bf16)
        )


def token_backward(
    head_dim,
    scal,
    back_branch,
    out_rows,
    qkv,
    bias,
    token_back,
    first,
    tokens,
    w_qkv,
    grad_qkv,
    back_first,
    grad_norm,
    distance,
    w_nat,
    tb,
    back_mixed,
    back_qkv,
    key_sum,
    band,
):
    places, rows, width = back_branch.shape
    heads, span = bias.shape
    lanes = heads * head_dim
    scale = head_dim ** (-0.5)
    rows_in_order(scal, w_nat, w_qkv)
    bias_blocks(tb, [bias[h : h + 1, :] for h in range(heads)])
    for q in range(places):
        back_mixed[aligned(place_of(scal, q) * rows, rows), :] = dot_rt(
            back_branch[q], out_rows[...]
        ).astype(bf16)
    key_sum[...] = token_back[...]
    for h in range(heads):
        key_at, value_at = head_cols(1, h, heads, head_dim), head_cols(2, h, heads, head_dim)
        query_at, read_at = head_cols(0, h, heads, head_dim), slice(h * head_dim, (h + 1) * head_dim)
        for c in reversed(range(places)):
            count = min(span, (c + 1) * rows)
            low, high = (c + 1) * rows - count, (c + 1) * rows
            last = c * rows if c == places - 1 else 0
            query, back = qkv[c * rows : high, query_at], back_mixed[c * rows : high, read_at]
            keys = qkv[low:high, key_at]
            probs = window_probs(scal, query, keys, tb[h], last, scale)
            back_probs = dot_rt(back, qkv[low:high, value_at])
            row_dot = jnp.sum(probs * back_probs, axis=-1, keepdims=True)
            back_scores = probs * (back_probs - row_dot)
            if c == places - 1:
                band[...] = back_scores
            else:
                band[:, span - count :] += back_scores
            raw = (back_scores * scale).astype(bf16)
            back_qkv[c * rows : high, query_at] = dot(raw, keys).astype(bf16)
            key_to = slice(key_at.start - lanes, key_at.stop - lanes)
            value_to = slice(value_at.start - lanes, value_at.stop - lanes)
            key_sum[low:high, key_to] += dot_lt(raw, query)
            key_sum[low:high, value_to] += dot_lt(probs.astype(bf16), back)
        distance[h : h + 1, :] = jnp.sum(by_distance(band[...]), axis=0, keepdims=True)
    back_qkv[:, lanes:] = key_sum[...].astype(bf16)
    for start in range(0, width, 256):
        put_rows(
            scal,
            grad_qkv,
            start,
            dot_lt(first[:, start : start + 256], back_qkv[...]).astype(bf16),
        )
    gain_sum, shift_sum = None, None
    for q in range(places):
        back = dot_rt(back_qkv[aligned(place_of(scal, q) * rows, rows), :], w_nat[...])
        back_first[q] = back.astype(bf16)
        hat, _ = normalized(tokens[q].astype(f32))
        gain_term = jnp.sum(back * hat, axis=0, keepdims=True)
        shift_term = jnp.sum(back, axis=0, keepdims=True)
        gain_sum = gain_term if q == 0 else gain_sum + gain_term
        shift_sum = shift_term if q == 0 else shift_sum + shift_term
    grad_norm[0:1, :] = gain_sum
    grad_norm[1:2, :] = shift_sum


def flip_low(i):
    return i + 1 - 2 * (i % 2)


class Mover:
    def __init__(self, send, recv):
        self.send, self.recv, self.sends, self.recvs = send, recv, 0, 0

    def send_slot(self):
        self.sends += 1
        return self.sends - 1

    def recv_slot(self):
        self.recvs += 1
        return self.recvs - 1

    def copy(self, source, target, device, send_slot, recv_slot):
        return pltpu.make_async_remote_copy(
            src_ref=source,
            dst_ref=target,
            send_sem=self.send.at[send_slot],
            recv_sem=self.recv.at[recv_slot],
            device_id=device,
            device_id_type=pl.DeviceIdType.MESH,
        )

    def __call__(self, source, target, device):
        return self.copy(source, target, device, self.send_slot(), self.recv_slot())


class Links:
    def __init__(self):
        self.d, self.s = lax.axis_index("dp"), lax.axis_index("state")
        z, y = self.d // 2, self.d % 2
        self.over_z = [2 * (z + 1 - 2 * (z % 2)) + y, 2 * ((z + 2) % 4) + y, 2 * (3 - z) + y]
        self.over_y = flip_low(self.d)
        self.core, self.x = flip_low(self.s), (self.s + 2) % 4
        self.to_core, self.to_x = (self.d, self.core), (self.d, self.x)
        self.to_y = (self.over_y, self.s)
        self.to_z = [(other, self.s) for other in self.over_z]
        self.in_middle = (z == 1) | (z == 2)
        self.far_middle = 2 * (2 - z // 2) + y
        self.far_end = 2 * (3 - 3 * (z // 2)) + y
        self.to_far, self.to_far_end = (self.far_middle, self.s), (self.far_end, self.s)
        self.z, self.z_rest = z, [i // 2 for i in (self.over_z[0], self.far_middle, self.far_end)]

    def greet(self):
        barrier = pltpu.get_barrier_semaphore()
        partners = [self.to_core, self.to_x, self.to_y, *self.to_z]
        for partner in partners:
            pl.semaphore_signal(
                barrier, inc=1, device_id=partner, device_id_type=pl.DeviceIdType.MESH
            )
        pl.semaphore_wait(barrier, len(partners))


class GroupGather:
    def __init__(self, mover, links, whole, at, source=None):
        self.links, self.parts = links, [links.s, links.core, links.x, flip_low(links.x)]
        own = whole.at[at(links.s)]
        source = own if source is None else source
        across = whole.at[at(links.x)]
        self.over_x = mover(source, own, links.to_x)
        self.beside = mover(source, own, links.to_core)
        self.passed = mover(across, across, links.to_core)

    def start(self):
        self.over_x.start()
        self.beside.start()

    def forward(self):
        self.over_x.wait_recv()
        self.passed.start()

    def finish(self):
        self.beside.wait_recv()
        self.passed.wait_recv()

    def sent(self):
        for copy in (self.over_x, self.beside, self.passed):
            copy.wait_send()


class WeightGather:
    def __init__(self, mover, links, whole, at, source):
        own = whole.at[at(links.d)]
        self.links = links
        near, far = mover.send_slot(), mover.send_slot()
        slots = [mover.recv_slot() for _ in range(3)]
        self.near = mover.copy(source, own, links.to_z[0], near, slots[0])
        self.far = [mover.copy(source, own, links.to_far, far, slots[k]) for k in (1, 2)]
        self.own_y = mover(source, own, links.to_y)
        self.passed, self.relayed = [], [None]
        for k, other in enumerate((links.over_z[0], links.far_middle, links.far_end)):
            block = whole.at[at(other)]
            self.passed.append(mover(block, block, links.to_y))
            if k:
                self.relayed.append(
                    mover.copy(block, block, links.to_z[0], mover.send_slot(), slots[k])
                )

    def start_z(self):
        self.near.start()

        @pl.when(self.links.in_middle)
        def _():
            self.far[0].start()

        @pl.when(jnp.logical_not(self.links.in_middle))
        def _():
            self.far[1].start()

    def start_y(self):
        self.own_y.start()

    def pass_on(self, k):
        if k == 0:
            self.near.wait_recv()
        else:
            self.relayed[k].wait_recv()
        self.passed[k].start()

    def pass_middle(self, *ks):
        @pl.when(self.links.in_middle)
        def _():
            for k in ks:
                if k:
                    self.relayed[k].wait_recv()
                    self.relayed[k].start()
                    self.passed[k].start()
                else:
                    self.pass_on(0)

    def pass_end(self, *ks):
        @pl.when(jnp.logical_not(self.links.in_middle))
        def _():
            for k in ks:
                self.pass_on(k)

    def finish(self):
        self.own_y.wait_recv()
        for copy in self.passed:
            copy.wait_recv()

    def sent(self):
        for copy in (self.near, self.far[0], self.own_y, *self.passed):
            copy.wait_send()

        @pl.when(self.links.in_middle)
        def _():
            for copy in self.relayed[1:]:
                copy.wait_send()


class PairGather:
    def __init__(self, mover, links, whole, at, pair, source):
        own = whole.at[at(links.d)]
        self.links = links
        self.own_y = mover(source, own, links.to_y)
        both = whole.at[pair(links.z)]
        near, far = mover.send_slot(), mover.send_slot()
        slots = [mover.recv_slot() for _ in range(3)]
        self.near = mover.copy(both, both, links.to_z[0], near, slots[0])
        self.far = [mover.copy(both, both, links.to_far, far, slots[k]) for k in (1, 2)]
        self.relayed = [None]
        for k in (1, 2):
            other = whole.at[pair(links.z_rest[k])]
            self.relayed.append(
                mover.copy(other, other, links.to_z[0], mover.send_slot(), slots[k])
            )

    def start_y(self):
        self.own_y.start()

    def start_z(self):
        self.own_y.wait_recv()
        self.near.start()

        @pl.when(self.links.in_middle)
        def _():
            self.far[0].start()

        @pl.when(jnp.logical_not(self.links.in_middle))
        def _():
            self.far[1].start()

    def pass_middle(self, *ks):
        @pl.when(self.links.in_middle)
        def _():
            for k in ks:
                if k:
                    self.relayed[k].wait_recv()
                    self.relayed[k].start()
                else:
                    self.near.wait_recv()

    def pass_end(self, *ks):
        @pl.when(jnp.logical_not(self.links.in_middle))
        def _():
            for k in ks:
                if k:
                    self.relayed[k].wait_recv()
                else:
                    self.near.wait_recv()

    def sent(self):
        for copy in (self.own_y, self.near, self.far[0]):
            copy.wait_send()

        @pl.when(self.links.in_middle)
        def _():
            for copy in self.relayed[1:]:
                copy.wait_send()


class GroupSum:
    def __init__(self, mover, links, partial, at, beside, across):
        self.partial, self.at, self.links = partial, at, links
        self.from_core, self.from_x = beside, across
        diagonal = flip_low(links.x)
        self.far = mover(partial.at[at(diagonal)], beside.at[1], links.to_core)
        self.near = mover(partial.at[at(links.core)], beside.at[0], links.to_core)
        self.over = mover(partial.at[at(links.x)], across, links.to_x)

    def start(self):
        self.far.start()
        self.near.start()

    def keep(self):
        self.near.wait_recv()
        pair = self.partial[self.at(self.links.s)].astype(f32) + self.from_core[0].astype(f32)
        self.from_core[0] = pair.astype(bf16)

    def finish_kept(self):
        self.over.wait_recv()
        return self.from_core[0].astype(f32) + self.from_x[...].astype(f32)

    def middle(self):
        self.far.wait_recv()
        place = self.at(self.links.x)
        total = self.partial[place].astype(f32) + self.from_core[1].astype(f32)
        self.partial[place] = total.astype(bf16)
        self.over.start()

    def finish(self):
        self.near.wait_recv()
        pair = self.partial[self.at(self.links.s)].astype(f32) + self.from_core[0].astype(f32)
        self.over.wait_recv()
        return pair + self.from_x[...].astype(f32)

    def sent(self):
        for copy in (self.far, self.near, self.over):
            copy.wait_send()


class BlockSum:
    def __init__(self, mover, links, partial, from_core, from_x, summed, start, half):
        core = links.s % 2

        def half_at(i):
            return (pl.ds(pl.multiple_of(start + i * half, half), half), slice(None))

        self.partial, self.summed, self.mine = partial, summed, half_at(core)
        self.from_core, self.from_x = from_core, from_x
        self.beside = mover(partial.at[half_at(1 - core)], from_core, links.to_core)
        self.over = mover(partial.at[self.mine], from_x, links.to_x)
        self.back = mover(summed.at[self.mine], summed.at[self.mine], links.to_core)

    def start(self):
        self.beside.start()

    def middle(self):
        self.beside.wait_recv()
        pair = self.partial[self.mine].astype(f32) + self.from_core[...].astype(f32)
        self.partial[self.mine] = pair.astype(bf16)
        self.over.start()

    def total(self):
        self.over.wait_recv()
        return self.partial[self.mine].astype(f32) + self.from_x[...].astype(f32)

    def share(self, value):
        self.summed[self.mine] = value.astype(bf16)
        self.back.start()

    def finish(self):
        self.back.wait_recv()

    def sent(self):
        for copy in (self.beside, self.over, self.back):
            copy.wait_send()


class LineSum:
    def __init__(self, mover, links, grads, places, from_z):
        self.links, self.grads, self.places, self.from_z = links, grads, places, from_z
        sends, slots = [mover.send_slot() for _ in range(3)], [mover.recv_slot() for _ in range(4)]
        blocks = [grads.at[place] for place in places]
        self.to_near = [
            mover.copy(blocks[k], from_z.at[k], links.to_z[0], sends[k], slots[k]) for k in range(3)
        ]
        self.onward = [None] + [
            mover.copy(blocks[k], from_z.at[3], device, sends[k], slots[3])
            for k, device in ((1, links.to_far), (2, links.to_far_end))
        ]

    def send_z(self, k):
        if k == 0:
            self.to_near[0].start()
        else:

            @pl.when(jnp.logical_not(self.links.in_middle))
            def _():
                self.to_near[k].start()

    def combine(self, k):
        @pl.when(self.links.in_middle)
        def _():
            self.to_near[k].wait_recv()
            total = self.grads[self.places[k]].astype(f32) + self.from_z[k].astype(f32)
            self.grads[self.places[k]] = total.astype(bf16)
            self.onward[k].start()

    def arrived_z(self):
        self.to_near[0].wait_recv()
        near = self.from_z[0].astype(f32)
        self.onward[1].wait_recv()
        return near + self.from_z[3].astype(f32)

    def sent(self):
        for copy in self.to_near:
            copy.wait_send()


class WeightSum(LineSum):
    def __init__(self, mover, links, grads, at, from_y, from_z):
        others = [links.over_z[0], links.far_middle, links.far_end]
        super().__init__(mover, links, grads, [at(i) for i in others], from_z)
        self.own, self.from_y = at(links.d), from_y
        self.over_y = [
            mover(grads.at[at(flip_low(i))], from_y.at[k], links.to_y)
            for k, i in enumerate([links.d, *others])
        ]

    def start(self):
        for k in (2, 3, 1, 0):
            self.over_y[k].start()

    def forward(self, *order):
        for k in order:
            self.over_y[k + 1].wait_recv()
            place = self.places[k]
            total = self.grads[place].astype(f32) + self.from_y[k + 1].astype(f32)
            self.grads[place] = total.astype(bf16)
            self.send_z(k)

    def finish(self):
        self.over_y[0].wait_recv()
        total = self.grads[self.own].astype(f32) + self.from_y[0].astype(f32)
        return total + self.arrived_z()

    def sent(self):
        super().sent()
        for copy in self.over_y:
            copy.wait_send()


class PairSum(LineSum):
    def __init__(self, mover, links, grads, at, pair, from_y, from_z):
        super().__init__(mover, links, grads, [pair(i) for i in links.z_rest], from_z)
        self.own_pair, self.own, self.from_y = pair(links.z), at(links.d), from_y
        self.over_y = mover(grads.at[at(links.over_y)], from_y, links.to_y)

    def start(self):
        for k in (1, 2, 0):
            self.send_z(k)

    def middle(self):
        total = self.grads[self.own_pair].astype(f32) + self.arrived_z()
        self.grads[self.own_pair] = total.astype(bf16)
        self.over_y.start()

    def finish(self):
        self.over_y.wait_recv()
        return self.grads[self.own].astype(f32) + self.from_y[...].astype(f32)

    def sent(self):
        super().sent()
        self.over_y.wait_send()


class SmallSum:
    def __init__(self, mover, links, value, arrived):
        self.value, self.arrived = value, arrived
        partners = [links.to_core, links.to_x, links.to_z[0], links.to_z[1], links.to_y]
        self.copies = [mover(value.at[k], arrived.at[k], to) for k, to in enumerate(partners)]

    def start(self):
        self.copies[0].start()

    def step(self, k):
        self.copies[k].wait_recv()
        self.value[k + 1] = self.value[k] + self.arrived[k]
        if k + 1 < len(self.copies):
            self.copies[k + 1].start()

    def sent(self):
        for copy in self.copies:
            copy.wait_send()


LAYER_COPIES = 160


def layer(
    head_dim,
    length,
    tokens,
    state,
    cot,
    state_cot,
    w_qkv,
    w_out,
    w_sqkv,
    w_sout,
    w_up,
    w_down,
    buckets,
    rel_table,
    gains,
    shifts,
    gate_bias,
    home_output,
    home_next_state,
    home_grad_tokens,
    home_grad_state,
    home_grad_qkv,
    home_grad_out,
    home_grad_sqkv,
    home_grad_sout,
    home_grad_up,
    home_grad_down,
    home_grad_rel,
    home_grad_norm,
    send_sem,
    recv_sem,
    local_sem,
    slab,
    qkv_nat,
    sqkv_nat,
    out_nat,
    sout_nat,
    up_nat,
    down_nat,
    tok_all,
    cot_all,
    state_all,
    mixed,
    read_all,
    hid,
    first,
    qkv,
    second,
    sqkv,
    back_read,
    back_sqkv,
    own_sum,
    key_sum,
    res_own,
    hat_half,
    inverse_half,
    tb,
    band,
    out_rows,
    state_grads,
    down_grads,
    y_state,
    y_down,
    y_up,
    y_out,
    y_sout,
    z_state,
    z_down,
    z_up,
    z_out,
    z_sout,
    beside_rows,
    across_rows,
    beside_ffn,
    across_ffn,
    small,
    small_in,
    distance,
    landed,
    credit,
    by_bucket,
    home_sem,
    output,
    next_state,
    grad_tokens,
    grad_state,
    grad_qkv,
    grad_out,
    grad_sqkv,
    grad_sout,
    grad_up,
    grad_down,
    grad_rel,
    grad_norm,
):
    rows, width = tokens.shape
    state_rows = state.shape[0]
    heads, _, span = tb.shape
    lanes = heads * head_dim
    depth = w_qkv.shape[0]
    inner_width = up_nat.shape[1]
    all_states = 4 * state_rows
    group_rows = 4 * rows
    scale = head_dim ** (-0.5)
    links = Links()
    s, d = links.s, links.d
    mover = Mover(send_sem, recv_sem)
    back_qkv, back_second, back_input = sqkv_nat, out_nat, sout_nat
    ffn_partial, back_first, back_branch = up_nat, down_nat, cot_all
    slope, up_grads = state_all, state_all
    back_state, ship = down_grads, slab
    hidden, token_grads = hid, hid

    def block(i, size):
        if isinstance(i, int):
            return slice(i * size, (i + 1) * size)
        return pl.ds(pl.multiple_of(i * size, size), size)

    def own_rows(size):
        return lambda i: (block(i, size), slice(None))

    def own_lanes(size):
        return lambda i: (slice(None), block(i, size))

    def cot_rows(i):
        if isinstance(i, int):
            start = all_states + i * state_rows
            return (slice(start, start + state_rows), slice(None))
        return (pl.ds(pl.multiple_of(all_states + i * state_rows, state_rows), state_rows), slice(None))

    own_columns = block(s, lanes)

    def own_out(i):
        return (block(i, depth), own_columns)

    def pair_last(i):
        return (block(i, 2 * depth), slice(3 * lanes, 4 * lanes))

    def last_lanes(i):
        return (block(i, depth), slice(3 * lanes, 4 * lanes))

    def first_lanes(i):
        return (block(i, depth), slice(0, 3 * lanes))

    to_slab = []
    for k, shard in enumerate((w_qkv, w_sqkv)):
        core_slot = 1 - links.core % 2 + links.core // 2
        x_slot = 2 - 2 * (links.x // 2)
        to_slab.append(
            (
                mover(
                    shard.at[:, block(2 - 2 * (s % 2), lanes)],
                    slab.at[k, :, block(x_slot, lanes)],
                    links.to_x,
                ),
                mover(
                    shard.at[:, lanes : 2 * lanes],
                    slab.at[k, :, block(core_slot, lanes)],
                    links.to_core,
                ),
            )
        )
    get_tokens = GroupGather(mover, links, tok_all, own_rows(rows), tokens)
    get_state = GroupGather(mover, links, state_all, own_rows(state_rows), state)
    get_scot = GroupGather(mover, links, state_all, cot_rows, state_cot)
    get_cot = GroupGather(mover, links, cot_all, own_rows(rows), cot)
    dp_sout = WeightGather(mover, links, sout_nat, own_out, w_sout)
    dp_out = WeightGather(mover, links, out_nat, own_out, w_out)
    dp_qkv = WeightGather(mover, links, qkv_nat, own_rows(depth), slab.at[0])
    dp_sqkv = WeightGather(mover, links, sqkv_nat, own_rows(depth), slab.at[1])
    dp_up = WeightGather(mover, links, up_nat, own_rows(depth), w_up)
    top, bottom = slice(0, inner_width // 2), slice(inner_width // 2, inner_width)
    dp_down = WeightGather(
        mover, links, down_nat, lambda i: (top, block(i, depth)), w_down.at[top, :]
    )
    dp_pair = PairGather(
        mover,
        links,
        down_nat,
        lambda i: (bottom, block(i, depth)),
        lambda i: (bottom, block(i, 2 * depth)),
        w_down.at[bottom, :],
    )
    get_sout = GroupGather(mover, links, sout_nat, own_lanes(lanes))
    get_out = [
        GroupGather(mover, links, out_nat, lambda i, at=at: (at, block(i, lanes)))
        for at in (slice(0, width // 2), slice(width // 2, width))
    ]
    get_mixed = GroupGather(mover, links, mixed, own_lanes(lanes))
    get_read = GroupGather(mover, links, read_all, own_lanes(lanes))
    sum_state = GroupSum(
        mover,
        links,
        back_state,
        own_rows(state_rows),
        beside_ffn.at[:, 0:state_rows, :],
        across_ffn.at[0:state_rows, :],
    )
    half = rows // 2
    block_sums = [
        BlockSum(
            mover,
            links,
            back_second,
            beside_rows.at[i // 2, i % 2 * half : (i % 2 + 1) * half, :],
            across_rows.at[i // 2, i % 2 * half : (i % 2 + 1) * half, :],
            back_branch,
            i * rows,
            half,
        )
        for i in range(4)
    ]
    sum_ffn = GroupSum(mover, links, ffn_partial, own_rows(rows), beside_ffn, across_ffn)
    sum_first = GroupSum(
        mover, links, back_first, own_rows(rows), beside_rows, across_rows.at[0]
    )
    dp_state = WeightSum(mover, links, state_grads, first_lanes, y_state, z_state)
    dp_grad_sout = PairSum(mover, links, state_grads, last_lanes, pair_last, y_sout, z_sout)
    dp_grad_down = WeightSum(mover, links, down_grads, own_lanes(depth), y_down, z_down)
    up_cut = inner_width * 3 // 4
    dp_grad_up, dp_grad_up_last = [
        WeightSum(
            mover,
            links,
            up_grads,
            lambda i, at=at: (block(i, depth), at),
            y_up.at[:, :, at],
            z_up.at[:, :, at],
        )
        for at in (slice(0, up_cut), slice(up_cut, inner_width))
    ]
    dp_grad_out = WeightSum(mover, links, token_grads, last_lanes, y_out, z_out)
    dp_grad_qkv = WeightSum(mover, links, token_grads, first_lanes, y_state, z_state)
    sum_small = SmallSum(mover, links, small, small_in)
    to_owner = [
        (
            mover(
                ship.at[k, :, block(2 - 2 * (s // 2), lanes)],
                landed.at[k, :, block(2 - 2 * (s % 2), lanes)],
                links.to_x,
            ),
            mover(
                ship.at[k, :, block(1 - s % 2 + s // 2, lanes)],
                landed.at[k, :, lanes : 2 * lanes],
                links.to_core,
            ),
        )
        for k in range(2)
    ]
    assert max(mover.sends, mover.recvs) == LAYER_COPIES
    leaving = []

    def send_home(staged, home):
        copy = pltpu.make_async_copy(staged, home, home_sem.at[len(leaving)])
        leaving.append(copy)
        copy.start()


    local = []
    for source, target in (
        (w_qkv.at[:, block(2 * (s % 2), lanes)], slab.at[0, :, block((s + 1) // 2, lanes)]),
        (w_sqkv.at[:, block(2 * (s % 2), lanes)], slab.at[1, :, block((s + 1) // 2, lanes)]),
        (tokens, tok_all.at[block(s, rows), :]),
        (state, state_all.at[block(s, state_rows), :]),
        (state_cot, state_all.at[cot_rows(s)]),
        (cot, cot_all.at[block(s, rows), :]),
        (w_up, up_nat.at[block(d, depth), :]),
        (w_down, down_nat.at[:, block(d, depth)]),
        (w_out, out_nat.at[block(d, depth), own_columns]),
        (w_sout, sout_nat.at[block(d, depth), own_columns]),
    ):
        local.append(pltpu.make_async_copy(source, target, local_sem.at[len(local)]))

    links.greet()
    for over_x, beside in to_slab:
        over_x.start()
        beside.start()
    dp_sout.start_y()
    dp_out.start_y()
    get_tokens.start()
    for copy in local:
        copy.start()
    small[0] = jnp.zeros(small.shape[1:], f32)
    key_sum[...] = jnp.zeros_like(key_sum)
    own_sum[...] = jnp.zeros_like(own_sum)
    for k, gather in enumerate((dp_qkv, dp_sqkv)):
        for copy in (*to_slab[k],):
            copy.wait_recv()
        local[k].wait()
        if k == 0:
            gather.start_z()
            gather.start_y()
    get_state.start()
    qkv_nat[block(d, depth), :] = slab[0]
    sqkv_nat[block(d, depth), :] = slab[1]
    for copy in local[2:]:
        copy.wait()

    def token_norm(i):
        at = block(i, rows)
        hat, _ = normalized(tok_all[at, :].astype(f32))
        first[at, :] = (hat * gains[0:1, :] + shifts[0:1, :]).astype(bf16)

    token_norm(s)
    onehot = jnp.where(
        lax.broadcasted_iota(jnp.int32, (rel_table.shape[1], buckets.shape[1]), 0) == buckets[...],
        1.0,
        0.0,
    )
    turned = jnp.where(
        lax.broadcasted_iota(jnp.int32, (span, buckets.shape[1]), 0)
        + lax.broadcasted_iota(jnp.int32, (span, buckets.shape[1]), 1)
        == buckets.shape[1],
        1.0,
        0.0,
    )
    by_bucket[...] = dot_rt(turned.astype(bf16), onehot.astype(bf16))
    bias = lax.dot_general(
        rel_table[...],
        by_bucket[...],
        (((1,), (1,)), ((), ())),
        precision=lax.Precision.HIGHEST,
        preferred_element_type=f32,
    )
    column = lax.broadcasted_iota(jnp.int32, bias.shape, 1)
    distance[...] = jnp.where((column > 0) & (column <= span - rows), bias, masked_value)
    bias_blocks(tb, [distance[pl.ds(s * heads + h, 1), :] for h in range(heads)])
    distance[...] = jnp.zeros_like(distance)
    get_tokens.beside.wait_recv()
    token_norm(links.core)
    dp_qkv.pass_on(0)
    dp_qkv.pass_middle(1, 2)
    dp_sout.start_z()
    dp_qkv.pass_end(1)
    get_tokens.forward()
    get_scot.start()
    dp_sqkv.start_z()
    token_norm(links.x)
    dp_sout.pass_on(0)
    dp_sout.pass_middle(1, 2)
    dp_qkv.pass_end(2)
    dp_sqkv.start_y()
    dp_sout.pass_end(1, 2)
    get_tokens.passed.wait_recv()
    token_norm(flip_low(links.x))
    get_state.forward()
    get_cot.start()
    dp_sqkv.pass_on(0)
    dp_sqkv.pass_middle(1)
    dp_out.start_z()
    dp_pair.start_y()
    dp_qkv.finish()
    dp_sqkv.pass_middle(2)

    def token_qkv(i):
        at = block(i, rows)
        qkv[at, :] = dot(first[at, :], qkv_nat[...]).astype(bf16)

    for i in range(4):
        token_qkv(i)
    for c in range(4):
        count = min(span, (c + 1) * rows)
        low, high = (c + 1) * rows - count, (c + 1) * rows
        last = c * rows if c == 3 else 0
        parts = []
        for h in range(heads):
            probs = window_probs(
                (0, length[0]),
                qkv[c * rows : high, head_cols(0, h, heads, head_dim)],
                qkv[low:high, head_cols(1, h, heads, head_dim)],
                tb[h],
                last,
                scale,
            )
            parts.append(
                dot(probs.astype(bf16), qkv[low:high, head_cols(2, h, heads, head_dim)])
            )
        mixed[c * rows : high, own_columns] = jnp.concatenate(parts, axis=1).astype(bf16)
        if c == 0:
            dp_sout.finish()
            get_sout.start()
            dp_up.start_z()
        elif c == 1:
            dp_sqkv.pass_end(1)
            dp_out.pass_on(0)
            dp_down.start_z()
        elif c == 2:
            dp_sqkv.pass_end(2)
            dp_out.pass_middle(1, 2)
    get_mixed.start()
    dp_out.pass_end(1)
    dp_up.start_y()
    get_scot.forward()

    get_state.finish()

    def state_norms(i):
        at = block(i, state_rows)
        hat, _ = normalized(state_all[at, :].astype(f32))
        hid[at, :] = (hat * gains[2:3, :] + shifts[2:3, :]).astype(bf16)

    for i in range(4):
        state_norms(i)
    dp_sqkv.finish()
    state_norm, back_update = slice(0, all_states), slice(all_states, 2 * all_states)
    sqkv[...] = dot(hid[state_norm, :], sqkv_nat[...]).astype(bf16)
    dp_out.pass_end(2)
    dp_up.pass_on(0)
    dp_up.pass_middle(1)
    dp_pair.start_z()
    dp_down.start_y()

    def state_read(i):
        at = block(i, state_rows)
        parts = []
        for h in range(heads):
            own, token = state_probs(
                (0, length[0]),
                sqkv[at, head_cols(0, h, heads, head_dim)],
                sqkv[:, head_cols(1, h, heads, head_dim)],
                qkv[:, head_cols(1, h, heads, head_dim)],
                scale,
            )
            parts.append(
                dot(own.astype(bf16), sqkv[:, head_cols(2, h, heads, head_dim)])
                + dot(token.astype(bf16), qkv[:, head_cols(2, h, heads, head_dim)])
            )
        read_all[at, own_columns] = jnp.concatenate(parts, axis=1).astype(bf16)

    for i in range(4):
        state_read(i)
        if i == 0:
            dp_out.finish()
            get_out[0].start()
        elif i == 1:
            dp_up.pass_middle(2)
            dp_up.pass_end(1)
    get_read.start()
    get_out[1].start()
    dp_down.pass_on(0)
    dp_down.pass_middle(1)
    dp_up.pass_end(2)
    get_cot.forward()
    get_sout.forward()

    gate = jax.nn.sigmoid(gate_bias[...])
    get_scot.finish()

    def updates(i):
        hid[cot_rows(i)] = ((1.0 - gate) * state_all[cot_rows(i)].astype(f32)).astype(bf16)

    for i in range(4):
        updates(i)
    get_sout.finish()
    back_read[...] = dot_rt(hid[back_update, :], sout_nat[block(s, lanes), :]).astype(bf16)

    def state_back(h):
        key_at, value_at = head_cols(1, h, heads, head_dim), head_cols(2, h, heads, head_dim)
        query_at, read_at = head_cols(0, h, heads, head_dim), head_cols(0, h, heads, head_dim)

        def one(i):
            at = block(i, state_rows)
            query, back = sqkv[at, query_at], back_read[at, read_at]
            own, token = state_probs(
                (0, length[0]), query, sqkv[:, key_at], qkv[:, key_at], scale
            )
            back_own = dot_rt(back, sqkv[:, value_at])
            back_token = dot_rt(back, qkv[:, value_at])
            row_dot = jnp.sum(own * back_own, axis=-1, keepdims=True) + jnp.sum(
                token * back_token, axis=-1, keepdims=True
            )
            own_raw = (own * (back_own - row_dot) * scale).astype(bf16)
            token_raw = (token * (back_token - row_dot) * scale).astype(bf16)
            back_sqkv[at, query_at] = (
                dot(own_raw, sqkv[:, key_at]) + dot(token_raw, qkv[:, key_at])
            ).astype(bf16)
            key_to = slice(key_at.start - lanes, key_at.stop - lanes)
            value_to = slice(value_at.start - lanes, value_at.stop - lanes)
            own_sum[:, key_to] += dot_lt(own_raw, query)
            own_sum[:, value_to] += dot_lt(own.astype(bf16), back)
            key_sum[:, key_to] += dot_lt(token_raw, query)
            key_sum[:, value_to] += dot_lt(token.astype(bf16), back)

        for i in range(4):
            one(i)

    for h in range(heads):
        state_back(h)
        if h == 0:
            dp_down.pass_middle(2)
            dp_down.pass_end(1)
            dp_pair.pass_middle(0, 1)
            get_mixed.forward()
            get_out[0].forward()
    back_sqkv[:, lanes:] = own_sum[...].astype(bf16)

    back_state[0:all_states, :] = dot_rt(back_sqkv[...], sqkv_nat[...]).astype(bf16)
    sum_state.start()
    dp_down.pass_end(2)
    dp_pair.pass_middle(2)
    get_read.forward()

    for start in range(0, width, 256):
        at = slice(start, start + 256)
        state_grads[at, 0 : 3 * lanes] = dot_lt(hid[state_norm, at], back_sqkv[...]).astype(bf16)
    dp_state.start()
    sum_state.middle()
    sum_state.keep()
    get_out[1].forward()

    get_read.finish()
    update = dot(read_all[block(s, state_rows), :], sout_nat[...])
    held = state_all[block(s, state_rows), :].astype(f32)
    own_cot = state_all[cot_rows(s)].astype(f32)
    next_state[...] = (gate * held + (1.0 - gate) * update).astype(bf16)
    send_home(next_state, home_next_state)
    small[0, 6:7, :] = jnp.sum(own_cot * (held - update), axis=0, keepdims=True) * (
        gate * (1.0 - gate)
    )
    state_grads[:, 3 * lanes : 4 * lanes] = dot_lt(
        read_all[...], hid[back_update, own_columns]
    ).astype(bf16)

    get_read.sent()
    own_state, own_scot = slice(0, state_rows), slice(state_rows, 2 * state_rows)
    again = [
        pltpu.make_async_copy(source, read_all.at[place, :], local_sem.at[k])
        for k, (source, place) in enumerate(((state, own_state), (state_cot, own_scot)))
    ]
    for copy in again:
        copy.start()
    dp_grad_sout.start()

    get_mixed.finish()
    for gather in get_out:
        gather.finish()
    dp_up.finish()
    get_cot.finish()
    for gather in (get_state, get_scot, get_sout, dp_sout, *get_out, dp_out, dp_sqkv):
        gather.sent()
    out_rows[...] = out_nat[block(s, lanes), :]

    def ffn_rows(i):
        at = block(i, rows)
        total = tok_all[at, :].astype(f32) + dot(mixed[at, :], out_nat[...])

        @pl.when(i == s)
        def _():
            res_own[...] = total

        hat, inverse = normalized(total)
        normed = (hat * gains[1:2, :] + shifts[1:2, :]).astype(bf16)
        second[at, :] = normed
        own_half = block(i, half)
        upper = s % 2 == 0
        hat_half[own_half, :] = jnp.where(upper, hat[:half], hat[half:]).astype(bf16)
        inverse_half[own_half, :] = jnp.broadcast_to(
            jnp.where(upper, inverse[:half], inverse[half:]), (half, 128)
        )
        inner = dot(normed, up_nat[...])
        root = 0.7978845608028654
        square = inner * inner
        bend = jnp.tanh(inner * (root + (root * 0.044715) * square))
        open_part = 0.5 + 0.5 * bend
        hidden[at, :] = (inner * open_part).astype(bf16)
        slope[at, :] = (
            open_part
            + (inner - inner * bend * bend) * (0.5 * root + (1.5 * root * 0.044715) * square)
        ).astype(bf16)

    for i in range(4):
        ffn_rows(i)

    sum_state.sent()

    def down_columns(i):
        at = block(i, 256)
        down_grads[:, at] = dot_lt(hidden[...], cot_all[:, at]).astype(bf16)

    for i in range(width // 256):
        down_columns(i)
    dp_grad_down.start()
    get_cot.sent()
    for copy in again:
        copy.wait()
    hat_state, inverse_state = normalized(read_all[own_state, :].astype(f32))
    back_own_state = sum_state.finish_kept()
    small[0, 2:3, :] = jnp.sum(back_own_state * hat_state, axis=0, keepdims=True)
    small[0, 5:6, :] = jnp.sum(back_own_state, axis=0, keepdims=True)
    grad_state[...] = (
        gate * read_all[own_scot, :].astype(f32)
        + normed_back(back_own_state, hat_state, inverse_state, gains[2:3, :])
    ).astype(bf16)
    send_home(grad_state, home_grad_state)
    dp_down.finish()
    dp_pair.pass_end(0, 1, 2)

    def ffn_back_rows(i):
        at = block(i, rows)
        inner = (dot_rt(cot_all[at, :], down_nat[...]) * slope[at, :].astype(f32)).astype(bf16)
        back_input[at, :] = inner
        back_second[at, :] = dot_rt(inner, up_nat[...]).astype(bf16)
        block_sums[i].start()

    def up_columns(i):
        at = block(i, 256)
        up_grads[at, :] = dot_lt(second[:, at], back_input[...]).astype(bf16)

    def ffn_out_rows(i):
        at = block(i, rows)
        ffn_partial[at, :] = dot(hidden[at, :], down_nat[...]).astype(bf16)

    def norm_rows(i):
        back = block_sums[i].total()
        at = block(i, half)
        hat = hat_half[at, :].astype(f32)
        small[0, 1:2, :] += 0.5 * jnp.sum(back * hat, axis=0, keepdims=True)
        small[0, 4:5, :] += 0.5 * jnp.sum(back, axis=0, keepdims=True)
        kept_cot = cot_all[block_sums[i].mine].astype(f32)
        block_sums[i].share(
            kept_cot + normed_back(back, hat, inverse_half[at, 0:1], gains[1:2, :])
        )

    def window_back(c):
        block_sums[c].finish()
        count = min(span, (c + 1) * rows)
        low, high = (c + 1) * rows - count, (c + 1) * rows
        last = c * rows if c == 3 else 0
        at = block(c, rows)
        back_mixed = dot_rt(back_branch[at, :], out_rows[...]).astype(bf16)
        for h in range(heads):
            key_at, value_at = head_cols(1, h, heads, head_dim), head_cols(2, h, heads, head_dim)
            query_at = head_cols(0, h, heads, head_dim)
            query, back = qkv[at, query_at], back_mixed[:, query_at]
            keys = qkv[low:high, key_at]
            probs = window_probs((0, length[0]), query, keys, tb[h], last, scale)
            back_probs = dot_rt(back, qkv[low:high, value_at])
            row_dot = jnp.sum(probs * back_probs, axis=-1, keepdims=True)
            back_scores = probs * (back_probs - row_dot)
            if c == 0:
                band[h] = jnp.zeros(band.shape[1:], f32)
            band[h, :, span - count :] += back_scores
            raw = (back_scores * scale).astype(bf16)
            back_qkv[at, query_at] = dot(raw, keys).astype(bf16)
            key_to = slice(key_at.start - lanes, key_at.stop - lanes)
            value_to = slice(value_at.start - lanes, value_at.stop - lanes)
            key_sum[low:high, key_to] += dot_lt(raw, query)
            key_sum[low:high, value_to] += dot_lt(probs.astype(bf16), back)

    ffn_back_rows(0)
    ffn_back_rows(1)
    block_sums[0].middle()
    ffn_back_rows(2)
    block_sums[1].middle()
    ffn_back_rows(3)
    block_sums[2].middle()
    for k in (1, 2):
        dp_grad_sout.combine(k)
    block_sums[3].middle()
    dp_state.forward(1)
    for i in range(width // 256):
        up_columns(i)
    dp_grad_sout.middle()
    dp_grad_up.start()
    dp_up.sent()
    dp_state.forward(2)
    for i in range(4):
        ffn_out_rows(i)
    sum_ffn.start()
    dp_down.sent()
    dp_pair.sent()
    norm_rows(0)
    dp_state.forward(0)
    norm_rows(1)
    window_back(0)
    dp_state.combine(1)
    dp_state.combine(2)
    sum_ffn.middle()
    norm_rows(2)
    window_back(1)
    dp_grad_down.forward(1)
    norm_rows(3)
    window_back(2)
    dp_grad_down.forward(2)
    state_total = dp_state.finish()
    for partner in (links.to_y, *links.to_z):
        pl.semaphore_signal(credit, inc=1, device_id=partner, device_id_type=pl.DeviceIdType.MESH)
    dp_qkv.sent()
    ship[1] = state_total.astype(bf16)
    grad_sqkv[:, block(2 * (s % 2), lanes)] = ship[1, :, block((s + 1) // 2, lanes)]
    for copy in to_owner[1]:
        copy.start()
    window_back(3)
    dp_grad_down.forward(0)
    back_qkv[:, lanes:] = key_sum[...].astype(bf16)
    small[0, 0:1, :] = jnp.zeros((1, width), f32)
    small[0, 3:4, :] = jnp.zeros((1, width), f32)

    def qkv_grads(i):
        at = block(i, 256)
        token_grads[at, 0 : 3 * lanes] = dot_lt(first[:, at], back_qkv[...]).astype(bf16)

    def first_partial(i):
        at = block(i, rows)
        back = dot_rt(back_qkv[at, :], qkv_nat[...])
        back_first[at, :] = back.astype(bf16)
        hat, _ = normalized(tok_all[at, :].astype(f32))
        small[0, 0:1, :] += jnp.sum(back * hat, axis=0, keepdims=True)
        small[0, 3:4, :] += jnp.sum(back, axis=0, keepdims=True)

    def land(k, grads):
        for copy in to_owner[k]:
            copy.wait_recv()
        grads[:, lanes : 2 * lanes] = landed[k, :, lanes : 2 * lanes]
        x_at = block(2 - 2 * (s % 2), lanes)
        grads[:, x_at] = landed[k, :, x_at]

    token_grads[:, 3 * lanes : 4 * lanes] = dot_lt(
        mixed[...], back_branch[:, own_columns]
    ).astype(bf16)
    dp_grad_out.start()
    for i in range(width // 256):
        qkv_grads(i)
    pl.semaphore_wait(credit, 4)
    dp_grad_qkv.start()
    dp_grad_up_last.start()
    dp_grad_up.forward(1)
    dp_grad_down.combine(1)
    for h in range(heads):
        distance[pl.ds(s * heads + h, 1), :] = jnp.sum(by_distance(band[h]), axis=0, keepdims=True)
    small[0, 8:16, 0 : by_bucket.shape[1]] = lax.dot_general(
        distance[...],
        by_bucket[...],
        (((1,), (0,)), ((), ())),
        precision=lax.Precision.HIGHEST,
        preferred_element_type=f32,
    )
    dp_grad_up.forward(2)
    for i in range(4):
        first_partial(i)
    sum_small.start()
    sum_first.start()
    dp_grad_down.combine(2)
    dp_grad_up.forward(0)
    output[...] = (res_own[...] + sum_ffn.finish()).astype(bf16)
    send_home(output, home_output)
    sum_small.step(0)
    sum_first.middle()
    grad_down[...] = dp_grad_down.finish().astype(bf16)
    send_home(grad_down, home_grad_down)
    dp_grad_up.combine(1)
    sum_small.step(1)
    dp_grad_out.forward(1, 2, 0)
    dp_grad_up.combine(2)
    for k in (1, 2):
        dp_grad_out.combine(k)
    dp_grad_qkv.forward(1)
    sum_small.step(2)
    dp_grad_qkv.forward(2)
    hat_first, inverse_first = normalized(tok_all[block(s, rows), :].astype(f32))
    back_own_first = sum_first.finish()
    grad_tokens[...] = (
        back_branch[block(s, rows), :].astype(f32)
        + normed_back(back_own_first, hat_first, inverse_first, gains[0:1, :])
    ).astype(bf16)
    send_home(grad_tokens, home_grad_tokens)
    dp_grad_qkv.combine(1)
    dp_grad_qkv.forward(0)
    grad_sout[...] = dp_grad_sout.finish().astype(bf16)
    send_home(grad_sout, home_grad_sout)
    dp_grad_qkv.combine(2)
    sum_small.step(3)
    dp_grad_up_last.forward(1)
    dp_grad_up_last.forward(2)
    grad_up[:, 0:up_cut] = dp_grad_up.finish().astype(bf16)
    send_home(grad_up.at[:, 0:up_cut], home_grad_up.at[:, 0:up_cut])
    dp_grad_up_last.forward(0)
    dp_grad_up_last.combine(1)
    dp_grad_up_last.combine(2)
    land(1, grad_sqkv)
    send_home(grad_sqkv, home_grad_sqkv)
    grad_out[...] = dp_grad_out.finish().astype(bf16)
    send_home(grad_out, home_grad_out)
    ship[0] = dp_grad_qkv.finish().astype(bf16)
    for copy in to_owner[0]:
        copy.start()
    grad_qkv[:, block(2 * (s % 2), lanes)] = ship[0, :, block((s + 1) // 2, lanes)]
    sum_small.step(4)
    grad_norm[...] = small[5, 0:8, :]
    grad_rel[...] = small[5, 8:16, 0:128]
    send_home(grad_norm, home_grad_norm)
    send_home(grad_rel, home_grad_rel)
    grad_up[:, up_cut:] = dp_grad_up_last.finish().astype(bf16)
    send_home(grad_up.at[:, up_cut:], home_grad_up.at[:, up_cut:])
    land(0, grad_qkv)
    send_home(grad_qkv, home_grad_qkv)
    for over_x, beside in (*to_slab, *to_owner):
        over_x.wait_send()
        beside.wait_send()
    for used in (
        get_tokens,
        get_mixed,
        *block_sums,
        sum_ffn,
        sum_first,
        dp_state,
        dp_grad_sout,
        dp_grad_down,
        dp_grad_up,
        dp_grad_up_last,
        dp_grad_out,
        dp_grad_qkv,
        sum_small,
    ):
        used.sent()
    for copy in leaving:
        copy.wait()


def settle(*refs):
    values, results, rest = refs[:12], refs[12:26], refs[26:]
    held, widened, (read_sem, write_sem) = rest[:10], rest[10:16], rest[16:]
    reads = [pltpu.make_async_copy(values[k], held[k], read_sem.at[k]) for k in range(10)]
    for copy in reads:
        copy.start()
    writes = []
    for k in range(10):
        reads[k].wait()
        target = results[k].at[0] if len(results[k].shape) == 3 else results[k]
        ready = held[k]
        if k >= 4:
            ready = widened[k - 4]
            ready[...] = held[k][...].astype(f32)
        writes.append(pltpu.make_async_copy(ready, target, write_sem.at[k]))
        writes[-1].start()
    rel, gain, shift, gate = results[10:]
    grad_rel, grad_norm = values[10:]
    rel[...] = grad_rel[:, 0 : rel.shape[1]]
    gain[...] = grad_norm[0:3, :]
    shift[...] = grad_norm[3:6, :]
    gate[...] = grad_norm[6, :]
    for copy in writes:
        copy.wait()


def norm_back(values, back, gain):
    hat, inverse = normalized(values)
    return normed_back(back, hat, inverse, gain)


def per_device(
    tokens,
    state_in,
    cotangent,
    state_cotangent,
    seq_len,
    bucket_table,
    w_qkv,
    w_out,
    w_sqkv,
    w_sout,
    w_up,
    w_down,
    rel_table,
    norm_gain,
    norm_shift,
    gate_bias,
):
    rows, width = tokens.shape
    bucket_count, head_count = rel_table.shape
    window = bucket_table.shape[0]
    state_rows = state_in.shape[1]
    places = lax.axis_size("state")
    assert places == len(PLACES)
    dp_count = lax.axis_size("dp")
    here, dp_here = lax.axis_index("state"), lax.axis_index("dp")
    head_dim = width // head_count
    heads = head_count // places
    lanes = heads * head_dim
    span = window + rows
    group_rows = rows * places
    all_states = state_rows * places
    inner_width = w_up.shape[1]
    hops = dp_count == len(DP_PLACES)
    blocks = dp_count if hops else 1

    def swap(value, axis, bit):
        count = lax.axis_size(axis)
        return lax.ppermute(value, axis, [(i, i ^ bit) for i in range(count)])

    def from_group(value):
        pair = jnp.stack([value, swap(value, "state", 2)])
        return jnp.concatenate([pair, swap(pair, "state", 1)], axis=0)

    def list_from_group(value):
        across = swap(value, "state", 2)
        return [value, across, swap(value, "state", 1), swap(across, "state", 1)]

    def sum_to_owner(partial):
        half = partial.shape[0] // 2
        pair = partial[:half].astype(f32) + swap(partial[half:], "state", 1).astype(f32)
        return pair[0] + swap(pair[1].astype(bf16), "state", 2).astype(f32)

    def from_dp(block, axis):
        if not hops:
            return lax.all_gather(block, "dp", axis=axis, tiled=True)[None]
        gathered = block[None]
        for bit in DP_STEPS:
            gathered = jnp.concatenate([gathered, swap(gathered, "dp", bit)], axis=0)
        return gathered

    def sum_over_dp(partial, axis):
        if not hops:
            return lax.psum_scatter(partial[0], "dp", scatter_dimension=axis, tiled=True).astype(f32)
        for bit in reversed(DP_STEPS):
            half = partial.shape[0] // 2
            arrived = swap(partial[half:], "dp", bit)
            total = partial[:half].astype(f32) + arrived.astype(f32)
            partial = total.astype(bf16)
        return total[0]

    def sum_over_all(vector):
        if not hops:
            return lax.psum(vector, ("dp", "state"))
        for axis, bit in (("state", 1), ("state", 2), ("dp", 1), ("dp", 2), ("dp", 4)):
            vector = vector + swap(vector, axis, bit)
        return vector

    even = here % 2 == 0

    def pick(*by_place):
        value = by_place[-1]
        for i in reversed(range(places - 1)):
            value = jnp.where(here == i, by_place[i], value)
        return value

    def to_heads(shard):
        left, middle, right = (shard[:, i * lanes : (i + 1) * lanes] for i in range(3))
        own = jnp.where(even, left, right)
        across = swap(jnp.where(even, right, left), "state", 2)
        beside = swap(middle, "state", 1)
        query = pick(own, beside, across, across)
        keys = pick(beside, own, own, beside)
        values = pick(across, across, beside, own)
        return jnp.concatenate([query, keys, values], axis=1)

    def from_heads(grads):
        query, keys, values = (grads[:, i * lanes : (i + 1) * lanes] for i in range(3))
        own = pick(query, keys, keys, values)
        beside = swap(pick(keys, query, values, keys), "state", 1)
        across = swap(pick(values, values, query, query), "state", 2)
        return jnp.concatenate(
            [jnp.where(even, own, across), beside, jnp.where(even, across, own)], axis=1
        )

    if hops:
        block_list = dp_here ^ jnp.array(DP_PLACES, jnp.int32)
        position_list = jnp.array(
            [DP_PLACES.index(i) for i in range(dp_count)], jnp.int32
        )[dp_here ^ jnp.arange(dp_count)]
    else:
        block_list = position_list = jnp.zeros((1,), jnp.int32)
    scal = jnp.concatenate(
        [here[None].astype(jnp.int32), seq_len.astype(jnp.int32), block_list, position_list]
    ).astype(jnp.int32)

    gains = [norm_gain[i : i + 1] for i in range(3)]
    shifts = [norm_shift[i : i + 1] for i in range(3)]

    depth = w_qkv.shape[0]
    if hops:
        whole = pl.BlockSpec(memory_space=pltpu.VMEM)
        anywhere = pl.BlockSpec(memory_space=pl.ANY)
        vmem = lambda shape, kind=bf16: pltpu.VMEM(shape, kind)
        square = vmem((width, width))
        grad_blocks = lambda kind: [
            vmem(shape, kind)
            for shape in (
                (depth, 3 * lanes),
                (depth, lanes),
                (depth, 3 * lanes),
                (depth, lanes),
                (depth, inner_width),
                (inner_width, depth),
            )
        ]
        summed = pl.pallas_call(
            functools.partial(layer, head_dim),
            out_shape=[
                out((rows, width)),
                out((state_rows, width)),
                out((rows, width)),
                out((state_rows, width)),
                out((depth, 3 * lanes)),
                out((depth, lanes)),
                out((depth, 3 * lanes)),
                out((depth, lanes)),
                out((depth, inner_width)),
                out((inner_width, depth)),
                out((head_count, 128), f32),
                out((8, width), f32),
            ],
            in_specs=[pl.BlockSpec(memory_space=pltpu.SMEM)] + [anywhere] * 10 + [whole] * 5,
            out_specs=[anywhere] * 12,
            scratch_shapes=[
                pltpu.SemaphoreType.DMA((LAYER_COPIES,)),
                pltpu.SemaphoreType.DMA((LAYER_COPIES,)),
                pltpu.SemaphoreType.DMA((16,)),
                vmem((2, depth, 3 * lanes)),
                vmem((width, 3 * lanes)),
                vmem((width, 3 * lanes)),
                square,
                square,
                vmem((width, inner_width)),
                vmem((inner_width, width)),
                vmem((group_rows, width)),
                vmem((group_rows, width)),
                vmem((2 * all_states, width)),
                vmem((group_rows, width)),
                vmem((all_states, width)),
                vmem((2 * all_states, width)),
                vmem((group_rows, width)),
                vmem((group_rows, 3 * lanes)),
                vmem((group_rows, width)),
                vmem((all_states, 3 * lanes)),
                vmem((all_states, lanes)),
                vmem((all_states, 3 * lanes)),
                vmem((all_states, 2 * lanes), f32),
                vmem((group_rows, 2 * lanes), f32),
                vmem((rows, width), f32),
                vmem((group_rows // 2, width)),
                vmem((group_rows // 2, 128), f32),
                vmem((heads, rows, span), f32),
                vmem((heads, rows, span), f32),
                vmem((lanes, width)),
                square,
                vmem((inner_width, width)),
                vmem((4, depth, 3 * lanes)),
                vmem((4, inner_width, depth)),
                vmem((4, depth, inner_width)),
                vmem((4, depth, lanes)),
                vmem((depth, lanes)),
                vmem((4, depth, 3 * lanes)),
                vmem((4, inner_width, depth)),
                vmem((4, depth, inner_width)),
                vmem((4, depth, lanes)),
                vmem((4, 2 * depth, lanes)),
                vmem((2, rows, width)),
                vmem((2, rows, width)),
                vmem((2, rows, width)),
                vmem((rows, width)),
                vmem((6, 16, width), f32),
                vmem((5, 16, width), f32),
                vmem((8, span), f32),
                vmem((2, depth, 3 * lanes)),
                pltpu.SemaphoreType.REGULAR,
                vmem((span, bucket_count), f32),
                pltpu.SemaphoreType.DMA((16,)),
                vmem((rows, width)),
                vmem((state_rows, width)),
                vmem((rows, width)),
                vmem((state_rows, width)),
                *grad_blocks(bf16),
                vmem((head_count, 128), f32),
                vmem((8, width), f32),
            ],
            compiler_params=pltpu.CompilerParams(
                collective_id=0, has_side_effects=True, vmem_limit_bytes=64 << 20
            ),
            name="layer",
        )(
            seq_len,
            tokens,
            state_in[0],
            cotangent,
            state_cotangent[0],
            w_qkv,
            w_out,
            w_sqkv,
            w_sout,
            w_up,
            w_down,
            bucket_table[None],
            rel_table.T,
            norm_gain,
            norm_shift,
            gate_bias[None],
        )
        results = pl.pallas_call(
            settle,
            out_shape=[
                out((rows, width)),
                out((1, state_rows, width)),
                out((rows, width)),
                out((1, state_rows, width)),
                out((depth, 3 * lanes), f32),
                out((depth, lanes), f32),
                out((depth, 3 * lanes), f32),
                out((depth, lanes), f32),
                out((depth, inner_width), f32),
                out((inner_width, depth), f32),
                out((head_count, bucket_count), f32),
                out((3, width), f32),
                out((3, width), f32),
                out((width,), f32),
            ],
            in_specs=[anywhere] * 10 + [whole] * 2,
            out_specs=[anywhere] * 10 + [whole] * 4,
            scratch_shapes=[
                vmem((rows, width)),
                vmem((state_rows, width)),
                vmem((rows, width)),
                vmem((state_rows, width)),
                *grad_blocks(bf16),
                *grad_blocks(f32),
                pltpu.SemaphoreType.DMA((10,)),
                pltpu.SemaphoreType.DMA((10,)),
            ],
            compiler_params=pltpu.CompilerParams(vmem_limit_bytes=60 << 20),
            name="settle",
        )(*summed)
        return (*results[:10], results[10].T, *results[11:])

    lookup = (bucket_table[:, None] == jnp.arange(bucket_count)[None, :]).astype(f32)
    own_table = lax.dynamic_slice_in_dim(rel_table, here * heads, heads, 1)
    bias_rows = jnp.dot(
        own_table.T, lookup.T, precision=lax.Precision.HIGHEST, preferred_element_type=f32
    )
    bias = jnp.concatenate(
        [
            jnp.full((heads, 1), masked_value, f32),
            bias_rows[:, ::-1],
            jnp.full((heads, span - window - 1), masked_value, f32),
        ],
        axis=1,
    )
    both = to_heads(jnp.concatenate([w_qkv, w_sqkv], axis=0))
    full_qkv = from_dp(both[:depth], 0)
    all_tokens = from_group(tokens)
    full_sqkv = from_dp(both[depth:], 0)
    all_state = from_group(state_in[0])
    all_cot = from_group(cotangent)
    all_state_cot = from_group(state_cotangent[0])
    outs_pair = from_dp(jnp.concatenate([w_out, w_sout], axis=1), 0)
    half = outs_pair.shape[2] // 2
    full_sout = list_from_group(outs_pair[:, :, half:])
    full_out = list_from_group(outs_pair[:, :, :half])
    full_up = from_dp(w_up, 0)
    full_down = from_dp(w_down, 1)

    first, qkv, mixed = call(
        functools.partial(token_forward, head_dim),
        "token_forward",
        [out((group_rows, width)), out((group_rows, 3 * lanes)), out((places, rows, lanes))],
        [pltpu.VMEM((width, 3 * lanes), bf16), pltpu.VMEM((heads, rows, span), f32)],
        2 * group_rows * width * 3 * lanes,
        group_rows * span * heads,
        scal,
        all_tokens,
        gains[0],
        shifts[0],
        full_qkv,
        bias,
    )
    mixed_parts = list_from_group(mixed)

    state_norm, sqkv, read = call(
        functools.partial(state_forward, head_dim),
        "state_forward",
        [
            out((all_states, width)),
            out((all_states, 3 * lanes)),
            out((places, state_rows, lanes)),
        ],
        [pltpu.VMEM((width, 3 * lanes), bf16)],
        2 * all_states * width * 3 * lanes,
        all_states * (all_states + group_rows) * heads,
        scal,
        all_state,
        gains[2],
        shifts[2],
        full_sqkv,
        qkv,
    )
    read_parts = list_from_group(read)

    next_state, grad_gate, grad_sout, token_back, grad_sqkv, back_state_norm, state_sums = call(
        functools.partial(state_backward, head_dim),
        "state_backward",
        [
            out((state_rows, width)),
            out((1, width), f32),
            out((blocks, width // blocks, lanes)),
            out((group_rows, 2 * lanes), f32),
            out((blocks, width // blocks, 3 * lanes)),
            out((places, state_rows, width)),
            out((2, width), f32),
        ],
        [
            pltpu.VMEM((width, 3 * lanes), bf16),
            pltpu.VMEM((width, width), bf16),
            pltpu.VMEM((all_states, width), bf16),
            pltpu.VMEM((all_states, lanes), bf16),
            pltpu.VMEM((all_states, 3 * lanes), bf16),
            pltpu.VMEM((all_states, 2 * lanes), f32),
        ],
        4 * all_states * width * 4 * lanes,
        all_states * (all_states + group_rows) * heads,
        scal,
        state_in[0],
        all_state_cot,
        gate_bias[None],
        all_state,
        *read_parts,
        *full_sout,
        sqkv,
        qkv,
        state_norm,
        full_sqkv,
    )
    residual, second, hidden, slope, out_rows, grad_down = call(
        ffn_up,
        "ffn_up",
        [
            out((places, rows, width), f32),
            out((group_rows, width)),
            out((group_rows, inner_width)),
            out((group_rows, inner_width)),
            out((lanes, width)),
            out((blocks, inner_width, width // blocks)),
        ],
        [pltpu.VMEM((width, width), bf16), pltpu.VMEM((width, inner_width), bf16)],
        2 * group_rows * width * (width + 2 * inner_width),
        group_rows * inner_width,
        scal,
        all_tokens,
        *mixed_parts,
        *full_out,
        gains[1],
        shifts[1],
        full_up,
        all_cot,
    )

    back_second, back_input, mid_sums = call(
        ffn_back,
        "ffn_back",
        [
            out((places, rows, width)),
            out((group_rows, inner_width)),
            out((2, width), f32),
        ],
        [pltpu.VMEM((inner_width, width), bf16), pltpu.VMEM((width, inner_width), bf16)],
        4 * group_rows * width * inner_width,
        0,
        scal,
        all_cot,
        full_down,
        full_up,
        slope,
        residual,
    )
    residual_own = residual[0]
    own_grad_sout = sum_over_dp(grad_sout, 0)
    own_grad_sqkv = sum_over_dp(grad_sqkv, 0)
    back_state = sum_to_owner(back_state_norm)
    gate_open = jax.nn.sigmoid(gate_bias)
    grad_state = (
        gate_open * state_cotangent[0].astype(f32)
        + norm_back(state_in[0].astype(f32), back_state, norm_gain[2])
    ).astype(bf16)

    own_grad_down = sum_over_dp(grad_down, 1)
    back_second = sum_to_owner(back_second)
    back_residual = cotangent.astype(f32) + norm_back(residual_own, back_second, norm_gain[1])
    back_branch = from_group(back_residual.astype(bf16))

    ffn_partial, grad_up = call(
        ffn_rest,
        "ffn_rest",
        [out((places, rows, width)), out((blocks, width // blocks, inner_width))],
        [pltpu.VMEM((inner_width, width), bf16)],
        4 * group_rows * width * inner_width,
        0,
        scal,
        hidden,
        full_down,
        second,
        back_input,
    )
    own_grad_up = sum_over_dp(grad_up, 0)
    output = (residual_own + sum_to_owner(ffn_partial)).astype(bf16)

    (grad_out,) = call(
        out_grad,
        "out_grad",
        [out((blocks, width // blocks, lanes))],
        [],
        2 * group_rows * width * lanes,
        0,
        scal,
        back_branch,
        *mixed_parts,
    )
    own_grad_out = sum_over_dp(grad_out, 0)

    grad_qkv, back_first, first_sums, distance = call(
        functools.partial(token_backward, head_dim),
        "token_backward",
        [
            out((blocks, width // blocks, 3 * lanes)),
            out((places, rows, width)),
            out((2, width), f32),
            out((heads, span), f32),
        ],
        [
            pltpu.VMEM((width, 3 * lanes), bf16),
            pltpu.VMEM((heads, rows, span), f32),
            pltpu.VMEM((group_rows, lanes), bf16),
            pltpu.VMEM((group_rows, 3 * lanes), bf16),
            pltpu.VMEM((group_rows, 2 * lanes), f32),
            pltpu.VMEM((rows, span), f32),
        ],
        2 * group_rows * width * 7 * lanes,
        group_rows * span * heads,
        scal,
        back_branch,
        out_rows,
        qkv,
        bias,
        token_back,
        first,
        all_tokens,
        full_qkv,
    )
    back_first = sum_to_owner(back_first)
    grad_tokens = (
        norm_back(tokens.astype(f32), back_first, norm_gain[0]) + back_residual
    ).astype(bf16)
    own_grad_qkv = sum_over_dp(grad_qkv, 0)
    both_grads = from_heads(
        jnp.concatenate([own_grad_qkv, own_grad_sqkv], axis=0).astype(bf16)
    ).astype(f32)

    per_distance = distance[:, 1 : window + 1][:, ::-1]
    own_rel = jnp.dot(
        per_distance, lookup, precision=lax.Precision.HIGHEST, preferred_element_type=f32
    ).T
    grad_rel = lax.dynamic_update_slice_in_dim(
        jnp.zeros((bucket_count, head_count), f32), own_rel, here * heads, 1
    )
    small = [
        jnp.stack([first_sums[0], mid_sums[0], state_sums[0]]),
        jnp.stack([first_sums[1], mid_sums[1], state_sums[1]]),
        grad_gate[0],
        grad_rel,
    ]
    packed = sum_over_all(jnp.concatenate([v.reshape(-1, 128) for v in small], axis=0))
    unpacked, start = [], 0
    for v in small:
        count = v.size // 128
        unpacked.append(packed[start : start + count].reshape(v.shape))
        start += count
    return (
        output,
        next_state[None],
        grad_tokens,
        grad_state[None],
        both_grads[:depth],
        own_grad_out,
        both_grads[depth:],
        own_grad_sout,
        own_grad_up,
        own_grad_down,
        unpacked[3],
        unpacked[0],
        unpacked[1],
        unpacked[2],
    )


def solution(mesh):
    rows_spec = P(("dp", "state"), None)
    state_spec = P("dp", "state", None)
    weight_spec = P("dp", "state")
    return jax.shard_map(
        per_device,
        mesh=mesh,
        in_specs=(
            rows_spec,
            state_spec,
            rows_spec,
            state_spec,
            P("dp"),
            P(),
            weight_spec,
            weight_spec,
            weight_spec,
            weight_spec,
            weight_spec,
            P("state", "dp"),
            P(),
            P(),
            P(),
            P(),
        ),
        out_specs=(
            rows_spec,
            state_spec,
            rows_spec,
            state_spec,
            weight_spec,
            weight_spec,
            weight_spec,
            weight_spec,
            weight_spec,
            P("state", "dp"),
            P(),
            P(),
            P(),
            P(),
        ),
        check_vma=False,
    )
```
